32 devices in a mesh: ctx: 8 (over y, x, core), fsdp: 4 (over z).
Axes of the slice: x: 2, y: 2, z: 4, core: 2. Of those that a mesh axis runs over, the one named last changes fastest.
Arguments:
- tokens: bfloat16 [4, 1536, 2048], P('fsdp', 'ctx'), may hold values from -6 to 6
- lengths: int32 [4, 2], P('fsdp'), may hold values from 1 to 1535, as said below
- deal: int32 [4, 8, 8], P('fsdp'), may hold values from 0 to 7, each once within a row
- attn_gain: bfloat16 [2048], P('fsdp'), may hold values from 0.5 to 1.5
- query_weight: bfloat16 [2048, 2048], P('fsdp'), may hold values from -0.5 to 0.5
- key_matrix: bfloat16 [2048, 512], P('fsdp'), may hold values from -0.5 to 0.5
- value_matrix: bfloat16 [2048, 512], P('fsdp'), may hold values from -0.125 to 0.125
- out_weight: bfloat16 [2048, 2048], P('fsdp'), may hold values from -1.5 to 1.5
- mlp_gain: bfloat16 [2048], P('fsdp'), may hold values from 0.5 to 1.5
- gate_weight: bfloat16 [2048, 8192], P('fsdp'), may hold values from -0.125 to 0.125
- up_weight: bfloat16 [2048, 8192], P('fsdp'), may hold values from -0.125 to 0.125
- down_weight: bfloat16 [8192, 2048], P('fsdp'), may hold values from -0.25 to 0.25
- cotangent: bfloat16 [4, 1536, 2048], P('fsdp', 'ctx'), may hold values from -6 to 6
Outputs:
- activations: bfloat16 [4, 1536, 2048], P('fsdp', 'ctx')
- token_grad: float32 [4, 1536, 2048], P('fsdp', 'ctx')
- attn_gain_grad: float32 [2048], P('fsdp')
- query_grad: float32 [2048, 2048], P('fsdp')
- key_grad: float32 [2048, 512], P('fsdp')
- value_grad: float32 [2048, 512], P('fsdp')
- out_grad: float32 [2048, 2048], P('fsdp')
- mlp_gain_grad: float32 [2048], P('fsdp')
- gate_grad: float32 [2048, 8192], P('fsdp')
- up_grad: float32 [2048, 8192], P('fsdp')
- down_grad: float32 [8192, 2048], P('fsdp')
The draws below stay inside these ranges and needn't reach their ends.
Inputs may be any that keep to these rules, and one draw needn't show every extreme that they name: Each row holds the lengths of the two sequences of one group laid end to end; they sum to 1536 and the longer holds at least 1024 tokens. deal[f, i, k] is the device along ctx that holds, in dealt order, the k-th block of 24 tokens of ctx device i of group f; each row is a permutation.
All inputs are finite; a program needn't handle non-finite values.
Results may differ from the reference program's by a relative error of at most 0.024.
Values may be sent and summed in bfloat16 or wider, within the bound.
A program may use at most 576 MiB of HBM per device.

```python
import jax
import jax.numpy as jnp
from jax import lax

MODEL_WIDTH = 2048
QUERY_HEADS = 32
KEY_VALUE_HEADS = 8
HEAD_SIZE = 64
FF = 8192
TOK_DEV = 192
GROUPS = 4
GROUP_TOKENS = 1536
LONGEST = 1024
N_CTX = 8


def draw_lengths(key, part):
    key = jax.random.fold_in(key, 17)
    key_long, key_side, key_pick = jax.random.split(key, 3)
    longer = jax.random.randint(key_long, (GROUPS,), LONGEST, GROUP_TOKENS)
    chosen = jax.random.randint(key_pick, (), 0, GROUPS)
    longer = jnp.where(jnp.arange(GROUPS) == chosen, GROUP_TOKENS - 1, longer)
    side_pick = jax.random.randint(key_side, (GROUPS,), 0, 2)
    first_len = jnp.where(side_pick == 1, longer, GROUP_TOKENS - longer)
    return jnp.stack([first_len, GROUP_TOKENS - first_len], axis=1).astype(jnp.int32)


def shard_levels(key, shape, cuts, low, largest):
    factor_of = 1.0
    for dim, blocks in cuts:
        steps = jax.random.uniform(jax.random.fold_in(jax.random.fold_in(key, 6), dim), (blocks,), jnp.float32, low / len(cuts), largest / len(cuts))
        factor_of = factor_of * jnp.repeat(jnp.exp(steps), shape[dim] // blocks).reshape((-1,) + (1,) * (len(shape) - 1 - dim))
    return factor_of


def noise(key, extent, spread, bound, cuts=(), kind=jnp.bfloat16):
    loudness = shard_levels(key, extent, cuts, -0.22, 0.18) if cuts else 1.0
    entries = jax.random.normal(key, extent, jnp.float32) * spread * loudness
    return jnp.minimum(jnp.maximum(entries, -bound), bound).astype(kind)


def setup_inputs(seed: int = 0) -> dict:
    splits = jax.random.split(jax.random.key(seed), 14)
    tokens = noise(splits[0], (GROUPS, GROUP_TOKENS, MODEL_WIDTH), 1.0, 6.0, ((0, 4), (1, 8)))
    lengths = draw_lengths(jax.random.fold_in(splits[13], 71), 0)
    deal = jax.vmap(lambda own: jax.random.permutation(own, N_CTX))(jax.random.split(splits[2], GROUPS * N_CTX)).reshape((GROUPS, N_CTX, N_CTX)).astype(jnp.int32)
    attn_gain = jnp.clip(1.0 + 0.1 * jax.random.normal(splits[3], (MODEL_WIDTH,), jnp.float32), 0.5, 1.5).astype(jnp.bfloat16)
    query_weight = noise(splits[4], (MODEL_WIDTH, QUERY_HEADS * HEAD_SIZE), (MODEL_WIDTH // 16) ** -0.5, 0.5, ((0, 4),))
    key_matrix = noise(splits[5], (MODEL_WIDTH, KEY_VALUE_HEADS * HEAD_SIZE), (MODEL_WIDTH // 16) ** -0.5, 0.5, ((0, 4),))
    value_matrix = noise(splits[6], (MODEL_WIDTH, KEY_VALUE_HEADS * HEAD_SIZE), MODEL_WIDTH ** -0.5, 0.125, ((0, 4),))
    out_weight = noise(splits[7], (QUERY_HEADS * HEAD_SIZE, MODEL_WIDTH), 16 ** -0.5, 1.5, ((0, 4),))
    mlp_gain = jnp.clip(1.0 + 0.1 * jax.random.normal(splits[8], (MODEL_WIDTH,), jnp.float32), 0.5, 1.5).astype(jnp.bfloat16)
    gate_weight = noise(splits[9], (MODEL_WIDTH, FF), MODEL_WIDTH ** -0.5, 0.125, ((0, 4),))
    up_weight = noise(splits[10], (MODEL_WIDTH, FF), MODEL_WIDTH ** -0.5, 0.125, ((0, 4),))
    down_weight = noise(splits[11], (FF, MODEL_WIDTH), (FF // 16) ** -0.5, 0.25, ((0, 4),))
    cotangent = noise(splits[12], (GROUPS, GROUP_TOKENS, MODEL_WIDTH), 1.0, 6.0, ((0, 4), (1, 8)))
    return dict(tokens=tokens, lengths=lengths, deal=deal, attn_gain=attn_gain, query_weight=query_weight, key_matrix=key_matrix, value_matrix=value_matrix, out_weight=out_weight, mlp_gain=mlp_gain, gate_weight=gate_weight, up_weight=up_weight, down_weight=down_weight, cotangent=cotangent)


EPSILON = 1e-05
ROPE_BASE = 10000000.0
SCORE_SCALE = 0.015625
RESIDUAL_SCALE = 0.22
NEGATIVE_BIG = -1e+30
HIGHEST = lax.Precision.HIGHEST

@jax.custom_vjp
def low(v):
    return lax.optimization_barrier(v.astype(jnp.bfloat16)).astype(jnp.float32)

@jax.custom_vjp
def low_back(v):
    return v

def low_keep(v):
    return (low(v), None)

def low_pass(kept, grad):
    return (grad,)

def back_keep(v):
    return (v, None)

def back_low(kept, grad):
    return (low(grad),)
low.defvjp(low_keep, low_pass)
low_back.defvjp(back_keep, back_low)

def matrix_product(left_op, right_op):
    return jnp.dot(left_op, right_op, precision=HIGHEST, preferred_element_type=jnp.float32)

def rms_norm(rows_in, gain_row):
    scale_col = lax.rsqrt(lax.optimization_barrier(jnp.mean(rows_in * rows_in, axis=-1, keepdims=True)) + EPSILON)
    return rows_in * scale_col * gain_row

def rotary(positions):
    freq_index = jnp.arange(HEAD_SIZE // 2, dtype=jnp.float32)
    inverse = ROPE_BASE ** (-2.0 * freq_index / HEAD_SIZE)
    angles = positions.astype(jnp.float32)[:, None] * inverse[None, :]
    return (jnp.cos(angles)[:, None, :], jnp.sin(angles)[:, None, :])

def apply_rotary(heads_in, cosine_values, sine_values):
    first_half = heads_in[..., :HEAD_SIZE // 2]
    second_half = heads_in[..., HEAD_SIZE // 2:]
    return jnp.concatenate([first_half * cosine_values - second_half * sine_values, second_half * cosine_values + first_half * sine_values], axis=-1)

def given_table(deal_rows, n_ctx, tokens_per_device):
    block_rows = tokens_per_device // n_ctx
    slot_ids = jnp.arange(n_ctx, dtype=jnp.int32)
    matched = deal_rows[:, :, None] == slot_ids[None, None, :]
    source_slot = lax.optimization_barrier(jnp.sum(jnp.where(matched, slot_ids[None, :, None], 0), axis=1))
    first_block = slot_ids[:, None] * n_ctx + source_slot
    offsets = jnp.arange(block_rows, dtype=jnp.int32)
    table = first_block.T[:, :, None] * block_rows + offsets[None, None, :]
    return table.reshape(n_ctx, tokens_per_device).astype(jnp.int32)

def attend(query_rotated, key_rot, value_matrix_rows, segment):
    block_length = min(512, GROUP_TOKENS)
    count_of_blocks = GROUP_TOKENS // block_length
    key_index = jnp.arange(GROUP_TOKENS, dtype=jnp.int32)

    @jax.checkpoint
    def one_block(packed_tokens):
        query_block, segment_blk, index_blk = packed_tokens
        grouped_rows = query_block.reshape(block_length, KEY_VALUE_HEADS, QUERY_HEADS // KEY_VALUE_HEADS, HEAD_SIZE)
        scores = low_back(jnp.einsum('qgrd,kgd->grqk', grouped_rows, key_rot, precision=HIGHEST) * SCORE_SCALE)
        allowed = (segment_blk[:, None] == segment[None, :]) & (index_blk[:, None] >= key_index[None, :])
        prob_rows = low(jax.nn.softmax(jnp.where(allowed, scores, NEGATIVE_BIG), axis=-1))
        block_out = jnp.einsum('grqk,kgd->qgrd', prob_rows, value_matrix_rows, precision=HIGHEST)
        return block_out.reshape(block_length, QUERY_HEADS * HEAD_SIZE)
    block_outs = lax.map(one_block, (query_rotated.reshape(count_of_blocks, block_length, QUERY_HEADS, HEAD_SIZE), segment.reshape(count_of_blocks, block_length), key_index.reshape(count_of_blocks, block_length)))
    return block_outs.reshape(GROUP_TOKENS, QUERY_HEADS * HEAD_SIZE)

def layer_group(rows_per_group, segment, position, params):
    attn_gain, query_weight, key_matrix, value_matrix, out_weight, mlp_gain, gate_weight, up_weight, down_weight = params
    normalized_rows = low(rms_norm(rows_per_group, attn_gain))
    queries = low_back(matrix_product(normalized_rows, query_weight)).reshape(GROUP_TOKENS, QUERY_HEADS, HEAD_SIZE)
    keys_before_rotary = low_back(matrix_product(normalized_rows, key_matrix)).reshape(GROUP_TOKENS, KEY_VALUE_HEADS, HEAD_SIZE)
    value_matrix_rows = low(low_back(matrix_product(normalized_rows, value_matrix))).reshape(GROUP_TOKENS, KEY_VALUE_HEADS, HEAD_SIZE)
    cosine_values, sine_values = rotary(position)
    query_rotated = low(apply_rotary(queries, cosine_values, sine_values))
    key_rot = low(apply_rotary(keys_before_rotary, cosine_values, sine_values))
    attended = low(low_back(attend(query_rotated, key_rot, value_matrix_rows, segment)))
    hidden = rows_per_group + RESIDUAL_SCALE * low_back(matrix_product(attended, out_weight))
    normed2 = low(rms_norm(hidden, mlp_gain))
    gate_rows = low_back(matrix_product(normed2, gate_weight))
    up_rows = low_back(matrix_product(normed2, up_weight))
    mixed_rows = low(jax.nn.silu(gate_rows) * up_rows)
    return hidden + RESIDUAL_SCALE * low_back(matrix_product(mixed_rows, down_weight))

def reference(tokens, lengths, deal, attn_gain, query_weight, key_matrix, value_matrix, out_weight, mlp_gain, gate_weight, up_weight, down_weight, cotangent):
    given_pos = jnp.arange(GROUP_TOKENS, dtype=jnp.int32)
    first_len = lengths[:, 0:1].astype(jnp.int32)
    segment = (given_pos[None, :] >= first_len).astype(jnp.int32)
    position = (given_pos[None, :] - segment * first_len).astype(jnp.int32)
    dealt_index = jax.vmap(lambda deal_block: given_table(deal_block, N_CTX, TOK_DEV))(deal).reshape(GROUPS, GROUP_TOKENS)

    def forward(token_rows, gain_a, weight_q, weight_k, weight_v, weight_o, gain_m, weight_g, weight_u, weight_d):
        params = (gain_a, weight_q, weight_k, weight_v, weight_o, gain_m, weight_g, weight_u, weight_d)
        results = lax.map(lambda packed_tokens: layer_group(packed_tokens[0], packed_tokens[1], packed_tokens[2], params), (token_rows, segment, position))
        return jnp.take_along_axis(results, dealt_index[:, :, None], axis=1)
    outputs, pullback = jax.vjp(forward, tokens.astype(jnp.float32), attn_gain.astype(jnp.float32), query_weight.astype(jnp.float32), key_matrix.astype(jnp.float32), value_matrix.astype(jnp.float32), out_weight.astype(jnp.float32), mlp_gain.astype(jnp.float32), gate_weight.astype(jnp.float32), up_weight.astype(jnp.float32), down_weight.astype(jnp.float32))
    grads = pullback(cotangent.astype(jnp.float32))
    return (outputs.astype(jnp.bfloat16), grads[0], grads[1], grads[2], grads[3], grads[4], grads[5], grads[6], grads[7], grads[8], grads[9])
```

```python
import jax
import jax.numpy as jnp
from jax import lax
from jax.experimental import pallas as pl
from jax.experimental.pallas import tpu as pltpu
from jax.sharding import PartitionSpec as P

QUERY_HEADS = 32
KEY_VALUE_HEADS = 8
HEAD_SIZE = 64
EPSILON = 1e-05
ROPE_BASE = 10000000.0
SCORE_SCALE = 0.015625
RESIDUAL_SCALE = 0.22
NEGATIVE_BIG = -1e30
LANES = 128
ROWS = 256
BF16 = jnp.bfloat16
F32 = jnp.float32
VMEM_LIMIT = 56 * 1024 * 1024


def dot_nn(a, b):
    return lax.dot_general(a, b, (((1,), (0,)), ((), ())), preferred_element_type=F32)


def dot_nt(a, b):
    return lax.dot_general(a, b, (((1,), (1,)), ((), ())), preferred_element_type=F32)


def dot_tn(a, b):
    return lax.dot_general(a, b, (((0,), (0,)), ((), ())), preferred_element_type=F32)


def swap_halves(x):
    lane = lax.broadcasted_iota(jnp.int32, x.shape, 1)
    first = lax.rem(lane, HEAD_SIZE) < HEAD_SIZE // 2
    return jnp.where(first, pltpu.roll(x, LANES - HEAD_SIZE // 2, 1), pltpu.roll(x, HEAD_SIZE // 2, 1))


def low_half(shape):
    return lax.broadcasted_iota(jnp.int32, shape, 1) < HEAD_SIZE


def mask_bias(first_len, row0, rows, cols):
    query = row0 + lax.broadcasted_iota(jnp.int32, (rows, cols), 0)
    key = lax.broadcasted_iota(jnp.int32, (rows, cols), 1)
    start = jnp.where(query >= first_len, first_len, 0)
    return jnp.where((key <= query) & (key >= start), 0.0, NEGATIVE_BIG)


def attention_forward_kernel(length_ref, q_ref, kv_ref, cos_ref, sin_ref, out_ref, q_out, k_out, v_out, lse_ref):
    pair = pl.program_id(0)
    tokens = q_ref.shape[0]
    cos, sin = cos_ref[...], sin_ref[...]

    @pl.when(pair == 0)
    def _():
        kv = kv_ref[...]
        turned = pltpu.roll(kv, HEAD_SIZE, 1)
        low = low_half(kv.shape)
        k = jnp.where(low, kv, turned)
        k_out[...] = (k * cos + swap_halves(k) * sin).astype(BF16)
        v_out[...] = jnp.where(low, turned, kv).astype(BF16)

    q = q_ref[...]
    q_out[...] = ((q * cos + swap_halves(q) * sin) * SCORE_SCALE).astype(BF16)
    first_len = length_ref[0]
    for block in range(tokens // ROWS):
        rows = pl.ds(block * ROWS, ROWS)
        end = (block + 1) * ROWS
        bias = mask_bias(first_len, block * ROWS, ROWS, end)
        query = q_out[rows, :]
        low = low_half(query.shape)
        keys, values = k_out[:end, :], v_out[:end, :]
        parts = []
        for half in range(2):
            chosen = low if half == 0 else jnp.logical_not(low)
            scores = dot_nt(jnp.where(chosen, query, jnp.zeros_like(query)), keys) + bias
            top = jnp.max(scores, axis=-1, keepdims=True)
            weights = jnp.exp(scores - top)
            total = jnp.sum(weights, axis=-1, keepdims=True)
            probs = (weights * (1.0 / total)).astype(BF16)
            parts.append(dot_nn(probs, values))
            lse_ref[0, rows, half : half + 1] = top + jnp.log(total)
        out_ref[rows, :] = jnp.where(low_half(parts[0].shape), parts[0], parts[1]).astype(BF16)


def attention_forward(qkv, cos, sin, lengths, heads):
    tokens = qkv.shape[0]
    pairs = heads // 2
    return pl.pallas_call(
        attention_forward_kernel,
        grid=(pairs,),
        in_specs=[
            pl.BlockSpec(memory_space=pltpu.SMEM),
            pl.BlockSpec((tokens, LANES), lambda j: (0, j)),
            pl.BlockSpec((tokens, LANES), lambda j: (0, pairs)),
            pl.BlockSpec((tokens, LANES), lambda j: (0, 0)),
            pl.BlockSpec((tokens, LANES), lambda j: (0, 0)),
        ],
        out_specs=[
            pl.BlockSpec((tokens, LANES), lambda j: (0, j)),
            pl.BlockSpec((tokens, LANES), lambda j: (0, j)),
            pl.BlockSpec((tokens, LANES), lambda j: (0, 0)),
            pl.BlockSpec((tokens, LANES), lambda j: (0, 0)),
            pl.BlockSpec((1, tokens, LANES), lambda j: (j, 0, 0)),
        ],
        out_shape=[
            jax.ShapeDtypeStruct((tokens, pairs * LANES), BF16),
            jax.ShapeDtypeStruct((tokens, pairs * LANES), BF16),
            jax.ShapeDtypeStruct((tokens, LANES), BF16),
            jax.ShapeDtypeStruct((tokens, LANES), BF16),
            jax.ShapeDtypeStruct((pairs, tokens, LANES), F32),
        ],
        compiler_params=pltpu.CompilerParams(vmem_limit_bytes=VMEM_LIMIT),
        cost_estimate=pl.CostEstimate(
            flops=4 * tokens * tokens * LANES * heads // 2,
            bytes_accessed=12 * tokens * pairs * LANES,
            transcendentals=tokens * tokens * heads // 2,
        ),
        name="attend",
    )(lengths, qkv, qkv, cos, sin)


def attention_backward_kernel(length_ref, g_ref, q_ref, k_ref, v_ref, lse_ref, cos_ref, sin_ref, dq_ref, dkv_ref, dk_sum, dv_sum):
    pair = pl.program_id(0)
    tokens = q_ref.shape[0]

    @pl.when(pair == 0)
    def _():
        dk_sum[...] = jnp.zeros_like(dk_sum)
        dv_sum[...] = jnp.zeros_like(dv_sum)

    first_len = length_ref[0]
    for block in range(tokens // ROWS):
        rows = pl.ds(block * ROWS, ROWS)
        end = (block + 1) * ROWS
        bias = mask_bias(first_len, block * ROWS, ROWS, end)
        query, grad = q_ref[rows, :], g_ref[rows, :]
        low = low_half(query.shape)
        keys, values = k_ref[:end, :], v_ref[:end, :]
        parts = []
        for half in range(2):
            chosen = low if half == 0 else jnp.logical_not(low)
            own_query = jnp.where(chosen, query, jnp.zeros_like(query))
            own_grad = jnp.where(chosen, grad, jnp.zeros_like(grad))
            scores = dot_nt(own_query, keys) + bias
            probs = jnp.exp(scores - lse_ref[0, rows, half : half + 1])
            prob_grad = dot_nt(own_grad, values)
            delta = jnp.sum(probs * prob_grad, axis=-1, keepdims=True)
            score_grad = (probs * (prob_grad - delta)).astype(BF16)
            parts.append(dot_nn(score_grad, keys))
            dk_sum[:end, :] += dot_tn(score_grad, own_query)
            dv_sum[:end, :] += dot_tn(probs.astype(BF16), own_grad)
        dq = jnp.where(low_half(parts[0].shape), parts[0], parts[1]) * SCORE_SCALE
        dq_ref[rows, :] = (dq * cos_ref[rows, :] - swap_halves(dq) * sin_ref[rows, :]).astype(BF16)

    @pl.when(pair == pl.num_programs(0) - 1)
    def _():
        dk = dk_sum[...]
        dk = dk + pltpu.roll(dk, HEAD_SIZE, 1)
        dk = dk * cos_ref[...] - swap_halves(dk) * sin_ref[...]
        dv = dv_sum[...]
        dv = dv + pltpu.roll(dv, HEAD_SIZE, 1)
        dkv_ref[...] = jnp.where(low_half(dk.shape), dk, dv).astype(BF16)


def attention_backward(grads, q_rot, k_rot, v_rows, lse, cos, sin, lengths):
    tokens = q_rot.shape[0]
    pairs = q_rot.shape[1] // LANES
    one = pl.BlockSpec((tokens, LANES), lambda j: (0, 0))
    each = pl.BlockSpec((tokens, LANES), lambda j: (0, j))
    return pl.pallas_call(
        attention_backward_kernel,
        grid=(pairs,),
        in_specs=[
            pl.BlockSpec(memory_space=pltpu.SMEM),
            each,
            each,
            one,
            one,
            pl.BlockSpec((1, tokens, LANES), lambda j: (j, 0, 0)),
            one,
            one,
        ],
        out_specs=[each, one],
        out_shape=[
            jax.ShapeDtypeStruct((tokens, pairs * LANES), BF16),
            jax.ShapeDtypeStruct((tokens, LANES), BF16),
        ],
        scratch_shapes=[pltpu.VMEM((tokens, LANES), F32), pltpu.VMEM((tokens, LANES), F32)],
        compiler_params=pltpu.CompilerParams(vmem_limit_bytes=VMEM_LIMIT),
        cost_estimate=pl.CostEstimate(
            flops=10 * tokens * tokens * LANES * pairs,
            bytes_accessed=12 * tokens * pairs * LANES,
            transcendentals=tokens * tokens * pairs,
        ),
        name="attend_back",
    )(lengths, grads, q_rot, k_rot, v_rows, lse, cos, sin)


def own_columns(array, index, width):
    return lax.dynamic_slice_in_dim(array, index * width, width, axis=1)


def local(
    tokens,
    lengths,
    deal,
    attn_gain,
    query_weight,
    key_matrix,
    value_matrix,
    out_weight,
    mlp_gain,
    gate_weight,
    up_weight,
    down_weight,
    cotangent,
):
    n_ctx = lax.axis_size("ctx")
    n_fsdp = lax.axis_size("fsdp")
    me = lax.axis_index("ctx")
    plane = lax.axis_index("fsdp")
    per_device, width = tokens.shape[1], tokens.shape[2]
    total = per_device * n_ctx
    block_rows = per_device // n_ctx
    heads = QUERY_HEADS // n_ctx
    sharing = n_ctx // KEY_VALUE_HEADS
    own_width = width // n_ctx
    ff = gate_weight.shape[1]
    slab = ff // (n_fsdp * n_ctx)
    own_ff = slab * n_fsdp
    rows_shard = query_weight.shape[0]

    kv_head = me // sharing
    qkv_shard = jnp.concatenate(
        [
            own_columns(query_weight, me, heads * HEAD_SIZE),
            own_columns(key_matrix, kv_head, HEAD_SIZE),
            own_columns(value_matrix, kv_head, HEAD_SIZE),
        ],
        axis=1,
    )
    w_qkv = lax.all_gather(qkv_shard, "fsdp", axis=0, tiled=True)
    gains = lax.all_gather(jnp.stack([attn_gain, mlp_gain]), "fsdp", axis=1, tiled=True).astype(F32)
    w_out = lax.all_gather(own_columns(out_weight, me, own_width), "fsdp", axis=0, tiled=True)

    def ff_columns(array):
        picked = lax.dynamic_index_in_dim(
            array.reshape(rows_shard, n_fsdp, n_ctx, slab), me, 2, keepdims=False
        )
        return picked.reshape(rows_shard, own_ff)

    w_gate = lax.all_gather(ff_columns(gate_weight), "fsdp", axis=0, tiled=True)
    w_up = lax.all_gather(ff_columns(up_weight), "fsdp", axis=0, tiled=True)
    w_down = lax.all_gather(
        lax.dynamic_slice_in_dim(down_weight, me * slab, slab, axis=0), "fsdp", axis=0, tiled=True
    )

    first_len = lengths[0, 0]
    given = jnp.arange(total, dtype=jnp.int32)
    position = given - jnp.where(given >= first_len, first_len, 0)
    freq_index = jnp.arange(HEAD_SIZE // 2, dtype=F32)
    inverse = ROPE_BASE ** (-2.0 * freq_index / HEAD_SIZE)
    angles = position.astype(F32)[:, None] * inverse[None, :]
    cos, sin = jnp.cos(angles), jnp.sin(angles)
    cos_table = jnp.concatenate([cos, cos, cos, cos], axis=1)
    sin_table = jnp.concatenate([-sin, sin, -sin, sin], axis=1)

    deal_rows = deal[0]
    slot_ids = jnp.arange(n_ctx, dtype=jnp.int32)
    dealt_of_given = (deal_rows * n_ctx + slot_ids[:, None]).reshape(-1)
    matched = deal_rows[:, :, None] == slot_ids[None, None, :]
    source_slot = jnp.sum(jnp.where(matched, slot_ids[None, :, None], 0), axis=1)
    given_of_dealt = (slot_ids[:, None] * n_ctx + source_slot).T.reshape(-1)

    def reorder(array, table):
        blocks = array.reshape(n_ctx * n_ctx, block_rows, array.shape[1])
        return jnp.take(blocks, table, axis=0).reshape(array.shape)

    x = lax.all_gather(tokens[0], "ctx", axis=0, tiled=True).astype(F32)
    grad_result = reorder(lax.all_gather(cotangent[0], "ctx", axis=0, tiled=True), dealt_of_given)
    r1 = lax.rsqrt(jnp.mean(x * x, axis=-1, keepdims=True) + EPSILON)
    normed = (x * r1 * gains[0]).astype(BF16)
    qkv = dot_nn(normed, w_qkv)
    attended, q_rot, k_rot, v_rows, lse = attention_forward(qkv, cos_table, sin_table, lengths[0], heads)
    attended_all = lax.all_gather(attended, "ctx", axis=1, tiled=True)
    hidden_own = own_columns(x, me, own_width) + RESIDUAL_SCALE * dot_nn(attended_all, w_out)
    hidden = lax.all_gather(hidden_own.astype(BF16), "ctx", axis=1, tiled=True).astype(F32)
    r2 = lax.rsqrt(jnp.mean(hidden * hidden, axis=-1, keepdims=True) + EPSILON)
    normed2 = (hidden * r2 * gains[1]).astype(BF16)
    gate = dot_nn(normed2, w_gate)
    up = dot_nn(normed2, w_up)
    sig = jax.nn.sigmoid(gate)
    mixed = (gate * sig * up).astype(BF16)

    mlp_grad = (RESIDUAL_SCALE * grad_result.astype(F32)).astype(BF16)

    def settle(left, right):
        return lax.psum_scatter(dot_tn(left, right).astype(BF16), "fsdp", scatter_dimension=0, tiled=True)

    down_part = settle(mixed, mlp_grad)
    mixed_grad = dot_nt(mlp_grad, w_down)
    gate_rows_grad = (mixed_grad * up * sig * (1.0 + gate * (1.0 - sig))).astype(BF16)
    up_rows_grad = (mixed_grad * gate * sig).astype(BF16)
    gate_part = settle(normed2, gate_rows_grad)
    up_part = settle(normed2, up_rows_grad)
    normed2_grad = dot_nt(gate_rows_grad, w_gate) + dot_nt(up_rows_grad, w_up)
    weighted2 = normed2_grad * gains[1]
    mlp_gain_part = jnp.sum(normed2_grad * hidden * r2, axis=0)
    hidden_part = r2 * weighted2 - hidden * r2**3 * jnp.mean(weighted2 * hidden, axis=-1, keepdims=True)
    hidden_grad = lax.psum_scatter(
        hidden_part.astype(BF16), "ctx", scatter_dimension=1, tiled=True
    ).astype(F32) + own_columns(grad_result, me, own_width).astype(F32)
    branch_grad = (RESIDUAL_SCALE * hidden_grad).astype(BF16)
    out_part = settle(attended_all, branch_grad)
    attended_grad = lax.psum_scatter(
        dot_nt(branch_grad, w_out).astype(BF16), "ctx", scatter_dimension=1, tiled=True
    )
    dq, dkv = attention_backward(attended_grad, q_rot, k_rot, v_rows, lse, cos_table, sin_table, lengths[0])
    dqkv = jnp.concatenate([dq, dkv], axis=1)
    qkv_part = settle(normed, dqkv)
    normed_grad = dot_nt(dqkv, w_qkv)
    weighted1 = normed_grad * gains[0]
    attn_gain_part = jnp.sum(normed_grad * x * r1, axis=0)
    token_part = r1 * weighted1 - x * r1**3 * jnp.mean(weighted1 * x, axis=-1, keepdims=True)
    spread = jnp.zeros((total, width), F32)
    spread = lax.dynamic_update_slice_in_dim(spread, hidden_grad, me * own_width, axis=1)
    token_grad = lax.psum_scatter(
        (token_part + spread).astype(BF16), "ctx", scatter_dimension=0, tiled=True
    ).astype(F32)[None]

    mixed_dealt = reorder(mixed, given_of_dealt)
    hidden_spread = jnp.zeros((total, width), F32)
    hidden_spread = lax.dynamic_update_slice_in_dim(
        hidden_spread, reorder(hidden_own, given_of_dealt), me * own_width, axis=1
    )
    result_part = hidden_spread + RESIDUAL_SCALE * dot_nn(mixed_dealt, w_down)
    activations = lax.psum_scatter(result_part.astype(BF16), "ctx", scatter_dimension=0, tiled=True)[None]

    def whole(part):
        return lax.all_gather(part, "ctx", axis=0, tiled=False)

    qkv_all = whole(qkv_part).astype(F32)
    split = heads * HEAD_SIZE
    query_grad = qkv_all[:, :, :split].transpose(1, 0, 2).reshape(rows_shard, width)

    def shared_heads(pieces):
        pieces = pieces.reshape(KEY_VALUE_HEADS, sharing, rows_shard, HEAD_SIZE).sum(axis=1)
        return pieces.transpose(1, 0, 2).reshape(rows_shard, KEY_VALUE_HEADS * HEAD_SIZE)

    key_grad = shared_heads(qkv_all[:, :, split : split + HEAD_SIZE])
    value_grad = shared_heads(qkv_all[:, :, split + HEAD_SIZE :])
    out_grad = whole(out_part).transpose(1, 0, 2).reshape(rows_shard, width).astype(F32)

    def ff_whole(part):
        pieces = whole(part).reshape(n_ctx, rows_shard, n_fsdp, slab)
        return pieces.transpose(1, 2, 0, 3).reshape(rows_shard, ff).astype(F32)

    gate_grad = ff_whole(gate_part)
    up_grad = ff_whole(up_part)
    down_grad = whole(down_part).reshape(n_ctx * slab, width).astype(F32)
    gain_totals = lax.psum(jnp.stack([attn_gain_part, mlp_gain_part]), ("ctx", "fsdp"))
    own_gains = lax.dynamic_slice_in_dim(gain_totals, plane * rows_shard, rows_shard, axis=1)
    return (
        activations,
        token_grad,
        own_gains[0],
        query_grad,
        key_grad,
        value_grad,
        out_grad,
        own_gains[1],
        gate_grad,
        up_grad,
        down_grad,
    )


def solution(mesh):
    rows = P("fsdp", None)
    block = P("fsdp", "ctx", None)
    gain = P("fsdp")
    return jax.shard_map(
        local,
        mesh=mesh,
        in_specs=(block, rows, P("fsdp", None, None), gain, rows, rows, rows, rows, gain, rows, rows, rows, block),
        out_specs=(block, block, gain, rows, rows, rows, rows, gain, rows, rows, rows),
        check_vma=False,
    )
```

```python
import jax
import jax.numpy as jnp
from jax import lax
from jax.experimental import pallas as pl
from jax.experimental.pallas import tpu as pltpu
from jax.sharding import PartitionSpec as P

QUERY_HEADS = 32
KEY_VALUE_HEADS = 8
HEAD_SIZE = 64
EPSILON = 1e-05
ROPE_BASE = 10000000.0
SCORE_SCALE = 0.015625
RESIDUAL_SCALE = 0.22
NEGATIVE_BIG = -1e30
LANES = 128
ROWS = 256
BF16 = jnp.bfloat16
F32 = jnp.float32
VMEM_LIMIT = 56 * 1024 * 1024


def dot_nn(a, b):
    return lax.dot_general(a, b, (((1,), (0,)), ((), ())), preferred_element_type=F32)


def dot_nt(a, b):
    return lax.dot_general(a, b, (((1,), (1,)), ((), ())), preferred_element_type=F32)


def dot_tn(a, b):
    return lax.dot_general(a, b, (((0,), (0,)), ((), ())), preferred_element_type=F32)


def swap_halves(x):
    lane = lax.broadcasted_iota(jnp.int32, x.shape, 1)
    first = lax.rem(lane, HEAD_SIZE) < HEAD_SIZE // 2
    return jnp.where(first, pltpu.roll(x, LANES - HEAD_SIZE // 2, 1), pltpu.roll(x, HEAD_SIZE // 2, 1))


def low_half(shape):
    return lax.broadcasted_iota(jnp.int32, shape, 1) < HEAD_SIZE


def mask_bias(first_len, row0, rows, cols):
    query = row0 + lax.broadcasted_iota(jnp.int32, (rows, cols), 0)
    key = lax.broadcasted_iota(jnp.int32, (rows, cols), 1)
    start = jnp.where(query >= first_len, first_len, 0)
    return jnp.where((key <= query) & (key >= start), 0.0, NEGATIVE_BIG)


def attention_forward_kernel(length_ref, q_ref, kv_ref, cos_ref, sin_ref, out_ref, q_out, k_out, v_out, lse_ref):
    pair = pl.program_id(0)
    tokens = q_ref.shape[0]
    cos, sin = cos_ref[...], sin_ref[...]

    @pl.when(pair == 0)
    def _():
        kv = kv_ref[...]
        turned = pltpu.roll(kv, HEAD_SIZE, 1)
        low = low_half(kv.shape)
        k = jnp.where(low, kv, turned)
        k_out[...] = (k * cos + swap_halves(k) * sin).astype(BF16)
        v_out[...] = jnp.where(low, turned, kv).astype(BF16)

    q = q_ref[...]
    q_out[...] = ((q * cos + swap_halves(q) * sin) * SCORE_SCALE).astype(BF16)
    first_len = length_ref[0]
    for block in range(tokens // ROWS):
        rows = pl.ds(block * ROWS, ROWS)
        end = (block + 1) * ROWS
        bias = mask_bias(first_len, block * ROWS, ROWS, end)
        query = q_out[rows, :]
        low = low_half(query.shape)
        keys, values = k_out[:end, :], v_out[:end, :]
        parts = []
        for half in range(2):
            chosen = low if half == 0 else jnp.logical_not(low)
            scores = dot_nt(jnp.where(chosen, query, jnp.zeros_like(query)), keys) + bias
            top = jnp.max(scores, axis=-1, keepdims=True)
            weights = jnp.exp(scores - top)
            total = jnp.sum(weights, axis=-1, keepdims=True)
            probs = (weights * (1.0 / total)).astype(BF16)
            parts.append(dot_nn(probs, values))
            lse_ref[0, rows, half : half + 1] = top + jnp.log(total)
        out_ref[rows, :] = jnp.where(low_half(parts[0].shape), parts[0], parts[1]).astype(BF16)


def attention_forward(qkv, cos, sin, lengths, heads):
    tokens = qkv.shape[0]
    pairs = heads // 2
    return pl.pallas_call(
        attention_forward_kernel,
        grid=(pairs,),
        in_specs=[
            pl.BlockSpec(memory_space=pltpu.SMEM),
            pl.BlockSpec((tokens, LANES), lambda j: (0, j)),
            pl.BlockSpec((tokens, LANES), lambda j: (0, pairs)),
            pl.BlockSpec((tokens, LANES), lambda j: (0, 0)),
            pl.BlockSpec((tokens, LANES), lambda j: (0, 0)),
        ],
        out_specs=[
            pl.BlockSpec((tokens, LANES), lambda j: (0, j)),
            pl.BlockSpec((tokens, LANES), lambda j: (0, j)),
            pl.BlockSpec((tokens, LANES), lambda j: (0, 0)),
            pl.BlockSpec((tokens, LANES), lambda j: (0, 0)),
            pl.BlockSpec((1, tokens, LANES), lambda j: (j, 0, 0)),
        ],
        out_shape=[
            jax.ShapeDtypeStruct((tokens, pairs * LANES), BF16),
            jax.ShapeDtypeStruct((tokens, pairs * LANES), BF16),
            jax.ShapeDtypeStruct((tokens, LANES), BF16),
            jax.ShapeDtypeStruct((tokens, LANES), BF16),
            jax.ShapeDtypeStruct((pairs, tokens, LANES), F32),
        ],
        compiler_params=pltpu.CompilerParams(vmem_limit_bytes=VMEM_LIMIT),
        cost_estimate=pl.CostEstimate(
            flops=4 * tokens * tokens * LANES * heads // 2,
            bytes_accessed=12 * tokens * pairs * LANES,
            transcendentals=tokens * tokens * heads // 2,
        ),
        name="attend",
    )(lengths, qkv, qkv, cos, sin)


def attention_backward_kernel(length_ref, g_ref, q_ref, k_ref, v_ref, lse_ref, cos_ref, sin_ref, dq_ref, dkv_ref, dk_sum, dv_sum):
    pair = pl.program_id(0)
    tokens = q_ref.shape[0]

    @pl.when(pair == 0)
    def _():
        dk_sum[...] = jnp.zeros_like(dk_sum)
        dv_sum[...] = jnp.zeros_like(dv_sum)

    first_len = length_ref[0]
    for block in range(tokens // ROWS):
        rows = pl.ds(block * ROWS, ROWS)
        end = (block + 1) * ROWS
        bias = mask_bias(first_len, block * ROWS, ROWS, end)
        query, grad = q_ref[rows, :], g_ref[rows, :]
        low = low_half(query.shape)
        keys, values = k_ref[:end, :], v_ref[:end, :]
        parts = []
        for half in range(2):
            chosen = low if half == 0 else jnp.logical_not(low)
            own_query = jnp.where(chosen, query, jnp.zeros_like(query))
            own_grad = jnp.where(chosen, grad, jnp.zeros_like(grad))
            scores = dot_nt(own_query, keys) + bias
            probs = jnp.exp(scores - lse_ref[0, rows, half : half + 1])
            prob_grad = dot_nt(own_grad, values)
            delta = jnp.sum(probs * prob_grad, axis=-1, keepdims=True)
            score_grad = (probs * (prob_grad - delta)).astype(BF16)
            parts.append(dot_nn(score_grad, keys))
            dk_sum[:end, :] += dot_tn(score_grad, own_query)
            dv_sum[:end, :] += dot_tn(probs.astype(BF16), own_grad)
        dq = jnp.where(low_half(parts[0].shape), parts[0], parts[1]) * SCORE_SCALE
        dq_ref[rows, :] = (dq * cos_ref[rows, :] - swap_halves(dq) * sin_ref[rows, :]).astype(BF16)

    @pl.when(pair == pl.num_programs(0) - 1)
    def _():
        dk = dk_sum[...]
        dk = dk + pltpu.roll(dk, HEAD_SIZE, 1)
        dk = dk * cos_ref[...] - swap_halves(dk) * sin_ref[...]
        dv = dv_sum[...]
        dv = dv + pltpu.roll(dv, HEAD_SIZE, 1)
        dkv_ref[...] = jnp.where(low_half(dk.shape), dk, dv).astype(BF16)


def attention_backward(grads, q_rot, k_rot, v_rows, lse, cos, sin, lengths):
    tokens = q_rot.shape[0]
    pairs = q_rot.shape[1] // LANES
    one = pl.BlockSpec((tokens, LANES), lambda j: (0, 0))
    each = pl.BlockSpec((tokens, LANES), lambda j: (0, j))
    return pl.pallas_call(
        attention_backward_kernel,
        grid=(pairs,),
        in_specs=[
            pl.BlockSpec(memory_space=pltpu.SMEM),
            each,
            each,
            one,
            one,
            pl.BlockSpec((1, tokens, LANES), lambda j: (j, 0, 0)),
            one,
            one,
        ],
        out_specs=[each, one],
        out_shape=[
            jax.ShapeDtypeStruct((tokens, pairs * LANES), BF16),
            jax.ShapeDtypeStruct((tokens, LANES), BF16),
        ],
        scratch_shapes=[pltpu.VMEM((tokens, LANES), F32), pltpu.VMEM((tokens, LANES), F32)],
        compiler_params=pltpu.CompilerParams(vmem_limit_bytes=VMEM_LIMIT),
        cost_estimate=pl.CostEstimate(
            flops=10 * tokens * tokens * LANES * pairs,
            bytes_accessed=12 * tokens * pairs * LANES,
            transcendentals=tokens * tokens * pairs,
        ),
        name="attend_back",
    )(lengths, grads, q_rot, k_rot, v_rows, lse, cos, sin)


def row_block(width):
    return pl.BlockSpec((ROWS, width), lambda i: (i, 0))


def fixed(*shape):
    return pl.BlockSpec(shape, lambda i: (0,) * len(shape))


def params():
    return pltpu.CompilerParams(vmem_limit_bytes=VMEM_LIMIT)


def cost(flops, *arrays):
    moved = sum(a.size * a.dtype.itemsize for a in arrays)
    return pl.CostEstimate(flops=flops, bytes_accessed=moved, transcendentals=0)


def project_kernel(x_ref, gain_ref, w_ref, normed_ref, qkv_ref):
    x = x_ref[...].astype(F32)
    r1 = lax.rsqrt(jnp.mean(x * x, axis=-1, keepdims=True) + EPSILON)
    normed = (x * r1 * gain_ref[...]).astype(BF16)
    normed_ref[...] = normed
    qkv_ref[...] = dot_nn(normed, w_ref[...])


def project(x, gain, w_qkv):
    total, width = x.shape
    columns = w_qkv.shape[1]
    out_shape = [jax.ShapeDtypeStruct((total, width), BF16), jax.ShapeDtypeStruct((total, columns), F32)]
    return pl.pallas_call(
        project_kernel,
        grid=(total // ROWS,),
        in_specs=[row_block(width), fixed(1, width), fixed(width, columns)],
        out_specs=[row_block(width), row_block(columns)],
        out_shape=out_shape,
        compiler_params=params(),
        cost_estimate=cost(2 * total * width * columns, x, w_qkv, *out_shape),
        name="project",
    )(x, gain, w_qkv)


def out_kernel(me_ref, x_ref, att_ref, w_ref, hidden_ref):
    own_width = hidden_ref.shape[1]
    acc = jnp.zeros(hidden_ref.shape, F32)
    for c in range(att_ref.shape[0]):
        acc += dot_nn(att_ref[c], w_ref[c])
    start = pl.multiple_of(me_ref[0] * own_width, LANES)
    x = x_ref[:, pl.ds(start, own_width)].astype(F32)
    hidden_ref[...] = (x + RESIDUAL_SCALE * acc).astype(BF16)


def out_projection(me, x, att_all, w_out):
    n, total, own = att_all.shape
    width = x.shape[1]
    own_width = w_out.shape[1]
    w_heads = w_out.reshape(n, own, own_width)
    out_shape = jax.ShapeDtypeStruct((total, own_width), BF16)
    return pl.pallas_call(
        out_kernel,
        grid=(total // ROWS,),
        in_specs=[
            pl.BlockSpec(memory_space=pltpu.SMEM),
            row_block(width),
            pl.BlockSpec((n, ROWS, own), lambda i: (0, i, 0)),
            fixed(n, own, own_width),
        ],
        out_specs=row_block(own_width),
        out_shape=out_shape,
        compiler_params=params(),
        cost_estimate=cost(2 * total * width * own_width, x, att_all, w_out, out_shape),
        name="out_projection",
    )(me, x, att_all, w_heads)


def join(ref):
    return jnp.concatenate([ref[c].astype(F32) for c in range(ref.shape[0])], axis=1)


def mlp_kernel(hidden_ref, gain_ref, gate_ref, up_ref, normed_ref, a_ref, b_ref, mixed_ref):
    hidden = join(hidden_ref)
    r2 = lax.rsqrt(jnp.mean(hidden * hidden, axis=-1, keepdims=True) + EPSILON)
    normed = (hidden * r2 * gain_ref[...]).astype(BF16)
    normed_ref[...] = normed
    gate = dot_nn(normed, gate_ref[...])
    up = dot_nn(normed, up_ref[...])
    sig = jax.nn.sigmoid(gate)
    silu = gate * sig
    mixed_ref[...] = (silu * up).astype(BF16)
    b_ref[...] = silu.astype(BF16)
    a_ref[...] = (up * sig * (1.0 + gate * (1.0 - sig))).astype(BF16)


def mlp_forward(hidden_all, gain, w_gate, w_up):
    n, total, own = hidden_all.shape
    width, own_ff = w_gate.shape
    wide = jax.ShapeDtypeStruct((total, width), BF16)
    narrow = jax.ShapeDtypeStruct((total, own_ff), BF16)
    return pl.pallas_call(
        mlp_kernel,
        grid=(total // ROWS,),
        in_specs=[
            pl.BlockSpec((n, ROWS, own), lambda i: (0, i, 0)),
            fixed(1, width),
            fixed(width, own_ff),
            fixed(width, own_ff),
        ],
        out_specs=[row_block(width), row_block(own_ff), row_block(own_ff), row_block(own_ff)],
        out_shape=[wide, narrow, narrow, narrow],
        compiler_params=params(),
        cost_estimate=cost(4 * total * width * own_ff, hidden_all, w_gate, w_up, wide, narrow, narrow, narrow),
        name="mlp_forward",
    )(hidden_all, gain, w_gate, w_up)


def mlp_back_kernel(
    grad_ref, a_ref, b_ref, hidden_ref, gain_ref, gate_ref, up_ref, down_ref, ggrad_ref, ugrad_ref, part_ref, gain_out
):
    mixed_grad = dot_nt(grad_ref[...], down_ref[...])
    ggrad = (mixed_grad * a_ref[...].astype(F32)).astype(BF16)
    ugrad = (mixed_grad * b_ref[...].astype(F32)).astype(BF16)
    ggrad_ref[...] = ggrad
    ugrad_ref[...] = ugrad
    normed_grad = dot_nt(ggrad, gate_ref[...]) + dot_nt(ugrad, up_ref[...])
    hidden = join(hidden_ref)
    r2 = lax.rsqrt(jnp.mean(hidden * hidden, axis=-1, keepdims=True) + EPSILON)
    gain_part = jnp.sum(normed_grad * (hidden * r2), axis=0, keepdims=True)

    @pl.when(pl.program_id(0) == 0)
    def _():
        gain_out[...] = jnp.zeros_like(gain_out)

    gain_out[...] += gain_part
    weighted = normed_grad * gain_ref[...]
    mean = jnp.mean(weighted * hidden, axis=-1, keepdims=True)
    part = r2 * weighted - hidden * (r2 * r2 * r2 * mean)
    own = part_ref.shape[2]
    for c in range(part_ref.shape[0]):
        part_ref[c] = part[:, c * own : (c + 1) * own].astype(BF16)


def mlp_backward(mlp_grad, a, b, hidden_all, gain, w_gate, w_up, w_down):
    n, total, own = hidden_all.shape
    width, own_ff = w_gate.shape
    narrow = jax.ShapeDtypeStruct((total, own_ff), BF16)
    planes = pl.BlockSpec((n, ROWS, own), lambda i: (0, i, 0))
    return pl.pallas_call(
        mlp_back_kernel,
        grid=(total // ROWS,),
        in_specs=[
            row_block(width),
            row_block(own_ff),
            row_block(own_ff),
            planes,
            fixed(1, width),
            fixed(width, own_ff),
            fixed(width, own_ff),
            fixed(own_ff, width),
        ],
        out_specs=[row_block(own_ff), row_block(own_ff), planes, fixed(1, width)],
        out_shape=[narrow, narrow, jax.ShapeDtypeStruct((n, total, own), BF16), jax.ShapeDtypeStruct((1, width), F32)],
        compiler_params=params(),
        cost_estimate=cost(6 * total * width * own_ff, mlp_grad, hidden_all, hidden_all, w_gate, w_up, w_down, a, b, a, b),
        name="mlp_backward",
    )(mlp_grad, a, b, hidden_all, gain, w_gate, w_up, w_down)


def branch_kernel(part_ref, grad_ref, w_ref, hidden_ref, branch_ref, out_ref):
    hidden_grad = part_ref[...].astype(F32) + grad_ref[...].astype(F32)
    hidden_ref[...] = hidden_grad
    branch = (RESIDUAL_SCALE * hidden_grad).astype(BF16)
    branch_ref[...] = branch
    own = out_ref.shape[2]
    for c in range(out_ref.shape[0]):
        out_ref[c] = dot_nt(branch, w_ref[c]).astype(BF16)


def branch_backward(hidden_part, grad_own, w_out, n):
    total, own_width = hidden_part.shape
    own = w_out.shape[0] // n
    w_heads = w_out.reshape(n, own, own_width)
    return pl.pallas_call(
        branch_kernel,
        grid=(total // ROWS,),
        in_specs=[row_block(own_width), row_block(own_width), fixed(n, own, own_width)],
        out_specs=[row_block(own_width), row_block(own_width), pl.BlockSpec((n, ROWS, own), lambda i: (0, i, 0))],
        out_shape=[
            jax.ShapeDtypeStruct((total, own_width), F32),
            jax.ShapeDtypeStruct((total, own_width), BF16),
            jax.ShapeDtypeStruct((n, total, own), BF16),
        ],
        compiler_params=params(),
        cost_estimate=cost(2 * total * own_width * own * n, hidden_part, hidden_part, hidden_part, w_out),
        name="branch_backward",
    )(hidden_part, grad_own, w_heads)


def token_kernel(me_ref, dq_ref, dkv_ref, w_ref, x_ref, gain_ref, hidden_ref, part_ref, gain_out):
    split = dq_ref.shape[1]
    normed_grad = dot_nt(dq_ref[...], w_ref[:, :split]) + dot_nt(dkv_ref[...], w_ref[:, split:])
    x = x_ref[...].astype(F32)
    r1 = lax.rsqrt(jnp.mean(x * x, axis=-1, keepdims=True) + EPSILON)

    @pl.when(pl.program_id(0) == 0)
    def _():
        gain_out[...] = jnp.zeros_like(gain_out)

    gain_out[...] += jnp.sum(normed_grad * (x * r1), axis=0, keepdims=True)
    weighted = normed_grad * gain_ref[...]
    mean = jnp.mean(weighted * x, axis=-1, keepdims=True)
    part = r1 * weighted - x * (r1 * r1 * r1 * mean)
    own_width = hidden_ref.shape[1]
    for c in range(part.shape[1] // own_width):
        piece = part[:, c * own_width : (c + 1) * own_width]
        piece = piece + jnp.where(me_ref[0] == c, hidden_ref[...], 0.0)
        part_ref[:, c * own_width : (c + 1) * own_width] = piece.astype(BF16)


def token_backward(me, dq, dkv, w_qkv, x, gain, hidden_grad):
    total, width = x.shape
    own_width = hidden_grad.shape[1]
    return pl.pallas_call(
        token_kernel,
        grid=(total // ROWS,),
        in_specs=[
            pl.BlockSpec(memory_space=pltpu.SMEM),
            row_block(dq.shape[1]),
            row_block(dkv.shape[1]),
            fixed(*w_qkv.shape),
            row_block(width),
            fixed(1, width),
            row_block(own_width),
        ],
        out_specs=[row_block(width), fixed(1, width)],
        out_shape=[jax.ShapeDtypeStruct((total, width), BF16), jax.ShapeDtypeStruct((1, width), F32)],
        compiler_params=params(),
        cost_estimate=cost(2 * total * width * w_qkv.shape[1], x, x, w_qkv, dq, dkv, hidden_grad),
        name="token_backward",
    )(me, dq, dkv, w_qkv, x, gain, hidden_grad)


def spread_kernel(in_ref, out_ref):
    out_ref[...] = in_ref[0].astype(F32)


def spread_columns(pieces, slab, groups):
    n, rows, _ = pieces.shape
    out_shape = jax.ShapeDtypeStruct((rows, groups * n * slab), F32)
    return pl.pallas_call(
        spread_kernel,
        grid=(groups, n),
        in_specs=[pl.BlockSpec((1, rows, slab), lambda f, c: (c, 0, f))],
        out_specs=pl.BlockSpec((rows, slab), lambda f, c: (0, f * n + c)),
        out_shape=out_shape,
        compiler_params=params(),
        cost_estimate=cost(0, pieces, out_shape),
        name="spread_columns",
    )(pieces)


def gather_planes(shards):
    n_planes = lax.axis_size("fsdp")
    plane = lax.axis_index("fsdp")
    ups, downs = [], []
    up = down = shards
    for step in range(n_planes - 1):
        up = lax.ppermute(up, "fsdp", [(q, q + 1) for q in range(step, n_planes - 1)])
        down = lax.ppermute(down, "fsdp", [(q + 1, q) for q in range(n_planes - 1 - step)])
        ups.append(up)
        downs.append(down)

    def order(p):
        return lambda own, ups, downs: jnp.concatenate([ups[p - 1 - j] if j < p else own if j == p else downs[j - p - 1] for j in range(n_planes)], axis=0)

    return lax.switch(plane, [order(p) for p in range(n_planes)], shards, ups, downs), ups


def settle_planes(part):
    n_planes = lax.axis_size("fsdp")
    plane = lax.axis_index("fsdp")
    rows = part.shape[0] // n_planes

    def block(index):
        return lax.dynamic_slice_in_dim(part, jnp.clip(index, 0, n_planes - 1) * rows, rows, axis=0)

    def chain(index_of, pair):
        got = None
        for step in range(n_planes - 1):
            value = block(index_of(step))
            if got is not None:
                value = value + got
            got = lax.ppermute(value, "fsdp", [pair(q) for q in range(step + 1)])
        return got

    last = n_planes - 1
    from_below = chain(lambda s: last - s + plane, lambda q: (q, q + 1))
    from_above = chain(lambda s: s - last + plane, lambda q: (last - q, last - q - 1))
    return (block(plane).astype(F32) + from_below.astype(F32) + from_above.astype(F32)).astype(part.dtype)


def own_columns(array, index, width):
    return lax.dynamic_slice_in_dim(array, index * width, width, axis=1)


def after(value, *others):
    return lax.optimization_barrier((value, *others))[0]


def local(
    tokens,
    lengths,
    deal,
    attn_gain,
    query_weight,
    key_matrix,
    value_matrix,
    out_weight,
    mlp_gain,
    gate_weight,
    up_weight,
    down_weight,
    cotangent,
):
    n_ctx = lax.axis_size("ctx")
    n_fsdp = lax.axis_size("fsdp")
    me = lax.axis_index("ctx")
    me_array = me.astype(jnp.int32).reshape(1)
    per_device, width = tokens.shape[1], tokens.shape[2]
    total = per_device * n_ctx
    block_rows = per_device // n_ctx
    heads = QUERY_HEADS // n_ctx
    sharing = n_ctx // KEY_VALUE_HEADS
    own_width = width // n_ctx
    ff = gate_weight.shape[1]
    slab = ff // (n_fsdp * n_ctx)
    rows_shard = query_weight.shape[0]

    kv_head = me // sharing
    split = heads * HEAD_SIZE
    attn_shard = jnp.concatenate(
        [
            own_columns(query_weight, me, split),
            own_columns(key_matrix, kv_head, HEAD_SIZE),
            own_columns(value_matrix, kv_head, HEAD_SIZE),
            own_columns(out_weight, me, own_width),
        ],
        axis=1,
    )

    def ff_columns(array):
        return jnp.concatenate([own_columns(array, f * n_ctx + me, slab) for f in range(n_fsdp)], axis=1)

    gain_shard = jnp.stack([attn_gain, mlp_gain]).reshape(1, 2 * rows_shard)
    gains_all, _ = gather_planes(gain_shard)
    gains = gains_all.reshape(n_fsdp, 2, rows_shard).transpose(1, 0, 2).reshape(2, 1, width).astype(F32)
    w_attn, first = gather_planes(attn_shard)
    w_qkv, w_out = w_attn[:, : split + 2 * HEAD_SIZE], w_attn[:, split + 2 * HEAD_SIZE :]
    w_gate, second = gather_planes(after(ff_columns(gate_weight), first[0]))
    w_up, second = gather_planes(after(ff_columns(up_weight), first[0]))
    w_down, _ = gather_planes(
        after(lax.dynamic_slice_in_dim(down_weight, me * slab, slab, axis=0), second[1])
    )

    first_len = lengths[0, 0]
    given = jnp.arange(total, dtype=jnp.int32)
    position = given - jnp.where(given >= first_len, first_len, 0)
    freq_index = jnp.arange(HEAD_SIZE // 2, dtype=F32)
    inverse = ROPE_BASE ** (-2.0 * freq_index / HEAD_SIZE)
    angles = position.astype(F32)[:, None] * inverse[None, :]
    cos, sin = jnp.cos(angles), jnp.sin(angles)
    cos_table = jnp.concatenate([cos, cos, cos, cos], axis=1)
    sin_table = jnp.concatenate([-sin, sin, -sin, sin], axis=1)

    deal_rows = deal[0]
    slot_ids = jnp.arange(n_ctx, dtype=jnp.int32)
    dealt_of_given = (deal_rows * n_ctx + slot_ids[:, None]).reshape(-1)
    matched = deal_rows[:, :, None] == slot_ids[None, None, :]
    source_slot = jnp.sum(jnp.where(matched, slot_ids[None, :, None], 0), axis=1)
    given_of_dealt = (slot_ids[:, None] * n_ctx + source_slot).T.reshape(-1)

    def reorder(array, table):
        blocks = array.reshape(n_ctx * n_ctx, block_rows, array.shape[1])
        return jnp.take(blocks, table, axis=0, mode="clip").reshape(array.shape)

    x = lax.all_gather(tokens[0], "ctx", axis=0, tiled=True)
    normed, qkv = project(x, gains[0], w_qkv)
    attended, q_rot, k_rot, v_rows, lse = attention_forward(qkv, cos_table, sin_table, lengths[0], heads)
    attended_all = lax.all_gather(attended, "ctx", axis=0, tiled=False)
    hidden_own = out_projection(me_array, x, attended_all, w_out)
    hidden_all = lax.all_gather(hidden_own, "ctx", axis=0, tiled=False)
    cotangent_all = lax.all_gather(after(cotangent[0], attended), "ctx", axis=0, tiled=True)
    grad_result = reorder(cotangent_all, dealt_of_given)
    normed2, a, b, mixed = mlp_forward(hidden_all, gains[1], w_gate, w_up)

    mlp_grad = (RESIDUAL_SCALE * grad_result.astype(F32)).astype(BF16)

    def settle(left, right):
        return settle_planes(dot_tn(left, right).astype(BF16))

    down_part = settle(mixed, mlp_grad)
    ggrad, ugrad, hidden_part, mlp_gain_part = mlp_backward(
        mlp_grad, a, b, hidden_all, gains[1], w_gate, w_up, w_down
    )
    hidden_sum = lax.psum_scatter(hidden_part, "ctx", scatter_dimension=0, tiled=False)
    gate_part = settle(normed2, ggrad)
    up_part = settle(normed2, ugrad)
    hidden_grad, branch_grad, attended_part = branch_backward(
        hidden_sum, own_columns(grad_result, me, own_width), w_out, n_ctx
    )
    attended_grad = lax.psum_scatter(attended_part, "ctx", scatter_dimension=0, tiled=False)
    out_part = settle_planes(
        jnp.einsum("ctk,to->cko", attended_all, branch_grad, preferred_element_type=F32)
        .astype(BF16)
        .reshape(width, own_width)
    )
    dq, dkv = attention_backward(attended_grad, q_rot, k_rot, v_rows, lse, cos_table, sin_table, lengths[0])
    qkv_part = settle(normed, jnp.concatenate([dq, dkv], axis=1))
    token_part, attn_gain_part = token_backward(me_array, dq, dkv, w_qkv, x, gains[0], hidden_grad)
    token_grad = lax.psum_scatter(token_part, "ctx", scatter_dimension=0, tiled=True).astype(F32)[None]

    both = jnp.concatenate([mixed, (hidden_own.astype(F32) * (1.0 / RESIDUAL_SCALE)).astype(BF16)], axis=1)
    column = lax.broadcasted_iota(jnp.int32, (own_width, width), 1) - me * own_width
    place = (column == lax.broadcasted_iota(jnp.int32, (own_width, width), 0)).astype(BF16)
    result_part = RESIDUAL_SCALE * dot_nn(reorder(both, given_of_dealt), jnp.concatenate([w_down, place], axis=0))
    activations = lax.psum_scatter(
        after(result_part.astype(BF16), attended_grad), "ctx", scatter_dimension=0, tiled=True
    )[None]

    def whole(part):
        return lax.all_gather(part, "ctx", axis=0, tiled=False)

    down_grad = whole(down_part).reshape(n_ctx * slab, width).astype(F32)
    if slab % LANES == 0:
        gate_grad = spread_columns(whole(gate_part), slab, n_fsdp)
        up_grad = spread_columns(whole(up_part), slab, n_fsdp)
    else:

        def ff_whole(part):
            pieces = whole(part).reshape(n_ctx, rows_shard, n_fsdp, slab)
            return pieces.transpose(1, 2, 0, 3).reshape(rows_shard, ff).astype(F32)

        gate_grad = ff_whole(gate_part)
        up_grad = ff_whole(up_part)
    out_grad = spread_columns(whole(out_part), own_width, 1)
    qkv_all = whole(qkv_part)
    query_grad = spread_columns(qkv_all, split, 1)

    def shared_heads(pieces):
        pieces = pieces.astype(F32).reshape(KEY_VALUE_HEADS, sharing, rows_shard, HEAD_SIZE).sum(axis=1)
        return pieces.transpose(1, 0, 2).reshape(rows_shard, KEY_VALUE_HEADS * HEAD_SIZE)

    key_grad = shared_heads(qkv_all[:, :, split : split + HEAD_SIZE])
    value_grad = shared_heads(qkv_all[:, :, split + HEAD_SIZE :])

    gain_parts = jnp.concatenate([attn_gain_part, mlp_gain_part], axis=0)
    step = 1
    while step < n_ctx:
        gain_parts = gain_parts + lax.ppermute(gain_parts, "ctx", [(c, c ^ step) for c in range(n_ctx)])
        step *= 2
    gain_rows = gain_parts.reshape(2, n_fsdp, rows_shard).transpose(1, 0, 2).reshape(n_fsdp, 2 * rows_shard)
    own_gains = settle_planes(gain_rows).reshape(2, rows_shard)
    return (
        activations,
        token_grad,
        own_gains[0],
        query_grad,
        key_grad,
        value_grad,
        out_grad,
        own_gains[1],
        gate_grad,
        up_grad,
        down_grad,
    )


def solution(mesh):
    rows = P("fsdp", None)
    block = P("fsdp", "ctx", None)
    gain = P("fsdp")
    return jax.shard_map(
        local,
        mesh=mesh,
        in_specs=(block, rows, P("fsdp", None, None), gain, rows, rows, rows, rows, gain, rows, rows, rows, block),
        out_specs=(block, block, gain, rows, rows, rows, rows, gain, rows, rows, rows),
        check_vma=False,
    )
```

```python
import functools

import jax
import jax.numpy as jnp
from jax import lax
from jax.experimental import pallas as pl
from jax.experimental.pallas import tpu as pltpu
from jax.sharding import PartitionSpec as P

QUERY_HEADS = 32
KEY_VALUE_HEADS = 8
HEAD_SIZE = 64
EPSILON = 1e-05
ROPE_BASE = 10000000.0
SCORE_SCALE = 0.015625
RESIDUAL_SCALE = 0.22
NEGATIVE_BIG = -1e30
LANES = 128
ROWS = 256
BF16 = jnp.bfloat16
F32 = jnp.float32
VMEM_LIMIT = 56 * 1024 * 1024


def dot_nn(a, b):
    return lax.dot_general(a, b, (((1,), (0,)), ((), ())), preferred_element_type=F32)


def dot_nt(a, b):
    return lax.dot_general(a, b, (((1,), (1,)), ((), ())), preferred_element_type=F32)


def dot_tn(a, b):
    return lax.dot_general(a, b, (((0,), (0,)), ((), ())), preferred_element_type=F32)


def swap_halves(x):
    lane = lax.broadcasted_iota(jnp.int32, x.shape, 1)
    first = lax.rem(lane, HEAD_SIZE) < HEAD_SIZE // 2
    return jnp.where(first, pltpu.roll(x, LANES - HEAD_SIZE // 2, 1), pltpu.roll(x, HEAD_SIZE // 2, 1))


def low_half(shape):
    return lax.broadcasted_iota(jnp.int32, shape, 1) < HEAD_SIZE


def mask_bias(first_len, row0, rows, cols):
    query = row0 + lax.broadcasted_iota(jnp.int32, (rows, cols), 0)
    key = lax.broadcasted_iota(jnp.int32, (rows, cols), 1)
    start = jnp.where(query >= first_len, first_len, 0)
    return jnp.where((key <= query) & (key >= start), 0.0, NEGATIVE_BIG)


def attention_backward_kernel(length_ref, g_ref, q_ref, k_ref, v_ref, lse_ref, cos_ref, sin_ref, dq_ref, dkv_ref, dk_sum, dv_sum):
    pair = pl.program_id(0)
    tokens = q_ref.shape[0]

    @pl.when(pair == 0)
    def _():
        dk_sum[...] = jnp.zeros_like(dk_sum)
        dv_sum[...] = jnp.zeros_like(dv_sum)

    first_len = length_ref[0]
    for block in range(tokens // ROWS):
        rows = pl.ds(block * ROWS, ROWS)
        end = (block + 1) * ROWS
        bias = mask_bias(first_len, block * ROWS, ROWS, end)
        query, grad = q_ref[rows, :], g_ref[rows, :]
        low = low_half(query.shape)
        keys, values = k_ref[:end, :], v_ref[:end, :]
        parts = []
        for half in range(2):
            chosen = low if half == 0 else jnp.logical_not(low)
            own_query = jnp.where(chosen, query, jnp.zeros_like(query))
            own_grad = jnp.where(chosen, grad, jnp.zeros_like(grad))
            scores = dot_nt(own_query, keys) + bias
            probs = jnp.exp(scores - lse_ref[0, rows, half : half + 1])
            prob_grad = dot_nt(own_grad, values)
            delta = jnp.sum(probs * prob_grad, axis=-1, keepdims=True)
            score_grad = (probs * (prob_grad - delta)).astype(BF16)
            parts.append(dot_nn(score_grad, keys))
            dk_sum[:end, :] += dot_tn(score_grad, own_query)
            dv_sum[:end, :] += dot_tn(probs.astype(BF16), own_grad)
        dq = jnp.where(low_half(parts[0].shape), parts[0], parts[1]) * SCORE_SCALE
        dq_ref[rows, :] = (dq * cos_ref[rows, :] - swap_halves(dq) * sin_ref[rows, :]).astype(BF16)

    @pl.when(pair == pl.num_programs(0) - 1)
    def _():
        dk = dk_sum[...]
        dk = dk + pltpu.roll(dk, HEAD_SIZE, 1)
        dk = dk * cos_ref[...] - swap_halves(dk) * sin_ref[...]
        dv = dv_sum[...]
        dv = dv + pltpu.roll(dv, HEAD_SIZE, 1)
        dkv_ref[...] = jnp.where(low_half(dk.shape), dk, dv).astype(BF16)


def attention_backward(grads, q_rot, k_rot, v_rows, lse, cos, sin, lengths):
    tokens = q_rot.shape[0]
    pairs = q_rot.shape[1] // LANES
    one = pl.BlockSpec((tokens, LANES), lambda j: (0, 0))
    each = pl.BlockSpec((tokens, LANES), lambda j: (0, j))
    return pl.pallas_call(
        attention_backward_kernel,
        grid=(pairs,),
        in_specs=[
            pl.BlockSpec(memory_space=pltpu.SMEM),
            each,
            each,
            one,
            one,
            pl.BlockSpec((1, tokens, LANES), lambda j: (j, 0, 0)),
            one,
            one,
        ],
        out_specs=[each, one],
        out_shape=[
            jax.ShapeDtypeStruct((tokens, pairs * LANES), BF16),
            jax.ShapeDtypeStruct((tokens, LANES), BF16),
        ],
        scratch_shapes=[pltpu.VMEM((tokens, LANES), F32), pltpu.VMEM((tokens, LANES), F32)],
        compiler_params=pltpu.CompilerParams(vmem_limit_bytes=VMEM_LIMIT),
        cost_estimate=pl.CostEstimate(
            flops=10 * tokens * tokens * LANES * pairs,
            bytes_accessed=12 * tokens * pairs * LANES,
            transcendentals=tokens * tokens * pairs,
        ),
        name="attend_back",
    )(lengths, grads, q_rot, k_rot, v_rows, lse, cos, sin)


def row_block(width):
    return pl.BlockSpec((ROWS, width), lambda i: (i, 0))


def fixed(*shape):
    return pl.BlockSpec(shape, lambda i: (0,) * len(shape))


def params():
    return pltpu.CompilerParams(vmem_limit_bytes=VMEM_LIMIT)


def cost(flops, *arrays):
    moved = sum(a.size * a.dtype.itemsize for a in arrays)
    return pl.CostEstimate(flops=flops, bytes_accessed=moved, transcendentals=0)


def mlp_back_kernel(
    grad_ref, a_ref, b_ref, hidden_ref, gain_ref, gate_ref, up_ref, down_ref, ggrad_ref, ugrad_ref, part_ref, gain_out
):
    mixed_grad = dot_nt(grad_ref[...], down_ref[...])
    ggrad = (mixed_grad * a_ref[...].astype(F32)).astype(BF16)
    ugrad = (mixed_grad * b_ref[...].astype(F32)).astype(BF16)
    ggrad_ref[...] = ggrad
    ugrad_ref[...] = ugrad
    normed_grad = dot_nt(ggrad, gate_ref[...]) + dot_nt(ugrad, up_ref[...])
    hidden = hidden_ref[...].astype(F32)
    r2 = lax.rsqrt(jnp.mean(hidden * hidden, axis=-1, keepdims=True) + EPSILON)
    gain_part = jnp.sum(normed_grad * (hidden * r2), axis=0, keepdims=True)

    @pl.when(pl.program_id(0) == 0)
    def _():
        gain_out[...] = jnp.zeros_like(gain_out)

    gain_out[...] += gain_part
    weighted = normed_grad * gain_ref[...]
    mean = jnp.mean(weighted * hidden, axis=-1, keepdims=True)
    part = r2 * weighted - hidden * (r2 * r2 * r2 * mean)
    own = part_ref.shape[2]
    for c in range(part_ref.shape[0]):
        part_ref[c] = part[:, c * own : (c + 1) * own].astype(BF16)


def mlp_backward(n, mlp_grad, a, b, hidden_all, gain, w_gate, w_up, w_down):
    total, width = hidden_all.shape
    own = width // n
    own_ff = w_gate.shape[1]
    narrow = jax.ShapeDtypeStruct((total, own_ff), BF16)
    planes = pl.BlockSpec((n, ROWS, own), lambda i: (0, i, 0))
    return pl.pallas_call(
        mlp_back_kernel,
        grid=(total // ROWS,),
        in_specs=[
            row_block(width),
            row_block(own_ff),
            row_block(own_ff),
            row_block(width),
            fixed(1, width),
            fixed(width, own_ff),
            fixed(width, own_ff),
            fixed(own_ff, width),
        ],
        out_specs=[row_block(own_ff), row_block(own_ff), planes, fixed(1, width)],
        out_shape=[narrow, narrow, jax.ShapeDtypeStruct((n, total, own), BF16), jax.ShapeDtypeStruct((1, width), F32)],
        compiler_params=params(),
        cost_estimate=cost(6 * total * width * own_ff, mlp_grad, hidden_all, hidden_all, w_gate, w_up, w_down, a, b, a, b),
        name="mlp_backward",
    )(mlp_grad, a, b, hidden_all, gain, w_gate, w_up, w_down)


def branch_kernel(part_ref, grad_ref, w_ref, hidden_ref, branch_ref, out_ref):
    hidden_grad = part_ref[...].astype(F32) + grad_ref[...].astype(F32)
    hidden_ref[...] = hidden_grad
    branch = (RESIDUAL_SCALE * hidden_grad).astype(BF16)
    branch_ref[...] = branch
    own = out_ref.shape[2]
    for c in range(out_ref.shape[0]):
        out_ref[c] = dot_nt(branch, w_ref[c]).astype(BF16)


def branch_backward(hidden_part, grad_own, w_out, n):
    total, own_width = hidden_part.shape
    own = w_out.shape[0] // n
    w_heads = w_out.reshape(n, own, own_width)
    return pl.pallas_call(
        branch_kernel,
        grid=(total // ROWS,),
        in_specs=[row_block(own_width), row_block(own_width), fixed(n, own, own_width)],
        out_specs=[row_block(own_width), row_block(own_width), pl.BlockSpec((n, ROWS, own), lambda i: (0, i, 0))],
        out_shape=[
            jax.ShapeDtypeStruct((total, own_width), F32),
            jax.ShapeDtypeStruct((total, own_width), BF16),
            jax.ShapeDtypeStruct((n, total, own), BF16),
        ],
        compiler_params=params(),
        cost_estimate=cost(2 * total * own_width * own * n, hidden_part, hidden_part, hidden_part, w_out),
        name="branch_backward",
    )(hidden_part, grad_own, w_heads)


def token_kernel(me_ref, dq_ref, dkv_ref, w_ref, x_ref, gain_ref, hidden_ref, part_ref, gain_out):
    split = dq_ref.shape[1]
    normed_grad = dot_nt(dq_ref[...], w_ref[:, :split]) + dot_nt(dkv_ref[...], w_ref[:, split:])
    x = x_ref[...].astype(F32)
    r1 = lax.rsqrt(jnp.mean(x * x, axis=-1, keepdims=True) + EPSILON)

    @pl.when(pl.program_id(0) == 0)
    def _():
        gain_out[...] = jnp.zeros_like(gain_out)

    gain_out[...] += jnp.sum(normed_grad * (x * r1), axis=0, keepdims=True)
    weighted = normed_grad * gain_ref[...]
    mean = jnp.mean(weighted * x, axis=-1, keepdims=True)
    part = r1 * weighted - x * (r1 * r1 * r1 * mean)
    own_width = hidden_ref.shape[1]
    for c in range(part.shape[1] // own_width):
        piece = part[:, c * own_width : (c + 1) * own_width]
        piece = piece + jnp.where(me_ref[0] == c, hidden_ref[...], 0.0)
        part_ref[:, c * own_width : (c + 1) * own_width] = piece.astype(BF16)


def token_backward(me, dq, dkv, w_qkv, x, gain, hidden_grad):
    total, width = x.shape
    own_width = hidden_grad.shape[1]
    return pl.pallas_call(
        token_kernel,
        grid=(total // ROWS,),
        in_specs=[
            pl.BlockSpec(memory_space=pltpu.SMEM),
            row_block(dq.shape[1]),
            row_block(dkv.shape[1]),
            fixed(*w_qkv.shape),
            row_block(width),
            fixed(1, width),
            row_block(own_width),
        ],
        out_specs=[row_block(width), fixed(1, width)],
        out_shape=[jax.ShapeDtypeStruct((total, width), BF16), jax.ShapeDtypeStruct((1, width), F32)],
        compiler_params=params(),
        cost_estimate=cost(2 * total * width * w_qkv.shape[1], x, x, w_qkv, dq, dkv, hidden_grad),
        name="token_backward",
    )(me, dq, dkv, w_qkv, x, gain, hidden_grad)


def spread_kernel(in_ref, out_ref):
    out_ref[...] = in_ref[0].astype(F32)


def spread_columns(pieces, slab, groups):
    n, rows, _ = pieces.shape
    out_shape = jax.ShapeDtypeStruct((rows, groups * n * slab), F32)
    return pl.pallas_call(
        spread_kernel,
        grid=(groups, n),
        in_specs=[pl.BlockSpec((1, rows, slab), lambda f, c: (c, 0, f))],
        out_specs=pl.BlockSpec((rows, slab), lambda f, c: (0, f * n + c)),
        out_shape=out_shape,
        compiler_params=params(),
        cost_estimate=cost(0, pieces, out_shape),
        name="spread_columns",
    )(pieces)


MESH = pl.DeviceIdType.MESH


class Chain:
    def __init__(self, slot, planes, plane, send_sem, recv_sem):
        self.slot, self.planes, self.plane = slot, planes, plane
        self.send_sem, self.recv_sem = send_sem, recv_sem

    def copy(self, way, step, shard, to):
        return pltpu.make_async_remote_copy(
            src_ref=self.slot(shard),
            dst_ref=self.slot(shard),
            send_sem=self.send_sem.at[way, step],
            recv_sem=self.recv_sem.at[way, step],
            device_id={"fsdp": to},
            device_id_type=MESH,
        )

    def moves(self, step):
        p, last = self.plane, self.planes - 1
        return (
            (0, (p >= step) & (p < last), p - step, p + 1, p >= step + 1, p - 1 - step),
            (1, (p + step <= last) & (p > 0), p + step, p - 1, p + step + 1 <= last, p + 1 + step),
        )

    def start(self, step):
        for way, sends, shard, to, _, _ in self.moves(step):

            @pl.when(sends)
            def _(way=way, shard=shard, to=to):
                self.copy(way, step, shard, to).start()

    def arrive(self, step):
        for way, _, _, _, receives, shard in self.moves(step):

            @pl.when(receives)
            def _(way=way, shard=shard):
                self.copy(way, step, shard, self.plane).wait_recv()

    def advance(self, step):
        self.arrive(step - 1)
        self.start(step)

    def drain(self):
        for step in range(self.planes - 1):
            for way, sends, shard, to, _, _ in self.moves(step):

                @pl.when(sends)
                def _(way=way, shard=shard, to=to, step=step):
                    self.copy(way, step, shard, to).wait_send()


class Spread:
    def __init__(self, src, slot, n, me, send_sem, recv_sem):
        self.src, self.slot, self.n, self.me = src, slot, n, me
        self.send_sem, self.recv_sem = send_sem, recv_sem
        self.chips = n // 2
        self.chip, self.core = me // 2, lax.rem(me, 2)
        self.partner = me + 1 - 2 * self.core

    def at(self, k):
        return lax.rem(self.chip + k, self.chips) * 2 + self.core

    def copy(self, src, owner, sem, to):
        return pltpu.make_async_remote_copy(
            src_ref=src,
            dst_ref=self.slot(owner),
            send_sem=self.send_sem.at[sem],
            recv_sem=self.recv_sem.at[sem],
            device_id={"ctx": to},
            device_id_type=MESH,
        )

    def out(self, k):
        return self.copy(self.src, self.me, k, self.at(k))

    def relay(self, k):
        owner = self.at(self.chips - k) if k else self.me
        src = self.slot(owner) if k else self.src
        return self.copy(src, owner, self.chips + k, self.partner)

    def start(self):
        for k in range(1, self.chips):
            self.out(k).start()
        self.relay(0).start()

    def pass_on(self):
        for k in range(1, self.chips):
            self.copy(self.src, self.at(self.chips - k), k, self.me).wait_recv()
            self.relay(k).start()

    def finish(self):
        other = 1 - 2 * self.core
        for k in range(self.chips):
            owner = (self.at(self.chips - k) if k else self.me) + other
            self.copy(self.slot(owner), owner, self.chips + k, self.me).wait_recv()

    def drain(self):
        for k in range(1, self.chips):
            self.out(k).wait_send()
        for k in range(self.chips):
            self.relay(k).wait_send()


def greet(n, planes, me, plane, across):
    barrier = pltpu.get_barrier_semaphore()
    chips = n // 2
    core = lax.rem(me, 2)
    others = [lax.rem(me // 2 + k, chips) * 2 + core for k in range(1, chips)] + [me + 1 - 2 * core]
    for other in others:
        pl.semaphore_signal(barrier, inc=1, device_id={"ctx": other}, device_id_type=MESH)
    if across:

        @pl.when(plane > 0)
        def _():
            pl.semaphore_signal(barrier, inc=1, device_id={"fsdp": plane - 1}, device_id_type=MESH)

        @pl.when(plane < planes - 1)
        def _():
            pl.semaphore_signal(barrier, inc=1, device_id={"fsdp": plane + 1}, device_id_type=MESH)

    count = len(others)
    if across:
        count = count + (plane > 0).astype(jnp.int32) + (plane < planes - 1).astype(jnp.int32)
    pl.semaphore_wait(barrier, count)


def forward_kernel(
    n,
    planes,
    heads,
    length_ref,
    tokens_ref,
    attn_shard,
    gate_shard,
    up_shard,
    down_shard,
    gain_shard,
    cos_ref,
    sin_ref,
    x_out,
    normed_out,
    q_out,
    k_out,
    v_out,
    lse_out,
    att_out,
    hid_out,
    normed2_out,
    a_out,
    b_out,
    mixed_out,
    attn_out,
    gate_out,
    up_out,
    down_out,
    gain_out,
    w_attn,
    w_gate,
    w_up,
    w_down,
    gains,
    x_all,
    qkv,
    q_rot,
    k_rot,
    v_rows,
    lse,
    own_att,
    att_all,
    own_hid,
    wide,
    narrow,
    z_send,
    z_recv,
    c_send,
    c_recv,
    keep_sem,
    wide_sem,
    narrow_sem,
):
    me, plane = lax.axis_index("ctx"), lax.axis_index("fsdp")
    per_device, width = tokens_ref.shape
    total = x_all.shape[0]
    rows_shard = attn_shard.shape[0]
    own = own_att.shape[1]
    own_width = own_hid.shape[1]
    columns = qkv.shape[1]
    blocks = total // ROWS
    pairs = heads // 2

    local_copies = []

    def keep(src, dst, index):
        copy = pltpu.make_async_copy(src, dst, keep_sem.at[index])
        copy.start()
        local_copies.append(copy)

    def chain(index, ref, rows):
        return Chain(lambda s: ref.at[pl.ds(s * rows, rows)], planes, plane, z_send.at[index], z_recv.at[index])

    attn_chain = chain(0, w_attn, rows_shard)
    gate_chain = chain(1, w_gate, rows_shard)
    up_chain = chain(2, w_up, rows_shard)
    down_chain = chain(3, w_down, down_shard.shape[0])
    gain_chain = chain(4, gains, gain_shard.shape[0])
    first = (attn_chain, attn_shard, 0), (gain_chain, gain_shard, 1), (gate_chain, gate_shard, 2), (up_chain, up_shard, 3), (down_chain, down_shard, 4)
    loads = [pltpu.make_async_copy(shard, c.slot(plane), keep_sem.at[i]) for c, shard, i in first]
    for load in loads:
        load.start()
    own_x = pltpu.make_async_copy(tokens_ref, x_all.at[pl.ds(me * per_device, per_device)], keep_sem.at[5])
    own_x.start()
    greet(n, planes, me, plane, True)
    loads[0].wait()
    attn_chain.start(0)
    loads[1].wait()
    gain_chain.start(0)
    x_spread = Spread(
        tokens_ref, lambda c: x_all.at[pl.ds(c * per_device, per_device)], n, me, c_send.at[0], c_recv.at[0]
    )
    x_spread.start()
    for load in loads[2:]:
        load.wait()
    own_x.wait()
    for step in range(1, planes - 1):
        attn_chain.advance(step)
        gain_chain.advance(step)
    gate_chain.start(0)
    up_chain.start(0)
    x_spread.pass_on()
    x_spread.finish()
    x_copy = pltpu.make_async_copy(x_all, x_out, keep_sem.at[0])
    x_copy.start()
    attn_chain.arrive(planes - 2)
    gain_chain.arrive(planes - 2)
    keep(w_attn, attn_out, 1)
    keep(gains, gain_out, 2)
    half = gain_shard.shape[1] // 2
    step_rows = gain_shard.shape[0]
    attn_gain = jnp.concatenate([gains[f * step_rows : f * step_rows + 1, :half] for f in range(planes)], axis=1)
    mlp_gain = jnp.concatenate([gains[f * step_rows : f * step_rows + 1, half:] for f in range(planes)], axis=1)

    def staged(stage, sem, slot, out, rows, wait_before):
        copy = pltpu.make_async_copy(stage.at[slot], out.at[rows], sem.at[slot])
        return copy.wait() if wait_before else copy.start()

    def project_block(i, _):
        rows = pl.ds(pl.multiple_of(i * ROWS, ROWS), ROWS)
        slot = lax.rem(i, 2)

        @pl.when(i >= 2)
        def _():
            staged(wide, wide_sem, slot, normed_out, rows, True)

        own_hid[rows, :] = x_all[rows, pl.ds(pl.multiple_of(me * own_width, LANES), own_width)]
        x = x_all[rows, :].astype(F32)
        r1 = lax.rsqrt(jnp.mean(x * x, axis=-1, keepdims=True) + EPSILON)
        normed = (x * r1 * attn_gain).astype(BF16)
        wide[slot] = normed
        staged(wide, wide_sem, slot, normed_out, rows, False)
        qkv[rows, :] = dot_nn(normed, w_attn[:, :columns])
        return 0

    lax.fori_loop(0, blocks, project_block, 0)
    for i in range(max(blocks - 2, 0), blocks):
        staged(wide, wide_sem, i % 2, normed_out, pl.ds(i * ROWS, ROWS), True)

    split = columns - LANES
    cos, sin = cos_ref[...], sin_ref[...]
    kv = qkv[:, split:]
    turned = pltpu.roll(kv, HEAD_SIZE, 1)
    low = low_half(kv.shape)
    k = jnp.where(low, kv, turned)
    k_rot[...] = (k * cos + swap_halves(k) * sin).astype(BF16)
    v_rows[...] = jnp.where(low, turned, kv).astype(BF16)
    keep(k_rot, k_out, 3)
    keep(v_rows, v_out, 4)
    first_len = length_ref[0]

    def attend_pair(pair, _):
        lanes = pl.ds(pl.multiple_of(pair * LANES, LANES), LANES)
        q = qkv[:, lanes]
        q_rot[:, lanes] = ((q * cos_ref[...] + swap_halves(q) * sin_ref[...]) * SCORE_SCALE).astype(BF16)
        for block in range(blocks):
            rows = pl.ds(block * ROWS, ROWS)
            end = (block + 1) * ROWS
            bias = mask_bias(first_len, block * ROWS, ROWS, end)
            query = q_rot[rows, lanes]
            lower = low_half(query.shape)
            keys, values = k_rot[:end, :], v_rows[:end, :]
            parts = []
            for side in range(2):
                chosen = lower if side == 0 else jnp.logical_not(lower)
                scores = dot_nt(jnp.where(chosen, query, jnp.zeros_like(query)), keys) + bias
                top = jnp.max(scores, axis=-1, keepdims=True)
                weights = jnp.exp(scores - top)
                whole = jnp.sum(weights, axis=-1, keepdims=True)
                probs = (weights * (1.0 / whole)).astype(BF16)
                parts.append(dot_nn(probs, values))
                lse[pair, rows, side : side + 1] = top + jnp.log(whole)
            own_att[rows, lanes] = jnp.where(low_half(parts[0].shape), parts[0], parts[1]).astype(BF16)
        return 0

    lax.fori_loop(0, pairs, attend_pair, 0)
    att_spread = Spread(own_att, lambda c: att_all.at[c], n, me, c_send.at[1], c_recv.at[1])
    x_copy.wait()
    x_spread.drain()
    att_spread.start()
    own_a = pltpu.make_async_copy(own_att, att_all.at[me], keep_sem.at[5])
    own_a.start()
    keep(q_rot, q_out, 6)
    keep(lse, lse_out, 7)
    if planes > 2:
        gate_chain.advance(1)
        up_chain.advance(1)
    att_spread.pass_on()
    own_a.wait()
    att_spread.finish()
    keep(att_all, att_out, 8)

    def out_block(i, _):
        rows = pl.ds(pl.multiple_of(i * ROWS, ROWS), ROWS)
        acc = jnp.zeros((ROWS, own_width), F32)
        for c in range(n):
            acc += dot_nn(att_all[c, rows, :], w_attn[c * own : (c + 1) * own, columns:])
        own_hid[rows, :] = (own_hid[rows, :].astype(F32) + RESIDUAL_SCALE * acc).astype(BF16)
        return 0

    lax.fori_loop(0, blocks, out_block, 0)
    def hid_slot(c):
        return x_all.at[:, pl.ds(pl.multiple_of(c * own_width, LANES), own_width)]

    hid_spread = Spread(own_hid, hid_slot, n, me, c_send.at[2], c_recv.at[2])
    hid_spread.start()
    own_h = pltpu.make_async_copy(own_hid, hid_slot(me), keep_sem.at[5])
    own_h.start()
    for step in range(2, planes - 1):
        gate_chain.advance(step)
        up_chain.advance(step)
    down_chain.start(0)
    hid_spread.pass_on()
    own_h.wait()
    hid_spread.finish()
    keep(x_all, hid_out, 9)
    gate_chain.arrive(planes - 2)
    up_chain.arrive(planes - 2)
    keep(w_gate, gate_out, 10)
    keep(w_up, up_out, 11)
    if planes > 2:
        down_chain.advance(1)

    def mlp_copies(i, rows, wait):
        slot = lax.rem(i, 2)
        staged(wide, wide_sem, slot, normed2_out, rows, wait)
        for j, out in enumerate((a_out, b_out, mixed_out)):
            staged(narrow.at[j], narrow_sem.at[j], slot, out, rows, wait)

    def mlp_block(i, _):
        rows = pl.ds(pl.multiple_of(i * ROWS, ROWS), ROWS)
        slot = lax.rem(i, 2)

        @pl.when(i >= 2)
        def _():
            mlp_copies(i, rows, True)

        hidden = x_all[rows, :].astype(F32)
        r2 = lax.rsqrt(jnp.mean(hidden * hidden, axis=-1, keepdims=True) + EPSILON)
        normed = (hidden * r2 * mlp_gain).astype(BF16)
        wide[slot] = normed
        gate = dot_nn(normed, w_gate[...])
        up = dot_nn(normed, w_up[...])
        sig = jax.nn.sigmoid(gate)
        silu = gate * sig
        narrow[2, slot] = (silu * up).astype(BF16)
        narrow[1, slot] = silu.astype(BF16)
        narrow[0, slot] = (up * sig * (1.0 + gate * (1.0 - sig))).astype(BF16)
        mlp_copies(i, rows, False)
        return 0

    lax.fori_loop(0, blocks, mlp_block, 0)
    for step in range(2, planes - 1):
        down_chain.advance(step)
    for i in range(max(blocks - 2, 0), blocks):
        mlp_copies(i, pl.ds(i * ROWS, ROWS), True)
    down_chain.arrive(planes - 2)
    keep(w_down, down_out, 12)
    for c in (attn_chain, gain_chain, gate_chain, up_chain, down_chain):
        c.drain()
    for s in (att_spread, hid_spread):
        s.drain()
    for copy in local_copies:
        copy.wait()


def forward(n, planes, heads, lengths, tokens, attn_shard, gate_shard, up_shard, down_shard, gain_shard, cos, sin):
    per_device, width = tokens.shape
    total = per_device * n
    own = heads * HEAD_SIZE
    columns = own + 2 * HEAD_SIZE
    own_width = attn_shard.shape[1] - columns
    own_ff = gate_shard.shape[1]
    rows_shard = attn_shard.shape[0]
    pairs = heads // 2
    weights = [
        ((planes * rows_shard, attn_shard.shape[1]), BF16),
        ((planes * rows_shard, own_ff), BF16),
        ((planes * rows_shard, own_ff), BF16),
        ((planes * down_shard.shape[0], width), BF16),
        ((planes * gain_shard.shape[0], gain_shard.shape[1]), F32),
    ]
    outs = [
        ((total, width), BF16),
        ((total, width), BF16),
        ((total, own), BF16),
        ((total, LANES), BF16),
        ((total, LANES), BF16),
        ((pairs, total, LANES), F32),
        ((n, total, own), BF16),
        ((total, width), BF16),
        ((total, width), BF16),
        ((total, own_ff), BF16),
        ((total, own_ff), BF16),
        ((total, own_ff), BF16),
    ] + weights
    scratch = weights + [
        ((total, width), BF16),
        ((total, columns), F32),
        ((total, own), BF16),
        ((total, LANES), BF16),
        ((total, LANES), BF16),
        ((pairs, total, LANES), F32),
        ((total, own), BF16),
        ((n, total, own), BF16),
        ((total, own_width), BF16),
        ((2, ROWS, width), BF16),
        ((3, 2, ROWS, own_ff), BF16),
    ]
    steps = max(planes - 1, 1)
    dma = pltpu.SemaphoreType.DMA
    anywhere = pl.BlockSpec(memory_space=pl.ANY)
    vmem = pl.BlockSpec(memory_space=pltpu.VMEM)
    return pl.pallas_call(
        functools.partial(forward_kernel, n, planes, heads),
        in_specs=[pl.BlockSpec(memory_space=pltpu.SMEM), vmem] + [anywhere] * 5 + [vmem] * 2,
        out_specs=[anywhere] * len(outs),
        out_shape=[jax.ShapeDtypeStruct(*o) for o in outs],
        scratch_shapes=[pltpu.VMEM(*s) for s in scratch]
        + [dma((5, 2, steps)), dma((5, 2, steps)), dma((3, n)), dma((3, n)), dma((16,)), dma((2,)), dma((3, 2))],
        compiler_params=pltpu.CompilerParams(
            vmem_limit_bytes=VMEM_LIMIT, collective_id=1, has_side_effects=True
        ),
        cost_estimate=pl.CostEstimate(
            flops=2 * total * width * (columns + own_width + 2 * own_ff),
            bytes_accessed=60 * 1024 * 1024,
            transcendentals=0,
        ),
        name="forward",
    )(lengths, tokens, attn_shard, gate_shard, up_shard, down_shard, gain_shard, cos, sin)


def own_columns(array, index, width):
    return lax.dynamic_slice_in_dim(array, index * width, width, axis=1)


def after(value, *others):
    return lax.optimization_barrier((value, *others))[0]


def local(
    tokens,
    lengths,
    deal,
    attn_gain,
    query_weight,
    key_matrix,
    value_matrix,
    out_weight,
    mlp_gain,
    gate_weight,
    up_weight,
    down_weight,
    cotangent,
):
    n_ctx = lax.axis_size("ctx")
    n_fsdp = lax.axis_size("fsdp")
    me = lax.axis_index("ctx")
    me_array = me.astype(jnp.int32).reshape(1)
    per_device, width = tokens.shape[1], tokens.shape[2]
    total = per_device * n_ctx
    block_rows = per_device // n_ctx
    heads = QUERY_HEADS // n_ctx
    sharing = n_ctx // KEY_VALUE_HEADS
    own_width = width // n_ctx
    ff = gate_weight.shape[1]
    slab = ff // (n_fsdp * n_ctx)
    rows_shard = query_weight.shape[0]

    kv_head = me // sharing
    split = heads * HEAD_SIZE
    attn_shard = jnp.concatenate(
        [
            own_columns(query_weight, me, split),
            own_columns(key_matrix, kv_head, HEAD_SIZE),
            own_columns(value_matrix, kv_head, HEAD_SIZE),
            own_columns(out_weight, me, own_width),
        ],
        axis=1,
    )

    def ff_columns(array):
        return jnp.concatenate([own_columns(array, f * n_ctx + me, slab) for f in range(n_fsdp)], axis=1)

    gain_shard = jnp.tile(jnp.concatenate([attn_gain, mlp_gain]).astype(F32)[None], (8, 1))

    first_len = lengths[0, 0]
    given = jnp.arange(total, dtype=jnp.int32)
    position = given - jnp.where(given >= first_len, first_len, 0)
    freq_index = jnp.arange(HEAD_SIZE // 2, dtype=F32)
    inverse = ROPE_BASE ** (-2.0 * freq_index / HEAD_SIZE)
    angles = position.astype(F32)[:, None] * inverse[None, :]
    cos, sin = jnp.cos(angles), jnp.sin(angles)
    cos_table = jnp.concatenate([cos, cos, cos, cos], axis=1)
    sin_table = jnp.concatenate([-sin, sin, -sin, sin], axis=1)

    deal_rows = deal[0]
    slot_ids = jnp.arange(n_ctx, dtype=jnp.int32)
    dealt_of_given = (deal_rows * n_ctx + slot_ids[:, None]).reshape(-1)
    matched = deal_rows[:, :, None] == slot_ids[None, None, :]
    source_slot = jnp.sum(jnp.where(matched, slot_ids[None, :, None], 0), axis=1)
    given_of_dealt = (slot_ids[:, None] * n_ctx + source_slot).T.reshape(-1)

    def reorder(array, table):
        blocks = array.reshape(n_ctx * n_ctx, block_rows, array.shape[1])
        return jnp.take(blocks, table, axis=0, mode="clip").reshape(array.shape)

    cotangent_all = lax.all_gather(cotangent[0], "ctx", axis=0, tiled=True)
    (
        x, normed, q_rot, k_rot, v_rows, lse, attended_all, hidden_all, normed2, a, b, mixed, w_attn, w_gate, w_up, w_down, gains_all,
    ) = forward(
        n_ctx,
        n_fsdp,
        heads,
        lengths[0],
        tokens[0],
        attn_shard,
        ff_columns(gate_weight),
        ff_columns(up_weight),
        lax.dynamic_slice_in_dim(down_weight, me * slab, slab, axis=0),
        gain_shard,
        cos_table,
        sin_table,
    )
    w_qkv, w_out = w_attn[:, : split + 2 * HEAD_SIZE], w_attn[:, split + 2 * HEAD_SIZE :]
    gains = gains_all.reshape(n_fsdp, 8, 2, rows_shard)[:, 0].transpose(1, 0, 2).reshape(2, 1, width)
    hidden_own = own_columns(hidden_all, me, own_width)
    grad_result = reorder(cotangent_all, dealt_of_given)

    mlp_grad = (RESIDUAL_SCALE * grad_result.astype(F32)).astype(BF16)

    def settle(left, right):
        return lax.psum_scatter(dot_tn(left, right).astype(BF16), "fsdp", scatter_dimension=0, tiled=True)

    down_part = settle(mixed, mlp_grad)
    ggrad, ugrad, hidden_part, mlp_gain_part = mlp_backward(
        n_ctx, mlp_grad, a, b, hidden_all, gains[1], w_gate, w_up, w_down
    )
    hidden_sum = lax.psum_scatter(hidden_part, "ctx", scatter_dimension=0, tiled=False)
    gate_part = settle(normed2, ggrad)
    up_part = settle(normed2, ugrad)
    hidden_grad, branch_grad, attended_part = branch_backward(
        hidden_sum, own_columns(grad_result, me, own_width), w_out, n_ctx
    )
    attended_grad = lax.psum_scatter(attended_part, "ctx", scatter_dimension=0, tiled=False)
    out_part = lax.psum_scatter(
        jnp.einsum("ctk,to->cko", attended_all, branch_grad, preferred_element_type=F32)
        .astype(BF16)
        .reshape(width, own_width),
        "fsdp",
        scatter_dimension=0,
        tiled=True,
    )
    dq, dkv = attention_backward(attended_grad, q_rot, k_rot, v_rows, lse, cos_table, sin_table, lengths[0])
    qkv_part = settle(normed, jnp.concatenate([dq, dkv], axis=1))
    token_part, attn_gain_part = token_backward(me_array, dq, dkv, w_qkv, x, gains[0], hidden_grad)
    token_grad = lax.psum_scatter(token_part, "ctx", scatter_dimension=0, tiled=True).astype(F32)[None]

    both = jnp.concatenate([mixed, (hidden_own.astype(F32) * (1.0 / RESIDUAL_SCALE)).astype(BF16)], axis=1)
    column = lax.broadcasted_iota(jnp.int32, (own_width, width), 1) - me * own_width
    place = (column == lax.broadcasted_iota(jnp.int32, (own_width, width), 0)).astype(BF16)
    result_part = RESIDUAL_SCALE * dot_nn(reorder(both, given_of_dealt), jnp.concatenate([w_down, place], axis=0))
    activations = lax.psum_scatter(
        after(result_part.astype(BF16), attended_grad), "ctx", scatter_dimension=0, tiled=True
    )[None]

    def whole(part):
        return lax.all_gather(part, "ctx", axis=0, tiled=False)

    down_grad = whole(down_part).reshape(n_ctx * slab, width).astype(F32)
    if slab % LANES == 0:
        gate_grad = spread_columns(whole(gate_part), slab, n_fsdp)
        up_grad = spread_columns(whole(up_part), slab, n_fsdp)
    else:

        def ff_whole(part):
            pieces = whole(part).reshape(n_ctx, rows_shard, n_fsdp, slab)
            return pieces.transpose(1, 2, 0, 3).reshape(rows_shard, ff).astype(F32)

        gate_grad = ff_whole(gate_part)
        up_grad = ff_whole(up_part)
    out_grad = spread_columns(whole(out_part), own_width, 1)
    qkv_all = whole(qkv_part)
    query_grad = spread_columns(qkv_all, split, 1)

    def shared_heads(pieces):
        pieces = pieces.astype(F32).reshape(KEY_VALUE_HEADS, sharing, rows_shard, HEAD_SIZE).sum(axis=1)
        return pieces.transpose(1, 0, 2).reshape(rows_shard, KEY_VALUE_HEADS * HEAD_SIZE)

    key_grad = shared_heads(qkv_all[:, :, split : split + HEAD_SIZE])
    value_grad = shared_heads(qkv_all[:, :, split + HEAD_SIZE :])

    gain_parts = jnp.concatenate([attn_gain_part, mlp_gain_part], axis=0)
    step = 1
    while step < n_ctx:
        gain_parts = gain_parts + lax.ppermute(gain_parts, "ctx", [(c, c ^ step) for c in range(n_ctx)])
        step *= 2
    gain_rows = gain_parts.reshape(2, n_fsdp, rows_shard).transpose(1, 0, 2).reshape(n_fsdp, 2 * rows_shard)
    own_gains = lax.psum_scatter(gain_rows, "fsdp", scatter_dimension=0, tiled=True).reshape(2, rows_shard)
    return (
        activations,
        token_grad,
        own_gains[0],
        query_grad,
        key_grad,
        value_grad,
        out_grad,
        own_gains[1],
        gate_grad,
        up_grad,
        down_grad,
    )


def solution(mesh):
    rows = P("fsdp", None)
    block = P("fsdp", "ctx", None)
    gain = P("fsdp")
    return jax.shard_map(
        local,
        mesh=mesh,
        in_specs=(block, rows, P("fsdp", None, None), gain, rows, rows, rows, rows, gain, rows, rows, rows, block),
        out_specs=(block, block, gain, rows, rows, rows, rows, gain, rows, rows, rows),
        check_vma=False,
    )
```

```python
import functools

import jax
import jax.numpy as jnp
from jax import lax
from jax.experimental import pallas as pl
from jax.experimental.pallas import tpu as pltpu
from jax.sharding import PartitionSpec as P

QUERY_HEADS = 32
KEY_VALUE_HEADS = 8
HEAD_SIZE = 64
EPSILON = 1e-05
ROPE_BASE = 10000000.0
SCORE_SCALE = 0.015625
RESIDUAL_SCALE = 0.22
NEGATIVE_BIG = -1e30
LANES = 128
ROWS = 256
BF16 = jnp.bfloat16
F32 = jnp.float32
VMEM_LIMIT = 56 * 1024 * 1024


def dot_nn(a, b):
    return lax.dot_general(a, b, (((1,), (0,)), ((), ())), preferred_element_type=F32)


def dot_nt(a, b):
    return lax.dot_general(a, b, (((1,), (1,)), ((), ())), preferred_element_type=F32)


def dot_tn(a, b):
    return lax.dot_general(a, b, (((0,), (0,)), ((), ())), preferred_element_type=F32)


def swap_halves(x):
    lane = lax.broadcasted_iota(jnp.int32, x.shape, 1)
    first = lax.rem(lane, HEAD_SIZE) < HEAD_SIZE // 2
    return jnp.where(first, pltpu.roll(x, LANES - HEAD_SIZE // 2, 1), pltpu.roll(x, HEAD_SIZE // 2, 1))


def low_half(shape):
    return lax.broadcasted_iota(jnp.int32, shape, 1) < HEAD_SIZE


def mask_bias(first_len, row0, rows, cols):
    query = row0 + lax.broadcasted_iota(jnp.int32, (rows, cols), 0)
    key = lax.broadcasted_iota(jnp.int32, (rows, cols), 1)
    start = jnp.where(query >= first_len, first_len, 0)
    return jnp.where((key <= query) & (key >= start), 0.0, NEGATIVE_BIG)


def attention_backward_kernel(length_ref, g_ref, q_ref, k_ref, v_ref, lse_ref, cos_ref, sin_ref, dq_ref, dkv_ref, dk_sum, dv_sum):
    pair = pl.program_id(0)
    tokens = q_ref.shape[0]

    @pl.when(pair == 0)
    def _():
        dk_sum[...] = jnp.zeros_like(dk_sum)
        dv_sum[...] = jnp.zeros_like(dv_sum)

    first_len = length_ref[0]
    for block in range(tokens // ROWS):
        rows = pl.ds(block * ROWS, ROWS)
        end = (block + 1) * ROWS
        bias = mask_bias(first_len, block * ROWS, ROWS, end)
        query, grad = q_ref[rows, :], g_ref[rows, :]
        low = low_half(query.shape)
        keys, values = k_ref[:end, :], v_ref[:end, :]
        parts = []
        for half in range(2):
            chosen = low if half == 0 else jnp.logical_not(low)
            own_query = jnp.where(chosen, query, jnp.zeros_like(query))
            own_grad = jnp.where(chosen, grad, jnp.zeros_like(grad))
            scores = dot_nt(own_query, keys) + bias
            probs = jnp.exp(scores - lse_ref[0, rows, half : half + 1])
            prob_grad = dot_nt(own_grad, values)
            delta = jnp.sum(probs * prob_grad, axis=-1, keepdims=True)
            score_grad = (probs * (prob_grad - delta)).astype(BF16)
            parts.append(dot_nn(score_grad, keys))
            dk_sum[:end, :] += dot_tn(score_grad, own_query)
            dv_sum[:end, :] += dot_tn(probs.astype(BF16), own_grad)
        dq = jnp.where(low_half(parts[0].shape), parts[0], parts[1]) * SCORE_SCALE
        dq_ref[rows, :] = (dq * cos_ref[rows, :] - swap_halves(dq) * sin_ref[rows, :]).astype(BF16)

    @pl.when(pair == pl.num_programs(0) - 1)
    def _():
        dk = dk_sum[...]
        dk = dk + pltpu.roll(dk, HEAD_SIZE, 1)
        dk = dk * cos_ref[...] - swap_halves(dk) * sin_ref[...]
        dv = dv_sum[...]
        dv = dv + pltpu.roll(dv, HEAD_SIZE, 1)
        dkv_ref[...] = jnp.where(low_half(dk.shape), dk, dv).astype(BF16)


def attention_backward(grads, q_rot, k_rot, v_rows, lse, cos, sin, lengths):
    tokens = q_rot.shape[0]
    pairs = q_rot.shape[1] // LANES
    one = pl.BlockSpec((tokens, LANES), lambda j: (0, 0))
    each = pl.BlockSpec((tokens, LANES), lambda j: (0, j))
    return pl.pallas_call(
        attention_backward_kernel,
        grid=(pairs,),
        in_specs=[
            pl.BlockSpec(memory_space=pltpu.SMEM),
            each,
            each,
            one,
            one,
            pl.BlockSpec((1, tokens, LANES), lambda j: (j, 0, 0)),
            one,
            one,
        ],
        out_specs=[each, one],
        out_shape=[
            jax.ShapeDtypeStruct((tokens, pairs * LANES), BF16),
            jax.ShapeDtypeStruct((tokens, LANES), BF16),
        ],
        scratch_shapes=[pltpu.VMEM((tokens, LANES), F32), pltpu.VMEM((tokens, LANES), F32)],
        compiler_params=pltpu.CompilerParams(vmem_limit_bytes=VMEM_LIMIT),
        cost_estimate=pl.CostEstimate(
            flops=10 * tokens * tokens * LANES * pairs,
            bytes_accessed=12 * tokens * pairs * LANES,
            transcendentals=tokens * tokens * pairs,
        ),
        name="attend_back",
    )(lengths, grads, q_rot, k_rot, v_rows, lse, cos, sin)


def row_block(width):
    return pl.BlockSpec((ROWS, width), lambda i: (i, 0))


def fixed(*shape):
    return pl.BlockSpec(shape, lambda i: (0,) * len(shape))


def params():
    return pltpu.CompilerParams(vmem_limit_bytes=VMEM_LIMIT)


def cost(flops, *arrays):
    moved = sum(a.size * a.dtype.itemsize for a in arrays)
    return pl.CostEstimate(flops=flops, bytes_accessed=moved, transcendentals=0)


def mlp_back_kernel(
    grad_ref, a_ref, b_ref, hidden_ref, gain_ref, gate_ref, up_ref, down_ref, ggrad_ref, ugrad_ref, part_ref, gain_out
):
    mixed_grad = dot_nt(grad_ref[...], down_ref[...])
    ggrad = (mixed_grad * a_ref[...].astype(F32)).astype(BF16)
    ugrad = (mixed_grad * b_ref[...].astype(F32)).astype(BF16)
    ggrad_ref[...] = ggrad
    ugrad_ref[...] = ugrad
    normed_grad = dot_nt(ggrad, gate_ref[...]) + dot_nt(ugrad, up_ref[...])
    hidden = hidden_ref[...].astype(F32)
    r2 = lax.rsqrt(jnp.mean(hidden * hidden, axis=-1, keepdims=True) + EPSILON)
    gain_part = jnp.sum(normed_grad * (hidden * r2), axis=0, keepdims=True)

    @pl.when(pl.program_id(0) == 0)
    def _():
        gain_out[...] = jnp.zeros_like(gain_out)

    gain_out[...] += gain_part
    weighted = normed_grad * gain_ref[...]
    mean = jnp.mean(weighted * hidden, axis=-1, keepdims=True)
    part = r2 * weighted - hidden * (r2 * r2 * r2 * mean)
    own = part_ref.shape[2]
    for c in range(part_ref.shape[0]):
        part_ref[c] = part[:, c * own : (c + 1) * own].astype(BF16)


def mlp_backward(n, mlp_grad, a, b, hidden_all, gain, w_gate, w_up, w_down):
    total, width = hidden_all.shape
    own = width // n
    own_ff = w_gate.shape[1]
    narrow = jax.ShapeDtypeStruct((total, own_ff), BF16)
    planes = pl.BlockSpec((n, ROWS, own), lambda i: (0, i, 0))
    return pl.pallas_call(
        mlp_back_kernel,
        grid=(total // ROWS,),
        in_specs=[
            row_block(width),
            row_block(own_ff),
            row_block(own_ff),
            row_block(width),
            fixed(1, width),
            fixed(width, own_ff),
            fixed(width, own_ff),
            fixed(own_ff, width),
        ],
        out_specs=[row_block(own_ff), row_block(own_ff), planes, fixed(1, width)],
        out_shape=[narrow, narrow, jax.ShapeDtypeStruct((n, total, own), BF16), jax.ShapeDtypeStruct((1, width), F32)],
        compiler_params=params(),
        cost_estimate=cost(6 * total * width * own_ff, mlp_grad, hidden_all, hidden_all, w_gate, w_up, w_down, a, b, a, b),
        name="mlp_backward",
    )(mlp_grad, a, b, hidden_all, gain, w_gate, w_up, w_down)


def branch_kernel(part_ref, grad_ref, w_ref, hidden_ref, branch_ref, out_ref):
    hidden_grad = part_ref[...].astype(F32) + grad_ref[...].astype(F32)
    hidden_ref[...] = hidden_grad
    branch = (RESIDUAL_SCALE * hidden_grad).astype(BF16)
    branch_ref[...] = branch
    own = out_ref.shape[2]
    for c in range(out_ref.shape[0]):
        out_ref[c] = dot_nt(branch, w_ref[c]).astype(BF16)


def branch_backward(hidden_part, grad_own, w_out, n):
    total, own_width = hidden_part.shape
    own = w_out.shape[0] // n
    w_heads = w_out.reshape(n, own, own_width)
    return pl.pallas_call(
        branch_kernel,
        grid=(total // ROWS,),
        in_specs=[row_block(own_width), row_block(own_width), fixed(n, own, own_width)],
        out_specs=[row_block(own_width), row_block(own_width), pl.BlockSpec((n, ROWS, own), lambda i: (0, i, 0))],
        out_shape=[
            jax.ShapeDtypeStruct((total, own_width), F32),
            jax.ShapeDtypeStruct((total, own_width), BF16),
            jax.ShapeDtypeStruct((n, total, own), BF16),
        ],
        compiler_params=params(),
        cost_estimate=cost(2 * total * own_width * own * n, hidden_part, hidden_part, hidden_part, w_out),
        name="branch_backward",
    )(hidden_part, grad_own, w_heads)


def token_kernel(me_ref, dq_ref, dkv_ref, w_ref, x_ref, gain_ref, hidden_ref, part_ref, gain_out):
    split = dq_ref.shape[1]
    normed_grad = dot_nt(dq_ref[...], w_ref[:, :split]) + dot_nt(dkv_ref[...], w_ref[:, split:])
    x = x_ref[...].astype(F32)
    r1 = lax.rsqrt(jnp.mean(x * x, axis=-1, keepdims=True) + EPSILON)

    @pl.when(pl.program_id(0) == 0)
    def _():
        gain_out[...] = jnp.zeros_like(gain_out)

    gain_out[...] += jnp.sum(normed_grad * (x * r1), axis=0, keepdims=True)
    weighted = normed_grad * gain_ref[...]
    mean = jnp.mean(weighted * x, axis=-1, keepdims=True)
    part = r1 * weighted - x * (r1 * r1 * r1 * mean)
    own_width = hidden_ref.shape[1]
    for c in range(part.shape[1] // own_width):
        piece = part[:, c * own_width : (c + 1) * own_width]
        piece = piece + jnp.where(me_ref[0] == c, hidden_ref[...], 0.0)
        part_ref[:, c * own_width : (c + 1) * own_width] = piece.astype(BF16)


def token_backward(me, dq, dkv, w_qkv, x, gain, hidden_grad):
    total, width = x.shape
    own_width = hidden_grad.shape[1]
    return pl.pallas_call(
        token_kernel,
        grid=(total // ROWS,),
        in_specs=[
            pl.BlockSpec(memory_space=pltpu.SMEM),
            row_block(dq.shape[1]),
            row_block(dkv.shape[1]),
            fixed(*w_qkv.shape),
            row_block(width),
            fixed(1, width),
            row_block(own_width),
        ],
        out_specs=[row_block(width), fixed(1, width)],
        out_shape=[jax.ShapeDtypeStruct((total, width), BF16), jax.ShapeDtypeStruct((1, width), F32)],
        compiler_params=params(),
        cost_estimate=cost(2 * total * width * w_qkv.shape[1], x, x, w_qkv, dq, dkv, hidden_grad),
        name="token_backward",
    )(me, dq, dkv, w_qkv, x, gain, hidden_grad)


def spread_kernel(in_ref, out_ref):
    slab = in_ref.shape[2]
    for c in range(in_ref.shape[0]):
        out_ref[:, c * slab : (c + 1) * slab] = in_ref[c].astype(F32)


def spread_columns(pieces, slab, groups):
    n, rows, _ = pieces.shape
    tile = 128
    out_shape = jax.ShapeDtypeStruct((rows, groups * n * slab), F32)
    return pl.pallas_call(
        spread_kernel,
        grid=(groups, rows // tile),
        in_specs=[pl.BlockSpec((n, tile, slab), lambda f, r: (0, r, f))],
        out_specs=pl.BlockSpec((tile, n * slab), lambda f, r: (r, f)),
        out_shape=out_shape,
        compiler_params=params(),
        cost_estimate=cost(0, pieces, out_shape),
        name="spread_columns",
    )(pieces)


MESH = pl.DeviceIdType.MESH


class Chain:
    def __init__(self, slot, planes, plane, send_sem, recv_sem):
        self.slot, self.planes, self.plane = slot, planes, plane
        self.send_sem, self.recv_sem = send_sem, recv_sem

    def copy(self, way, step, shard, to):
        return pltpu.make_async_remote_copy(
            src_ref=self.slot(shard),
            dst_ref=self.slot(shard),
            send_sem=self.send_sem.at[way, step],
            recv_sem=self.recv_sem.at[way, step],
            device_id={"fsdp": to},
            device_id_type=MESH,
        )

    def moves(self, step):
        p, last = self.plane, self.planes - 1
        return (
            (0, (p >= step) & (p < last), p - step, p + 1, p >= step + 1, p - 1 - step),
            (1, (p + step <= last) & (p > 0), p + step, p - 1, p + step + 1 <= last, p + 1 + step),
        )

    def start(self, step):
        for way, sends, shard, to, _, _ in self.moves(step):

            @pl.when(sends)
            def _(way=way, shard=shard, to=to):
                self.copy(way, step, shard, to).start()

    def arrive(self, step):
        for way, _, _, _, receives, shard in self.moves(step):

            @pl.when(receives)
            def _(way=way, shard=shard):
                self.copy(way, step, shard, self.plane).wait_recv()

    def advance(self, step):
        self.arrive(step - 1)
        self.start(step)

    def drain(self):
        for step in range(self.planes - 1):
            for way, sends, shard, to, _, _ in self.moves(step):

                @pl.when(sends)
                def _(way=way, shard=shard, to=to, step=step):
                    self.copy(way, step, shard, to).wait_send()


class Spread:
    def __init__(self, src, slot, n, me, send_sem, recv_sem):
        self.src, self.slot, self.n, self.me = src, slot, n, me
        self.send_sem, self.recv_sem = send_sem, recv_sem
        self.chips = n // 2
        self.chip, self.core = me // 2, lax.rem(me, 2)
        self.partner = me + 1 - 2 * self.core

    def at(self, k):
        return lax.rem(self.chip + k, self.chips) * 2 + self.core

    def copy(self, src, owner, sem, to):
        return pltpu.make_async_remote_copy(
            src_ref=src,
            dst_ref=self.slot(owner),
            send_sem=self.send_sem.at[sem],
            recv_sem=self.recv_sem.at[sem],
            device_id={"ctx": to},
            device_id_type=MESH,
        )

    def out(self, k):
        return self.copy(self.src, self.me, k, self.at(k))

    def relay(self, k):
        owner = self.at(self.chips - k) if k else self.me
        src = self.slot(owner) if k else self.src
        return self.copy(src, owner, self.chips + k, self.partner)

    def start(self):
        for k in range(1, self.chips):
            self.out(k).start()
        self.relay(0).start()

    def pass_on(self):
        for k in range(1, self.chips):
            self.copy(self.src, self.at(self.chips - k), k, self.me).wait_recv()
            self.relay(k).start()

    def finish(self):
        other = 1 - 2 * self.core
        for k in range(self.chips):
            owner = (self.at(self.chips - k) if k else self.me) + other
            self.copy(self.slot(owner), owner, self.chips + k, self.me).wait_recv()

    def drain(self):
        for k in range(1, self.chips):
            self.out(k).wait_send()
        for k in range(self.chips):
            self.relay(k).wait_send()


def greet(n, planes, me, plane, across):
    barrier = pltpu.get_barrier_semaphore()
    chips = n // 2
    core = lax.rem(me, 2)
    others = [lax.rem(me // 2 + k, chips) * 2 + core for k in range(1, chips)] + [me + 1 - 2 * core]
    for other in others:
        pl.semaphore_signal(barrier, inc=1, device_id={"ctx": other}, device_id_type=MESH)
    if across:

        @pl.when(plane > 0)
        def _():
            pl.semaphore_signal(barrier, inc=1, device_id={"fsdp": plane - 1}, device_id_type=MESH)

        @pl.when(plane < planes - 1)
        def _():
            pl.semaphore_signal(barrier, inc=1, device_id={"fsdp": plane + 1}, device_id_type=MESH)

    count = len(others)
    if across:
        count = count + (plane > 0).astype(jnp.int32) + (plane < planes - 1).astype(jnp.int32)
    pl.semaphore_wait(barrier, count)


def forward_kernel(
    n,
    planes,
    heads,
    length_ref,
    tokens_ref,
    attn_shard,
    gate_shard,
    up_shard,
    down_shard,
    gain_shard,
    cos_ref,
    sin_ref,
    x_out,
    normed_out,
    q_out,
    k_out,
    v_out,
    lse_out,
    att_out,
    hid_out,
    normed2_out,
    a_out,
    b_out,
    mixed_out,
    attn_out,
    gate_out,
    up_out,
    down_out,
    gain_out,
    w_attn,
    w_gate,
    w_up,
    w_down,
    gains,
    x_all,
    qkv,
    q_rot,
    k_rot,
    v_rows,
    lse,
    own_att,
    att_all,
    own_hid,
    wide,
    narrow,
    z_send,
    z_recv,
    c_send,
    c_recv,
    keep_sem,
    wide_sem,
    narrow_sem,
):
    me, plane = lax.axis_index("ctx"), lax.axis_index("fsdp")
    per_device, width = tokens_ref.shape
    total = x_all.shape[0]
    rows_shard = attn_shard.shape[0]
    own = own_att.shape[1]
    own_width = own_hid.shape[1]
    columns = qkv.shape[1]
    blocks = total // ROWS
    pairs = heads // 2

    local_copies = []

    def keep(src, dst, index):
        copy = pltpu.make_async_copy(src, dst, keep_sem.at[index])
        copy.start()
        local_copies.append(copy)

    def chain(index, ref, rows):
        return Chain(lambda s: ref.at[pl.ds(s * rows, rows)], planes, plane, z_send.at[index], z_recv.at[index])

    attn_chain = chain(0, w_attn, rows_shard)
    gate_chain = chain(1, w_gate, rows_shard)
    up_chain = chain(2, w_up, rows_shard)
    down_chain = chain(3, w_down, down_shard.shape[0])
    gain_chain = chain(4, gains, gain_shard.shape[0])
    first = (attn_chain, attn_shard, 0), (gain_chain, gain_shard, 1), (gate_chain, gate_shard, 2), (up_chain, up_shard, 3), (down_chain, down_shard, 4)
    loads = [pltpu.make_async_copy(shard, c.slot(plane), keep_sem.at[i]) for c, shard, i in first]
    for load in loads:
        load.start()
    own_x = pltpu.make_async_copy(tokens_ref, x_all.at[pl.ds(me * per_device, per_device)], keep_sem.at[5])
    own_x.start()
    greet(n, planes, me, plane, True)
    loads[0].wait()
    attn_chain.start(0)
    loads[1].wait()
    gain_chain.start(0)
    x_spread = Spread(
        tokens_ref, lambda c: x_all.at[pl.ds(c * per_device, per_device)], n, me, c_send.at[0], c_recv.at[0]
    )
    x_spread.start()
    for load in loads[2:]:
        load.wait()
    own_x.wait()
    for step in range(1, planes - 1):
        attn_chain.advance(step)
        gain_chain.advance(step)
    gate_chain.start(0)
    up_chain.start(0)
    x_spread.pass_on()
    x_spread.finish()
    x_copy = pltpu.make_async_copy(x_all, x_out, keep_sem.at[0])
    x_copy.start()
    attn_chain.arrive(planes - 2)
    gain_chain.arrive(planes - 2)
    keep(w_attn, attn_out, 1)
    keep(gains, gain_out, 2)
    half = gain_shard.shape[1] // 2
    step_rows = gain_shard.shape[0]
    attn_gain = jnp.concatenate([gains[f * step_rows : f * step_rows + 1, :half] for f in range(planes)], axis=1)
    mlp_gain = jnp.concatenate([gains[f * step_rows : f * step_rows + 1, half:] for f in range(planes)], axis=1)

    def staged(stage, sem, slot, out, rows, wait_before):
        copy = pltpu.make_async_copy(stage.at[slot], out.at[rows], sem.at[slot])
        return copy.wait() if wait_before else copy.start()

    def project_block(i, _):
        rows = pl.ds(pl.multiple_of(i * ROWS, ROWS), ROWS)
        slot = lax.rem(i, 2)

        @pl.when(i >= 2)
        def _():
            staged(wide, wide_sem, slot, normed_out, rows, True)

        own_hid[rows, :] = x_all[rows, pl.ds(pl.multiple_of(me * own_width, LANES), own_width)]
        x = x_all[rows, :].astype(F32)
        r1 = lax.rsqrt(jnp.mean(x * x, axis=-1, keepdims=True) + EPSILON)
        normed = (x * r1 * attn_gain).astype(BF16)
        wide[slot] = normed
        staged(wide, wide_sem, slot, normed_out, rows, False)
        qkv[rows, :] = dot_nn(normed, w_attn[:, :columns])
        return 0

    lax.fori_loop(0, blocks, project_block, 0)
    for i in range(max(blocks - 2, 0), blocks):
        staged(wide, wide_sem, i % 2, normed_out, pl.ds(i * ROWS, ROWS), True)

    split = columns - LANES
    cos, sin = cos_ref[...], sin_ref[...]
    kv = qkv[:, split:]
    turned = pltpu.roll(kv, HEAD_SIZE, 1)
    low = low_half(kv.shape)
    k = jnp.where(low, kv, turned)
    k_rot[...] = (k * cos + swap_halves(k) * sin).astype(BF16)
    v_rows[...] = jnp.where(low, turned, kv).astype(BF16)
    keep(k_rot, k_out, 3)
    keep(v_rows, v_out, 4)
    first_len = length_ref[0]

    def attend_pair(pair, _):
        lanes = pl.ds(pl.multiple_of(pair * LANES, LANES), LANES)
        q = qkv[:, lanes]
        q_rot[:, lanes] = ((q * cos_ref[...] + swap_halves(q) * sin_ref[...]) * SCORE_SCALE).astype(BF16)
        for block in range(blocks):
            rows = pl.ds(block * ROWS, ROWS)
            end = (block + 1) * ROWS
            bias = mask_bias(first_len, block * ROWS, ROWS, end)
            query = q_rot[rows, lanes]
            lower = low_half(query.shape)
            keys, values = k_rot[:end, :], v_rows[:end, :]
            parts = []
            for side in range(2):
                chosen = lower if side == 0 else jnp.logical_not(lower)
                scores = dot_nt(jnp.where(chosen, query, jnp.zeros_like(query)), keys) + bias
                top = jnp.max(scores, axis=-1, keepdims=True)
                weights = jnp.exp(scores - top)
                whole = jnp.sum(weights, axis=-1, keepdims=True)
                probs = (weights * (1.0 / whole)).astype(BF16)
                parts.append(dot_nn(probs, values))
                lse[pair, rows, side : side + 1] = top + jnp.log(whole)
            own_att[rows, lanes] = jnp.where(low_half(parts[0].shape), parts[0], parts[1]).astype(BF16)
        return 0

    lax.fori_loop(0, pairs, attend_pair, 0)
    att_spread = Spread(own_att, lambda c: att_all.at[c], n, me, c_send.at[1], c_recv.at[1])
    x_copy.wait()
    x_spread.drain()
    att_spread.start()
    own_a = pltpu.make_async_copy(own_att, att_all.at[me], keep_sem.at[5])
    own_a.start()
    keep(q_rot, q_out, 6)
    keep(lse, lse_out, 7)
    if planes > 2:
        gate_chain.advance(1)
        up_chain.advance(1)
    att_spread.pass_on()
    own_a.wait()
    att_spread.finish()
    keep(att_all, att_out, 8)

    def out_block(i, _):
        rows = pl.ds(pl.multiple_of(i * ROWS, ROWS), ROWS)
        acc = jnp.zeros((ROWS, own_width), F32)
        for c in range(n):
            acc += dot_nn(att_all[c, rows, :], w_attn[c * own : (c + 1) * own, columns:])
        own_hid[rows, :] = (own_hid[rows, :].astype(F32) + RESIDUAL_SCALE * acc).astype(BF16)
        return 0

    lax.fori_loop(0, blocks, out_block, 0)
    def hid_slot(c):
        return x_all.at[:, pl.ds(pl.multiple_of(c * own_width, LANES), own_width)]

    hid_spread = Spread(own_hid, hid_slot, n, me, c_send.at[2], c_recv.at[2])
    hid_spread.start()
    own_h = pltpu.make_async_copy(own_hid, hid_slot(me), keep_sem.at[5])
    own_h.start()
    for step in range(2, planes - 1):
        gate_chain.advance(step)
        up_chain.advance(step)
    down_chain.start(0)
    hid_spread.pass_on()
    own_h.wait()
    hid_spread.finish()
    keep(x_all, hid_out, 9)
    gate_chain.arrive(planes - 2)
    up_chain.arrive(planes - 2)
    keep(w_gate, gate_out, 10)
    keep(w_up, up_out, 11)
    if planes > 2:
        down_chain.advance(1)

    def mlp_copies(i, rows, wait):
        slot = lax.rem(i, 2)
        staged(wide, wide_sem, slot, normed2_out, rows, wait)
        for j, out in enumerate((a_out, b_out, mixed_out)):
            staged(narrow.at[j], narrow_sem.at[j], slot, out, rows, wait)

    def mlp_block(i, _):
        rows = pl.ds(pl.multiple_of(i * ROWS, ROWS), ROWS)
        slot = lax.rem(i, 2)

        @pl.when(i >= 2)
        def _():
            mlp_copies(i, rows, True)

        hidden = x_all[rows, :].astype(F32)
        r2 = lax.rsqrt(jnp.mean(hidden * hidden, axis=-1, keepdims=True) + EPSILON)
        normed = (hidden * r2 * mlp_gain).astype(BF16)
        wide[slot] = normed
        gate = dot_nn(normed, w_gate[...])
        up = dot_nn(normed, w_up[...])
        sig = jax.nn.sigmoid(gate)
        silu = gate * sig
        narrow[2, slot] = (silu * up).astype(BF16)
        narrow[1, slot] = silu.astype(BF16)
        narrow[0, slot] = (up * sig * (1.0 + gate * (1.0 - sig))).astype(BF16)
        mlp_copies(i, rows, False)
        return 0

    lax.fori_loop(0, blocks, mlp_block, 0)
    for step in range(2, planes - 1):
        down_chain.advance(step)
    for i in range(max(blocks - 2, 0), blocks):
        mlp_copies(i, pl.ds(i * ROWS, ROWS), True)
    down_chain.arrive(planes - 2)
    keep(w_down, down_out, 12)
    for c in (attn_chain, gain_chain, gate_chain, up_chain, down_chain):
        c.drain()
    for s in (att_spread, hid_spread):
        s.drain()
    for copy in local_copies:
        copy.wait()


def forward(n, planes, heads, lengths, tokens, attn_shard, gate_shard, up_shard, down_shard, gain_shard, cos, sin):
    per_device, width = tokens.shape
    total = per_device * n
    own = heads * HEAD_SIZE
    columns = own + 2 * HEAD_SIZE
    own_width = attn_shard.shape[1] - columns
    own_ff = gate_shard.shape[1]
    rows_shard = attn_shard.shape[0]
    pairs = heads // 2
    weights = [
        ((planes * rows_shard, attn_shard.shape[1]), BF16),
        ((planes * rows_shard, own_ff), BF16),
        ((planes * rows_shard, own_ff), BF16),
        ((planes * down_shard.shape[0], width), BF16),
        ((planes * gain_shard.shape[0], gain_shard.shape[1]), F32),
    ]
    outs = [
        ((total, width), BF16),
        ((total, width), BF16),
        ((total, own), BF16),
        ((total, LANES), BF16),
        ((total, LANES), BF16),
        ((pairs, total, LANES), F32),
        ((n, total, own), BF16),
        ((total, width), BF16),
        ((total, width), BF16),
        ((total, own_ff), BF16),
        ((total, own_ff), BF16),
        ((total, own_ff), BF16),
    ] + weights
    scratch = weights + [
        ((total, width), BF16),
        ((total, columns), F32),
        ((total, own), BF16),
        ((total, LANES), BF16),
        ((total, LANES), BF16),
        ((pairs, total, LANES), F32),
        ((total, own), BF16),
        ((n, total, own), BF16),
        ((total, own_width), BF16),
        ((2, ROWS, width), BF16),
        ((3, 2, ROWS, own_ff), BF16),
    ]
    steps = max(planes - 1, 1)
    dma = pltpu.SemaphoreType.DMA
    anywhere = pl.BlockSpec(memory_space=pl.ANY)
    vmem = pl.BlockSpec(memory_space=pltpu.VMEM)
    return pl.pallas_call(
        functools.partial(forward_kernel, n, planes, heads),
        in_specs=[pl.BlockSpec(memory_space=pltpu.SMEM), vmem] + [anywhere] * 5 + [vmem] * 2,
        out_specs=[anywhere] * len(outs),
        out_shape=[jax.ShapeDtypeStruct(*o) for o in outs],
        scratch_shapes=[pltpu.VMEM(*s) for s in scratch]
        + [dma((5, 2, steps)), dma((5, 2, steps)), dma((3, n)), dma((3, n)), dma((16,)), dma((2,)), dma((3, 2))],
        compiler_params=pltpu.CompilerParams(
            vmem_limit_bytes=VMEM_LIMIT, collective_id=1, has_side_effects=True
        ),
        cost_estimate=pl.CostEstimate(
            flops=2 * total * width * (columns + own_width + 2 * own_ff),
            bytes_accessed=60 * 1024 * 1024,
            transcendentals=0,
        ),
        name="forward",
    )(lengths, tokens, attn_shard, gate_shard, up_shard, down_shard, gain_shard, cos, sin)


CHUNK = 64


def add_into(dst, src):
    def step(i, _):
        rows = pl.ds(pl.multiple_of(i * CHUNK, CHUNK), CHUNK)
        dst[rows, :] = (dst[rows, :].astype(F32) + src[rows, :].astype(F32)).astype(dst.dtype)
        return 0

    if dst.shape[0] <= CHUNK:
        dst[...] = dst[...] + src[...]
    else:
        lax.fori_loop(0, dst.shape[0] // CHUNK, step, 0)


def fetch(src, dst, sem):
    copy = pltpu.make_async_copy(src, dst, sem)
    copy.start()
    copy.wait()


class Settle:
    def __init__(self, block, landed, stage, planes, plane, send_sem, recv_sem, load_sem):
        self.block, self.landed, self.stage = block, landed, stage
        self.planes, self.plane = planes, plane
        self.send_sem, self.recv_sem, self.load_sem = send_sem, recv_sem, load_sem

    def slot(self, way, shard, at):
        return shard if way == 0 else jnp.where(shard == at, self.planes, shard)

    def sends(self, step):
        p, last = self.plane, self.planes - 1
        return (
            (0, (p <= step) & (p < last), last - step + p, p + 1),
            (1, (last - p <= step) & (p > 0), step - last + p, p - 1),
        )

    def receives(self, step):
        p, last = self.plane, self.planes - 1
        return (
            (0, (p >= 1) & (p - 1 <= step), last - step + p - 1),
            (1, (p <= last - 1) & (last - p - 1 <= step), step - last + p + 1),
        )

    def copy(self, way, step, shard, to):
        return pltpu.make_async_remote_copy(
            src_ref=self.block(shard),
            dst_ref=self.landed.at[self.slot(way, shard, to)],
            send_sem=self.send_sem.at[way, step],
            recv_sem=self.recv_sem.at[way, step],
            device_id={"fsdp": to},
            device_id_type=MESH,
        )

    def start(self, step=0):
        for way, active, shard, to in self.sends(step):

            @pl.when(active)
            def _(way=way, shard=shard, to=to):
                self.copy(way, step, shard, to).start()

    def take(self, step):
        for way, active, shard in self.receives(step):

            @pl.when(active)
            def _(way=way, shard=shard):
                self.copy(way, step, shard, self.plane).wait_recv()
                fetch(self.landed.at[self.slot(way, shard, self.plane)], self.stage, self.load_sem)
                add_into(self.block(shard), self.stage)

    def advance(self, step):
        self.take(step - 1)
        self.start(step)

    def drain(self):
        for step in range(self.planes - 1):
            for way, active, shard, to in self.sends(step):

                @pl.when(active)
                def _(way=way, shard=shard, to=to, step=step):
                    self.copy(way, step, shard, to).wait_send()


class Scatter:
    def __init__(self, block, near, far, stage, n, me, send_sem, recv_sem, load_sem):
        self.block, self.near, self.far, self.stage = block, near, far, stage
        self.send_sem, self.recv_sem, self.load_sem = send_sem, recv_sem, load_sem
        self.chips = n // 2
        self.me, self.chip, self.core = me, me // 2, lax.rem(me, 2)

    def target(self, k, core):
        return lax.rem(self.chip + k, self.chips) * 2 + core

    def copy(self, k, sem, src, dst, to):
        return pltpu.make_async_remote_copy(
            src_ref=src,
            dst_ref=dst.at[k],
            send_sem=self.send_sem.at[sem],
            recv_sem=self.recv_sem.at[sem],
            device_id={"ctx": to},
            device_id_type=MESH,
        )

    def first(self, k):
        other = 1 - self.core
        return self.copy(k, k, self.block(self.target(k, other)), self.near, self.chip * 2 + other)

    def second(self, k):
        target = self.target(k, self.core)
        return self.copy(k, self.chips + k, self.block(target), self.far, target)

    def start(self):
        for k in range(self.chips):
            self.first(k).start()

    def pass_on(self):
        for k in range(1, self.chips):
            self.first(k).wait_recv()
            fetch(self.near.at[k], self.stage, self.load_sem)
            add_into(self.block(self.target(k, self.core)), self.stage)
            self.second(k).start()

    def finish(self, total):
        self.first(0).wait_recv()
        fetch(self.near.at[0], self.stage, self.load_sem)
        add_into(total, self.stage)
        for k in range(1, self.chips):
            self.second(k).wait_recv()
            fetch(self.far.at[k], self.stage, self.load_sem)
            add_into(total, self.stage)

    def drain(self):
        for k in range(self.chips):
            self.first(k).wait_send()
        for k in range(1, self.chips):
            self.second(k).wait_send()


def backward_kernel(
    n,
    planes,
    heads,
    length_ref,
    grad_in,
    mixed_in,
    a_in,
    b_in,
    hidden_in,
    normed2_in,
    normed_in,
    x_in,
    att_in,
    q_in,
    k_in,
    v_in,
    lse_in,
    cos_in,
    sin_in,
    attn_in,
    gate_in,
    up_in,
    down_in,
    gain_in,
    token_out,
    gain_out,
    down_all,
    gate_all,
    up_all,
    out_all,
    qkv_all,
    near1,
    far1,
    near2,
    far2,
    near3,
    far3,
    down_landed,
    gate_landed,
    up_landed,
    out_landed,
    qkv_landed,
    w_attn,
    w_gate,
    w_up,
    w_down,
    p_down,
    gains,
    grad,
    a_v,
    b_v,
    part,
    hid_stage,
    stage_tall,
    stage_wide,
    stage_col,
    hidden_grad,
    lse,
    cos,
    sin,
    dk_sum,
    dv_sum,
    gain_own,
    gain_all,
    gain_landed,
    gain_stage,
    z_send,
    z_recv,
    s_send,
    s_recv,
    g_send,
    g_recv,
    load_sem,
    hid_sem,
    add_sem,
):
    me, plane = lax.axis_index("ctx"), lax.axis_index("fsdp")
    total, width = grad.shape
    per_device = total // n
    own = heads * HEAD_SIZE
    own_width = width // n
    own_ff = a_v.shape[1]
    rows_shard = width // planes
    slab = own_ff // planes
    blocks = total // ROWS
    pairs = heads // 2
    columns = own + LANES
    last = planes - 2

    def load(src, dst, index):
        copy = pltpu.make_async_copy(src, dst, load_sem.at[index])
        copy.start()
        return copy

    mixed_loads = [load(mixed_in.at[:, pl.ds(d * own_width, own_width)], part.at[d], d) for d in range(own_ff // own_width)]
    grad_load = load(grad_in, grad, 8)
    down_load = load(down_in, w_down, 9)
    gate_load = load(gate_in, w_gate, 10)
    up_load = load(up_in, w_up, 11)
    a_load = load(a_in, a_v, 12)
    b_load = load(b_in, b_v, 13)
    attn_load = load(attn_in, w_attn, 14)
    gain_load = load(gain_in, gains, 15)
    greet(n, planes, me, plane, True)

    def settle(index, block, landed, stage):
        return Settle(block, landed, stage, planes, plane, z_send.at[index], z_recv.at[index], add_sem)

    def rows_of(ref, rows):
        return lambda d: ref.at[pl.ds(pl.multiple_of(d * rows, rows), rows)]

    def out_block_of(d):
        return w_down.at[pl.ds(0, rows_shard), pl.ds(pl.multiple_of(d * own_width, LANES), own_width)]

    def qkv_block_of(d):
        return w_down.at[pl.ds(rows_shard, rows_shard), pl.ds(pl.multiple_of(d * columns, LANES), columns)]

    def gain_block_of(d):
        return gain_own.at[:, pl.ds(pl.multiple_of(d * rows_shard, LANES), rows_shard)]

    down_sum = settle(0, rows_of(p_down, slab), down_landed, stage_wide)
    gate_sum = settle(1, rows_of(w_gate, rows_shard), gate_landed, stage_tall)
    up_sum = settle(2, rows_of(w_up, rows_shard), up_landed, stage_tall)
    out_sum = settle(3, out_block_of, out_landed, stage_tall.at[:, pl.ds(0, own_width)])
    qkv_sum = settle(4, qkv_block_of, qkv_landed, stage_tall.at[:, pl.ds(0, columns)])
    gain_sum = settle(5, gain_block_of, gain_landed, gain_stage)

    def spread(index, src, dst):
        return Spread(src, lambda c: dst.at[c], n, me, g_send.at[index], g_recv.at[index])

    spreads = []

    def give(index, sums, dst):
        sums.take(last)
        src = sums.block(plane)
        mine = load(src, dst.at[me], 16 + index)
        out = spread(index, src, dst)
        out.start()
        spreads.append((out, mine))
        return out

    def scatter(index, block, near, far, stage):
        return Scatter(block, near, far, stage, n, me, s_send.at[index], s_recv.at[index], add_sem)

    grad_load.wait()

    def scale_block(i, _):
        rows = pl.ds(pl.multiple_of(i * ROWS, ROWS), ROWS)
        grad[rows, :] = (RESIDUAL_SCALE * grad[rows, :].astype(F32)).astype(BF16)
        return 0

    lax.fori_loop(0, blocks, scale_block, 0)
    for copy in mixed_loads:
        copy.wait()

    def down_block(d, _):
        p_down[pl.ds(pl.multiple_of(d * own_width, own_width), own_width), :] = dot_tn(part[d], grad[...]).astype(BF16)
        return 0

    lax.fori_loop(0, own_ff // own_width, down_block, 0)
    down_sum.start()

    for copy in (down_load, gate_load, up_load, a_load, b_load, attn_load, gain_load):
        copy.wait()
    half = gains.shape[1] // 2
    attn_gain = jnp.concatenate([gains[f * 8 : f * 8 + 1, :half] for f in range(planes)], axis=1)
    mlp_gain = jnp.concatenate([gains[f * 8 : f * 8 + 1, half:] for f in range(planes)], axis=1)
    gain_own[...] = jnp.zeros_like(gain_own)

    def stream(src, i, wait):
        rows = pl.ds(pl.multiple_of(i * ROWS, ROWS), ROWS)
        slot = lax.rem(i, 2)
        copy = pltpu.make_async_copy(src.at[rows], hid_stage.at[slot], hid_sem.at[slot])
        return copy.wait() if wait else copy.start()

    stream(hidden_in, jnp.int32(0), False)

    def mlp_block(i, _):
        rows = pl.ds(pl.multiple_of(i * ROWS, ROWS), ROWS)

        @pl.when(i + 1 < blocks)
        def _():
            stream(hidden_in, i + 1, False)

        mixed_grad = dot_nt(grad[rows, :], w_down[...])
        ggrad = (mixed_grad * a_v[rows, :].astype(F32)).astype(BF16)
        ugrad = (mixed_grad * b_v[rows, :].astype(F32)).astype(BF16)
        a_v[rows, :] = ggrad
        b_v[rows, :] = ugrad
        normed_grad = dot_nt(ggrad, w_gate[...]) + dot_nt(ugrad, w_up[...])
        stream(hidden_in, i, True)
        hidden = hid_stage[lax.rem(i, 2)].astype(F32)
        r2 = lax.rsqrt(jnp.mean(hidden * hidden, axis=-1, keepdims=True) + EPSILON)
        gain_own[0:1, :] += jnp.sum(normed_grad * (hidden * r2), axis=0, keepdims=True)
        weighted = normed_grad * mlp_gain
        mean = jnp.mean(weighted * hidden, axis=-1, keepdims=True)
        piece = r2 * weighted - hidden * (r2 * r2 * r2 * mean)
        for c in range(n):
            part[c, rows, :] = piece[:, c * own_width : (c + 1) * own_width].astype(BF16)
        return 0

    lax.fori_loop(0, blocks, mlp_block, 0)
    first = scatter(0, lambda c: part.at[c], near1, far1, stage_col)
    first.start()
    normed2_load = load(normed2_in, grad, 8)
    down_sum.advance(1)
    normed2_load.wait()

    def columns_times(right, out):
        def block(j, _):
            lanes = pl.ds(pl.multiple_of(j * ROWS, ROWS), ROWS)
            out[lanes, :] = dot_tn(grad[:, lanes], right[...]).astype(BF16)
            return 0

        lax.fori_loop(0, width // ROWS, block, 0)

    columns_times(a_v, w_gate)
    gate_sum.start()
    first.pass_on()
    columns_times(b_v, w_up)
    up_sum.start()

    att_loads = [load(att_in.at[c], grad.at[:, pl.ds(c * own, own)], c) for c in range(n)]
    own_grad = load(grad_in.at[:, pl.ds(pl.multiple_of(me * own_width, LANES), own_width)], b_v.at[:, pl.ds(LANES, own_width)], 8)
    q_load = load(q_in, a_v.at[:, pl.ds(0, own)], 9)
    k_load = load(k_in, a_v.at[:, pl.ds(own, LANES)], 10)
    v_load = load(v_in, a_v.at[:, pl.ds(own + LANES, LANES)], 11)
    lse_load = load(lse_in, lse, 12)
    cos_load = load(cos_in, cos, 13)
    sin_load = load(sin_in, sin, 14)
    own_grad.wait()

    def begin(i, _):
        rows = pl.ds(pl.multiple_of(i * ROWS, ROWS), ROWS)
        hidden_grad[rows, :] = b_v[rows, LANES : LANES + own_width].astype(F32) + part[me, rows, :].astype(F32)
        return 0

    lax.fori_loop(0, blocks, begin, 0)
    first.finish(hidden_grad)
    first.drain()
    if planes > 3:
        down_sum.advance(2)

    def branch_block(i, _):
        rows = pl.ds(pl.multiple_of(i * ROWS, ROWS), ROWS)
        branch = (RESIDUAL_SCALE * hidden_grad[rows, :]).astype(BF16)
        b_v[rows, LANES : LANES + own_width] = branch
        for c in range(n):
            part[c, rows, :] = dot_nt(branch, w_attn[c * own : (c + 1) * own, columns:]).astype(BF16)
        return 0

    lax.fori_loop(0, blocks, branch_block, 0)
    second = scatter(1, lambda c: part.at[c], near2, far2, stage_col)
    second.start()
    gate_sum.advance(1)
    for copy in att_loads:
        copy.wait()
    heads_per_shard = rows_shard // own
    for c in range(n):
        place = out_block_of(c // heads_per_shard).at[pl.ds((c % heads_per_shard) * own, own)]
        place[...] = dot_tn(grad[:, c * own : (c + 1) * own], b_v[:, LANES : LANES + own_width]).astype(BF16)
    second.pass_on()
    up_sum.advance(1)
    out_sum.start()
    normed_load = load(normed_in, grad, 15)
    down_give = give(0, down_sum, down_all)
    second.finish(part.at[me])
    if planes > 3:
        gate_sum.advance(2)

    for copy in (q_load, k_load, v_load, lse_load, cos_load, sin_load):
        copy.wait()
    dk_sum[...] = jnp.zeros_like(dk_sum)
    dv_sum[...] = jnp.zeros_like(dv_sum)
    first_len = length_ref[0]
    dq_at = own + 2 * LANES

    def attend_pair(pair, _):
        lanes = pl.ds(pl.multiple_of(pair * LANES, LANES), LANES)
        dq_lanes = pl.ds(pl.multiple_of(dq_at + pair * LANES, LANES), LANES)
        for block in range(blocks):
            rows = pl.ds(block * ROWS, ROWS)
            end = (block + 1) * ROWS
            bias = mask_bias(first_len, block * ROWS, ROWS, end)
            query, grads = a_v[rows, lanes], part[me, rows, lanes]
            low = low_half(query.shape)
            keys, values = a_v[:end, own : own + LANES], a_v[:end, own + LANES : own + 2 * LANES]
            parts = []
            for side in range(2):
                chosen = low if side == 0 else jnp.logical_not(low)
                own_query = jnp.where(chosen, query, jnp.zeros_like(query))
                own_grads = jnp.where(chosen, grads, jnp.zeros_like(grads))
                scores = dot_nt(own_query, keys) + bias
                probs = jnp.exp(scores - lse[pair, rows, side : side + 1])
                prob_grad = dot_nt(own_grads, values)
                delta = jnp.sum(probs * prob_grad, axis=-1, keepdims=True)
                score_grad = (probs * (prob_grad - delta)).astype(BF16)
                parts.append(dot_nn(score_grad, keys))
                dk_sum[:end, :] += dot_tn(score_grad, own_query)
                dv_sum[:end, :] += dot_tn(probs.astype(BF16), own_grads)
            dq = jnp.where(low_half(parts[0].shape), parts[0], parts[1]) * SCORE_SCALE
            a_v[rows, dq_lanes] = (dq * cos[rows, :] - swap_halves(dq) * sin[rows, :]).astype(BF16)
        return 0

    lax.fori_loop(0, pairs, attend_pair, 0)
    dk = dk_sum[...]
    dk = dk + pltpu.roll(dk, HEAD_SIZE, 1)
    dk = dk * cos[...] - swap_halves(dk) * sin[...]
    dv = dv_sum[...]
    dv = dv + pltpu.roll(dv, HEAD_SIZE, 1)
    b_v[:, :LANES] = jnp.where(low_half(dk.shape), dk, dv).astype(BF16)
    if planes > 3:
        up_sum.advance(2)
    out_sum.advance(1)

    normed_load.wait()
    dq_end = dq_at + own
    for d in range(planes):
        for j in range(rows_shard // ROWS):
            lanes = slice(d * rows_shard + j * ROWS, d * rows_shard + (j + 1) * ROWS)
            place = qkv_block_of(d).at[pl.ds(j * ROWS, ROWS)]
            place[:, :own] = dot_tn(grad[:, lanes], a_v[:, dq_at:dq_end]).astype(BF16)
            place[:, own:] = dot_tn(grad[:, lanes], b_v[:, :LANES]).astype(BF16)
    qkv_sum.start()
    if planes > 3:
        out_sum.advance(2)
    down_give.pass_on()

    stream(x_in, jnp.int32(0), False)

    def token_block(i, _):
        rows = pl.ds(pl.multiple_of(i * ROWS, ROWS), ROWS)

        @pl.when(i + 1 < blocks)
        def _():
            stream(x_in, i + 1, False)

        normed_grad = dot_nt(a_v[rows, dq_at:dq_end], w_attn[:, :own]) + dot_nt(b_v[rows, :LANES], w_attn[:, own:columns])
        stream(x_in, i, True)
        x = hid_stage[lax.rem(i, 2)].astype(F32)
        r1 = lax.rsqrt(jnp.mean(x * x, axis=-1, keepdims=True) + EPSILON)
        gain_own[1:2, :] += jnp.sum(normed_grad * (x * r1), axis=0, keepdims=True)
        weighted = normed_grad * attn_gain
        mean = jnp.mean(weighted * x, axis=-1, keepdims=True)
        piece = r1 * weighted - x * (r1 * r1 * r1 * mean)
        for c in range(n):
            lanes = slice(c * own_width, (c + 1) * own_width)
            mine = jnp.where(me == c, hidden_grad[rows, :], 0.0)
            grad[rows, lanes] = (piece[:, lanes] + mine).astype(BF16)
        return 0

    lax.fori_loop(0, blocks, token_block, 0)

    def token_rows(c):
        return grad.at[pl.ds(pl.multiple_of(c * per_device, per_device), per_device)]

    third = scatter(2, token_rows, near3, far3, stage_wide.at[pl.ds(0, per_device)])
    third.start()
    gain_give = spread(5, gain_own, gain_all)
    gain_mine = load(gain_own, gain_all.at[me], 21)
    gain_give.start()
    qkv_sum.advance(1)
    gate_give = give(1, gate_sum, gate_all)
    third.pass_on()
    gain_give.pass_on()
    if planes > 3:
        qkv_sum.advance(2)
    up_give = give(2, up_sum, up_all)
    gain_give.finish()
    gain_mine.wait()
    gain_give.drain()
    gain_own[...] = sum(gain_all[c] for c in range(n))
    gain_sum.start()
    token_out[...] = token_rows(me)[...].astype(F32)
    third.finish(token_out)
    gain_sum.advance(1)
    out_give = give(3, out_sum, out_all)
    if planes > 3:
        gain_sum.advance(2)
    gate_give.pass_on()
    qkv_give = give(4, qkv_sum, qkv_all)
    up_give.pass_on()
    out_give.pass_on()
    gain_sum.take(last)
    gain_out[...] = gain_block_of(plane)[...]
    qkv_give.pass_on()
    for out, mine in spreads:
        out.finish()
        out.drain()
        mine.wait()
    for s in (second, third):
        s.drain()
    for s in (down_sum, gate_sum, up_sum, out_sum, qkv_sum, gain_sum):
        s.drain()


def backward(n, planes, heads, lengths, grad, saved, weights, cos, sin):
    x, normed, q_rot, k_rot, v_rows, lse, att_all, hidden, normed2, a, b, mixed = saved
    w_attn, w_gate, w_up, w_down, gains = weights
    total, width = grad.shape
    own = heads * HEAD_SIZE
    own_width = width // n
    own_ff = a.shape[1]
    rows_shard = width // planes
    slab = own_ff // planes
    columns = own + LANES
    chips = n // 2
    per_device = total // n
    col, row = (chips, total, own_width), (chips, per_device, width)
    outs = [
        ((per_device, width), F32),
        ((8, rows_shard), F32),
        ((n, slab, width), BF16),
        ((n, rows_shard, own_ff), BF16),
        ((n, rows_shard, own_ff), BF16),
        ((n, rows_shard, own_width), BF16),
        ((n, rows_shard, columns), BF16),
        (col, BF16),
        (col, BF16),
        (col, BF16),
        (col, BF16),
        (row, BF16),
        (row, BF16),
        ((planes + 1, slab, width), BF16),
        ((planes + 1, rows_shard, own_ff), BF16),
        ((planes + 1, rows_shard, own_ff), BF16),
        ((planes + 1, rows_shard, own_width), BF16),
        ((planes + 1, rows_shard, columns), BF16),
    ]
    scratch = [
        (w_attn.shape, BF16),
        (w_gate.shape, BF16),
        (w_up.shape, BF16),
        (w_down.shape, BF16),
        (w_down.shape, BF16),
        (gains.shape, F32),
        ((total, width), BF16),
        ((total, own_ff), BF16),
        ((total, own_ff), BF16),
        ((n, total, own_width), BF16),
        ((2, ROWS, width), BF16),
        ((rows_shard, own_ff), BF16),
        ((slab, width), BF16),
        ((total, own_width), BF16),
        ((total, own_width), F32),
        (lse.shape, F32),
        (cos.shape, F32),
        (sin.shape, F32),
        ((total, LANES), F32),
        ((total, LANES), F32),
        ((8, width), F32),
        ((n, 8, width), F32),
        ((planes + 1, 8, rows_shard), F32),
        ((8, rows_shard), F32),
    ]
    steps = planes - 1
    dma = pltpu.SemaphoreType.DMA
    anywhere = pl.BlockSpec(memory_space=pl.ANY)
    vmem = pl.BlockSpec(memory_space=pltpu.VMEM)
    return pl.pallas_call(
        functools.partial(backward_kernel, n, planes, heads),
        in_specs=[pl.BlockSpec(memory_space=pltpu.SMEM)] + [anywhere] * 20,
        out_specs=[vmem] * 2 + [anywhere] * (len(outs) - 2),
        out_shape=[jax.ShapeDtypeStruct(*o) for o in outs],
        scratch_shapes=[pltpu.VMEM(*s) for s in scratch]
        + [
            dma((6, 2, steps)),
            dma((6, 2, steps)),
            dma((3, n)),
            dma((3, n)),
            dma((6, n)),
            dma((6, n)),
            dma((24,)),
            dma((2,)),
            dma,
        ],
        compiler_params=pltpu.CompilerParams(
            vmem_limit_bytes=60 * 1024 * 1024, collective_id=2, has_side_effects=True
        ),
        cost_estimate=pl.CostEstimate(
            flops=16 * total * width * own_ff, bytes_accessed=100 * 1024 * 1024, transcendentals=0
        ),
        name="backward",
    )(
        lengths,
        grad,
        mixed,
        a,
        b,
        hidden,
        normed2,
        normed,
        x,
        att_all,
        q_rot,
        k_rot,
        v_rows,
        lse,
        cos,
        sin,
        w_attn,
        w_gate,
        w_up,
        w_down,
        gains,
    )[:7]


def kernel_fits(n, planes, total, width, own_ff):
    held = 4 * width * own_ff + 2 * total * width + 2 * total * own_ff
    return planes in (3, 4) and own_ff // planes >= total // n and n * own_ff >= 4 * width and 2 * held < 44 * 1024 * 1024 and (own_ff // planes) % LANES == 0


def own_columns(array, index, width):
    return lax.dynamic_slice_in_dim(array, index * width, width, axis=1)


def after(value, *others):
    return lax.optimization_barrier((value, *others))[0]


def local(
    tokens,
    lengths,
    deal,
    attn_gain,
    query_weight,
    key_matrix,
    value_matrix,
    out_weight,
    mlp_gain,
    gate_weight,
    up_weight,
    down_weight,
    cotangent,
):
    n_ctx = lax.axis_size("ctx")
    n_fsdp = lax.axis_size("fsdp")
    me = lax.axis_index("ctx")
    me_array = me.astype(jnp.int32).reshape(1)
    per_device, width = tokens.shape[1], tokens.shape[2]
    total = per_device * n_ctx
    block_rows = per_device // n_ctx
    heads = QUERY_HEADS // n_ctx
    sharing = n_ctx // KEY_VALUE_HEADS
    own_width = width // n_ctx
    ff = gate_weight.shape[1]
    slab = ff // (n_fsdp * n_ctx)
    own_ff = slab * n_fsdp
    rows_shard = query_weight.shape[0]

    kv_head = me // sharing
    split = heads * HEAD_SIZE
    attn_shard = jnp.concatenate(
        [
            own_columns(query_weight, me, split),
            own_columns(key_matrix, kv_head, HEAD_SIZE),
            own_columns(value_matrix, kv_head, HEAD_SIZE),
            own_columns(out_weight, me, own_width),
        ],
        axis=1,
    )

    def ff_columns(array):
        return jnp.concatenate([own_columns(array, f * n_ctx + me, slab) for f in range(n_fsdp)], axis=1)

    gain_shard = jnp.tile(jnp.concatenate([attn_gain, mlp_gain]).astype(F32)[None], (8, 1))

    first_len = lengths[0, 0]
    given = jnp.arange(total, dtype=jnp.int32)
    position = given - jnp.where(given >= first_len, first_len, 0)
    freq_index = jnp.arange(HEAD_SIZE // 2, dtype=F32)
    inverse = ROPE_BASE ** (-2.0 * freq_index / HEAD_SIZE)
    angles = position.astype(F32)[:, None] * inverse[None, :]
    cos, sin = jnp.cos(angles), jnp.sin(angles)
    cos_table = jnp.concatenate([cos, cos, cos, cos], axis=1)
    sin_table = jnp.concatenate([-sin, sin, -sin, sin], axis=1)

    deal_rows = deal[0]
    slot_ids = jnp.arange(n_ctx, dtype=jnp.int32)
    dealt_of_given = (deal_rows * n_ctx + slot_ids[:, None]).reshape(-1)
    matched = deal_rows[:, :, None] == slot_ids[None, None, :]
    source_slot = jnp.sum(jnp.where(matched, slot_ids[None, :, None], 0), axis=1)
    given_of_dealt = (slot_ids[:, None] * n_ctx + source_slot).T.reshape(-1)

    def reorder(array, table):
        blocks = array.reshape(n_ctx * n_ctx, block_rows, array.shape[1])
        return jnp.take(blocks, table, axis=0, mode="clip").reshape(array.shape)

    cotangent_all = lax.all_gather(cotangent[0], "ctx", axis=0, tiled=True)
    (
        x, normed, q_rot, k_rot, v_rows, lse, attended_all, hidden_all, normed2, a, b, mixed, w_attn, w_gate, w_up, w_down, gains_all,
    ) = forward(
        n_ctx,
        n_fsdp,
        heads,
        lengths[0],
        tokens[0],
        attn_shard,
        ff_columns(gate_weight),
        ff_columns(up_weight),
        lax.dynamic_slice_in_dim(down_weight, me * slab, slab, axis=0),
        gain_shard,
        cos_table,
        sin_table,
    )
    w_qkv, w_out = w_attn[:, : split + 2 * HEAD_SIZE], w_attn[:, split + 2 * HEAD_SIZE :]
    gains = gains_all.reshape(n_fsdp, 8, 2, rows_shard)[:, 0].transpose(1, 0, 2).reshape(2, 1, width)
    hidden_own = own_columns(hidden_all, me, own_width)
    grad_result = reorder(cotangent_all, dealt_of_given)

    both = jnp.concatenate([mixed, (hidden_own.astype(F32) * (1.0 / RESIDUAL_SCALE)).astype(BF16)], axis=1)
    column = lax.broadcasted_iota(jnp.int32, (own_width, width), 1) - me * own_width
    place = (column == lax.broadcasted_iota(jnp.int32, (own_width, width), 0)).astype(BF16)
    result_part = RESIDUAL_SCALE * dot_nn(reorder(both, given_of_dealt), jnp.concatenate([w_down, place], axis=0))
    activations = lax.psum_scatter(
        result_part.astype(BF16), "ctx", scatter_dimension=0, tiled=True
    )[None]

    if kernel_fits(n_ctx, n_fsdp, total, width, own_ff):
        token_grad, gain_rows, down_part, gate_part, up_part, out_part, qkv_part = backward(
            n_ctx,
            n_fsdp,
            heads,
            lengths[0],
            grad_result,
            (x, normed, q_rot, k_rot, v_rows, lse, attended_all, hidden_all, normed2, a, b, mixed),
            (w_attn, w_gate, w_up, w_down, gains_all),
            cos_table,
            sin_table,
        )
        token_grad = token_grad[None]
        own_gains = gain_rows[1::-1]
    else:
        mlp_grad = (RESIDUAL_SCALE * grad_result.astype(F32)).astype(BF16)

        def settle(left, right):
            return lax.psum_scatter(dot_tn(left, right).astype(BF16), "fsdp", scatter_dimension=0, tiled=True)

        down_part = settle(mixed, mlp_grad)
        ggrad, ugrad, hidden_part, mlp_gain_part = mlp_backward(
            n_ctx, mlp_grad, a, b, hidden_all, gains[1], w_gate, w_up, w_down
        )
        hidden_sum = lax.psum_scatter(hidden_part, "ctx", scatter_dimension=0, tiled=False)
        gate_part = settle(normed2, ggrad)
        up_part = settle(normed2, ugrad)
        hidden_grad, branch_grad, attended_part = branch_backward(
            hidden_sum, own_columns(grad_result, me, own_width), w_out, n_ctx
        )
        attended_grad = lax.psum_scatter(attended_part, "ctx", scatter_dimension=0, tiled=False)
        out_part = lax.psum_scatter(
            jnp.einsum("ctk,to->cko", attended_all, branch_grad, preferred_element_type=F32)
            .astype(BF16)
            .reshape(width, own_width),
            "fsdp",
            scatter_dimension=0,
            tiled=True,
        )
        dq, dkv = attention_backward(attended_grad, q_rot, k_rot, v_rows, lse, cos_table, sin_table, lengths[0])
        qkv_part = settle(normed, jnp.concatenate([dq, dkv], axis=1))
        token_part, attn_gain_part = token_backward(me_array, dq, dkv, w_qkv, x, gains[0], hidden_grad)
        token_grad = lax.psum_scatter(token_part, "ctx", scatter_dimension=0, tiled=True).astype(F32)[None]

        gain_parts = jnp.concatenate([attn_gain_part, mlp_gain_part], axis=0)
        step = 1
        while step < n_ctx:
            gain_parts = gain_parts + lax.ppermute(gain_parts, "ctx", [(c, c ^ step) for c in range(n_ctx)])
            step *= 2
        gain_rows = gain_parts.reshape(2, n_fsdp, rows_shard).transpose(1, 0, 2).reshape(n_fsdp, 2 * rows_shard)
        own_gains = lax.psum_scatter(gain_rows, "fsdp", scatter_dimension=0, tiled=True).reshape(2, rows_shard)
        down_part, gate_part, up_part, out_part, qkv_part = [
            lax.all_gather(p, "ctx", axis=0, tiled=False) for p in (down_part, gate_part, up_part, out_part, qkv_part)
        ]

    down_grad = down_part.reshape(n_ctx * slab, width).astype(F32)
    if slab % LANES == 0:
        gate_grad = spread_columns(gate_part, slab, n_fsdp)
        up_grad = spread_columns(up_part, slab, n_fsdp)
    else:

        def ff_whole(part):
            pieces = part.reshape(n_ctx, rows_shard, n_fsdp, slab)
            return pieces.transpose(1, 2, 0, 3).reshape(rows_shard, ff).astype(F32)

        gate_grad = ff_whole(gate_part)
        up_grad = ff_whole(up_part)
    out_grad = spread_columns(out_part, own_width, 1)
    qkv_all = qkv_part
    query_grad = spread_columns(qkv_all, split, 1)

    def shared_heads(pieces):
        pieces = pieces.astype(F32).reshape(KEY_VALUE_HEADS, sharing, rows_shard, HEAD_SIZE).sum(axis=1)
        return pieces.transpose(1, 0, 2).reshape(rows_shard, KEY_VALUE_HEADS * HEAD_SIZE)

    key_grad = shared_heads(qkv_all[:, :, split : split + HEAD_SIZE])
    value_grad = shared_heads(qkv_all[:, :, split + HEAD_SIZE :])

    return (
        activations,
        token_grad,
        own_gains[0],
        query_grad,
        key_grad,
        value_grad,
        out_grad,
        own_gains[1],
        gate_grad,
        up_grad,
        down_grad,
    )


def solution(mesh):
    rows = P("fsdp", None)
    block = P("fsdp", "ctx", None)
    gain = P("fsdp")
    return jax.shard_map(
        local,
        mesh=mesh,
        in_specs=(block, rows, P("fsdp", None, None), gain, rows, rows, rows, rows, gain, rows, rows, rows, block),
        out_specs=(block, block, gain, rows, rows, rows, rows, gain, rows, rows, rows),
        check_vma=False,
    )
```

```python
import functools

import jax
import jax.numpy as jnp
from jax import lax
from jax.experimental import pallas as pl
from jax.experimental.pallas import tpu as pltpu
from jax.sharding import PartitionSpec as P

QUERY_HEADS = 32
KEY_VALUE_HEADS = 8
HEAD_SIZE = 64
EPSILON = 1e-05
ROPE_BASE = 10000000.0
SCORE_SCALE = 0.015625
RESIDUAL_SCALE = 0.22
NEGATIVE_BIG = -1e30
LANES = 128
ROWS = 256
BF16 = jnp.bfloat16
F32 = jnp.float32
VMEM_LIMIT = 56 * 1024 * 1024


def dot_nn(a, b):
    return lax.dot_general(a, b, (((1,), (0,)), ((), ())), preferred_element_type=F32)


def dot_nt(a, b):
    return lax.dot_general(a, b, (((1,), (1,)), ((), ())), preferred_element_type=F32)


def dot_tn(a, b):
    return lax.dot_general(a, b, (((0,), (0,)), ((), ())), preferred_element_type=F32)


def swap_halves(x):
    lane = lax.broadcasted_iota(jnp.int32, x.shape, 1)
    first = lax.rem(lane, HEAD_SIZE) < HEAD_SIZE // 2
    return jnp.where(first, pltpu.roll(x, LANES - HEAD_SIZE // 2, 1), pltpu.roll(x, HEAD_SIZE // 2, 1))


def low_half(shape):
    return lax.broadcasted_iota(jnp.int32, shape, 1) < HEAD_SIZE


def mask_bias(first_len, row0, rows, cols):
    query = row0 + lax.broadcasted_iota(jnp.int32, (rows, cols), 0)
    key = lax.broadcasted_iota(jnp.int32, (rows, cols), 1)
    start = jnp.where(query >= first_len, first_len, 0)
    return jnp.where((key <= query) & (key >= start), 0.0, NEGATIVE_BIG)


def attention_backward_kernel(length_ref, g_ref, q_ref, k_ref, v_ref, lse_ref, cos_ref, sin_ref, dq_ref, dkv_ref, dk_sum, dv_sum):
    pair = pl.program_id(0)
    tokens = q_ref.shape[0]

    @pl.when(pair == 0)
    def _():
        dk_sum[...] = jnp.zeros_like(dk_sum)
        dv_sum[...] = jnp.zeros_like(dv_sum)

    first_len = length_ref[0]
    for block in range(tokens // ROWS):
        rows = pl.ds(block * ROWS, ROWS)
        end = (block + 1) * ROWS
        bias = mask_bias(first_len, block * ROWS, ROWS, end)
        query, grad = q_ref[rows, :], g_ref[rows, :]
        low = low_half(query.shape)
        keys, values = k_ref[:end, :], v_ref[:end, :]
        parts = []
        for half in range(2):
            chosen = low if half == 0 else jnp.logical_not(low)
            own_query = jnp.where(chosen, query, jnp.zeros_like(query))
            own_grad = jnp.where(chosen, grad, jnp.zeros_like(grad))
            scores = dot_nt(own_query, keys) + bias
            probs = jnp.exp(scores - lse_ref[0, rows, half : half + 1])
            prob_grad = dot_nt(own_grad, values)
            delta = jnp.sum(probs * prob_grad, axis=-1, keepdims=True)
            score_grad = (probs * (prob_grad - delta)).astype(BF16)
            parts.append(dot_nn(score_grad, keys))
            dk_sum[:end, :] += dot_tn(score_grad, own_query)
            dv_sum[:end, :] += dot_tn(probs.astype(BF16), own_grad)
        dq = jnp.where(low_half(parts[0].shape), parts[0], parts[1]) * SCORE_SCALE
        dq_ref[rows, :] = (dq * cos_ref[rows, :] - swap_halves(dq) * sin_ref[rows, :]).astype(BF16)

    @pl.when(pair == pl.num_programs(0) - 1)
    def _():
        dk = dk_sum[...]
        dk = dk + pltpu.roll(dk, HEAD_SIZE, 1)
        dk = dk * cos_ref[...] - swap_halves(dk) * sin_ref[...]
        dv = dv_sum[...]
        dv = dv + pltpu.roll(dv, HEAD_SIZE, 1)
        dkv_ref[...] = jnp.where(low_half(dk.shape), dk, dv).astype(BF16)


def attention_backward(grads, q_rot, k_rot, v_rows, lse, cos, sin, lengths):
    tokens = q_rot.shape[0]
    pairs = q_rot.shape[1] // LANES
    one = pl.BlockSpec((tokens, LANES), lambda j: (0, 0))
    each = pl.BlockSpec((tokens, LANES), lambda j: (0, j))
    return pl.pallas_call(
        attention_backward_kernel,
        grid=(pairs,),
        in_specs=[
            pl.BlockSpec(memory_space=pltpu.SMEM),
            each,
            each,
            one,
            one,
            pl.BlockSpec((1, tokens, LANES), lambda j: (j, 0, 0)),
            one,
            one,
        ],
        out_specs=[each, one],
        out_shape=[
            jax.ShapeDtypeStruct((tokens, pairs * LANES), BF16),
            jax.ShapeDtypeStruct((tokens, LANES), BF16),
        ],
        scratch_shapes=[pltpu.VMEM((tokens, LANES), F32), pltpu.VMEM((tokens, LANES), F32)],
        compiler_params=pltpu.CompilerParams(vmem_limit_bytes=VMEM_LIMIT),
        cost_estimate=pl.CostEstimate(
            flops=10 * tokens * tokens * LANES * pairs,
            bytes_accessed=12 * tokens * pairs * LANES,
            transcendentals=tokens * tokens * pairs,
        ),
        name="attend_back",
    )(lengths, grads, q_rot, k_rot, v_rows, lse, cos, sin)


def row_block(width):
    return pl.BlockSpec((ROWS, width), lambda i: (i, 0))


def fixed(*shape):
    return pl.BlockSpec(shape, lambda i: (0,) * len(shape))


def params():
    return pltpu.CompilerParams(vmem_limit_bytes=VMEM_LIMIT)


def cost(flops, *arrays):
    moved = sum(a.size * a.dtype.itemsize for a in arrays)
    return pl.CostEstimate(flops=flops, bytes_accessed=moved, transcendentals=0)


def mlp_back_kernel(
    grad_ref, a_ref, b_ref, hidden_ref, gain_ref, gate_ref, up_ref, down_ref, ggrad_ref, ugrad_ref, part_ref, gain_out
):
    mixed_grad = dot_nt(grad_ref[...], down_ref[...])
    ggrad = (mixed_grad * a_ref[...].astype(F32)).astype(BF16)
    ugrad = (mixed_grad * b_ref[...].astype(F32)).astype(BF16)
    ggrad_ref[...] = ggrad
    ugrad_ref[...] = ugrad
    normed_grad = dot_nt(ggrad, gate_ref[...]) + dot_nt(ugrad, up_ref[...])
    hidden = hidden_ref[...].astype(F32)
    r2 = lax.rsqrt(jnp.mean(hidden * hidden, axis=-1, keepdims=True) + EPSILON)
    gain_part = jnp.sum(normed_grad * (hidden * r2), axis=0, keepdims=True)

    @pl.when(pl.program_id(0) == 0)
    def _():
        gain_out[...] = jnp.zeros_like(gain_out)

    gain_out[...] += gain_part
    weighted = normed_grad * gain_ref[...]
    mean = jnp.mean(weighted * hidden, axis=-1, keepdims=True)
    part = r2 * weighted - hidden * (r2 * r2 * r2 * mean)
    own = part_ref.shape[2]
    for c in range(part_ref.shape[0]):
        part_ref[c] = part[:, c * own : (c + 1) * own].astype(BF16)


def mlp_backward(n, mlp_grad, a, b, hidden_all, gain, w_gate, w_up, w_down):
    total, width = hidden_all.shape
    own = width // n
    own_ff = w_gate.shape[1]
    narrow = jax.ShapeDtypeStruct((total, own_ff), BF16)
    planes = pl.BlockSpec((n, ROWS, own), lambda i: (0, i, 0))
    return pl.pallas_call(
        mlp_back_kernel,
        grid=(total // ROWS,),
        in_specs=[
            row_block(width),
            row_block(own_ff),
            row_block(own_ff),
            row_block(width),
            fixed(1, width),
            fixed(width, own_ff),
            fixed(width, own_ff),
            fixed(own_ff, width),
        ],
        out_specs=[row_block(own_ff), row_block(own_ff), planes, fixed(1, width)],
        out_shape=[narrow, narrow, jax.ShapeDtypeStruct((n, total, own), BF16), jax.ShapeDtypeStruct((1, width), F32)],
        compiler_params=params(),
        cost_estimate=cost(6 * total * width * own_ff, mlp_grad, hidden_all, hidden_all, w_gate, w_up, w_down, a, b, a, b),
        name="mlp_backward",
    )(mlp_grad, a, b, hidden_all, gain, w_gate, w_up, w_down)


def branch_kernel(part_ref, grad_ref, w_ref, hidden_ref, branch_ref, out_ref):
    hidden_grad = part_ref[...].astype(F32) + grad_ref[...].astype(F32)
    hidden_ref[...] = hidden_grad
    branch = (RESIDUAL_SCALE * hidden_grad).astype(BF16)
    branch_ref[...] = branch
    own = out_ref.shape[2]
    for c in range(out_ref.shape[0]):
        out_ref[c] = dot_nt(branch, w_ref[c]).astype(BF16)


def branch_backward(hidden_part, grad_own, w_out, n):
    total, own_width = hidden_part.shape
    own = w_out.shape[0] // n
    w_heads = w_out.reshape(n, own, own_width)
    return pl.pallas_call(
        branch_kernel,
        grid=(total // ROWS,),
        in_specs=[row_block(own_width), row_block(own_width), fixed(n, own, own_width)],
        out_specs=[row_block(own_width), row_block(own_width), pl.BlockSpec((n, ROWS, own), lambda i: (0, i, 0))],
        out_shape=[
            jax.ShapeDtypeStruct((total, own_width), F32),
            jax.ShapeDtypeStruct((total, own_width), BF16),
            jax.ShapeDtypeStruct((n, total, own), BF16),
        ],
        compiler_params=params(),
        cost_estimate=cost(2 * total * own_width * own * n, hidden_part, hidden_part, hidden_part, w_out),
        name="branch_backward",
    )(hidden_part, grad_own, w_heads)


def token_kernel(me_ref, dq_ref, dkv_ref, w_ref, x_ref, gain_ref, hidden_ref, part_ref, gain_out):
    split = dq_ref.shape[1]
    normed_grad = dot_nt(dq_ref[...], w_ref[:, :split]) + dot_nt(dkv_ref[...], w_ref[:, split:])
    x = x_ref[...].astype(F32)
    r1 = lax.rsqrt(jnp.mean(x * x, axis=-1, keepdims=True) + EPSILON)

    @pl.when(pl.program_id(0) == 0)
    def _():
        gain_out[...] = jnp.zeros_like(gain_out)

    gain_out[...] += jnp.sum(normed_grad * (x * r1), axis=0, keepdims=True)
    weighted = normed_grad * gain_ref[...]
    mean = jnp.mean(weighted * x, axis=-1, keepdims=True)
    part = r1 * weighted - x * (r1 * r1 * r1 * mean)
    own_width = hidden_ref.shape[1]
    for c in range(part.shape[1] // own_width):
        piece = part[:, c * own_width : (c + 1) * own_width]
        piece = piece + jnp.where(me_ref[0] == c, hidden_ref[...], 0.0)
        part_ref[:, c * own_width : (c + 1) * own_width] = piece.astype(BF16)


def token_backward(me, dq, dkv, w_qkv, x, gain, hidden_grad):
    total, width = x.shape
    own_width = hidden_grad.shape[1]
    return pl.pallas_call(
        token_kernel,
        grid=(total // ROWS,),
        in_specs=[
            pl.BlockSpec(memory_space=pltpu.SMEM),
            row_block(dq.shape[1]),
            row_block(dkv.shape[1]),
            fixed(*w_qkv.shape),
            row_block(width),
            fixed(1, width),
            row_block(own_width),
        ],
        out_specs=[row_block(width), fixed(1, width)],
        out_shape=[jax.ShapeDtypeStruct((total, width), BF16), jax.ShapeDtypeStruct((1, width), F32)],
        compiler_params=params(),
        cost_estimate=cost(2 * total * width * w_qkv.shape[1], x, x, w_qkv, dq, dkv, hidden_grad),
        name="token_backward",
    )(me, dq, dkv, w_qkv, x, gain, hidden_grad)


def spread_kernel(in_ref, out_ref):
    slab = in_ref.shape[2]
    for c in range(in_ref.shape[0]):
        out_ref[:, c * slab : (c + 1) * slab] = in_ref[c].astype(F32)


def spread_columns(pieces, slab, groups):
    n, rows, _ = pieces.shape
    tile = 128
    out_shape = jax.ShapeDtypeStruct((rows, groups * n * slab), F32)
    return pl.pallas_call(
        spread_kernel,
        grid=(groups, rows // tile),
        in_specs=[pl.BlockSpec((n, tile, slab), lambda f, r: (0, r, f))],
        out_specs=pl.BlockSpec((tile, n * slab), lambda f, r: (r, f)),
        out_shape=out_shape,
        compiler_params=params(),
        cost_estimate=cost(0, pieces, out_shape),
        name="spread_columns",
    )(pieces)


MESH = pl.DeviceIdType.MESH


class Chain:
    def __init__(self, slot, planes, plane, send_sem, recv_sem):
        self.slot, self.planes, self.plane = slot, planes, plane
        self.send_sem, self.recv_sem = send_sem, recv_sem

    def copy(self, way, step, shard, to):
        return pltpu.make_async_remote_copy(
            src_ref=self.slot(shard),
            dst_ref=self.slot(shard),
            send_sem=self.send_sem.at[way, step],
            recv_sem=self.recv_sem.at[way, step],
            device_id={"fsdp": to},
            device_id_type=MESH,
        )

    def moves(self, step):
        p, last = self.plane, self.planes - 1
        return (
            (0, (p >= step) & (p < last), p - step, p + 1, p >= step + 1, p - 1 - step),
            (1, (p + step <= last) & (p > 0), p + step, p - 1, p + step + 1 <= last, p + 1 + step),
        )

    def start(self, step):
        for way, sends, shard, to, _, _ in self.moves(step):

            @pl.when(sends)
            def _(way=way, shard=shard, to=to):
                self.copy(way, step, shard, to).start()

    def arrive(self, step):
        for way, _, _, _, receives, shard in self.moves(step):

            @pl.when(receives)
            def _(way=way, shard=shard):
                self.copy(way, step, shard, self.plane).wait_recv()

    def advance(self, step):
        self.arrive(step - 1)
        self.start(step)

    def drain(self):
        for step in range(self.planes - 1):
            for way, sends, shard, to, _, _ in self.moves(step):

                @pl.when(sends)
                def _(way=way, shard=shard, to=to, step=step):
                    self.copy(way, step, shard, to).wait_send()


class Spread:
    def __init__(self, src, slot, n, me, send_sem, recv_sem):
        self.src, self.slot, self.n, self.me = src, slot, n, me
        self.send_sem, self.recv_sem = send_sem, recv_sem
        self.chips = n // 2
        self.chip, self.core = me // 2, lax.rem(me, 2)
        self.partner = me + 1 - 2 * self.core

    def at(self, k):
        return lax.rem(self.chip + k, self.chips) * 2 + self.core

    def copy(self, src, owner, sem, to):
        return pltpu.make_async_remote_copy(
            src_ref=src,
            dst_ref=self.slot(owner),
            send_sem=self.send_sem.at[sem],
            recv_sem=self.recv_sem.at[sem],
            device_id={"ctx": to},
            device_id_type=MESH,
        )

    def out(self, k):
        return self.copy(self.src, self.me, k, self.at(k))

    def relay(self, k):
        owner = self.at(self.chips - k) if k else self.me
        src = self.slot(owner) if k else self.src
        return self.copy(src, owner, self.chips + k, self.partner)

    def start(self):
        for k in range(1, self.chips):
            self.out(k).start()
        self.relay(0).start()

    def pass_on(self):
        for k in range(1, self.chips):
            self.copy(self.src, self.at(self.chips - k), k, self.me).wait_recv()
            self.relay(k).start()

    def late(self):
        pass

    def finish(self):
        other = 1 - 2 * self.core
        for k in range(self.chips):
            owner = (self.at(self.chips - k) if k else self.me) + other
            self.copy(self.slot(owner), owner, self.chips + k, self.me).wait_recv()

    def drain(self):
        for k in range(1, self.chips):
            self.out(k).wait_send()
        for k in range(self.chips):
            self.relay(k).wait_send()


class Spread4:
    def __init__(self, src, slot, n, me, send_sem, recv_sem):
        self.src, self.slot, self.me = src, slot, me
        self.send_sem, self.recv_sem = send_sem, recv_sem
        self.core = lax.rem(me, 2)
        self.other = 1 - self.core
        chip = me // 2
        self.near, self.side, self.far = square(chip)
        self.chip = chip
        self.half = src.shape[0] // 2

    def copy(self, src, dst, sem, to):
        return pltpu.make_async_remote_copy(
            src_ref=src,
            dst_ref=dst,
            send_sem=self.send_sem.at[sem],
            recv_sem=self.recv_sem.at[sem],
            device_id={"ctx": to},
            device_id_type=MESH,
        )

    def part(self, owner, which):
        return self.slot(owner).at[pl.ds(which * self.half, self.half)]

    def out(self, sem):
        chip = self.near if sem == 1 else self.side
        return self.copy(self.src, self.slot(self.me), sem, chip * 2 + self.core)

    def onward(self, sem):
        origin, to, which = (self.near, self.side, 0) if sem == 3 else (self.side, self.near, 1)
        owner = origin * 2 + self.core
        return self.copy(self.part(owner, which), self.part(owner, which), sem, to * 2 + self.core)

    def relay(self, k):
        owner = (self.chip, self.near, self.side, self.far)[k] * 2 + self.core
        src = self.slot(owner) if k else self.src
        return self.copy(src, self.slot(owner), 4 + k, self.chip * 2 + self.other)

    def start(self):
        self.out(1).start()
        self.out(2).start()
        self.relay(0).start()

    def pass_on(self):
        for k, chip in ((1, self.near), (2, self.side)):
            owner = chip * 2 + self.core
            self.copy(self.src, self.slot(owner), k, self.me).wait_recv()
            self.onward(3 if k == 1 else 0).start()
            self.relay(k).start()

    def late(self):
        owner = self.far * 2 + self.core
        for sem, which in ((3, 0), (0, 1)):
            self.copy(self.part(owner, which), self.part(owner, which), sem, self.me).wait_recv()
        self.relay(3).start()

    def finish(self):
        for k, chip in enumerate((self.chip, self.near, self.side, self.far)):
            owner = chip * 2 + self.other
            self.copy(self.slot(owner), self.slot(owner), 4 + k, self.me).wait_recv()

    def drain(self):
        for sem in (1, 2):
            self.out(sem).wait_send()
        for sem in (3, 0):
            self.onward(sem).wait_send()
        for k in range(4):
            self.relay(k).wait_send()


def square(chip):
    return chip + 1 - 2 * lax.rem(chip, 2), chip + 2 - 4 * (chip // 2), 3 - chip


def spread_over(n, src, *rest):
    return (Spread4 if n == 8 and src.shape[0] % 32 == 0 else Spread)(src, *rest)


def greet(n, planes, me, plane, across):
    barrier = pltpu.get_barrier_semaphore()
    chips = n // 2
    core = lax.rem(me, 2)
    others = [lax.rem(me // 2 + k, chips) * 2 + core for k in range(1, chips)] + [me + 1 - 2 * core]
    for other in others:
        pl.semaphore_signal(barrier, inc=1, device_id={"ctx": other}, device_id_type=MESH)
    if across:

        @pl.when(plane > 0)
        def _():
            pl.semaphore_signal(barrier, inc=1, device_id={"fsdp": plane - 1}, device_id_type=MESH)

        @pl.when(plane < planes - 1)
        def _():
            pl.semaphore_signal(barrier, inc=1, device_id={"fsdp": plane + 1}, device_id_type=MESH)

    count = len(others)
    if across:
        count = count + (plane > 0).astype(jnp.int32) + (plane < planes - 1).astype(jnp.int32)
    pl.semaphore_wait(barrier, count)


def forward_kernel(
    n,
    planes,
    heads,
    length_ref,
    tokens_ref,
    attn_shard,
    gate_shard,
    up_shard,
    down_shard,
    gain_shard,
    cos_ref,
    sin_ref,
    x_out,
    normed_out,
    q_out,
    k_out,
    v_out,
    lse_out,
    att_out,
    hid_out,
    normed2_out,
    a_out,
    b_out,
    mixed_out,
    attn_out,
    gate_out,
    up_out,
    down_out,
    gain_out,
    w_attn,
    w_gate,
    w_up,
    w_down,
    gains,
    x_all,
    qkv,
    q_rot,
    k_rot,
    v_rows,
    lse,
    own_att,
    att_all,
    own_hid,
    wide,
    narrow,
    z_send,
    z_recv,
    c_send,
    c_recv,
    keep_sem,
    wide_sem,
    narrow_sem,
):
    me, plane = lax.axis_index("ctx"), lax.axis_index("fsdp")
    per_device, width = tokens_ref.shape
    total = x_all.shape[0]
    rows_shard = attn_shard.shape[0]
    own = own_att.shape[1]
    own_width = own_hid.shape[1]
    columns = qkv.shape[1]
    blocks = total // ROWS
    pairs = heads // 2

    local_copies = []

    def keep(src, dst, index):
        copy = pltpu.make_async_copy(src, dst, keep_sem.at[index])
        copy.start()
        local_copies.append(copy)

    def chain(index, ref, rows):
        return Chain(lambda s: ref.at[pl.ds(s * rows, rows)], planes, plane, z_send.at[index], z_recv.at[index])

    attn_chain = chain(0, w_attn, rows_shard)
    gate_chain = chain(1, w_gate, rows_shard)
    up_chain = chain(2, w_up, rows_shard)
    down_chain = chain(3, w_down, down_shard.shape[0])
    gain_chain = chain(4, gains, gain_shard.shape[0])
    first = (attn_chain, attn_shard, 0), (gain_chain, gain_shard, 1), (gate_chain, gate_shard, 2), (up_chain, up_shard, 3), (down_chain, down_shard, 4)
    loads = [pltpu.make_async_copy(shard, c.slot(plane), keep_sem.at[i]) for c, shard, i in first]
    for load in loads:
        load.start()
    own_x = pltpu.make_async_copy(tokens_ref, x_all.at[pl.ds(me * per_device, per_device)], keep_sem.at[5])
    own_x.start()
    greet(n, planes, me, plane, True)
    loads[0].wait()
    attn_chain.start(0)
    loads[1].wait()
    gain_chain.start(0)
    x_spread = spread_over(
        n, tokens_ref, lambda c: x_all.at[pl.ds(c * per_device, per_device)], n, me, c_send.at[0], c_recv.at[0]
    )
    x_spread.start()
    for load in loads[2:]:
        load.wait()
    own_x.wait()
    for step in range(1, planes - 1):
        attn_chain.advance(step)
        gain_chain.advance(step)
    gate_chain.start(0)
    up_chain.start(0)
    x_spread.pass_on()
    x_spread.late()
    x_spread.finish()
    x_copy = pltpu.make_async_copy(x_all, x_out, keep_sem.at[0])
    x_copy.start()
    attn_chain.arrive(planes - 2)
    gain_chain.arrive(planes - 2)
    keep(w_attn, attn_out, 1)
    keep(gains, gain_out, 2)
    half = gain_shard.shape[1] // 2
    step_rows = gain_shard.shape[0]
    attn_gain = jnp.concatenate([gains[f * step_rows : f * step_rows + 1, :half] for f in range(planes)], axis=1)
    mlp_gain = jnp.concatenate([gains[f * step_rows : f * step_rows + 1, half:] for f in range(planes)], axis=1)

    def staged(stage, sem, slot, out, rows, wait_before):
        copy = pltpu.make_async_copy(stage.at[slot], out.at[rows], sem.at[slot])
        return copy.wait() if wait_before else copy.start()

    def project_block(i, _):
        rows = pl.ds(pl.multiple_of(i * ROWS, ROWS), ROWS)
        slot = lax.rem(i, 2)

        @pl.when(i >= 2)
        def _():
            staged(wide, wide_sem, slot, normed_out, rows, True)

        own_hid[rows, :] = x_all[rows, pl.ds(pl.multiple_of(me * own_width, LANES), own_width)]
        x = x_all[rows, :].astype(F32)
        r1 = lax.rsqrt(jnp.mean(x * x, axis=-1, keepdims=True) + EPSILON)
        normed = (x * r1 * attn_gain).astype(BF16)
        wide[slot] = normed
        staged(wide, wide_sem, slot, normed_out, rows, False)
        qkv[rows, :] = dot_nn(normed, w_attn[:, :columns])
        return 0

    lax.fori_loop(0, blocks, project_block, 0)
    for i in range(max(blocks - 2, 0), blocks):
        staged(wide, wide_sem, i % 2, normed_out, pl.ds(i * ROWS, ROWS), True)

    split = columns - LANES
    cos, sin = cos_ref[...], sin_ref[...]
    kv = qkv[:, split:]
    turned = pltpu.roll(kv, HEAD_SIZE, 1)
    low = low_half(kv.shape)
    k = jnp.where(low, kv, turned)
    k_rot[...] = (k * cos + swap_halves(k) * sin).astype(BF16)
    v_rows[...] = jnp.where(low, turned, kv).astype(BF16)
    keep(k_rot, k_out, 3)
    keep(v_rows, v_out, 4)
    first_len = length_ref[0]

    def attend_pair(pair, _):
        lanes = pl.ds(pl.multiple_of(pair * LANES, LANES), LANES)
        q = qkv[:, lanes]
        q_rot[:, lanes] = ((q * cos_ref[...] + swap_halves(q) * sin_ref[...]) * SCORE_SCALE).astype(BF16)
        for block in range(blocks):
            rows = pl.ds(block * ROWS, ROWS)
            end = (block + 1) * ROWS
            bias = mask_bias(first_len, block * ROWS, ROWS, end)
            query = q_rot[rows, lanes]
            lower = low_half(query.shape)
            keys, values = k_rot[:end, :], v_rows[:end, :]
            parts = []
            for side in range(2):
                chosen = lower if side == 0 else jnp.logical_not(lower)
                scores = dot_nt(jnp.where(chosen, query, jnp.zeros_like(query)), keys) + bias
                top = jnp.max(scores, axis=-1, keepdims=True)
                weights = jnp.exp(scores - top)
                whole = jnp.sum(weights, axis=-1, keepdims=True)
                probs = (weights * (1.0 / whole)).astype(BF16)
                parts.append(dot_nn(probs, values))
                lse[pair, rows, side : side + 1] = top + jnp.log(whole)
            own_att[rows, lanes] = jnp.where(low_half(parts[0].shape), parts[0], parts[1]).astype(BF16)
        return 0

    lax.fori_loop(0, pairs, attend_pair, 0)
    att_spread = spread_over(n, own_att, lambda c: att_all.at[c], n, me, c_send.at[1], c_recv.at[1])
    x_copy.wait()
    x_spread.drain()
    att_spread.start()
    own_a = pltpu.make_async_copy(own_att, att_all.at[me], keep_sem.at[5])
    own_a.start()
    keep(q_rot, q_out, 6)
    keep(lse, lse_out, 7)
    if planes > 2:
        gate_chain.advance(1)
        up_chain.advance(1)
    att_spread.pass_on()
    att_spread.late()
    own_a.wait()
    att_spread.finish()
    keep(att_all, att_out, 8)

    def out_block(i, _):
        rows = pl.ds(pl.multiple_of(i * ROWS, ROWS), ROWS)
        acc = jnp.zeros((ROWS, own_width), F32)
        for c in range(n):
            acc += dot_nn(att_all[c, rows, :], w_attn[c * own : (c + 1) * own, columns:])
        own_hid[rows, :] = (own_hid[rows, :].astype(F32) + RESIDUAL_SCALE * acc).astype(BF16)
        return 0

    lax.fori_loop(0, blocks, out_block, 0)
    def hid_slot(c):
        return x_all.at[:, pl.ds(pl.multiple_of(c * own_width, LANES), own_width)]

    hid_spread = spread_over(n, own_hid, hid_slot, n, me, c_send.at[2], c_recv.at[2])
    hid_spread.start()
    own_h = pltpu.make_async_copy(own_hid, hid_slot(me), keep_sem.at[5])
    own_h.start()
    for step in range(2, planes - 1):
        gate_chain.advance(step)
        up_chain.advance(step)
    down_chain.start(0)
    hid_spread.pass_on()
    hid_spread.late()
    own_h.wait()
    hid_spread.finish()
    keep(x_all, hid_out, 9)
    gate_chain.arrive(planes - 2)
    up_chain.arrive(planes - 2)
    keep(w_gate, gate_out, 10)
    keep(w_up, up_out, 11)
    if planes > 2:
        down_chain.advance(1)

    def mlp_copies(i, rows, wait):
        slot = lax.rem(i, 2)
        staged(wide, wide_sem, slot, normed2_out, rows, wait)
        for j, out in enumerate((a_out, b_out, mixed_out)):
            staged(narrow.at[j], narrow_sem.at[j], slot, out, rows, wait)

    def mlp_block(i, _):
        rows = pl.ds(pl.multiple_of(i * ROWS, ROWS), ROWS)
        slot = lax.rem(i, 2)

        @pl.when(i >= 2)
        def _():
            mlp_copies(i, rows, True)

        hidden = x_all[rows, :].astype(F32)
        r2 = lax.rsqrt(jnp.mean(hidden * hidden, axis=-1, keepdims=True) + EPSILON)
        normed = (hidden * r2 * mlp_gain).astype(BF16)
        wide[slot] = normed
        gate = dot_nn(normed, w_gate[...])
        up = dot_nn(normed, w_up[...])
        sig = jax.nn.sigmoid(gate)
        silu = gate * sig
        narrow[2, slot] = (silu * up).astype(BF16)
        narrow[1, slot] = silu.astype(BF16)
        narrow[0, slot] = (up * sig * (1.0 + gate * (1.0 - sig))).astype(BF16)
        mlp_copies(i, rows, False)
        return 0

    lax.fori_loop(0, blocks, mlp_block, 0)
    for step in range(2, planes - 1):
        down_chain.advance(step)
    for i in range(max(blocks - 2, 0), blocks):
        mlp_copies(i, pl.ds(i * ROWS, ROWS), True)
    down_chain.arrive(planes - 2)
    keep(w_down, down_out, 12)
    for c in (attn_chain, gain_chain, gate_chain, up_chain, down_chain):
        c.drain()
    for s in (att_spread, hid_spread):
        s.drain()
    for copy in local_copies:
        copy.wait()


def forward(n, planes, heads, lengths, tokens, attn_shard, gate_shard, up_shard, down_shard, gain_shard, cos, sin):
    per_device, width = tokens.shape
    total = per_device * n
    own = heads * HEAD_SIZE
    columns = own + 2 * HEAD_SIZE
    own_width = attn_shard.shape[1] - columns
    own_ff = gate_shard.shape[1]
    rows_shard = attn_shard.shape[0]
    pairs = heads // 2
    weights = [
        ((planes * rows_shard, attn_shard.shape[1]), BF16),
        ((planes * rows_shard, own_ff), BF16),
        ((planes * rows_shard, own_ff), BF16),
        ((planes * down_shard.shape[0], width), BF16),
        ((planes * gain_shard.shape[0], gain_shard.shape[1]), F32),
    ]
    outs = [
        ((total, width), BF16),
        ((total, width), BF16),
        ((total, own), BF16),
        ((total, LANES), BF16),
        ((total, LANES), BF16),
        ((pairs, total, LANES), F32),
        ((n, total, own), BF16),
        ((total, width), BF16),
        ((total, width), BF16),
        ((total, own_ff), BF16),
        ((total, own_ff), BF16),
        ((total, own_ff), BF16),
    ] + weights
    scratch = weights + [
        ((total, width), BF16),
        ((total, columns), F32),
        ((total, own), BF16),
        ((total, LANES), BF16),
        ((total, LANES), BF16),
        ((pairs, total, LANES), F32),
        ((total, own), BF16),
        ((n, total, own), BF16),
        ((total, own_width), BF16),
        ((2, ROWS, width), BF16),
        ((3, 2, ROWS, own_ff), BF16),
    ]
    steps = max(planes - 1, 1)
    dma = pltpu.SemaphoreType.DMA
    anywhere = pl.BlockSpec(memory_space=pl.ANY)
    vmem = pl.BlockSpec(memory_space=pltpu.VMEM)
    return pl.pallas_call(
        functools.partial(forward_kernel, n, planes, heads),
        in_specs=[pl.BlockSpec(memory_space=pltpu.SMEM), vmem] + [anywhere] * 5 + [vmem] * 2,
        out_specs=[anywhere] * len(outs),
        out_shape=[jax.ShapeDtypeStruct(*o) for o in outs],
        scratch_shapes=[pltpu.VMEM(*s) for s in scratch]
        + [dma((5, 2, steps)), dma((5, 2, steps)), dma((3, n)), dma((3, n)), dma((16,)), dma((2,)), dma((3, 2))],
        compiler_params=pltpu.CompilerParams(
            vmem_limit_bytes=VMEM_LIMIT, collective_id=1, has_side_effects=True
        ),
        cost_estimate=pl.CostEstimate(
            flops=2 * total * width * (columns + own_width + 2 * own_ff),
            bytes_accessed=60 * 1024 * 1024,
            transcendentals=0,
        ),
        name="forward",
    )(lengths, tokens, attn_shard, gate_shard, up_shard, down_shard, gain_shard, cos, sin)


def add_into(dst, src):
    rows_in = dst.shape[0]
    chunk = 64 if rows_in % 64 == 0 else 32

    def step(i, _):
        rows = pl.ds(pl.multiple_of(i * chunk, chunk), chunk)
        dst[rows, :] = (dst[rows, :].astype(F32) + src[rows, :].astype(F32)).astype(dst.dtype)
        return 0

    if rows_in < chunk:
        dst[...] = dst[...] + src[...]
    else:
        lax.fori_loop(0, rows_in // chunk, step, 0)


def fetch(src, dst, sem):
    copy = pltpu.make_async_copy(src, dst, sem)
    copy.start()
    copy.wait()


class Settle:
    def __init__(self, block, landed, stage, planes, plane, send_sem, recv_sem, load_sem):
        self.block, self.landed, self.stage = block, landed, stage
        self.planes, self.plane = planes, plane
        self.send_sem, self.recv_sem, self.load_sem = send_sem, recv_sem, load_sem

    def slot(self, way, shard, at):
        return shard if way == 0 else jnp.where(shard == at, self.planes, shard)

    def sends(self, step):
        p, last = self.plane, self.planes - 1
        return (
            (0, (p <= step) & (p < last), last - step + p, p + 1),
            (1, (last - p <= step) & (p > 0), step - last + p, p - 1),
        )

    def receives(self, step):
        p, last = self.plane, self.planes - 1
        return (
            (0, (p >= 1) & (p - 1 <= step), last - step + p - 1),
            (1, (p <= last - 1) & (last - p - 1 <= step), step - last + p + 1),
        )

    def copy(self, way, step, shard, to):
        return pltpu.make_async_remote_copy(
            src_ref=self.block(shard),
            dst_ref=self.landed.at[self.slot(way, shard, to)],
            send_sem=self.send_sem.at[way, step],
            recv_sem=self.recv_sem.at[way, step],
            device_id={"fsdp": to},
            device_id_type=MESH,
        )

    def start(self, step=0):
        for way, active, shard, to in self.sends(step):

            @pl.when(active)
            def _(way=way, shard=shard, to=to):
                self.copy(way, step, shard, to).start()

    def take(self, step):
        for way, active, shard in self.receives(step):

            @pl.when(active)
            def _(way=way, shard=shard):
                self.copy(way, step, shard, self.plane).wait_recv()
                fetch(self.landed.at[self.slot(way, shard, self.plane)], self.stage, self.load_sem)
                add_into(self.block(shard), self.stage)

    def advance(self, step):
        self.take(step - 1)
        self.start(step)

    def drain(self):
        for step in range(self.planes - 1):
            for way, active, shard, to in self.sends(step):

                @pl.when(active)
                def _(way=way, shard=shard, to=to, step=step):
                    self.copy(way, step, shard, to).wait_send()


class Scatter:
    def __init__(self, block, near, far, stage, me, send_sem, recv_sem, load_sem):
        self.block, self.landed, self.far, self.stage = block, near, far, stage
        self.send_sem, self.recv_sem, self.load_sem = send_sem, recv_sem, load_sem
        self.core = lax.rem(me, 2)
        self.chip = me // 2
        self.chips = (self.chip, *square(self.chip))
        self.half = stage.shape[0] // 2

    def rows(self, which):
        return pl.ds(which * self.half, self.half)

    def own(self, k):
        return self.block(self.chips[k] * 2 + self.core)

    def copy(self, src, dst, sem, chip, core):
        return pltpu.make_async_remote_copy(
            src_ref=src,
            dst_ref=dst,
            send_sem=self.send_sem.at[sem],
            recv_sem=self.recv_sem.at[sem],
            device_id={"ctx": chip * 2 + core},
            device_id_type=MESH,
        )

    def first(self, k):
        other = 1 - self.core
        return self.copy(self.block(self.chips[k] * 2 + other), self.landed.at[k], k, self.chip, other)

    def second(self, k, to, which):
        place = self.far.at[to - 1 if k == to else 2, self.rows(which)]
        sem = 4 + 2 * (to - 1) + which if k == to else 7 + to
        return self.copy(self.own(k).at[self.rows(which)], place, sem, self.chips[to], self.core)

    def start(self):
        for k in (3, 1, 2, 0):
            self.first(k).start()

    def add(self, k):
        self.first(k).wait_recv()
        fetch(self.landed.at[k], self.stage, self.load_sem)
        add_into(self.own(k), self.stage)

    def pass_on(self):
        self.add(3)
        self.second(3, 1, 0).start()
        self.second(3, 2, 1).start()
        self.add(1)
        self.second(1, 1, 0).start()
        self.add(2)
        self.second(2, 2, 1).start()

    def late(self):
        for to, which, k in ((1, 0, 2), (2, 1, 1)):
            self.second(3, to, which).wait_recv()
            place = self.stage.at[self.rows(which)]
            fetch(self.far.at[2, self.rows(which)], place, self.load_sem)
            add_into(self.own(k).at[self.rows(which)], place)
            self.second(k, k, which).start()

    def finish(self, total):
        self.first(0).wait_recv()
        fetch(self.landed.at[0], self.stage, self.load_sem)
        add_into(total, self.stage)
        for k in (1, 2):
            for which in (0, 1):
                self.second(k, k, which).wait_recv()
            fetch(self.far.at[k - 1], self.stage, self.load_sem)
            add_into(total, self.stage)

    def drain(self):
        for k in range(4):
            self.first(k).wait_send()
        for k, to, which in ((3, 1, 0), (3, 2, 1), (1, 1, 0), (1, 1, 1), (2, 2, 0), (2, 2, 1)):
            self.second(k, to, which).wait_send()


def backward_kernel(
    n,
    planes,
    heads,
    length_ref,
    grad_in,
    mixed_in,
    a_in,
    b_in,
    hidden_in,
    normed2_in,
    normed_in,
    x_in,
    att_in,
    q_in,
    k_in,
    v_in,
    lse_in,
    cos_in,
    sin_in,
    attn_in,
    gate_in,
    up_in,
    down_in,
    gain_in,
    token_out,
    gain_out,
    down_all,
    gate_all,
    up_all,
    out_all,
    qkv_all,
    near1,
    far1,
    near2,
    far2,
    near3,
    far3,
    down_landed,
    gate_landed,
    up_landed,
    out_landed,
    qkv_landed,
    w_attn,
    w_gate,
    w_up,
    w_down,
    p_down,
    gains,
    grad,
    a_v,
    b_v,
    part,
    hid_stage,
    stage_tall,
    stage_wide,
    stage_col,
    hidden_grad,
    lse,
    cos,
    sin,
    dk_sum,
    dv_sum,
    gain_own,
    gain_all,
    gain_landed,
    gain_stage,
    z_send,
    z_recv,
    s_send,
    s_recv,
    g_send,
    g_recv,
    load_sem,
    hid_sem,
    add_sem,
):
    me, plane = lax.axis_index("ctx"), lax.axis_index("fsdp")
    total, width = grad.shape
    per_device = total // n
    own = heads * HEAD_SIZE
    own_width = width // n
    own_ff = a_v.shape[1]
    rows_shard = width // planes
    slab = own_ff // planes
    blocks = total // ROWS
    pairs = heads // 2
    columns = own + LANES
    last = planes - 2

    def load(src, dst, index):
        copy = pltpu.make_async_copy(src, dst, load_sem.at[index])
        copy.start()
        return copy

    mixed_loads = [load(mixed_in.at[:, pl.ds(d * own_width, own_width)], part.at[d], d) for d in range(own_ff // own_width)]
    grad_load = load(grad_in, grad, 8)
    down_load = load(down_in, w_down, 9)
    gate_load = load(gate_in, w_gate, 10)
    up_load = load(up_in, w_up, 11)
    a_load = load(a_in, a_v, 12)
    b_load = load(b_in, b_v, 13)
    attn_load = load(attn_in, w_attn, 14)
    gain_load = load(gain_in, gains, 15)
    greet(n, planes, me, plane, True)

    def settle(index, block, landed, stage):
        return Settle(block, landed, stage, planes, plane, z_send.at[index], z_recv.at[index], add_sem)

    def rows_of(ref, rows):
        return lambda d: ref.at[pl.ds(pl.multiple_of(d * rows, rows), rows)]

    def out_block_of(d):
        return w_down.at[pl.ds(0, rows_shard), pl.ds(pl.multiple_of(d * own_width, LANES), own_width)]

    def qkv_block_of(d):
        return w_down.at[pl.ds(rows_shard, rows_shard), pl.ds(pl.multiple_of(d * columns, LANES), columns)]

    def gain_block_of(d):
        return gain_own.at[:, pl.ds(pl.multiple_of(d * rows_shard, LANES), rows_shard)]

    down_sum = settle(0, rows_of(p_down, slab), down_landed, stage_wide)
    gate_sum = settle(1, rows_of(w_gate, rows_shard), gate_landed, stage_tall)
    up_sum = settle(2, rows_of(w_up, rows_shard), up_landed, stage_tall)
    out_sum = settle(3, out_block_of, out_landed, stage_tall.at[:, pl.ds(0, own_width)])
    qkv_sum = settle(4, qkv_block_of, qkv_landed, stage_tall.at[:, pl.ds(0, columns)])
    gain_sum = settle(5, gain_block_of, gain_landed, gain_stage)

    def spread(index, src, dst):
        return spread_over(n, src, lambda c: dst.at[c], n, me, g_send.at[index], g_recv.at[index])

    spreads = []

    def give(index, sums, dst):
        src = sums.block(plane)
        mine = load(src, dst.at[me], 16 + index)
        out = spread(index, src, dst)
        out.start()
        spreads.append((out, mine))
        return out

    def scatter(index, block, near, far, stage):
        return Scatter(block, near, far, stage, me, s_send.at[index], s_recv.at[index], add_sem)

    grad_load.wait()

    def scale_block(i, _):
        rows = pl.ds(pl.multiple_of(i * ROWS, ROWS), ROWS)
        grad[rows, :] = (RESIDUAL_SCALE * grad[rows, :].astype(F32)).astype(BF16)
        return 0

    lax.fori_loop(0, blocks, scale_block, 0)
    for copy in mixed_loads:
        copy.wait()

    def down_block(d, _):
        p_down[pl.ds(pl.multiple_of(d * own_width, own_width), own_width), :] = dot_tn(part[d], grad[...]).astype(BF16)
        return 0

    lax.fori_loop(0, own_ff // own_width, down_block, 0)
    down_sum.start()

    for copy in (down_load, gate_load, up_load, a_load, b_load, attn_load, gain_load):
        copy.wait()
    half = gains.shape[1] // 2
    attn_gain = jnp.concatenate([gains[f * 8 : f * 8 + 1, :half] for f in range(planes)], axis=1)
    mlp_gain = jnp.concatenate([gains[f * 8 : f * 8 + 1, half:] for f in range(planes)], axis=1)
    gain_own[...] = jnp.zeros_like(gain_own)

    def stream(src, i, wait):
        rows = pl.ds(pl.multiple_of(i * ROWS, ROWS), ROWS)
        slot = lax.rem(i, 2)
        copy = pltpu.make_async_copy(src.at[rows], hid_stage.at[slot], hid_sem.at[slot])
        return copy.wait() if wait else copy.start()

    stream(hidden_in, jnp.int32(0), False)

    def mlp_block(i, _):
        rows = pl.ds(pl.multiple_of(i * ROWS, ROWS), ROWS)

        @pl.when(i + 1 < blocks)
        def _():
            stream(hidden_in, i + 1, False)

        mixed_grad = dot_nt(grad[rows, :], w_down[...])
        ggrad = (mixed_grad * a_v[rows, :].astype(F32)).astype(BF16)
        ugrad = (mixed_grad * b_v[rows, :].astype(F32)).astype(BF16)
        a_v[rows, :] = ggrad
        b_v[rows, :] = ugrad
        normed_grad = dot_nt(ggrad, w_gate[...]) + dot_nt(ugrad, w_up[...])
        stream(hidden_in, i, True)

        @pl.when(i == blocks - 2)
        def _():
            down_sum.advance(1)

        hidden = hid_stage[lax.rem(i, 2)].astype(F32)
        r2 = lax.rsqrt(jnp.mean(hidden * hidden, axis=-1, keepdims=True) + EPSILON)
        gain_own[0:1, :] += jnp.sum(normed_grad * (hidden * r2), axis=0, keepdims=True)
        weighted = normed_grad * mlp_gain
        mean = jnp.mean(weighted * hidden, axis=-1, keepdims=True)
        piece = r2 * weighted - hidden * (r2 * r2 * r2 * mean)
        for c in range(n):
            part[c, rows, :] = piece[:, c * own_width : (c + 1) * own_width].astype(BF16)
        return 0

    lax.fori_loop(0, blocks, mlp_block, 0)
    first = scatter(0, lambda c: part.at[c], near1, far1, stage_col)
    first.start()
    normed2_load = load(normed2_in, grad, 8)
    normed2_load.wait()

    def columns_times(right, out):
        def block(j, _):
            lanes = pl.ds(pl.multiple_of(j * ROWS, ROWS), ROWS)
            out[lanes, :] = dot_tn(grad[:, lanes], right[...]).astype(BF16)
            return 0

        lax.fori_loop(0, width // ROWS, block, 0)

    columns_times(a_v, w_gate)
    gate_sum.start()
    first.pass_on()
    columns_times(b_v, w_up)
    first.late()
    down_sum.advance(2)

    att_loads = [load(att_in.at[c], grad.at[:, pl.ds(c * own, own)], c) for c in range(n)]
    own_grad = load(grad_in.at[:, pl.ds(pl.multiple_of(me * own_width, LANES), own_width)], b_v.at[:, pl.ds(LANES, own_width)], 8)
    q_load = load(q_in, a_v.at[:, pl.ds(0, own)], 9)
    k_load = load(k_in, a_v.at[:, pl.ds(own, LANES)], 10)
    v_load = load(v_in, a_v.at[:, pl.ds(own + LANES, LANES)], 11)
    lse_load = load(lse_in, lse, 12)
    cos_load = load(cos_in, cos, 13)
    sin_load = load(sin_in, sin, 14)
    own_grad.wait()

    def begin(i, _):
        rows = pl.ds(pl.multiple_of(i * ROWS, ROWS), ROWS)
        hidden_grad[rows, :] = b_v[rows, LANES : LANES + own_width].astype(F32) + part[me, rows, :].astype(F32)
        return 0

    lax.fori_loop(0, blocks, begin, 0)
    first.finish(hidden_grad)
    first.drain()

    def branch_block(i, _):
        rows = pl.ds(pl.multiple_of(i * ROWS, ROWS), ROWS)
        branch = (RESIDUAL_SCALE * hidden_grad[rows, :]).astype(BF16)
        b_v[rows, LANES : LANES + own_width] = branch
        for c in range(n):
            part[c, rows, :] = dot_nt(branch, w_attn[c * own : (c + 1) * own, columns:]).astype(BF16)
        return 0

    lax.fori_loop(0, blocks, branch_block, 0)
    second = scatter(1, lambda c: part.at[c], near2, far2, stage_col)
    second.start()
    gate_sum.advance(1)
    for copy in att_loads:
        copy.wait()
    heads_per_shard = rows_shard // own
    for c in range(n):
        place = out_block_of(c // heads_per_shard).at[pl.ds((c % heads_per_shard) * own, own)]
        place[...] = dot_tn(grad[:, c * own : (c + 1) * own], b_v[:, LANES : LANES + own_width]).astype(BF16)
    second.pass_on()
    normed_load = load(normed_in, grad, 15)
    down_sum.take(last)
    up_sum.start()
    second.late()
    second.finish(part.at[me])
    down_give = give(0, down_sum, down_all)
    gate_sum.advance(2)

    for copy in (q_load, k_load, v_load, lse_load, cos_load, sin_load):
        copy.wait()
    dk_sum[...] = jnp.zeros_like(dk_sum)
    dv_sum[...] = jnp.zeros_like(dv_sum)
    first_len = length_ref[0]
    dq_at = own + 2 * LANES

    def attend_pair(pair, _):
        lanes = pl.ds(pl.multiple_of(pair * LANES, LANES), LANES)
        dq_lanes = pl.ds(pl.multiple_of(dq_at + pair * LANES, LANES), LANES)
        for block in range(blocks):
            rows = pl.ds(block * ROWS, ROWS)
            end = (block + 1) * ROWS
            bias = mask_bias(first_len, block * ROWS, ROWS, end)
            query, grads = a_v[rows, lanes], part[me, rows, lanes]
            low = low_half(query.shape)
            keys, values = a_v[:end, own : own + LANES], a_v[:end, own + LANES : own + 2 * LANES]
            parts = []
            for side in range(2):
                chosen = low if side == 0 else jnp.logical_not(low)
                own_query = jnp.where(chosen, query, jnp.zeros_like(query))
                own_grads = jnp.where(chosen, grads, jnp.zeros_like(grads))
                scores = dot_nt(own_query, keys) + bias
                probs = jnp.exp(scores - lse[pair, rows, side : side + 1])
                prob_grad = dot_nt(own_grads, values)
                delta = jnp.sum(probs * prob_grad, axis=-1, keepdims=True)
                score_grad = (probs * (prob_grad - delta)).astype(BF16)
                parts.append(dot_nn(score_grad, keys))
                dk_sum[:end, :] += dot_tn(score_grad, own_query)
                dv_sum[:end, :] += dot_tn(probs.astype(BF16), own_grads)
            dq = jnp.where(low_half(parts[0].shape), parts[0], parts[1]) * SCORE_SCALE
            a_v[rows, dq_lanes] = (dq * cos[rows, :] - swap_halves(dq) * sin[rows, :]).astype(BF16)

        @pl.when(pair == 0)
        def _():
            down_give.pass_on()
            up_sum.advance(1)

        return 0

    lax.fori_loop(0, pairs, attend_pair, 0)
    dk = dk_sum[...]
    dk = dk + pltpu.roll(dk, HEAD_SIZE, 1)
    dk = dk * cos[...] - swap_halves(dk) * sin[...]
    dv = dv_sum[...]
    dv = dv + pltpu.roll(dv, HEAD_SIZE, 1)
    b_v[:, :LANES] = jnp.where(low_half(dk.shape), dk, dv).astype(BF16)
    down_give.late()
    gate_sum.take(last)
    gate_give = give(1, gate_sum, gate_all)
    up_sum.advance(2)
    out_sum.start()

    normed_load.wait()
    dq_end = dq_at + own
    for d in range(planes):
        for j in range(rows_shard // ROWS):
            lanes = slice(d * rows_shard + j * ROWS, d * rows_shard + (j + 1) * ROWS)
            place = qkv_block_of(d).at[pl.ds(j * ROWS, ROWS)]
            place[:, :own] = dot_tn(grad[:, lanes], a_v[:, dq_at:dq_end]).astype(BF16)
            place[:, own:] = dot_tn(grad[:, lanes], b_v[:, :LANES]).astype(BF16)
    gate_give.pass_on()
    out_sum.advance(1)
    qkv_sum.start()

    stream(x_in, jnp.int32(0), False)

    def token_block(i, _):
        rows = pl.ds(pl.multiple_of(i * ROWS, ROWS), ROWS)

        @pl.when(i + 1 < blocks)
        def _():
            stream(x_in, i + 1, False)

        normed_grad = dot_nt(a_v[rows, dq_at:dq_end], w_attn[:, :own]) + dot_nt(b_v[rows, :LANES], w_attn[:, own:columns])
        stream(x_in, i, True)
        x = hid_stage[lax.rem(i, 2)].astype(F32)
        r1 = lax.rsqrt(jnp.mean(x * x, axis=-1, keepdims=True) + EPSILON)
        gain_own[1:2, :] += jnp.sum(normed_grad * (x * r1), axis=0, keepdims=True)
        weighted = normed_grad * attn_gain
        mean = jnp.mean(weighted * x, axis=-1, keepdims=True)
        piece = r1 * weighted - x * (r1 * r1 * r1 * mean)
        for c in range(n):
            lanes = slice(c * own_width, (c + 1) * own_width)
            mine = jnp.where(me == c, hidden_grad[rows, :], 0.0)
            grad[rows, lanes] = (piece[:, lanes] + mine).astype(BF16)
        return 0

    lax.fori_loop(0, blocks, token_block, 0)

    def token_rows(c):
        return grad.at[pl.ds(pl.multiple_of(c * per_device, per_device), per_device)]

    third = scatter(2, token_rows, near3, far3, stage_wide.at[pl.ds(0, per_device)])
    third.start()
    gain_give = spread(5, gain_own, gain_all)
    gain_mine = load(gain_own, gain_all.at[me], 21)
    gain_give.start()
    gate_give.late()
    third.pass_on()
    out_sum.advance(2)
    gain_give.pass_on()
    up_sum.take(last)
    up_give = give(2, up_sum, up_all)
    third.late()
    qkv_sum.advance(1)
    gain_give.finish()
    gain_mine.wait()
    gain_give.drain()
    gain_own[...] = sum(gain_all[c] for c in range(n))
    gain_sum.start()
    token_out[...] = token_rows(me)[...].astype(F32)
    third.finish(token_out)
    out_sum.take(last)
    out_give = give(3, out_sum, out_all)
    up_give.pass_on()
    qkv_sum.advance(2)
    gain_sum.advance(1)
    out_give.pass_on()
    up_give.late()
    gain_sum.advance(2)
    out_give.late()
    qkv_sum.take(last)
    qkv_give = give(4, qkv_sum, qkv_all)
    gain_sum.take(last)
    gain_out[...] = gain_block_of(plane)[...]
    qkv_give.pass_on()
    qkv_give.late()
    for out, mine in spreads:
        out.finish()
        out.drain()
        mine.wait()
    for s in (second, third):
        s.drain()
    for s in (down_sum, gate_sum, up_sum, out_sum, qkv_sum, gain_sum):
        s.drain()


def backward(n, planes, heads, lengths, grad, saved, weights, cos, sin):
    x, normed, q_rot, k_rot, v_rows, lse, att_all, hidden, normed2, a, b, mixed = saved
    w_attn, w_gate, w_up, w_down, gains = weights
    total, width = grad.shape
    own = heads * HEAD_SIZE
    own_width = width // n
    own_ff = a.shape[1]
    rows_shard = width // planes
    slab = own_ff // planes
    columns = own + LANES
    chips = n // 2
    per_device = total // n
    col, row = (chips, total, own_width), (chips, per_device, width)
    outs = [
        ((per_device, width), F32),
        ((8, rows_shard), F32),
        ((n, slab, width), BF16),
        ((n, rows_shard, own_ff), BF16),
        ((n, rows_shard, own_ff), BF16),
        ((n, rows_shard, own_width), BF16),
        ((n, rows_shard, columns), BF16),
        (col, BF16),
        (col, BF16),
        (col, BF16),
        (col, BF16),
        (row, BF16),
        (row, BF16),
        ((planes + 1, slab, width), BF16),
        ((planes + 1, rows_shard, own_ff), BF16),
        ((planes + 1, rows_shard, own_ff), BF16),
        ((planes + 1, rows_shard, own_width), BF16),
        ((planes + 1, rows_shard, columns), BF16),
    ]
    scratch = [
        (w_attn.shape, BF16),
        (w_gate.shape, BF16),
        (w_up.shape, BF16),
        (w_down.shape, BF16),
        (w_down.shape, BF16),
        (gains.shape, F32),
        ((total, width), BF16),
        ((total, own_ff), BF16),
        ((total, own_ff), BF16),
        ((n, total, own_width), BF16),
        ((2, ROWS, width), BF16),
        ((rows_shard, own_ff), BF16),
        ((slab, width), BF16),
        ((total, own_width), BF16),
        ((total, own_width), F32),
        (lse.shape, F32),
        (cos.shape, F32),
        (sin.shape, F32),
        ((total, LANES), F32),
        ((total, LANES), F32),
        ((8, width), F32),
        ((n, 8, width), F32),
        ((planes + 1, 8, rows_shard), F32),
        ((8, rows_shard), F32),
    ]
    steps = planes - 1
    dma = pltpu.SemaphoreType.DMA
    anywhere = pl.BlockSpec(memory_space=pl.ANY)
    vmem = pl.BlockSpec(memory_space=pltpu.VMEM)
    return pl.pallas_call(
        functools.partial(backward_kernel, n, planes, heads),
        in_specs=[pl.BlockSpec(memory_space=pltpu.SMEM)] + [anywhere] * 20,
        out_specs=[vmem] * 2 + [anywhere] * (len(outs) - 2),
        out_shape=[jax.ShapeDtypeStruct(*o) for o in outs],
        scratch_shapes=[pltpu.VMEM(*s) for s in scratch]
        + [
            dma((6, 2, steps)),
            dma((6, 2, steps)),
            dma((3, 10)),
            dma((3, 10)),
            dma((6, n)),
            dma((6, n)),
            dma((24,)),
            dma((2,)),
            dma,
        ],
        compiler_params=pltpu.CompilerParams(
            vmem_limit_bytes=60 * 1024 * 1024, collective_id=2, has_side_effects=True
        ),
        cost_estimate=pl.CostEstimate(
            flops=16 * total * width * own_ff, bytes_accessed=100 * 1024 * 1024, transcendentals=0
        ),
        name="backward",
    )(
        lengths,
        grad,
        mixed,
        a,
        b,
        hidden,
        normed2,
        normed,
        x,
        att_all,
        q_rot,
        k_rot,
        v_rows,
        lse,
        cos,
        sin,
        w_attn,
        w_gate,
        w_up,
        w_down,
        gains,
    )[:7]


def kernel_fits(n, planes, total, width, own_ff):
    held = 4 * width * own_ff + 2 * total * width + 2 * total * own_ff
    return planes == 4 and n == 8 and own_ff // planes >= total // n and n * own_ff >= 4 * width and 2 * held < 44 * 1024 * 1024 and (own_ff // planes) % LANES == 0


def own_columns(array, index, width):
    return lax.dynamic_slice_in_dim(array, index * width, width, axis=1)


def after(value, *others):
    return lax.optimization_barrier((value, *others))[0]


def local(
    tokens,
    lengths,
    deal,
    attn_gain,
    query_weight,
    key_matrix,
    value_matrix,
    out_weight,
    mlp_gain,
    gate_weight,
    up_weight,
    down_weight,
    cotangent,
):
    n_ctx = lax.axis_size("ctx")
    n_fsdp = lax.axis_size("fsdp")
    me = lax.axis_index("ctx")
    me_array = me.astype(jnp.int32).reshape(1)
    per_device, width = tokens.shape[1], tokens.shape[2]
    total = per_device * n_ctx
    block_rows = per_device // n_ctx
    heads = QUERY_HEADS // n_ctx
    sharing = n_ctx // KEY_VALUE_HEADS
    own_width = width // n_ctx
    ff = gate_weight.shape[1]
    slab = ff // (n_fsdp * n_ctx)
    own_ff = slab * n_fsdp
    rows_shard = query_weight.shape[0]

    kv_head = me // sharing
    split = heads * HEAD_SIZE
    attn_shard = jnp.concatenate(
        [
            own_columns(query_weight, me, split),
            own_columns(key_matrix, kv_head, HEAD_SIZE),
            own_columns(value_matrix, kv_head, HEAD_SIZE),
            own_columns(out_weight, me, own_width),
        ],
        axis=1,
    )

    def ff_columns(array):
        return jnp.concatenate([own_columns(array, f * n_ctx + me, slab) for f in range(n_fsdp)], axis=1)

    gain_shard = jnp.tile(jnp.concatenate([attn_gain, mlp_gain]).astype(F32)[None], (8, 1))

    first_len = lengths[0, 0]
    given = jnp.arange(total, dtype=jnp.int32)
    position = given - jnp.where(given >= first_len, first_len, 0)
    freq_index = jnp.arange(HEAD_SIZE // 2, dtype=F32)
    inverse = ROPE_BASE ** (-2.0 * freq_index / HEAD_SIZE)
    angles = position.astype(F32)[:, None] * inverse[None, :]
    cos, sin = jnp.cos(angles), jnp.sin(angles)
    cos_table = jnp.concatenate([cos, cos, cos, cos], axis=1)
    sin_table = jnp.concatenate([-sin, sin, -sin, sin], axis=1)

    deal_rows = deal[0]
    slot_ids = jnp.arange(n_ctx, dtype=jnp.int32)
    dealt_of_given = (deal_rows * n_ctx + slot_ids[:, None]).reshape(-1)
    matched = deal_rows[:, :, None] == slot_ids[None, None, :]
    source_slot = jnp.sum(jnp.where(matched, slot_ids[None, :, None], 0), axis=1)
    given_of_dealt = (slot_ids[:, None] * n_ctx + source_slot).T.reshape(-1)

    def reorder(array, table):
        blocks = array.reshape(n_ctx * n_ctx, block_rows, array.shape[1])
        return jnp.take(blocks, table, axis=0, mode="clip").reshape(array.shape)

    cotangent_all = lax.all_gather(cotangent[0], "ctx", axis=0, tiled=True)
    (
        x, normed, q_rot, k_rot, v_rows, lse, attended_all, hidden_all, normed2, a, b, mixed, w_attn, w_gate, w_up, w_down, gains_all,
    ) = forward(
        n_ctx,
        n_fsdp,
        heads,
        lengths[0],
        tokens[0],
        attn_shard,
        ff_columns(gate_weight),
        ff_columns(up_weight),
        lax.dynamic_slice_in_dim(down_weight, me * slab, slab, axis=0),
        gain_shard,
        cos_table,
        sin_table,
    )
    w_qkv, w_out = w_attn[:, : split + 2 * HEAD_SIZE], w_attn[:, split + 2 * HEAD_SIZE :]
    gains = gains_all.reshape(n_fsdp, 8, 2, rows_shard)[:, 0].transpose(1, 0, 2).reshape(2, 1, width)
    hidden_own = own_columns(hidden_all, me, own_width)
    grad_result = reorder(cotangent_all, dealt_of_given)

    both = jnp.concatenate([mixed, (hidden_own.astype(F32) * (1.0 / RESIDUAL_SCALE)).astype(BF16)], axis=1)
    column = lax.broadcasted_iota(jnp.int32, (own_width, width), 1) - me * own_width
    place = (column == lax.broadcasted_iota(jnp.int32, (own_width, width), 0)).astype(BF16)
    result_part = RESIDUAL_SCALE * dot_nn(reorder(both, given_of_dealt), jnp.concatenate([w_down, place], axis=0))
    activations = lax.psum_scatter(
        result_part.astype(BF16), "ctx", scatter_dimension=0, tiled=True
    )[None]

    if kernel_fits(n_ctx, n_fsdp, total, width, own_ff):
        token_grad, gain_rows, down_part, gate_part, up_part, out_part, qkv_part = backward(
            n_ctx,
            n_fsdp,
            heads,
            lengths[0],
            grad_result,
            (x, normed, q_rot, k_rot, v_rows, lse, attended_all, hidden_all, normed2, a, b, mixed),
            (w_attn, w_gate, w_up, w_down, gains_all),
            cos_table,
            sin_table,
        )
        token_grad = token_grad[None]
        own_gains = gain_rows[1::-1]
    else:
        mlp_grad = (RESIDUAL_SCALE * grad_result.astype(F32)).astype(BF16)

        def settle(left, right):
            return lax.psum_scatter(dot_tn(left, right).astype(BF16), "fsdp", scatter_dimension=0, tiled=True)

        down_part = settle(mixed, mlp_grad)
        ggrad, ugrad, hidden_part, mlp_gain_part = mlp_backward(
            n_ctx, mlp_grad, a, b, hidden_all, gains[1], w_gate, w_up, w_down
        )
        hidden_sum = lax.psum_scatter(hidden_part, "ctx", scatter_dimension=0, tiled=False)
        gate_part = settle(normed2, ggrad)
        up_part = settle(normed2, ugrad)
        hidden_grad, branch_grad, attended_part = branch_backward(
            hidden_sum, own_columns(grad_result, me, own_width), w_out, n_ctx
        )
        attended_grad = lax.psum_scatter(attended_part, "ctx", scatter_dimension=0, tiled=False)
        out_part = lax.psum_scatter(
            jnp.einsum("ctk,to->cko", attended_all, branch_grad, preferred_element_type=F32)
            .astype(BF16)
            .reshape(width, own_width),
            "fsdp",
            scatter_dimension=0,
            tiled=True,
        )
        dq, dkv = attention_backward(attended_grad, q_rot, k_rot, v_rows, lse, cos_table, sin_table, lengths[0])
        qkv_part = settle(normed, jnp.concatenate([dq, dkv], axis=1))
        token_part, attn_gain_part = token_backward(me_array, dq, dkv, w_qkv, x, gains[0], hidden_grad)
        token_grad = lax.psum_scatter(token_part, "ctx", scatter_dimension=0, tiled=True).astype(F32)[None]

        gain_parts = jnp.concatenate([attn_gain_part, mlp_gain_part], axis=0)
        step = 1
        while step < n_ctx:
            gain_parts = gain_parts + lax.ppermute(gain_parts, "ctx", [(c, c ^ step) for c in range(n_ctx)])
            step *= 2
        gain_rows = gain_parts.reshape(2, n_fsdp, rows_shard).transpose(1, 0, 2).reshape(n_fsdp, 2 * rows_shard)
        own_gains = lax.psum_scatter(gain_rows, "fsdp", scatter_dimension=0, tiled=True).reshape(2, rows_shard)
        down_part, gate_part, up_part, out_part, qkv_part = [
            lax.all_gather(p, "ctx", axis=0, tiled=False) for p in (down_part, gate_part, up_part, out_part, qkv_part)
        ]

    down_grad = down_part.reshape(n_ctx * slab, width).astype(F32)
    if slab % LANES == 0:
        gate_grad = spread_columns(gate_part, slab, n_fsdp)
        up_grad = spread_columns(up_part, slab, n_fsdp)
    else:

        def ff_whole(part):
            pieces = part.reshape(n_ctx, rows_shard, n_fsdp, slab)
            return pieces.transpose(1, 2, 0, 3).reshape(rows_shard, ff).astype(F32)

        gate_grad = ff_whole(gate_part)
        up_grad = ff_whole(up_part)
    out_grad = spread_columns(out_part, own_width, 1)
    qkv_all = qkv_part
    query_grad = spread_columns(qkv_all, split, 1)

    def shared_heads(pieces):
        pieces = pieces.astype(F32).reshape(KEY_VALUE_HEADS, sharing, rows_shard, HEAD_SIZE).sum(axis=1)
        return pieces.transpose(1, 0, 2).reshape(rows_shard, KEY_VALUE_HEADS * HEAD_SIZE)

    key_grad = shared_heads(qkv_all[:, :, split : split + HEAD_SIZE])
    value_grad = shared_heads(qkv_all[:, :, split + HEAD_SIZE :])

    return (
        activations,
        token_grad,
        own_gains[0],
        query_grad,
        key_grad,
        value_grad,
        out_grad,
        own_gains[1],
        gate_grad,
        up_grad,
        down_grad,
    )


def solution(mesh):
    rows = P("fsdp", None)
    block = P("fsdp", "ctx", None)
    gain = P("fsdp")
    return jax.shard_map(
        local,
        mesh=mesh,
        in_specs=(block, rows, P("fsdp", None, None), gain, rows, rows, rows, rows, gain, rows, rows, rows, block),
        out_specs=(block, block, gain, rows, rows, rows, rows, gain, rows, rows, rows),
        check_vma=False,
    )
```

```python
import functools

import jax
import jax.numpy as jnp
from jax import lax
from jax.experimental import pallas as pl
from jax.experimental.pallas import tpu as pltpu
from jax.sharding import PartitionSpec as P

QUERY_HEADS = 32
KEY_VALUE_HEADS = 8
HEAD_SIZE = 64
EPSILON = 1e-05
ROPE_BASE = 10000000.0
SCORE_SCALE = 0.015625
RESIDUAL_SCALE = 0.22
NEGATIVE_BIG = -1e30
LANES = 128
ROWS = 256
BF16 = jnp.bfloat16
F32 = jnp.float32
VMEM_LIMIT = 59 * 1024 * 1024


def dot_nn(a, b):
    return lax.dot_general(a, b, (((1,), (0,)), ((), ())), preferred_element_type=F32)


def dot_nt(a, b):
    return lax.dot_general(a, b, (((1,), (1,)), ((), ())), preferred_element_type=F32)


def dot_tn(a, b):
    return lax.dot_general(a, b, (((0,), (0,)), ((), ())), preferred_element_type=F32)


def swap_halves(x):
    lane = lax.broadcasted_iota(jnp.int32, x.shape, 1)
    first = lax.rem(lane, HEAD_SIZE) < HEAD_SIZE // 2
    return jnp.where(first, pltpu.roll(x, LANES - HEAD_SIZE // 2, 1), pltpu.roll(x, HEAD_SIZE // 2, 1))


def low_half(shape):
    return lax.broadcasted_iota(jnp.int32, shape, 1) < HEAD_SIZE


def mask_bias(first_len, row0, rows, cols):
    query = row0 + lax.broadcasted_iota(jnp.int32, (rows, cols), 0)
    key = lax.broadcasted_iota(jnp.int32, (rows, cols), 1)
    start = jnp.where(query >= first_len, first_len, 0)
    return jnp.where((key <= query) & (key >= start), 0.0, NEGATIVE_BIG)


def attention_backward_kernel(length_ref, g_ref, q_ref, k_ref, v_ref, lse_ref, cos_ref, sin_ref, dq_ref, dkv_ref, dk_sum, dv_sum):
    pair = pl.program_id(0)
    tokens = q_ref.shape[0]

    @pl.when(pair == 0)
    def _():
        dk_sum[...] = jnp.zeros_like(dk_sum)
        dv_sum[...] = jnp.zeros_like(dv_sum)

    first_len = length_ref[0]
    for block in range(tokens // ROWS):
        rows = pl.ds(block * ROWS, ROWS)
        end = (block + 1) * ROWS
        bias = mask_bias(first_len, block * ROWS, ROWS, end)
        query, grad = q_ref[rows, :], g_ref[rows, :]
        low = low_half(query.shape)
        keys, values = k_ref[:end, :], v_ref[:end, :]
        parts = []
        for half in range(2):
            chosen = low if half == 0 else jnp.logical_not(low)
            own_query = jnp.where(chosen, query, jnp.zeros_like(query))
            own_grad = jnp.where(chosen, grad, jnp.zeros_like(grad))
            scores = dot_nt(own_query, keys) + bias
            probs = jnp.exp(scores - lse_ref[0, rows, half : half + 1])
            prob_grad = dot_nt(own_grad, values)
            delta = jnp.sum(probs * prob_grad, axis=-1, keepdims=True)
            score_grad = (probs * (prob_grad - delta)).astype(BF16)
            parts.append(dot_nn(score_grad, keys))
            dk_sum[:end, :] += dot_tn(score_grad, own_query)
            dv_sum[:end, :] += dot_tn(probs.astype(BF16), own_grad)
        dq = jnp.where(low_half(parts[0].shape), parts[0], parts[1]) * SCORE_SCALE
        dq_ref[rows, :] = (dq * cos_ref[rows, :] - swap_halves(dq) * sin_ref[rows, :]).astype(BF16)

    @pl.when(pair == pl.num_programs(0) - 1)
    def _():
        dk = dk_sum[...]
        dk = dk + pltpu.roll(dk, HEAD_SIZE, 1)
        dk = dk * cos_ref[...] - swap_halves(dk) * sin_ref[...]
        dv = dv_sum[...]
        dv = dv + pltpu.roll(dv, HEAD_SIZE, 1)
        dkv_ref[...] = jnp.where(low_half(dk.shape), dk, dv).astype(BF16)


def attention_backward(grads, q_rot, k_rot, v_rows, lse, cos, sin, lengths):
    tokens = q_rot.shape[0]
    pairs = q_rot.shape[1] // LANES
    one = pl.BlockSpec((tokens, LANES), lambda j: (0, 0))
    each = pl.BlockSpec((tokens, LANES), lambda j: (0, j))
    return pl.pallas_call(
        attention_backward_kernel,
        grid=(pairs,),
        in_specs=[
            pl.BlockSpec(memory_space=pltpu.SMEM),
            each,
            each,
            one,
            one,
            pl.BlockSpec((1, tokens, LANES), lambda j: (j, 0, 0)),
            one,
            one,
        ],
        out_specs=[each, one],
        out_shape=[
            jax.ShapeDtypeStruct((tokens, pairs * LANES), BF16),
            jax.ShapeDtypeStruct((tokens, LANES), BF16),
        ],
        scratch_shapes=[pltpu.VMEM((tokens, LANES), F32), pltpu.VMEM((tokens, LANES), F32)],
        compiler_params=pltpu.CompilerParams(vmem_limit_bytes=VMEM_LIMIT),
        cost_estimate=pl.CostEstimate(
            flops=10 * tokens * tokens * LANES * pairs,
            bytes_accessed=12 * tokens * pairs * LANES,
            transcendentals=tokens * tokens * pairs,
        ),
        name="attend_back",
    )(lengths, grads, q_rot, k_rot, v_rows, lse, cos, sin)


def row_block(width):
    return pl.BlockSpec((ROWS, width), lambda i: (i, 0))


def fixed(*shape):
    return pl.BlockSpec(shape, lambda i: (0,) * len(shape))


def params():
    return pltpu.CompilerParams(vmem_limit_bytes=VMEM_LIMIT)


def cost(flops, *arrays):
    moved = sum(a.size * a.dtype.itemsize for a in arrays)
    return pl.CostEstimate(flops=flops, bytes_accessed=moved, transcendentals=0)


def mlp_back_kernel(
    grad_ref, a_ref, b_ref, hidden_ref, gain_ref, gate_ref, up_ref, down_ref, ggrad_ref, ugrad_ref, part_ref, gain_out
):
    mixed_grad = dot_nt(grad_ref[...], down_ref[...])
    ggrad = (mixed_grad * a_ref[...].astype(F32)).astype(BF16)
    ugrad = (mixed_grad * b_ref[...].astype(F32)).astype(BF16)
    ggrad_ref[...] = ggrad
    ugrad_ref[...] = ugrad
    normed_grad = dot_nt(ggrad, gate_ref[...]) + dot_nt(ugrad, up_ref[...])
    hidden = hidden_ref[...].astype(F32)
    r2 = lax.rsqrt(jnp.mean(hidden * hidden, axis=-1, keepdims=True) + EPSILON)
    gain_part = jnp.sum(normed_grad * (hidden * r2), axis=0, keepdims=True)

    @pl.when(pl.program_id(0) == 0)
    def _():
        gain_out[...] = jnp.zeros_like(gain_out)

    gain_out[...] += gain_part
    weighted = normed_grad * gain_ref[...]
    mean = jnp.mean(weighted * hidden, axis=-1, keepdims=True)
    part = r2 * weighted - hidden * (r2 * r2 * r2 * mean)
    own = part_ref.shape[2]
    for c in range(part_ref.shape[0]):
        part_ref[c] = part[:, c * own : (c + 1) * own].astype(BF16)


def mlp_backward(n, mlp_grad, a, b, hidden_all, gain, w_gate, w_up, w_down):
    total, width = hidden_all.shape
    own = width // n
    own_ff = w_gate.shape[1]
    narrow = jax.ShapeDtypeStruct((total, own_ff), BF16)
    planes = pl.BlockSpec((n, ROWS, own), lambda i: (0, i, 0))
    return pl.pallas_call(
        mlp_back_kernel,
        grid=(total // ROWS,),
        in_specs=[
            row_block(width),
            row_block(own_ff),
            row_block(own_ff),
            row_block(width),
            fixed(1, width),
            fixed(width, own_ff),
            fixed(width, own_ff),
            fixed(own_ff, width),
        ],
        out_specs=[row_block(own_ff), row_block(own_ff), planes, fixed(1, width)],
        out_shape=[narrow, narrow, jax.ShapeDtypeStruct((n, total, own), BF16), jax.ShapeDtypeStruct((1, width), F32)],
        compiler_params=params(),
        cost_estimate=cost(6 * total * width * own_ff, mlp_grad, hidden_all, hidden_all, w_gate, w_up, w_down, a, b, a, b),
        name="mlp_backward",
    )(mlp_grad, a, b, hidden_all, gain, w_gate, w_up, w_down)


def branch_kernel(part_ref, grad_ref, w_ref, hidden_ref, branch_ref, out_ref):
    hidden_grad = part_ref[...].astype(F32) + grad_ref[...].astype(F32)
    hidden_ref[...] = hidden_grad
    branch = (RESIDUAL_SCALE * hidden_grad).astype(BF16)
    branch_ref[...] = branch
    own = out_ref.shape[2]
    for c in range(out_ref.shape[0]):
        out_ref[c] = dot_nt(branch, w_ref[c]).astype(BF16)


def branch_backward(hidden_part, grad_own, w_out, n):
    total, own_width = hidden_part.shape
    own = w_out.shape[0] // n
    w_heads = w_out.reshape(n, own, own_width)
    return pl.pallas_call(
        branch_kernel,
        grid=(total // ROWS,),
        in_specs=[row_block(own_width), row_block(own_width), fixed(n, own, own_width)],
        out_specs=[row_block(own_width), row_block(own_width), pl.BlockSpec((n, ROWS, own), lambda i: (0, i, 0))],
        out_shape=[
            jax.ShapeDtypeStruct((total, own_width), F32),
            jax.ShapeDtypeStruct((total, own_width), BF16),
            jax.ShapeDtypeStruct((n, total, own), BF16),
        ],
        compiler_params=params(),
        cost_estimate=cost(2 * total * own_width * own * n, hidden_part, hidden_part, hidden_part, w_out),
        name="branch_backward",
    )(hidden_part, grad_own, w_heads)


def token_kernel(me_ref, dq_ref, dkv_ref, w_ref, x_ref, gain_ref, hidden_ref, part_ref, gain_out):
    split = dq_ref.shape[1]
    normed_grad = dot_nt(dq_ref[...], w_ref[:, :split]) + dot_nt(dkv_ref[...], w_ref[:, split:])
    x = x_ref[...].astype(F32)
    r1 = lax.rsqrt(jnp.mean(x * x, axis=-1, keepdims=True) + EPSILON)

    @pl.when(pl.program_id(0) == 0)
    def _():
        gain_out[...] = jnp.zeros_like(gain_out)

    gain_out[...] += jnp.sum(normed_grad * (x * r1), axis=0, keepdims=True)
    weighted = normed_grad * gain_ref[...]
    mean = jnp.mean(weighted * x, axis=-1, keepdims=True)
    part = r1 * weighted - x * (r1 * r1 * r1 * mean)
    own_width = hidden_ref.shape[1]
    for c in range(part.shape[1] // own_width):
        piece = part[:, c * own_width : (c + 1) * own_width]
        piece = piece + jnp.where(me_ref[0] == c, hidden_ref[...], 0.0)
        part_ref[:, c * own_width : (c + 1) * own_width] = piece.astype(BF16)


def token_backward(me, dq, dkv, w_qkv, x, gain, hidden_grad):
    total, width = x.shape
    own_width = hidden_grad.shape[1]
    return pl.pallas_call(
        token_kernel,
        grid=(total // ROWS,),
        in_specs=[
            pl.BlockSpec(memory_space=pltpu.SMEM),
            row_block(dq.shape[1]),
            row_block(dkv.shape[1]),
            fixed(*w_qkv.shape),
            row_block(width),
            fixed(1, width),
            row_block(own_width),
        ],
        out_specs=[row_block(width), fixed(1, width)],
        out_shape=[jax.ShapeDtypeStruct((total, width), BF16), jax.ShapeDtypeStruct((1, width), F32)],
        compiler_params=params(),
        cost_estimate=cost(2 * total * width * w_qkv.shape[1], x, x, w_qkv, dq, dkv, hidden_grad),
        name="token_backward",
    )(me, dq, dkv, w_qkv, x, gain, hidden_grad)


def finish_kernel(slab, gate_ref, up_ref, down_ref, out_ref, qkv_ref, gate_out, up_out, down_out, out_out, q_out, k_out, v_out):
    n = gate_ref.shape[0]
    for src, dst, piece in ((gate_ref, gate_out, slab), (up_ref, up_out, slab), (out_ref, out_out, out_ref.shape[2])):
        for c in range(n):
            for f in range(src.shape[2] // piece):
                at = (f * n + c) * piece
                dst[:, at : at + piece] = src[c, :, f * piece : (f + 1) * piece].astype(F32)
    down_out[...] = down_ref[...].astype(F32)
    split = qkv_ref.shape[2] - LANES
    for c in range(n):
        q_out[:, c * split : (c + 1) * split] = qkv_ref[c, :, :split].astype(F32)
    for pair in range(n // 2):
        even = qkv_ref[2 * pair, :, split:].astype(F32)
        odd = qkv_ref[2 * pair + 1, :, split:].astype(F32)
        low = low_half(even.shape)
        lanes = slice(pair * LANES, (pair + 1) * LANES)
        k_out[:, lanes] = jnp.where(low, even, pltpu.roll(odd, HEAD_SIZE, 1))
        v_out[:, lanes] = jnp.where(low, pltpu.roll(even, HEAD_SIZE, 1), odd)


def finish(slab, gate, up, down, out, qkv):
    n, rows, own_ff = gate.shape
    width = n * out.shape[2]
    steps = 16
    tile, down_tile = rows // steps, down.shape[0] // steps
    kv = n * HEAD_SIZE

    def by_device(columns):
        return pl.BlockSpec((n, tile, columns), lambda i: (0, i, 0))

    def flat(height, columns):
        return pl.BlockSpec((height, columns), lambda i: (i, 0))

    outs = [
        (flat(tile, n * own_ff), (rows, n * own_ff)),
        (flat(tile, n * own_ff), (rows, n * own_ff)),
        (flat(down_tile, width), down.shape),
        (flat(tile, width), (rows, width)),
        (flat(tile, width), (rows, width)),
        (flat(tile, kv), (rows, kv)),
        (flat(tile, kv), (rows, kv)),
    ]
    return pl.pallas_call(
        functools.partial(finish_kernel, slab),
        grid=(steps,),
        in_specs=[
            by_device(own_ff),
            by_device(own_ff),
            flat(down_tile, width),
            by_device(out.shape[2]),
            by_device(qkv.shape[2]),
        ],
        out_specs=[spec for spec, _ in outs],
        out_shape=[jax.ShapeDtypeStruct(shape, F32) for _, shape in outs],
        compiler_params=params(),
        cost_estimate=cost(0, gate, gate, gate, up, up, up, down, down, down),
        name="finish",
    )(gate, up, down, out, qkv)


def spread_kernel(in_ref, out_ref):
    slab = in_ref.shape[2]
    for c in range(in_ref.shape[0]):
        out_ref[:, c * slab : (c + 1) * slab] = in_ref[c].astype(F32)


def spread_columns(pieces, slab, groups):
    n, rows, _ = pieces.shape
    tile = 128
    out_shape = jax.ShapeDtypeStruct((rows, groups * n * slab), F32)
    return pl.pallas_call(
        spread_kernel,
        grid=(groups, rows // tile),
        in_specs=[pl.BlockSpec((n, tile, slab), lambda f, r: (0, r, f))],
        out_specs=pl.BlockSpec((tile, n * slab), lambda f, r: (r, f)),
        out_shape=out_shape,
        compiler_params=params(),
        cost_estimate=cost(0, pieces, out_shape),
        name="spread_columns",
    )(pieces)


MESH = pl.DeviceIdType.MESH


class Chain:
    def __init__(self, slot, planes, plane, send_sem, recv_sem):
        self.slot, self.planes, self.plane = slot, planes, plane
        self.send_sem, self.recv_sem = send_sem, recv_sem

    def copy(self, way, step, shard, to):
        return pltpu.make_async_remote_copy(
            src_ref=self.slot(shard),
            dst_ref=self.slot(shard),
            send_sem=self.send_sem.at[way, step],
            recv_sem=self.recv_sem.at[way, step],
            device_id={"fsdp": to},
            device_id_type=MESH,
        )

    def moves(self, step):
        p, last = self.plane, self.planes - 1
        return (
            (0, (p >= step) & (p < last), p - step, p + 1, p >= step + 1, p - 1 - step),
            (1, (p + step <= last) & (p > 0), p + step, p - 1, p + step + 1 <= last, p + 1 + step),
        )

    def start(self, step):
        for way, sends, shard, to, _, _ in self.moves(step):

            @pl.when(sends)
            def _(way=way, shard=shard, to=to):
                self.copy(way, step, shard, to).start()

    def arrive(self, step):
        for way, _, _, _, receives, shard in self.moves(step):

            @pl.when(receives)
            def _(way=way, shard=shard):
                self.copy(way, step, shard, self.plane).wait_recv()

    def advance(self, step):
        self.arrive(step - 1)
        self.start(step)

    def drain(self):
        for step in range(self.planes - 1):
            for way, sends, shard, to, _, _ in self.moves(step):

                @pl.when(sends)
                def _(way=way, shard=shard, to=to, step=step):
                    self.copy(way, step, shard, to).wait_send()


class Spread:
    def __init__(self, src, slot, n, me, send_sem, recv_sem):
        self.src, self.slot, self.n, self.me = src, slot, n, me
        self.send_sem, self.recv_sem = send_sem, recv_sem
        self.chips = n // 2
        self.chip, self.core = me // 2, lax.rem(me, 2)
        self.partner = me + 1 - 2 * self.core

    def at(self, k):
        return lax.rem(self.chip + k, self.chips) * 2 + self.core

    def copy(self, src, owner, sem, to):
        return pltpu.make_async_remote_copy(
            src_ref=src,
            dst_ref=self.slot(owner),
            send_sem=self.send_sem.at[sem],
            recv_sem=self.recv_sem.at[sem],
            device_id={"ctx": to},
            device_id_type=MESH,
        )

    def out(self, k):
        return self.copy(self.src, self.me, k, self.at(k))

    def relay(self, k):
        owner = self.at(self.chips - k) if k else self.me
        src = self.slot(owner) if k else self.src
        return self.copy(src, owner, self.chips + k, self.partner)

    def start(self):
        for k in range(1, self.chips):
            self.out(k).start()
        self.relay(0).start()

    def pass_on(self):
        for k in range(1, self.chips):
            self.copy(self.src, self.at(self.chips - k), k, self.me).wait_recv()
            self.relay(k).start()

    def late(self):
        pass

    def finish(self):
        other = 1 - 2 * self.core
        for k in range(self.chips):
            owner = (self.at(self.chips - k) if k else self.me) + other
            self.copy(self.slot(owner), owner, self.chips + k, self.me).wait_recv()

    def drain(self):
        for k in range(1, self.chips):
            self.out(k).wait_send()
        for k in range(self.chips):
            self.relay(k).wait_send()


class Spread4:
    def __init__(self, src, slot, n, me, send_sem, recv_sem):
        self.src, self.slot, self.me = src, slot, me
        self.send_sem, self.recv_sem = send_sem, recv_sem
        self.core = lax.rem(me, 2)
        self.other = 1 - self.core
        chip = me // 2
        self.near, self.side, self.far = square(chip)
        self.chip = chip
        self.half = src.shape[0] // 2

    def copy(self, src, dst, sem, to):
        return pltpu.make_async_remote_copy(
            src_ref=src,
            dst_ref=dst,
            send_sem=self.send_sem.at[sem],
            recv_sem=self.recv_sem.at[sem],
            device_id={"ctx": to},
            device_id_type=MESH,
        )

    def part(self, owner, which):
        return self.slot(owner).at[pl.ds(which * self.half, self.half)]

    def out(self, sem):
        chip = self.near if sem == 1 else self.side
        return self.copy(self.src, self.slot(self.me), sem, chip * 2 + self.core)

    def onward(self, sem):
        origin, to, which = (self.near, self.side, 0) if sem == 3 else (self.side, self.near, 1)
        owner = origin * 2 + self.core
        return self.copy(self.part(owner, which), self.part(owner, which), sem, to * 2 + self.core)

    def relay(self, k):
        owner = (self.chip, self.near, self.side, self.far)[k] * 2 + self.core
        src = self.slot(owner) if k else self.src
        return self.copy(src, self.slot(owner), 4 + k, self.chip * 2 + self.other)

    def start(self):
        self.out(1).start()
        self.out(2).start()
        self.relay(0).start()

    def pass_on(self):
        for k, chip in ((1, self.near), (2, self.side)):
            owner = chip * 2 + self.core
            self.copy(self.src, self.slot(owner), k, self.me).wait_recv()
            self.onward(3 if k == 1 else 0).start()
            self.relay(k).start()

    def late(self):
        owner = self.far * 2 + self.core
        for sem, which in ((3, 0), (0, 1)):
            self.copy(self.part(owner, which), self.part(owner, which), sem, self.me).wait_recv()
        self.relay(3).start()

    def finish(self):
        for k, chip in enumerate((self.chip, self.near, self.side, self.far)):
            owner = chip * 2 + self.other
            self.copy(self.slot(owner), self.slot(owner), 4 + k, self.me).wait_recv()

    def drain(self):
        for sem in (1, 2):
            self.out(sem).wait_send()
        for sem in (3, 0):
            self.onward(sem).wait_send()
        for k in range(4):
            self.relay(k).wait_send()


def square(chip):
    return chip + 1 - 2 * lax.rem(chip, 2), chip + 2 - 4 * (chip // 2), 3 - chip


def spread_over(n, src, *rest):
    return (Spread4 if n == 8 and src.shape[0] % 32 == 0 else Spread)(src, *rest)


def greet(n, planes, me, plane, across):
    barrier = pltpu.get_barrier_semaphore()
    chips = n // 2
    core = lax.rem(me, 2)
    others = [lax.rem(me // 2 + k, chips) * 2 + core for k in range(1, chips)] + [me + 1 - 2 * core]
    for other in others:
        pl.semaphore_signal(barrier, inc=1, device_id={"ctx": other}, device_id_type=MESH)
    if across:

        @pl.when(plane > 0)
        def _():
            pl.semaphore_signal(barrier, inc=1, device_id={"fsdp": plane - 1}, device_id_type=MESH)

        @pl.when(plane < planes - 1)
        def _():
            pl.semaphore_signal(barrier, inc=1, device_id={"fsdp": plane + 1}, device_id_type=MESH)

    count = len(others)
    if across:
        count = count + (plane > 0).astype(jnp.int32) + (plane < planes - 1).astype(jnp.int32)
    pl.semaphore_wait(barrier, count)


def forward_kernel(
    n,
    planes,
    heads,
    length_ref,
    tokens_ref,
    attn_shard,
    gate_ref,
    up_ref,
    down_ref,
    gain_shard,
    cos_ref,
    sin_ref,
    x_out,
    normed_out,
    q_out,
    k_out,
    v_out,
    lse_out,
    att_out,
    hid_out,
    normed2_out,
    a_out,
    b_out,
    mixed_out,
    attn_out,
    gate_out,
    up_out,
    down_out,
    gain_out,
    w_attn,
    w_gate,
    w_up,
    w_down,
    gains,
    x_all,
    qkv,
    q_rot,
    k_rot,
    v_rows,
    lse,
    own_att,
    att_all,
    own_hid,
    own_scaled,
    wide,
    narrow,
    z_send,
    z_recv,
    c_send,
    c_recv,
    keep_sem,
    load_sem,
    wide_sem,
    narrow_sem,
):
    me, plane = lax.axis_index("ctx"), lax.axis_index("fsdp")
    per_device, width = tokens_ref.shape
    total = x_all.shape[0]
    rows_shard = attn_shard.shape[0]
    own = own_att.shape[1]
    own_width = own_hid.shape[1]
    columns = qkv.shape[1]
    blocks = total // ROWS
    pairs = heads // 2

    local_copies = []

    def keep(src, dst, index):
        copy = pltpu.make_async_copy(src, dst, keep_sem.at[index])
        copy.start()
        local_copies.append(copy)

    def chain(index, ref, rows):
        return Chain(lambda s: ref.at[pl.ds(s * rows, rows)], planes, plane, z_send.at[index], z_recv.at[index])

    attn_chain = chain(0, w_attn, rows_shard)
    gate_chain = chain(1, w_gate, rows_shard)
    up_chain = chain(2, w_up, rows_shard)
    slab = w_down.shape[0] // planes
    down_chain = chain(3, w_down, slab)
    gain_chain = chain(4, gains, gain_shard.shape[0])
    own_ff = w_gate.shape[1]
    loads = [
        pltpu.make_async_copy(shard, c.slot(plane), keep_sem.at[i])
        for i, (c, shard) in enumerate(((attn_chain, attn_shard), (gain_chain, gain_shard)))
    ]
    for ref, c, at in ((gate_ref, gate_chain, 0), (up_ref, up_chain, 1)):
        for f in range(ref.shape[1] // (n * slab)):
            src = ref.at[:, pl.ds(pl.multiple_of((f * n + me) * slab, LANES), slab)]
            dst = c.slot(plane).at[:, pl.ds(f * slab, slab)]
            loads.append(pltpu.make_async_copy(src, dst, load_sem.at[at, f]))
        if ref.shape[1] == own_ff:
            loads.append(pltpu.make_async_copy(ref, c.slot(plane), load_sem.at[at, 0]))
    down_src = down_ref if down_ref.shape[0] == slab else down_ref.at[pl.ds(pl.multiple_of(me * slab, slab), slab)]
    loads.append(pltpu.make_async_copy(down_src, down_chain.slot(plane), load_sem.at[2, 0]))
    for load in loads:
        load.start()
    own_x = pltpu.make_async_copy(tokens_ref, x_all.at[pl.ds(me * per_device, per_device)], keep_sem.at[5])
    own_x.start()
    greet(n, planes, me, plane, True)
    loads[0].wait()
    attn_chain.start(0)
    loads[1].wait()
    gain_chain.start(0)
    x_spread = spread_over(
        n, tokens_ref, lambda c: x_all.at[pl.ds(c * per_device, per_device)], n, me, c_send.at[0], c_recv.at[0]
    )
    x_spread.start()
    for load in loads[2:]:
        load.wait()
    own_x.wait()
    for step in range(1, planes - 1):
        attn_chain.advance(step)
        gain_chain.advance(step)
    gate_chain.start(0)
    up_chain.start(0)
    x_spread.pass_on()
    x_spread.late()
    x_spread.finish()
    x_copy = pltpu.make_async_copy(x_all, x_out, keep_sem.at[0])
    x_copy.start()
    attn_chain.arrive(planes - 2)
    gain_chain.arrive(planes - 2)
    keep(w_attn, attn_out, 1)
    keep(gains, gain_out, 2)
    half = gain_shard.shape[1] // 2
    step_rows = gain_shard.shape[0]
    attn_gain = jnp.concatenate([gains[f * step_rows : f * step_rows + 1, :half] for f in range(planes)], axis=1)
    mlp_gain = jnp.concatenate([gains[f * step_rows : f * step_rows + 1, half:] for f in range(planes)], axis=1)

    def staged(stage, sem, slot, out, rows, wait_before):
        copy = pltpu.make_async_copy(stage.at[slot], out.at[rows], sem.at[slot])
        return copy.wait() if wait_before else copy.start()

    def project_block(i, _):
        rows = pl.ds(pl.multiple_of(i * ROWS, ROWS), ROWS)
        slot = lax.rem(i, 2)

        @pl.when(i >= 2)
        def _():
            staged(wide, wide_sem, slot, normed_out, rows, True)

        own_hid[rows, :] = x_all[rows, pl.ds(pl.multiple_of(me * own_width, LANES), own_width)]
        x = x_all[rows, :].astype(F32)
        r1 = lax.rsqrt(jnp.mean(x * x, axis=-1, keepdims=True) + EPSILON)
        normed = (x * r1 * attn_gain).astype(BF16)
        wide[slot] = normed
        staged(wide, wide_sem, slot, normed_out, rows, False)
        qkv[rows, :] = dot_nn(normed, w_attn[:, :columns])
        return 0

    lax.fori_loop(0, blocks, project_block, 0)
    for i in range(max(blocks - 2, 0), blocks):
        staged(wide, wide_sem, i % 2, normed_out, pl.ds(i * ROWS, ROWS), True)

    split = columns - LANES
    cos, sin = cos_ref[...], sin_ref[...]
    kv = qkv[:, split:]
    turned = pltpu.roll(kv, HEAD_SIZE, 1)
    low = low_half(kv.shape)
    k = jnp.where(low, kv, turned)
    k_rot[...] = (k * cos + swap_halves(k) * sin).astype(BF16)
    v_rows[...] = jnp.where(low, turned, kv).astype(BF16)
    keep(k_rot, k_out, 3)
    keep(v_rows, v_out, 4)
    first_len = length_ref[0]

    def attend_pair(pair, _):
        lanes = pl.ds(pl.multiple_of(pair * LANES, LANES), LANES)
        q = qkv[:, lanes]
        q_rot[:, lanes] = ((q * cos_ref[...] + swap_halves(q) * sin_ref[...]) * SCORE_SCALE).astype(BF16)
        for block in range(blocks):
            rows = pl.ds(block * ROWS, ROWS)
            end = (block + 1) * ROWS
            bias = mask_bias(first_len, block * ROWS, ROWS, end)
            query = q_rot[rows, lanes]
            lower = low_half(query.shape)
            keys, values = k_rot[:end, :], v_rows[:end, :]
            parts = []
            for side in range(2):
                chosen = lower if side == 0 else jnp.logical_not(lower)
                scores = dot_nt(jnp.where(chosen, query, jnp.zeros_like(query)), keys) + bias
                top = jnp.max(scores, axis=-1, keepdims=True)
                weights = jnp.exp(scores - top)
                whole = jnp.sum(weights, axis=-1, keepdims=True)
                probs = (weights * (1.0 / whole)).astype(BF16)
                parts.append(dot_nn(probs, values))
                lse[pair, rows, side : side + 1] = top + jnp.log(whole)
            own_att[rows, lanes] = jnp.where(low_half(parts[0].shape), parts[0], parts[1]).astype(BF16)
        return 0

    lax.fori_loop(0, pairs, attend_pair, 0)
    att_spread = spread_over(n, own_att, lambda c: att_all.at[c], n, me, c_send.at[1], c_recv.at[1])
    x_copy.wait()
    x_spread.drain()
    att_spread.start()
    own_a = pltpu.make_async_copy(own_att, att_all.at[me], keep_sem.at[5])
    own_a.start()
    keep(q_rot, q_out, 6)
    keep(lse, lse_out, 7)
    if planes > 2:
        gate_chain.advance(1)
        up_chain.advance(1)
    att_spread.pass_on()
    att_spread.late()
    own_a.wait()
    att_spread.finish()
    keep(att_all, att_out, 8)

    def out_block(i, _):
        rows = pl.ds(pl.multiple_of(i * ROWS, ROWS), ROWS)
        acc = jnp.zeros((ROWS, own_width), F32)
        for c in range(n):
            acc += dot_nn(att_all[c, rows, :], w_attn[c * own : (c + 1) * own, columns:])
        hidden = own_hid[rows, :].astype(F32) + RESIDUAL_SCALE * acc
        own_hid[rows, :] = hidden.astype(BF16)
        own_scaled[rows, :] = (hidden * (1.0 / RESIDUAL_SCALE)).astype(BF16)
        return 0

    lax.fori_loop(0, blocks, out_block, 0)
    def hid_slot(c):
        return x_all.at[:, pl.ds(pl.multiple_of(c * own_width, LANES), own_width)]

    hid_spread = spread_over(n, own_hid, hid_slot, n, me, c_send.at[2], c_recv.at[2])
    hid_spread.start()
    keep(own_scaled, mixed_out.at[:, pl.ds(own_ff, own_width)], 13)
    own_h = pltpu.make_async_copy(own_hid, hid_slot(me), keep_sem.at[5])
    own_h.start()
    for step in range(2, planes - 1):
        gate_chain.advance(step)
        up_chain.advance(step)
    down_chain.start(0)
    hid_spread.pass_on()
    hid_spread.late()
    own_h.wait()
    hid_spread.finish()
    keep(x_all, hid_out, 9)
    gate_chain.arrive(planes - 2)
    up_chain.arrive(planes - 2)
    keep(w_gate, gate_out, 10)
    keep(w_up, up_out, 11)
    if planes > 2:
        down_chain.advance(1)

    def mlp_copies(i, rows, wait):
        slot = lax.rem(i, 2)
        staged(wide, wide_sem, slot, normed2_out, rows, wait)
        for j, out in enumerate((a_out, b_out, mixed_out.at[:, pl.ds(0, own_ff)])):
            staged(narrow.at[j], narrow_sem.at[j], slot, out, rows, wait)

    def mlp_block(i, _):
        rows = pl.ds(pl.multiple_of(i * ROWS, ROWS), ROWS)
        slot = lax.rem(i, 2)

        @pl.when(i >= 2)
        def _():
            mlp_copies(i, rows, True)

        hidden = x_all[rows, :].astype(F32)
        r2 = lax.rsqrt(jnp.mean(hidden * hidden, axis=-1, keepdims=True) + EPSILON)
        normed = (hidden * r2 * mlp_gain).astype(BF16)
        wide[slot] = normed
        gate = dot_nn(normed, w_gate[...])
        up = dot_nn(normed, w_up[...])
        sig = jax.nn.sigmoid(gate)
        silu = gate * sig
        narrow[2, slot] = (silu * up).astype(BF16)
        narrow[1, slot] = silu.astype(BF16)
        narrow[0, slot] = (up * sig * (1.0 + gate * (1.0 - sig))).astype(BF16)
        mlp_copies(i, rows, False)
        return 0

    lax.fori_loop(0, blocks, mlp_block, 0)
    for step in range(2, planes - 1):
        down_chain.advance(step)
    for i in range(max(blocks - 2, 0), blocks):
        mlp_copies(i, pl.ds(i * ROWS, ROWS), True)
    down_chain.arrive(planes - 2)
    keep(w_down, down_out, 12)
    for c in (attn_chain, gain_chain, gate_chain, up_chain, down_chain):
        c.drain()
    for s in (att_spread, hid_spread):
        s.drain()
    for copy in local_copies:
        copy.wait()


def forward(n, planes, heads, slab, lengths, tokens, attn_shard, gate, up, down, gain_shard, cos, sin):
    per_device, width = tokens.shape
    total = per_device * n
    own = heads * HEAD_SIZE
    columns = own + 2 * HEAD_SIZE
    own_width = attn_shard.shape[1] - columns
    own_ff = planes * slab
    rows_shard = attn_shard.shape[0]
    pairs = heads // 2
    weights = [
        ((planes * rows_shard, attn_shard.shape[1]), BF16),
        ((planes * rows_shard, own_ff), BF16),
        ((planes * rows_shard, own_ff), BF16),
        ((own_ff, width), BF16),
        ((planes * gain_shard.shape[0], gain_shard.shape[1]), F32),
    ]
    outs = [
        ((total, width), BF16),
        ((total, width), BF16),
        ((total, own), BF16),
        ((total, LANES), BF16),
        ((total, LANES), BF16),
        ((pairs, total, LANES), F32),
        ((n, total, own), BF16),
        ((total, width), BF16),
        ((total, width), BF16),
        ((total, own_ff), BF16),
        ((total, own_ff), BF16),
        ((total, own_ff + own_width), BF16),
    ] + weights
    scratch = weights + [
        ((total, width), BF16),
        ((total, columns), F32),
        ((total, own), BF16),
        ((total, LANES), BF16),
        ((total, LANES), BF16),
        ((pairs, total, LANES), F32),
        ((total, own), BF16),
        ((n, total, own), BF16),
        ((total, own_width), BF16),
        ((total, own_width), BF16),
        ((2, ROWS, width), BF16),
        ((3, 2, ROWS, own_ff), BF16),
    ]
    steps = max(planes - 1, 1)
    dma = pltpu.SemaphoreType.DMA
    anywhere = pl.BlockSpec(memory_space=pl.ANY)
    vmem = pl.BlockSpec(memory_space=pltpu.VMEM)
    return pl.pallas_call(
        functools.partial(forward_kernel, n, planes, heads),
        in_specs=[pl.BlockSpec(memory_space=pltpu.SMEM), vmem] + [anywhere] * 5 + [vmem] * 2,
        out_specs=[anywhere] * len(outs),
        out_shape=[jax.ShapeDtypeStruct(*o) for o in outs],
        scratch_shapes=[pltpu.VMEM(*s) for s in scratch]
        + [dma((5, 2, steps)), dma((5, 2, steps)), dma((3, n)), dma((3, n)), dma((16,)), dma((3, planes)), dma((2,)), dma((3, 2))],
        compiler_params=pltpu.CompilerParams(
            vmem_limit_bytes=VMEM_LIMIT, collective_id=1, has_side_effects=True
        ),
        cost_estimate=pl.CostEstimate(
            flops=2 * total * width * (columns + own_width + 2 * own_ff),
            bytes_accessed=60 * 1024 * 1024,
            transcendentals=0,
        ),
        name="forward",
    )(lengths, tokens, attn_shard, gate, up, down, gain_shard, cos, sin)


def add_into(dst, src):
    rows_in = dst.shape[0]
    chunk = 64 if rows_in % 64 == 0 else 32

    def step(i, _):
        rows = pl.ds(pl.multiple_of(i * chunk, chunk), chunk)
        dst[rows, :] = (dst[rows, :].astype(F32) + src[rows, :].astype(F32)).astype(dst.dtype)
        return 0

    if rows_in < chunk:
        dst[...] = dst[...] + src[...]
    else:
        lax.fori_loop(0, rows_in // chunk, step, 0)


def fetch(src, dst, sem):
    copy = pltpu.make_async_copy(src, dst, sem)
    copy.start()
    copy.wait()


class Settle:
    def __init__(self, block, landed, stage, planes, plane, send_sem, recv_sem, load_sem):
        self.block, self.landed, self.stage = block, landed, stage
        self.planes, self.plane = planes, plane
        self.send_sem, self.recv_sem, self.load_sem = send_sem, recv_sem, load_sem

    def slot(self, way, shard, at):
        return shard if way == 0 else jnp.where(shard == at, self.planes, shard)

    def sends(self, step):
        p, last = self.plane, self.planes - 1
        return (
            (0, (p <= step) & (p < last), last - step + p, p + 1),
            (1, (last - p <= step) & (p > 0), step - last + p, p - 1),
        )

    def receives(self, step):
        p, last = self.plane, self.planes - 1
        return (
            (0, (p >= 1) & (p - 1 <= step), last - step + p - 1),
            (1, (p <= last - 1) & (last - p - 1 <= step), step - last + p + 1),
        )

    def copy(self, way, step, shard, to):
        return pltpu.make_async_remote_copy(
            src_ref=self.block(shard),
            dst_ref=self.landed.at[self.slot(way, shard, to)],
            send_sem=self.send_sem.at[way, step],
            recv_sem=self.recv_sem.at[way, step],
            device_id={"fsdp": to},
            device_id_type=MESH,
        )

    def start(self, step=0):
        for way, active, shard, to in self.sends(step):

            @pl.when(active)
            def _(way=way, shard=shard, to=to):
                self.copy(way, step, shard, to).start()

    def take(self, step):
        for way, active, shard in self.receives(step):

            @pl.when(active)
            def _(way=way, shard=shard):
                self.copy(way, step, shard, self.plane).wait_recv()
                fetch(self.landed.at[self.slot(way, shard, self.plane)], self.stage, self.load_sem)
                add_into(self.block(shard), self.stage)

    def advance(self, step):
        self.take(step - 1)
        self.start(step)

    def drain(self):
        for step in range(self.planes - 1):
            for way, active, shard, to in self.sends(step):

                @pl.when(active)
                def _(way=way, shard=shard, to=to, step=step):
                    self.copy(way, step, shard, to).wait_send()


class Scatter:
    def __init__(self, block, near, far, stage, me, send_sem, recv_sem, load_sem):
        self.block, self.landed, self.far, self.stage = block, near, far, stage
        self.send_sem, self.recv_sem, self.load_sem = send_sem, recv_sem, load_sem
        self.core = lax.rem(me, 2)
        self.chip = me // 2
        self.chips = (self.chip, *square(self.chip))
        self.half = stage.shape[0] // 2

    def rows(self, which):
        return pl.ds(which * self.half, self.half)

    def own(self, k):
        return self.block(self.chips[k] * 2 + self.core)

    def copy(self, src, dst, sem, chip, core):
        return pltpu.make_async_remote_copy(
            src_ref=src,
            dst_ref=dst,
            send_sem=self.send_sem.at[sem],
            recv_sem=self.recv_sem.at[sem],
            device_id={"ctx": chip * 2 + core},
            device_id_type=MESH,
        )

    def first(self, k):
        other = 1 - self.core
        return self.copy(self.block(self.chips[k] * 2 + other), self.landed.at[k], k, self.chip, other)

    def second(self, k, to, which):
        place = self.far.at[to - 1 if k == to else 2, self.rows(which)]
        sem = 4 + 2 * (to - 1) + which if k == to else 7 + to
        return self.copy(self.own(k).at[self.rows(which)], place, sem, self.chips[to], self.core)

    def start(self):
        for k in (3, 1, 2, 0):
            self.first(k).start()

    def add(self, k):
        self.first(k).wait_recv()
        fetch(self.landed.at[k], self.stage, self.load_sem)
        add_into(self.own(k), self.stage)

    def pass_on(self):
        self.add(3)
        self.second(3, 1, 0).start()
        self.second(3, 2, 1).start()
        self.add(1)
        self.second(1, 1, 0).start()
        self.add(2)
        self.second(2, 2, 1).start()

    def late(self):
        for to, which, k in ((1, 0, 2), (2, 1, 1)):
            self.second(3, to, which).wait_recv()
            place = self.stage.at[self.rows(which)]
            fetch(self.far.at[2, self.rows(which)], place, self.load_sem)
            add_into(self.own(k).at[self.rows(which)], place)
            self.second(k, k, which).start()

    def finish(self, total):
        self.first(0).wait_recv()
        fetch(self.landed.at[0], self.stage, self.load_sem)
        add_into(total, self.stage)
        for k in (1, 2):
            for which in (0, 1):
                self.second(k, k, which).wait_recv()
            fetch(self.far.at[k - 1], self.stage, self.load_sem)
            add_into(total, self.stage)

    def drain(self):
        for k in range(4):
            self.first(k).wait_send()
        for k, to, which in ((3, 1, 0), (3, 2, 1), (1, 1, 0), (1, 1, 1), (2, 2, 0), (2, 2, 1)):
            self.second(k, to, which).wait_send()


def backward_kernel(
    n,
    planes,
    heads,
    length_ref,
    grad_in,
    mixed_in,
    a_in,
    b_in,
    hidden_in,
    normed2_in,
    normed_in,
    x_in,
    att_in,
    q_in,
    k_in,
    v_in,
    lse_in,
    cos_in,
    sin_in,
    attn_in,
    gate_in,
    up_in,
    down_in,
    gain_in,
    token_out,
    gain_out,
    down_all,
    gate_all,
    up_all,
    out_all,
    qkv_all,
    near1,
    far1,
    near2,
    far2,
    near3,
    far3,
    down_landed,
    gate_landed,
    up_landed,
    out_landed,
    qkv_landed,
    w_attn,
    w_gate,
    w_up,
    w_down,
    p_down,
    gains,
    grad,
    a_v,
    b_v,
    part,
    hid_stage,
    stage_tall,
    stage_wide,
    stage_col,
    hidden_grad,
    lse,
    cos,
    sin,
    dk_sum,
    dv_sum,
    gain_own,
    gain_all,
    gain_landed,
    gain_stage,
    z_send,
    z_recv,
    s_send,
    s_recv,
    g_send,
    g_recv,
    load_sem,
    hid_sem,
    add_sem,
):
    me, plane = lax.axis_index("ctx"), lax.axis_index("fsdp")
    total, width = grad.shape
    per_device = total // n
    own = heads * HEAD_SIZE
    own_width = width // n
    own_ff = a_v.shape[1]
    rows_shard = width // planes
    slab = own_ff // planes
    blocks = total // ROWS
    pairs = heads // 2
    columns = own + LANES
    last = planes - 2

    def load(src, dst, index):
        copy = pltpu.make_async_copy(src, dst, load_sem.at[index])
        copy.start()
        return copy

    mixed_loads = [load(mixed_in.at[:, pl.ds(d * own_width, own_width)], part.at[d], d) for d in range(own_ff // own_width)]
    grad_load = load(grad_in, grad, 8)
    down_load = load(down_in, w_down, 9)
    gate_load = load(gate_in, w_gate, 10)
    up_load = load(up_in, w_up, 11)
    a_load = load(a_in, a_v, 12)
    b_load = load(b_in, b_v, 13)
    attn_load = load(attn_in, w_attn, 14)
    gain_load = load(gain_in, gains, 15)
    greet(n, planes, me, plane, True)

    def settle(index, block, landed, stage):
        return Settle(block, landed, stage, planes, plane, z_send.at[index], z_recv.at[index], add_sem)

    def rows_of(ref, rows):
        return lambda d: ref.at[pl.ds(pl.multiple_of(d * rows, rows), rows)]

    def out_block_of(d):
        return w_down.at[pl.ds(0, rows_shard), pl.ds(pl.multiple_of(d * own_width, LANES), own_width)]

    def qkv_block_of(d):
        return w_down.at[pl.ds(rows_shard, rows_shard), pl.ds(pl.multiple_of(d * columns, LANES), columns)]

    def gain_block_of(d):
        return gain_own.at[:, pl.ds(pl.multiple_of(d * rows_shard, LANES), rows_shard)]

    down_sum = settle(0, rows_of(p_down, slab), down_landed, stage_wide)
    gate_sum = settle(1, rows_of(w_gate, rows_shard), gate_landed, stage_tall)
    up_sum = settle(2, rows_of(w_up, rows_shard), up_landed, stage_tall)
    out_sum = settle(3, out_block_of, out_landed, stage_tall.at[:, pl.ds(0, own_width)])
    qkv_sum = settle(4, qkv_block_of, qkv_landed, stage_tall.at[:, pl.ds(0, columns)])
    gain_sum = settle(5, gain_block_of, gain_landed, gain_stage)

    def spread(index, src, dst):
        return spread_over(n, src, lambda c: dst.at[c], n, me, g_send.at[index], g_recv.at[index])

    spreads = []

    def give(index, sums, dst):
        src = sums.block(plane)
        mine = load(src, dst.at[me], 16 + index)
        out = spread(index, src, dst)
        out.start()
        spreads.append((out, mine))
        return out

    def scatter(index, block, near, far, stage):
        return Scatter(block, near, far, stage, me, s_send.at[index], s_recv.at[index], add_sem)

    grad_load.wait()

    def scale_block(i, _):
        rows = pl.ds(pl.multiple_of(i * ROWS, ROWS), ROWS)
        grad[rows, :] = (RESIDUAL_SCALE * grad[rows, :].astype(F32)).astype(BF16)
        return 0

    lax.fori_loop(0, blocks, scale_block, 0)
    for copy in mixed_loads:
        copy.wait()

    def down_block(d, _):
        p_down[pl.ds(pl.multiple_of(d * own_width, own_width), own_width), :] = dot_tn(part[d], grad[...]).astype(BF16)
        return 0

    lax.fori_loop(0, own_ff // own_width, down_block, 0)
    down_sum.start()

    for copy in (down_load, gate_load, up_load, a_load, b_load, attn_load, gain_load):
        copy.wait()
    half = gains.shape[1] // 2
    attn_gain = jnp.concatenate([gains[f * 8 : f * 8 + 1, :half] for f in range(planes)], axis=1)
    mlp_gain = jnp.concatenate([gains[f * 8 : f * 8 + 1, half:] for f in range(planes)], axis=1)
    gain_own[...] = jnp.zeros_like(gain_own)

    def stream(src, i, wait):
        rows = pl.ds(pl.multiple_of(i * ROWS, ROWS), ROWS)
        slot = lax.rem(i, 2)
        copy = pltpu.make_async_copy(src.at[rows], hid_stage.at[slot], hid_sem.at[slot])
        return copy.wait() if wait else copy.start()

    stream(hidden_in, jnp.int32(0), False)

    def mlp_block(i, _):
        rows = pl.ds(pl.multiple_of(i * ROWS, ROWS), ROWS)

        @pl.when(i + 1 < blocks)
        def _():
            stream(hidden_in, i + 1, False)

        mixed_grad = dot_nt(grad[rows, :], w_down[...])
        ggrad = (mixed_grad * a_v[rows, :].astype(F32)).astype(BF16)
        ugrad = (mixed_grad * b_v[rows, :].astype(F32)).astype(BF16)
        a_v[rows, :] = ggrad
        b_v[rows, :] = ugrad
        normed_grad = dot_nt(ggrad, w_gate[...]) + dot_nt(ugrad, w_up[...])
        stream(hidden_in, i, True)

        @pl.when(i == blocks - 2)
        def _():
            down_sum.advance(1)

        hidden = hid_stage[lax.rem(i, 2)].astype(F32)
        r2 = lax.rsqrt(jnp.mean(hidden * hidden, axis=-1, keepdims=True) + EPSILON)
        gain_own[0:1, :] += jnp.sum(normed_grad * (hidden * r2), axis=0, keepdims=True)
        weighted = normed_grad * mlp_gain
        mean = jnp.mean(weighted * hidden, axis=-1, keepdims=True)
        piece = r2 * weighted - hidden * (r2 * r2 * r2 * mean)
        for c in range(n):
            part[c, rows, :] = piece[:, c * own_width : (c + 1) * own_width].astype(BF16)
        return 0

    lax.fori_loop(0, blocks, mlp_block, 0)
    first = scatter(0, lambda c: part.at[c], near1, far1, stage_col)
    first.start()
    normed2_load = load(normed2_in, grad, 8)
    normed2_load.wait()

    def columns_times(right, out):
        def block(j, _):
            lanes = pl.ds(pl.multiple_of(j * ROWS, ROWS), ROWS)
            out[lanes, :] = dot_tn(grad[:, lanes], right[...]).astype(BF16)
            return 0

        lax.fori_loop(0, width // ROWS, block, 0)

    columns_times(a_v, w_gate)
    gate_sum.start()
    first.pass_on()
    columns_times(b_v, w_up)
    first.late()
    down_sum.advance(2)

    att_loads = [load(att_in.at[c], grad.at[:, pl.ds(c * own, own)], c) for c in range(n)]
    own_grad = load(grad_in.at[:, pl.ds(pl.multiple_of(me * own_width, LANES), own_width)], b_v.at[:, pl.ds(LANES, own_width)], 8)
    q_load = load(q_in, a_v.at[:, pl.ds(0, own)], 9)
    k_load = load(k_in, a_v.at[:, pl.ds(own, LANES)], 10)
    v_load = load(v_in, a_v.at[:, pl.ds(own + LANES, LANES)], 11)
    lse_load = load(lse_in, lse, 12)
    cos_load = load(cos_in, cos, 13)
    sin_load = load(sin_in, sin, 14)
    own_grad.wait()

    def begin(i, _):
        rows = pl.ds(pl.multiple_of(i * ROWS, ROWS), ROWS)
        hidden_grad[rows, :] = b_v[rows, LANES : LANES + own_width].astype(F32) + part[me, rows, :].astype(F32)
        return 0

    lax.fori_loop(0, blocks, begin, 0)
    first.finish(hidden_grad)
    first.drain()

    def branch_block(i, _):
        rows = pl.ds(pl.multiple_of(i * ROWS, ROWS), ROWS)
        branch = (RESIDUAL_SCALE * hidden_grad[rows, :]).astype(BF16)
        b_v[rows, LANES : LANES + own_width] = branch
        for c in range(n):
            part[c, rows, :] = dot_nt(branch, w_attn[c * own : (c + 1) * own, columns:]).astype(BF16)
        return 0

    lax.fori_loop(0, blocks, branch_block, 0)
    second = scatter(1, lambda c: part.at[c], near2, far2, stage_col)
    second.start()
    gate_sum.advance(1)
    for copy in att_loads:
        copy.wait()
    heads_per_shard = rows_shard // own
    for c in range(n):
        place = out_block_of(c // heads_per_shard).at[pl.ds((c % heads_per_shard) * own, own)]
        place[...] = dot_tn(grad[:, c * own : (c + 1) * own], b_v[:, LANES : LANES + own_width]).astype(BF16)
    second.pass_on()
    normed_load = load(normed_in, grad, 15)
    down_sum.take(last)
    up_sum.start()
    second.late()
    second.finish(part.at[me])
    down_give = give(0, down_sum, down_all)
    gate_sum.advance(2)

    for copy in (q_load, k_load, v_load, lse_load, cos_load, sin_load):
        copy.wait()
    dk_sum[...] = jnp.zeros_like(dk_sum)
    dv_sum[...] = jnp.zeros_like(dv_sum)
    first_len = length_ref[0]
    dq_at = own + 2 * LANES

    def attend_pair(pair, _):
        lanes = pl.ds(pl.multiple_of(pair * LANES, LANES), LANES)
        dq_lanes = pl.ds(pl.multiple_of(dq_at + pair * LANES, LANES), LANES)
        for block in range(blocks):
            rows = pl.ds(block * ROWS, ROWS)
            end = (block + 1) * ROWS
            bias = mask_bias(first_len, block * ROWS, ROWS, end)
            query, grads = a_v[rows, lanes], part[me, rows, lanes]
            low = low_half(query.shape)
            keys, values = a_v[:end, own : own + LANES], a_v[:end, own + LANES : own + 2 * LANES]
            parts = []
            for side in range(2):
                chosen = low if side == 0 else jnp.logical_not(low)
                own_query = jnp.where(chosen, query, jnp.zeros_like(query))
                own_grads = jnp.where(chosen, grads, jnp.zeros_like(grads))
                scores = dot_nt(own_query, keys) + bias
                probs = jnp.exp(scores - lse[pair, rows, side : side + 1])
                prob_grad = dot_nt(own_grads, values)
                delta = jnp.sum(probs * prob_grad, axis=-1, keepdims=True)
                score_grad = (probs * (prob_grad - delta)).astype(BF16)
                parts.append(dot_nn(score_grad, keys))
                dk_sum[:end, :] += dot_tn(score_grad, own_query)
                dv_sum[:end, :] += dot_tn(probs.astype(BF16), own_grads)
            dq = jnp.where(low_half(parts[0].shape), parts[0], parts[1]) * SCORE_SCALE
            a_v[rows, dq_lanes] = (dq * cos[rows, :] - swap_halves(dq) * sin[rows, :]).astype(BF16)

        @pl.when(pair == 0)
        def _():
            down_give.pass_on()
            up_sum.advance(1)

        return 0

    lax.fori_loop(0, pairs, attend_pair, 0)
    dk = dk_sum[...]
    dk = dk + pltpu.roll(dk, HEAD_SIZE, 1)
    dk = dk * cos[...] - swap_halves(dk) * sin[...]
    dv = dv_sum[...]
    dv = dv + pltpu.roll(dv, HEAD_SIZE, 1)
    b_v[:, :LANES] = jnp.where(low_half(dk.shape), dk, dv).astype(BF16)
    down_give.late()
    gate_sum.take(last)
    gate_give = give(1, gate_sum, gate_all)
    up_sum.advance(2)
    out_sum.start()

    normed_load.wait()
    dq_end = dq_at + own
    for d in range(planes):
        for j in range(rows_shard // ROWS):
            lanes = slice(d * rows_shard + j * ROWS, d * rows_shard + (j + 1) * ROWS)
            place = qkv_block_of(d).at[pl.ds(j * ROWS, ROWS)]
            place[:, :own] = dot_tn(grad[:, lanes], a_v[:, dq_at:dq_end]).astype(BF16)
            place[:, own:] = dot_tn(grad[:, lanes], b_v[:, :LANES]).astype(BF16)
    gate_give.pass_on()
    out_sum.advance(1)
    qkv_sum.start()

    stream(x_in, jnp.int32(0), False)

    def token_block(i, _):
        rows = pl.ds(pl.multiple_of(i * ROWS, ROWS), ROWS)

        @pl.when(i + 1 < blocks)
        def _():
            stream(x_in, i + 1, False)

        normed_grad = dot_nt(a_v[rows, dq_at:dq_end], w_attn[:, :own]) + dot_nt(b_v[rows, :LANES], w_attn[:, own:columns])
        stream(x_in, i, True)
        x = hid_stage[lax.rem(i, 2)].astype(F32)
        r1 = lax.rsqrt(jnp.mean(x * x, axis=-1, keepdims=True) + EPSILON)
        gain_own[1:2, :] += jnp.sum(normed_grad * (x * r1), axis=0, keepdims=True)
        weighted = normed_grad * attn_gain
        mean = jnp.mean(weighted * x, axis=-1, keepdims=True)
        piece = r1 * weighted - x * (r1 * r1 * r1 * mean)
        for c in range(n):
            lanes = slice(c * own_width, (c + 1) * own_width)
            mine = jnp.where(me == c, hidden_grad[rows, :], 0.0)
            grad[rows, lanes] = (piece[:, lanes] + mine).astype(BF16)
        return 0

    lax.fori_loop(0, blocks, token_block, 0)

    def token_rows(c):
        return grad.at[pl.ds(pl.multiple_of(c * per_device, per_device), per_device)]

    third = scatter(2, token_rows, near3, far3, stage_wide.at[pl.ds(0, per_device)])
    third.start()
    gain_give = spread(5, gain_own, gain_all)
    gain_mine = load(gain_own, gain_all.at[me], 21)
    gain_give.start()
    gate_give.late()
    third.pass_on()
    out_sum.advance(2)
    gain_give.pass_on()
    up_sum.take(last)
    up_give = give(2, up_sum, up_all)
    third.late()
    qkv_sum.advance(1)
    gain_give.finish()
    gain_mine.wait()
    gain_give.drain()
    gain_own[...] = sum(gain_all[c] for c in range(n))
    gain_sum.start()
    token_out[...] = token_rows(me)[...].astype(F32)
    third.finish(token_out)
    out_sum.take(last)
    out_give = give(3, out_sum, out_all)
    up_give.pass_on()
    qkv_sum.advance(2)
    gain_sum.advance(1)
    out_give.pass_on()
    up_give.late()
    gain_sum.advance(2)
    out_give.late()
    qkv_sum.take(last)
    qkv_give = give(4, qkv_sum, qkv_all)
    gain_sum.take(last)
    gain_out[...] = gain_block_of(plane)[...]
    qkv_give.pass_on()
    qkv_give.late()
    for out, mine in spreads:
        out.finish()
        out.drain()
        mine.wait()
    for s in (second, third):
        s.drain()
    for s in (down_sum, gate_sum, up_sum, out_sum, qkv_sum, gain_sum):
        s.drain()


def backward(n, planes, heads, lengths, grad, saved, weights, cos, sin):
    x, normed, q_rot, k_rot, v_rows, lse, att_all, hidden, normed2, a, b, mixed = saved
    w_attn, w_gate, w_up, w_down, gains = weights
    total, width = grad.shape
    own = heads * HEAD_SIZE
    own_width = width // n
    own_ff = a.shape[1]
    rows_shard = width // planes
    slab = own_ff // planes
    columns = own + LANES
    chips = n // 2
    per_device = total // n
    col, row = (chips, total, own_width), (chips, per_device, width)
    outs = [
        ((per_device, width), F32),
        ((8, rows_shard), F32),
        ((n, slab, width), BF16),
        ((n, rows_shard, own_ff), BF16),
        ((n, rows_shard, own_ff), BF16),
        ((n, rows_shard, own_width), BF16),
        ((n, rows_shard, columns), BF16),
        (col, BF16),
        (col, BF16),
        (col, BF16),
        (col, BF16),
        (row, BF16),
        (row, BF16),
        ((planes + 1, slab, width), BF16),
        ((planes + 1, rows_shard, own_ff), BF16),
        ((planes + 1, rows_shard, own_ff), BF16),
        ((planes + 1, rows_shard, own_width), BF16),
        ((planes + 1, rows_shard, columns), BF16),
    ]
    scratch = [
        (w_attn.shape, BF16),
        (w_gate.shape, BF16),
        (w_up.shape, BF16),
        (w_down.shape, BF16),
        (w_down.shape, BF16),
        (gains.shape, F32),
        ((total, width), BF16),
        ((total, own_ff), BF16),
        ((total, own_ff), BF16),
        ((n, total, own_width), BF16),
        ((2, ROWS, width), BF16),
        ((rows_shard, own_ff), BF16),
        ((slab, width), BF16),
        ((total, own_width), BF16),
        ((total, own_width), F32),
        (lse.shape, F32),
        (cos.shape, F32),
        (sin.shape, F32),
        ((total, LANES), F32),
        ((total, LANES), F32),
        ((8, width), F32),
        ((n, 8, width), F32),
        ((planes + 1, 8, rows_shard), F32),
        ((8, rows_shard), F32),
    ]
    steps = planes - 1
    dma = pltpu.SemaphoreType.DMA
    anywhere = pl.BlockSpec(memory_space=pl.ANY)
    vmem = pl.BlockSpec(memory_space=pltpu.VMEM)
    return pl.pallas_call(
        functools.partial(backward_kernel, n, planes, heads),
        in_specs=[pl.BlockSpec(memory_space=pltpu.SMEM)] + [anywhere] * 20,
        out_specs=[vmem] * 2 + [anywhere] * (len(outs) - 2),
        out_shape=[jax.ShapeDtypeStruct(*o) for o in outs],
        scratch_shapes=[pltpu.VMEM(*s) for s in scratch]
        + [
            dma((6, 2, steps)),
            dma((6, 2, steps)),
            dma((3, 10)),
            dma((3, 10)),
            dma((6, n)),
            dma((6, n)),
            dma((24,)),
            dma((2,)),
            dma,
        ],
        compiler_params=pltpu.CompilerParams(
            vmem_limit_bytes=60 * 1024 * 1024, collective_id=2, has_side_effects=True
        ),
        cost_estimate=pl.CostEstimate(
            flops=16 * total * width * own_ff, bytes_accessed=100 * 1024 * 1024, transcendentals=0
        ),
        name="backward",
    )(
        lengths,
        grad,
        mixed,
        a,
        b,
        hidden,
        normed2,
        normed,
        x,
        att_all,
        q_rot,
        k_rot,
        v_rows,
        lse,
        cos,
        sin,
        w_attn,
        w_gate,
        w_up,
        w_down,
        gains,
    )[:7]


def kernel_fits(n, planes, total, width, own_ff):
    held = 4 * width * own_ff + 2 * total * width + 2 * total * own_ff
    return planes == 4 and n == 8 and own_ff // planes >= total // n and n * own_ff >= 4 * width and 2 * held < 44 * 1024 * 1024 and (own_ff // planes) % LANES == 0


def own_columns(array, index, width):
    return lax.dynamic_slice_in_dim(array, index * width, width, axis=1)


def after(value, *others):
    return lax.optimization_barrier((value, *others))[0]


def local(
    tokens,
    lengths,
    deal,
    attn_gain,
    query_weight,
    key_matrix,
    value_matrix,
    out_weight,
    mlp_gain,
    gate_weight,
    up_weight,
    down_weight,
    cotangent,
):
    n_ctx = lax.axis_size("ctx")
    n_fsdp = lax.axis_size("fsdp")
    me = lax.axis_index("ctx")
    me_array = me.astype(jnp.int32).reshape(1)
    per_device, width = tokens.shape[1], tokens.shape[2]
    total = per_device * n_ctx
    block_rows = per_device // n_ctx
    heads = QUERY_HEADS // n_ctx
    sharing = n_ctx // KEY_VALUE_HEADS
    own_width = width // n_ctx
    ff = gate_weight.shape[1]
    slab = ff // (n_fsdp * n_ctx)
    own_ff = slab * n_fsdp
    rows_shard = query_weight.shape[0]

    kv_head = me // sharing
    split = heads * HEAD_SIZE
    attn_shard = jnp.concatenate(
        [
            own_columns(query_weight, me, split),
            own_columns(key_matrix, kv_head, HEAD_SIZE),
            own_columns(value_matrix, kv_head, HEAD_SIZE),
            own_columns(out_weight, me, own_width),
        ],
        axis=1,
    )

    def ff_columns(array):
        return jnp.concatenate([own_columns(array, f * n_ctx + me, slab) for f in range(n_fsdp)], axis=1)

    gain_shard = jnp.tile(jnp.concatenate([attn_gain, mlp_gain]).astype(F32)[None], (8, 1))

    first_len = lengths[0, 0]
    given = jnp.arange(total, dtype=jnp.int32)
    position = given - jnp.where(given >= first_len, first_len, 0)
    freq_index = jnp.arange(HEAD_SIZE // 2, dtype=F32)
    inverse = ROPE_BASE ** (-2.0 * freq_index / HEAD_SIZE)
    turns = jnp.tile(inverse, 4)
    sign = jnp.tile(jnp.repeat(jnp.array([-1.0, 1.0], F32), HEAD_SIZE // 2), 2)
    angles = position.astype(F32)[:, None] * turns[None, :]
    cos_table = jnp.cos(angles)
    sin_table = jnp.sin(angles) * sign[None, :]

    deal_rows = deal[0]
    slot_ids = jnp.arange(n_ctx, dtype=jnp.int32)
    dealt_of_given = (deal_rows * n_ctx + slot_ids[:, None]).reshape(-1)
    matched = deal_rows[:, :, None] == slot_ids[None, None, :]
    source_slot = jnp.sum(jnp.where(matched, slot_ids[None, :, None], 0), axis=1)
    given_of_dealt = (slot_ids[:, None] * n_ctx + source_slot).T.reshape(-1)

    def reorder(array, table):
        blocks = array.reshape(n_ctx * n_ctx, block_rows, array.shape[1])
        return jnp.take(blocks, table, axis=0, mode="clip").reshape(array.shape)

    ff_weights = gate_weight, up_weight, down_weight
    if slab % LANES:
        ff_weights = (
            ff_columns(gate_weight),
            ff_columns(up_weight),
            lax.dynamic_slice_in_dim(down_weight, me * slab, slab, axis=0),
        )

    cotangent_all = lax.all_gather(cotangent[0], "ctx", axis=0, tiled=True)
    (
        x, normed, q_rot, k_rot, v_rows, lse, attended_all, hidden_all, normed2, a, b, both, w_attn, w_gate, w_up, w_down, gains_all,
    ) = forward(
        n_ctx,
        n_fsdp,
        heads,
        slab,
        lengths[0],
        tokens[0],
        attn_shard,
        *ff_weights,
        gain_shard,
        cos_table,
        sin_table,
    )
    w_qkv, w_out = w_attn[:, : split + 2 * HEAD_SIZE], w_attn[:, split + 2 * HEAD_SIZE :]
    gains = gains_all.reshape(n_fsdp, 8, 2, rows_shard)[:, 0].transpose(1, 0, 2).reshape(2, 1, width)
    grad_result = reorder(cotangent_all, dealt_of_given)

    column = lax.broadcasted_iota(jnp.int32, (own_width, width), 1) - me * own_width
    place = (column == lax.broadcasted_iota(jnp.int32, (own_width, width), 0)).astype(BF16)
    result_part = RESIDUAL_SCALE * dot_nn(reorder(both, given_of_dealt), jnp.concatenate([w_down, place], axis=0))
    activations = lax.psum_scatter(
        result_part.astype(BF16), "ctx", scatter_dimension=0, tiled=True
    )[None]

    if kernel_fits(n_ctx, n_fsdp, total, width, own_ff):
        token_grad, gain_rows, down_part, gate_part, up_part, out_part, qkv_part = backward(
            n_ctx,
            n_fsdp,
            heads,
            lengths[0],
            grad_result,
            (x, normed, q_rot, k_rot, v_rows, lse, attended_all, hidden_all, normed2, a, b, both),
            (w_attn, w_gate, w_up, w_down, gains_all),
            cos_table,
            sin_table,
        )
        token_grad = token_grad[None]
        own_gains = gain_rows[1::-1]
    else:
        mlp_grad = (RESIDUAL_SCALE * grad_result.astype(F32)).astype(BF16)

        def settle(left, right):
            return lax.psum_scatter(dot_tn(left, right).astype(BF16), "fsdp", scatter_dimension=0, tiled=True)

        down_part = settle(both[:, :own_ff], mlp_grad)
        ggrad, ugrad, hidden_part, mlp_gain_part = mlp_backward(
            n_ctx, mlp_grad, a, b, hidden_all, gains[1], w_gate, w_up, w_down
        )
        hidden_sum = lax.psum_scatter(hidden_part, "ctx", scatter_dimension=0, tiled=False)
        gate_part = settle(normed2, ggrad)
        up_part = settle(normed2, ugrad)
        hidden_grad, branch_grad, attended_part = branch_backward(
            hidden_sum, own_columns(grad_result, me, own_width), w_out, n_ctx
        )
        attended_grad = lax.psum_scatter(attended_part, "ctx", scatter_dimension=0, tiled=False)
        out_part = lax.psum_scatter(
            jnp.einsum("ctk,to->cko", attended_all, branch_grad, preferred_element_type=F32)
            .astype(BF16)
            .reshape(width, own_width),
            "fsdp",
            scatter_dimension=0,
            tiled=True,
        )
        dq, dkv = attention_backward(attended_grad, q_rot, k_rot, v_rows, lse, cos_table, sin_table, lengths[0])
        qkv_part = settle(normed, jnp.concatenate([dq, dkv], axis=1))
        token_part, attn_gain_part = token_backward(me_array, dq, dkv, w_qkv, x, gains[0], hidden_grad)
        token_grad = lax.psum_scatter(token_part, "ctx", scatter_dimension=0, tiled=True).astype(F32)[None]

        gain_parts = jnp.concatenate([attn_gain_part, mlp_gain_part], axis=0)
        step = 1
        while step < n_ctx:
            gain_parts = gain_parts + lax.ppermute(gain_parts, "ctx", [(c, c ^ step) for c in range(n_ctx)])
            step *= 2
        gain_rows = gain_parts.reshape(2, n_fsdp, rows_shard).transpose(1, 0, 2).reshape(n_fsdp, 2 * rows_shard)
        own_gains = lax.psum_scatter(gain_rows, "fsdp", scatter_dimension=0, tiled=True).reshape(2, rows_shard)
        down_part, gate_part, up_part, out_part, qkv_part = [
            lax.all_gather(p, "ctx", axis=0, tiled=False) for p in (down_part, gate_part, up_part, out_part, qkv_part)
        ]

    if slab % LANES == 0 and sharing == 1 and heads % 4 == 0:
        gate_grad, up_grad, down_grad, out_grad, query_grad, key_grad, value_grad = finish(
            slab, gate_part, up_part, down_part.reshape(n_ctx * slab, width), out_part, qkv_part
        )
    else:
        down_grad = down_part.reshape(n_ctx * slab, width).astype(F32)
        if slab % LANES == 0:
            gate_grad = spread_columns(gate_part, slab, n_fsdp)
            up_grad = spread_columns(up_part, slab, n_fsdp)
        else:

            def ff_whole(part):
                pieces = part.reshape(n_ctx, rows_shard, n_fsdp, slab)
                return pieces.transpose(1, 2, 0, 3).reshape(rows_shard, ff).astype(F32)

            gate_grad = ff_whole(gate_part)
            up_grad = ff_whole(up_part)
        out_grad = spread_columns(out_part, own_width, 1)
        qkv_all = qkv_part
        query_grad = spread_columns(qkv_all, split, 1)

        def shared_heads(pieces):
            pieces = pieces.astype(F32).reshape(KEY_VALUE_HEADS, sharing, rows_shard, HEAD_SIZE).sum(axis=1)
            return pieces.transpose(1, 0, 2).reshape(rows_shard, KEY_VALUE_HEADS * HEAD_SIZE)

        key_grad = shared_heads(qkv_all[:, :, split : split + HEAD_SIZE])
        value_grad = shared_heads(qkv_all[:, :, split + HEAD_SIZE :])

    return (
        activations,
        token_grad,
        own_gains[0],
        query_grad,
        key_grad,
        value_grad,
        out_grad,
        own_gains[1],
        gate_grad,
        up_grad,
        down_grad,
    )


def solution(mesh):
    rows = P("fsdp", None)
    block = P("fsdp", "ctx", None)
    gain = P("fsdp")
    return jax.shard_map(
        local,
        mesh=mesh,
        in_specs=(block, rows, P("fsdp", None, None), gain, rows, rows, rows, rows, gain, rows, rows, rows, block),
        out_specs=(block, block, gain, rows, rows, rows, rows, gain, rows, rows, rows),
        check_vma=False,
    )
```

```python
import functools

import jax
import jax.numpy as jnp
from jax import lax
from jax.experimental import pallas as pl
from jax.experimental.pallas import tpu as pltpu
from jax.sharding import PartitionSpec as P

QUERY_HEADS = 32
KEY_VALUE_HEADS = 8
HEAD_SIZE = 64
EPSILON = 1e-05
ROPE_BASE = 10000000.0
SCORE_SCALE = 0.015625
RESIDUAL_SCALE = 0.22
NEGATIVE_BIG = -1e30
LANES = 128
ROWS = 256
BF16 = jnp.bfloat16
F32 = jnp.float32
VMEM_LIMIT = 59 * 1024 * 1024


def dot_nn(a, b):
    return lax.dot_general(a, b, (((1,), (0,)), ((), ())), preferred_element_type=F32)


def dot_nt(a, b):
    return lax.dot_general(a, b, (((1,), (1,)), ((), ())), preferred_element_type=F32)


def dot_tn(a, b):
    return lax.dot_general(a, b, (((0,), (0,)), ((), ())), preferred_element_type=F32)


def swap_halves(x):
    lane = lax.broadcasted_iota(jnp.int32, x.shape, 1)
    first = lax.rem(lane, HEAD_SIZE) < HEAD_SIZE // 2
    return jnp.where(first, pltpu.roll(x, LANES - HEAD_SIZE // 2, 1), pltpu.roll(x, HEAD_SIZE // 2, 1))


def low_half(shape):
    return lax.broadcasted_iota(jnp.int32, shape, 1) < HEAD_SIZE


def mask_bias(first_len, row0, rows, cols):
    query = row0 + lax.broadcasted_iota(jnp.int32, (rows, cols), 0)
    key = lax.broadcasted_iota(jnp.int32, (rows, cols), 1)
    start = jnp.where(query >= first_len, first_len, 0)
    return jnp.where((key <= query) & (key >= start), 0.0, NEGATIVE_BIG)


def attention_backward_kernel(length_ref, g_ref, q_ref, k_ref, v_ref, lse_ref, cos_ref, sin_ref, dq_ref, dkv_ref, dk_sum, dv_sum):
    pair = pl.program_id(0)
    tokens = q_ref.shape[0]

    @pl.when(pair == 0)
    def _():
        dk_sum[...] = jnp.zeros_like(dk_sum)
        dv_sum[...] = jnp.zeros_like(dv_sum)

    first_len = length_ref[0]
    for block in range(tokens // ROWS):
        rows = pl.ds(block * ROWS, ROWS)
        end = (block + 1) * ROWS
        bias = mask_bias(first_len, block * ROWS, ROWS, end)
        query, grad = q_ref[rows, :], g_ref[rows, :]
        low = low_half(query.shape)
        keys, values = k_ref[:end, :], v_ref[:end, :]
        parts = []
        for half in range(2):
            chosen = low if half == 0 else jnp.logical_not(low)
            own_query = jnp.where(chosen, query, jnp.zeros_like(query))
            own_grad = jnp.where(chosen, grad, jnp.zeros_like(grad))
            scores = dot_nt(own_query, keys) + bias
            probs = jnp.exp(scores - lse_ref[0, rows, half : half + 1])
            prob_grad = dot_nt(own_grad, values)
            delta = jnp.sum(probs * prob_grad, axis=-1, keepdims=True)
            score_grad = (probs * (prob_grad - delta)).astype(BF16)
            parts.append(dot_nn(score_grad, keys))
            dk_sum[:end, :] += dot_tn(score_grad, own_query)
            dv_sum[:end, :] += dot_tn(probs.astype(BF16), own_grad)
        dq = jnp.where(low_half(parts[0].shape), parts[0], parts[1]) * SCORE_SCALE
        dq_ref[rows, :] = (dq * cos_ref[rows, :] - swap_halves(dq) * sin_ref[rows, :]).astype(BF16)

    @pl.when(pair == pl.num_programs(0) - 1)
    def _():
        dk = dk_sum[...]
        dk = dk + pltpu.roll(dk, HEAD_SIZE, 1)
        dk = dk * cos_ref[...] - swap_halves(dk) * sin_ref[...]
        dv = dv_sum[...]
        dv = dv + pltpu.roll(dv, HEAD_SIZE, 1)
        dkv_ref[...] = jnp.where(low_half(dk.shape), dk, dv).astype(BF16)


def attention_backward(grads, q_rot, k_rot, v_rows, lse, cos, sin, lengths):
    tokens = q_rot.shape[0]
    pairs = q_rot.shape[1] // LANES
    one = pl.BlockSpec((tokens, LANES), lambda j: (0, 0))
    each = pl.BlockSpec((tokens, LANES), lambda j: (0, j))
    return pl.pallas_call(
        attention_backward_kernel,
        grid=(pairs,),
        in_specs=[
            pl.BlockSpec(memory_space=pltpu.SMEM),
            each,
            each,
            one,
            one,
            pl.BlockSpec((1, tokens, LANES), lambda j: (j, 0, 0)),
            one,
            one,
        ],
        out_specs=[each, one],
        out_shape=[
            jax.ShapeDtypeStruct((tokens, pairs * LANES), BF16),
            jax.ShapeDtypeStruct((tokens, LANES), BF16),
        ],
        scratch_shapes=[pltpu.VMEM((tokens, LANES), F32), pltpu.VMEM((tokens, LANES), F32)],
        compiler_params=pltpu.CompilerParams(vmem_limit_bytes=VMEM_LIMIT),
        cost_estimate=pl.CostEstimate(
            flops=10 * tokens * tokens * LANES * pairs,
            bytes_accessed=12 * tokens * pairs * LANES,
            transcendentals=tokens * tokens * pairs,
        ),
        name="attend_back",
    )(lengths, grads, q_rot, k_rot, v_rows, lse, cos, sin)


def row_block(width):
    return pl.BlockSpec((ROWS, width), lambda i: (i, 0))


def fixed(*shape):
    return pl.BlockSpec(shape, lambda i: (0,) * len(shape))


def params():
    return pltpu.CompilerParams(vmem_limit_bytes=VMEM_LIMIT)


def cost(flops, *arrays):
    moved = sum(a.size * a.dtype.itemsize for a in arrays)
    return pl.CostEstimate(flops=flops, bytes_accessed=moved, transcendentals=0)


def mlp_back_kernel(
    grad_ref, a_ref, b_ref, hidden_ref, gain_ref, gate_ref, up_ref, down_ref, ggrad_ref, ugrad_ref, part_ref, gain_out
):
    mixed_grad = dot_nt(grad_ref[...], down_ref[...])
    ggrad = (mixed_grad * a_ref[...].astype(F32)).astype(BF16)
    ugrad = (mixed_grad * b_ref[...].astype(F32)).astype(BF16)
    ggrad_ref[...] = ggrad
    ugrad_ref[...] = ugrad
    normed_grad = dot_nt(ggrad, gate_ref[...]) + dot_nt(ugrad, up_ref[...])
    hidden = hidden_ref[...].astype(F32)
    r2 = lax.rsqrt(jnp.mean(hidden * hidden, axis=-1, keepdims=True) + EPSILON)
    gain_part = jnp.sum(normed_grad * (hidden * r2), axis=0, keepdims=True)

    @pl.when(pl.program_id(0) == 0)
    def _():
        gain_out[...] = jnp.zeros_like(gain_out)

    gain_out[...] += gain_part
    weighted = normed_grad * gain_ref[...]
    mean = jnp.mean(weighted * hidden, axis=-1, keepdims=True)
    part = r2 * weighted - hidden * (r2 * r2 * r2 * mean)
    own = part_ref.shape[2]
    for c in range(part_ref.shape[0]):
        part_ref[c] = part[:, c * own : (c + 1) * own].astype(BF16)


def mlp_backward(n, mlp_grad, a, b, hidden_all, gain, w_gate, w_up, w_down):
    total, width = hidden_all.shape
    own = width // n
    own_ff = w_gate.shape[1]
    narrow = jax.ShapeDtypeStruct((total, own_ff), BF16)
    planes = pl.BlockSpec((n, ROWS, own), lambda i: (0, i, 0))
    return pl.pallas_call(
        mlp_back_kernel,
        grid=(total // ROWS,),
        in_specs=[
            row_block(width),
            row_block(own_ff),
            row_block(own_ff),
            row_block(width),
            fixed(1, width),
            fixed(width, own_ff),
            fixed(width, own_ff),
            fixed(own_ff, width),
        ],
        out_specs=[row_block(own_ff), row_block(own_ff), planes, fixed(1, width)],
        out_shape=[narrow, narrow, jax.ShapeDtypeStruct((n, total, own), BF16), jax.ShapeDtypeStruct((1, width), F32)],
        compiler_params=params(),
        cost_estimate=cost(6 * total * width * own_ff, mlp_grad, hidden_all, hidden_all, w_gate, w_up, w_down, a, b, a, b),
        name="mlp_backward",
    )(mlp_grad, a, b, hidden_all, gain, w_gate, w_up, w_down)


def branch_kernel(part_ref, grad_ref, w_ref, hidden_ref, branch_ref, out_ref):
    hidden_grad = part_ref[...].astype(F32) + grad_ref[...].astype(F32)
    hidden_ref[...] = hidden_grad
    branch = (RESIDUAL_SCALE * hidden_grad).astype(BF16)
    branch_ref[...] = branch
    own = out_ref.shape[2]
    for c in range(out_ref.shape[0]):
        out_ref[c] = dot_nt(branch, w_ref[c]).astype(BF16)


def branch_backward(hidden_part, grad_own, w_out, n):
    total, own_width = hidden_part.shape
    own = w_out.shape[0] // n
    w_heads = w_out.reshape(n, own, own_width)
    return pl.pallas_call(
        branch_kernel,
        grid=(total // ROWS,),
        in_specs=[row_block(own_width), row_block(own_width), fixed(n, own, own_width)],
        out_specs=[row_block(own_width), row_block(own_width), pl.BlockSpec((n, ROWS, own), lambda i: (0, i, 0))],
        out_shape=[
            jax.ShapeDtypeStruct((total, own_width), F32),
            jax.ShapeDtypeStruct((total, own_width), BF16),
            jax.ShapeDtypeStruct((n, total, own), BF16),
        ],
        compiler_params=params(),
        cost_estimate=cost(2 * total * own_width * own * n, hidden_part, hidden_part, hidden_part, w_out),
        name="branch_backward",
    )(hidden_part, grad_own, w_heads)


def token_kernel(me_ref, dq_ref, dkv_ref, w_ref, x_ref, gain_ref, hidden_ref, part_ref, gain_out):
    split = dq_ref.shape[1]
    normed_grad = dot_nt(dq_ref[...], w_ref[:, :split]) + dot_nt(dkv_ref[...], w_ref[:, split:])
    x = x_ref[...].astype(F32)
    r1 = lax.rsqrt(jnp.mean(x * x, axis=-1, keepdims=True) + EPSILON)

    @pl.when(pl.program_id(0) == 0)
    def _():
        gain_out[...] = jnp.zeros_like(gain_out)

    gain_out[...] += jnp.sum(normed_grad * (x * r1), axis=0, keepdims=True)
    weighted = normed_grad * gain_ref[...]
    mean = jnp.mean(weighted * x, axis=-1, keepdims=True)
    part = r1 * weighted - x * (r1 * r1 * r1 * mean)
    own_width = hidden_ref.shape[1]
    for c in range(part.shape[1] // own_width):
        piece = part[:, c * own_width : (c + 1) * own_width]
        piece = piece + jnp.where(me_ref[0] == c, hidden_ref[...], 0.0)
        part_ref[:, c * own_width : (c + 1) * own_width] = piece.astype(BF16)


def token_backward(me, dq, dkv, w_qkv, x, gain, hidden_grad):
    total, width = x.shape
    own_width = hidden_grad.shape[1]
    return pl.pallas_call(
        token_kernel,
        grid=(total // ROWS,),
        in_specs=[
            pl.BlockSpec(memory_space=pltpu.SMEM),
            row_block(dq.shape[1]),
            row_block(dkv.shape[1]),
            fixed(*w_qkv.shape),
            row_block(width),
            fixed(1, width),
            row_block(own_width),
        ],
        out_specs=[row_block(width), fixed(1, width)],
        out_shape=[jax.ShapeDtypeStruct((total, width), BF16), jax.ShapeDtypeStruct((1, width), F32)],
        compiler_params=params(),
        cost_estimate=cost(2 * total * width * w_qkv.shape[1], x, x, w_qkv, dq, dkv, hidden_grad),
        name="token_backward",
    )(me, dq, dkv, w_qkv, x, gain, hidden_grad)


def finish_kernel(slab, gate_ref, up_ref, down_ref, out_ref, qkv_ref, gate_out, up_out, down_out, out_out, q_out, k_out, v_out):
    n = gate_ref.shape[0]
    for src, dst, piece in ((gate_ref, gate_out, slab), (up_ref, up_out, slab), (out_ref, out_out, out_ref.shape[2])):
        for c in range(n):
            for f in range(src.shape[2] // piece):
                at = (f * n + c) * piece
                dst[:, at : at + piece] = src[c, :, f * piece : (f + 1) * piece].astype(F32)
    down_out[...] = down_ref[...].astype(F32)
    split = qkv_ref.shape[2] - LANES
    for c in range(n):
        q_out[:, c * split : (c + 1) * split] = qkv_ref[c, :, :split].astype(F32)
    for pair in range(n // 2):
        even = qkv_ref[2 * pair, :, split:].astype(F32)
        odd = qkv_ref[2 * pair + 1, :, split:].astype(F32)
        low = low_half(even.shape)
        lanes = slice(pair * LANES, (pair + 1) * LANES)
        k_out[:, lanes] = jnp.where(low, even, pltpu.roll(odd, HEAD_SIZE, 1))
        v_out[:, lanes] = jnp.where(low, pltpu.roll(even, HEAD_SIZE, 1), odd)


def finish(slab, gate, up, down, out, qkv):
    n, rows, own_ff = gate.shape
    width = n * out.shape[2]
    steps = 16
    tile, down_tile = rows // steps, down.shape[0] // steps
    kv = n * HEAD_SIZE

    def by_device(columns):
        return pl.BlockSpec((n, tile, columns), lambda i: (0, i, 0))

    def flat(height, columns):
        return pl.BlockSpec((height, columns), lambda i: (i, 0))

    outs = [
        (flat(tile, n * own_ff), (rows, n * own_ff)),
        (flat(tile, n * own_ff), (rows, n * own_ff)),
        (flat(down_tile, width), down.shape),
        (flat(tile, width), (rows, width)),
        (flat(tile, width), (rows, width)),
        (flat(tile, kv), (rows, kv)),
        (flat(tile, kv), (rows, kv)),
    ]
    return pl.pallas_call(
        functools.partial(finish_kernel, slab),
        grid=(steps,),
        in_specs=[
            by_device(own_ff),
            by_device(own_ff),
            flat(down_tile, width),
            by_device(out.shape[2]),
            by_device(qkv.shape[2]),
        ],
        out_specs=[spec for spec, _ in outs],
        out_shape=[jax.ShapeDtypeStruct(shape, F32) for _, shape in outs],
        compiler_params=params(),
        cost_estimate=cost(0, gate, gate, gate, up, up, up, down, down, down),
        name="finish",
    )(gate, up, down, out, qkv)


def spread_kernel(in_ref, out_ref):
    slab = in_ref.shape[2]
    for c in range(in_ref.shape[0]):
        out_ref[:, c * slab : (c + 1) * slab] = in_ref[c].astype(F32)


def spread_columns(pieces, slab, groups):
    n, rows, _ = pieces.shape
    tile = 128
    out_shape = jax.ShapeDtypeStruct((rows, groups * n * slab), F32)
    return pl.pallas_call(
        spread_kernel,
        grid=(groups, rows // tile),
        in_specs=[pl.BlockSpec((n, tile, slab), lambda f, r: (0, r, f))],
        out_specs=pl.BlockSpec((tile, n * slab), lambda f, r: (r, f)),
        out_shape=out_shape,
        compiler_params=params(),
        cost_estimate=cost(0, pieces, out_shape),
        name="spread_columns",
    )(pieces)


MESH = pl.DeviceIdType.MESH


class Chain:
    def __init__(self, slot, planes, plane, send_sem, recv_sem):
        self.slot, self.planes, self.plane = slot, planes, plane
        self.send_sem, self.recv_sem = send_sem, recv_sem

    def copy(self, way, step, shard, to):
        return pltpu.make_async_remote_copy(
            src_ref=self.slot(shard),
            dst_ref=self.slot(shard),
            send_sem=self.send_sem.at[way, step],
            recv_sem=self.recv_sem.at[way, step],
            device_id={"fsdp": to},
            device_id_type=MESH,
        )

    def moves(self, step):
        p, last = self.plane, self.planes - 1
        return (
            (0, (p >= step) & (p < last), p - step, p + 1, p >= step + 1, p - 1 - step),
            (1, (p + step <= last) & (p > 0), p + step, p - 1, p + step + 1 <= last, p + 1 + step),
        )

    def start(self, step):
        for way, sends, shard, to, _, _ in self.moves(step):

            @pl.when(sends)
            def _(way=way, shard=shard, to=to):
                self.copy(way, step, shard, to).start()

    def arrive(self, step):
        for way, _, _, _, receives, shard in self.moves(step):

            @pl.when(receives)
            def _(way=way, shard=shard):
                self.copy(way, step, shard, self.plane).wait_recv()

    def advance(self, step):
        self.arrive(step - 1)
        self.start(step)

    def drain(self):
        for step in range(self.planes - 1):
            for way, sends, shard, to, _, _ in self.moves(step):

                @pl.when(sends)
                def _(way=way, shard=shard, to=to, step=step):
                    self.copy(way, step, shard, to).wait_send()


class Spread:
    def __init__(self, src, slot, n, me, send_sem, recv_sem):
        self.src, self.slot, self.n, self.me = src, slot, n, me
        self.send_sem, self.recv_sem = send_sem, recv_sem
        self.chips = n // 2
        self.chip, self.core = me // 2, lax.rem(me, 2)
        self.partner = me + 1 - 2 * self.core

    def at(self, k):
        return lax.rem(self.chip + k, self.chips) * 2 + self.core

    def copy(self, src, owner, sem, to):
        return pltpu.make_async_remote_copy(
            src_ref=src,
            dst_ref=self.slot(owner),
            send_sem=self.send_sem.at[sem],
            recv_sem=self.recv_sem.at[sem],
            device_id={"ctx": to},
            device_id_type=MESH,
        )

    def out(self, k):
        return self.copy(self.src, self.me, k, self.at(k))

    def relay(self, k):
        owner = self.at(self.chips - k) if k else self.me
        src = self.slot(owner) if k else self.src
        return self.copy(src, owner, self.chips + k, self.partner)

    def start(self):
        for k in range(1, self.chips):
            self.out(k).start()
        self.relay(0).start()

    def pass_on(self):
        for k in range(1, self.chips):
            self.copy(self.src, self.at(self.chips - k), k, self.me).wait_recv()
            self.relay(k).start()

    def late(self):
        pass

    def finish(self):
        other = 1 - 2 * self.core
        for k in range(self.chips):
            owner = (self.at(self.chips - k) if k else self.me) + other
            self.copy(self.slot(owner), owner, self.chips + k, self.me).wait_recv()

    def drain(self):
        for k in range(1, self.chips):
            self.out(k).wait_send()
        for k in range(self.chips):
            self.relay(k).wait_send()


class Spread4:
    def __init__(self, src, slot, n, me, send_sem, recv_sem):
        self.src, self.slot, self.me = src, slot, me
        self.send_sem, self.recv_sem = send_sem, recv_sem
        self.core = lax.rem(me, 2)
        self.other = 1 - self.core
        chip = me // 2
        self.near, self.side, self.far = square(chip)
        self.chip = chip
        self.half = src.shape[0] // 2

    def copy(self, src, dst, sem, to):
        return pltpu.make_async_remote_copy(
            src_ref=src,
            dst_ref=dst,
            send_sem=self.send_sem.at[sem],
            recv_sem=self.recv_sem.at[sem],
            device_id={"ctx": to},
            device_id_type=MESH,
        )

    def part(self, owner, which):
        return self.slot(owner).at[pl.ds(which * self.half, self.half)]

    def out(self, sem):
        chip = self.near if sem == 1 else self.side
        return self.copy(self.src, self.slot(self.me), sem, chip * 2 + self.core)

    def onward(self, sem):
        origin, to, which = (self.near, self.side, 0) if sem == 3 else (self.side, self.near, 1)
        owner = origin * 2 + self.core
        return self.copy(self.part(owner, which), self.part(owner, which), sem, to * 2 + self.core)

    def relay(self, k):
        owner = (self.chip, self.near, self.side, self.far)[k] * 2 + self.core
        src = self.slot(owner) if k else self.src
        return self.copy(src, self.slot(owner), 4 + k, self.chip * 2 + self.other)

    def start(self):
        self.out(1).start()
        self.out(2).start()
        self.relay(0).start()

    def pass_on(self):
        for k, chip in ((1, self.near), (2, self.side)):
            owner = chip * 2 + self.core
            self.copy(self.src, self.slot(owner), k, self.me).wait_recv()
            self.onward(3 if k == 1 else 0).start()
            self.relay(k).start()

    def late(self):
        owner = self.far * 2 + self.core
        for sem, which in ((3, 0), (0, 1)):
            self.copy(self.part(owner, which), self.part(owner, which), sem, self.me).wait_recv()
        self.relay(3).start()

    def finish(self):
        for k, chip in enumerate((self.chip, self.near, self.side, self.far)):
            owner = chip * 2 + self.other
            self.copy(self.slot(owner), self.slot(owner), 4 + k, self.me).wait_recv()

    def drain(self):
        for sem in (1, 2):
            self.out(sem).wait_send()
        for sem in (3, 0):
            self.onward(sem).wait_send()
        for k in range(4):
            self.relay(k).wait_send()


def square(chip):
    return chip + 1 - 2 * lax.rem(chip, 2), chip + 2 - 4 * (chip // 2), 3 - chip


def spread_over(n, src, *rest):
    return (Spread4 if n == 8 and src.shape[0] % 32 == 0 else Spread)(src, *rest)


def greet(n, planes, me, plane, across):
    barrier = pltpu.get_barrier_semaphore()
    chips = n // 2
    core = lax.rem(me, 2)
    others = [lax.rem(me // 2 + k, chips) * 2 + core for k in range(1, chips)] + [me + 1 - 2 * core]
    for other in others:
        pl.semaphore_signal(barrier, inc=1, device_id={"ctx": other}, device_id_type=MESH)
    if across:

        @pl.when(plane > 0)
        def _():
            pl.semaphore_signal(barrier, inc=1, device_id={"fsdp": plane - 1}, device_id_type=MESH)

        @pl.when(plane < planes - 1)
        def _():
            pl.semaphore_signal(barrier, inc=1, device_id={"fsdp": plane + 1}, device_id_type=MESH)

    count = len(others)
    if across:
        count = count + (plane > 0).astype(jnp.int32) + (plane < planes - 1).astype(jnp.int32)
    pl.semaphore_wait(barrier, count)


def forward_kernel(
    n,
    planes,
    heads,
    length_ref,
    tokens_ref,
    attn_shard,
    gate_ref,
    up_ref,
    down_ref,
    gain_shard,
    cos_ref,
    sin_ref,
    x_out,
    normed_out,
    q_out,
    k_out,
    v_out,
    lse_out,
    att_out,
    hid_out,
    normed2_out,
    a_out,
    b_out,
    mixed_out,
    attn_out,
    gate_out,
    up_out,
    down_out,
    gain_out,
    w_attn,
    w_gate,
    w_up,
    w_down,
    gains,
    x_all,
    qkv,
    q_rot,
    k_rot,
    v_rows,
    lse,
    own_att,
    att_all,
    own_hid,
    own_scaled,
    wide,
    narrow,
    z_send,
    z_recv,
    c_send,
    c_recv,
    keep_sem,
    load_sem,
    wide_sem,
    narrow_sem,
):
    me, plane = lax.axis_index("ctx"), lax.axis_index("fsdp")
    per_device, width = tokens_ref.shape
    total = x_all.shape[0]
    rows_shard = attn_shard.shape[0]
    own = own_att.shape[1]
    own_width = own_hid.shape[1]
    columns = qkv.shape[1]
    blocks = total // ROWS
    pairs = heads // 2

    local_copies = []

    def keep(src, dst, index):
        copy = pltpu.make_async_copy(src, dst, keep_sem.at[index])
        copy.start()
        local_copies.append(copy)

    def chain(index, ref, rows):
        return Chain(lambda s: ref.at[pl.ds(s * rows, rows)], planes, plane, z_send.at[index], z_recv.at[index])

    attn_chain = chain(0, w_attn, rows_shard)
    gate_chain = chain(1, w_gate, rows_shard)
    up_chain = chain(2, w_up, rows_shard)
    slab = w_down.shape[0] // planes
    down_chain = chain(3, w_down, slab)
    gain_chain = chain(4, gains, gain_shard.shape[0])
    own_ff = w_gate.shape[1]
    loads = [
        pltpu.make_async_copy(shard, c.slot(plane), keep_sem.at[i])
        for i, (c, shard) in enumerate(((attn_chain, attn_shard), (gain_chain, gain_shard)))
    ]
    for ref, c, at in ((gate_ref, gate_chain, 0), (up_ref, up_chain, 1)):
        for f in range(ref.shape[1] // (n * slab)):
            src = ref.at[:, pl.ds(pl.multiple_of((f * n + me) * slab, LANES), slab)]
            dst = c.slot(plane).at[:, pl.ds(f * slab, slab)]
            loads.append(pltpu.make_async_copy(src, dst, load_sem.at[at, f]))
        if ref.shape[1] == own_ff:
            loads.append(pltpu.make_async_copy(ref, c.slot(plane), load_sem.at[at, 0]))
    down_src = down_ref if down_ref.shape[0] == slab else down_ref.at[pl.ds(pl.multiple_of(me * slab, slab), slab)]
    loads.append(pltpu.make_async_copy(down_src, down_chain.slot(plane), load_sem.at[2, 0]))
    for load in loads:
        load.start()
    own_x = pltpu.make_async_copy(tokens_ref, x_all.at[pl.ds(me * per_device, per_device)], keep_sem.at[5])
    own_x.start()
    greet(n, planes, me, plane, True)
    loads[0].wait()
    attn_chain.start(0)
    loads[1].wait()
    gain_chain.start(0)
    x_spread = spread_over(
        n, tokens_ref, lambda c: x_all.at[pl.ds(c * per_device, per_device)], n, me, c_send.at[0], c_recv.at[0]
    )
    x_spread.start()
    for load in loads[2:]:
        load.wait()
    own_x.wait()
    for step in range(1, planes - 1):
        attn_chain.advance(step)
        gain_chain.advance(step)
    gate_chain.start(0)
    up_chain.start(0)
    x_spread.pass_on()
    x_spread.late()
    x_spread.finish()
    x_copy = pltpu.make_async_copy(x_all, x_out, keep_sem.at[0])
    x_copy.start()
    attn_chain.arrive(planes - 2)
    gain_chain.arrive(planes - 2)
    keep(w_attn, attn_out, 1)
    keep(gains, gain_out, 2)
    half = gain_shard.shape[1] // 2
    step_rows = gain_shard.shape[0]
    attn_gain = jnp.concatenate([gains[f * step_rows : f * step_rows + 1, :half] for f in range(planes)], axis=1)
    mlp_gain = jnp.concatenate([gains[f * step_rows : f * step_rows + 1, half:] for f in range(planes)], axis=1)

    def staged(stage, sem, slot, out, rows, wait_before):
        copy = pltpu.make_async_copy(stage.at[slot], out.at[rows], sem.at[slot])
        return copy.wait() if wait_before else copy.start()

    def project_block(i, _):
        rows = pl.ds(pl.multiple_of(i * ROWS, ROWS), ROWS)
        slot = lax.rem(i, 2)

        @pl.when(i >= 2)
        def _():
            staged(wide, wide_sem, slot, normed_out, rows, True)

        own_hid[rows, :] = x_all[rows, pl.ds(pl.multiple_of(me * own_width, LANES), own_width)]
        x = x_all[rows, :].astype(F32)
        r1 = lax.rsqrt(jnp.mean(x * x, axis=-1, keepdims=True) + EPSILON)
        normed = (x * r1 * attn_gain).astype(BF16)
        wide[slot] = normed
        staged(wide, wide_sem, slot, normed_out, rows, False)
        qkv[rows, :] = dot_nn(normed, w_attn[:, :columns])
        return 0

    lax.fori_loop(0, blocks, project_block, 0)
    for i in range(max(blocks - 2, 0), blocks):
        staged(wide, wide_sem, i % 2, normed_out, pl.ds(i * ROWS, ROWS), True)

    split = columns - LANES
    cos, sin = cos_ref[...], sin_ref[...]
    kv = qkv[:, split:]
    turned = pltpu.roll(kv, HEAD_SIZE, 1)
    low = low_half(kv.shape)
    k = jnp.where(low, kv, turned)
    k_rot[...] = (k * cos + swap_halves(k) * sin).astype(BF16)
    v_rows[...] = jnp.where(low, turned, kv).astype(BF16)
    keep(k_rot, k_out, 3)
    keep(v_rows, v_out, 4)
    first_len = length_ref[0]

    def attend_pair(pair, _):
        lanes = pl.ds(pl.multiple_of(pair * LANES, LANES), LANES)
        q = qkv[:, lanes]
        q_rot[:, lanes] = ((q * cos_ref[...] + swap_halves(q) * sin_ref[...]) * SCORE_SCALE).astype(BF16)
        for block in range(blocks):
            rows = pl.ds(block * ROWS, ROWS)
            end = (block + 1) * ROWS
            bias = mask_bias(first_len, block * ROWS, ROWS, end)
            query = q_rot[rows, lanes]
            lower = low_half(query.shape)
            keys, values = k_rot[:end, :], v_rows[:end, :]
            parts = []
            for side in range(2):
                chosen = lower if side == 0 else jnp.logical_not(lower)
                scores = dot_nt(jnp.where(chosen, query, jnp.zeros_like(query)), keys) + bias
                top = jnp.max(scores, axis=-1, keepdims=True)
                weights = jnp.exp(scores - top)
                whole = jnp.sum(weights, axis=-1, keepdims=True)
                probs = (weights * (1.0 / whole)).astype(BF16)
                parts.append(dot_nn(probs, values))
                lse[pair, rows, side : side + 1] = top + jnp.log(whole)
            own_att[rows, lanes] = jnp.where(low_half(parts[0].shape), parts[0], parts[1]).astype(BF16)
        return 0

    lax.fori_loop(0, pairs, attend_pair, 0)
    att_spread = spread_over(n, own_att, lambda c: att_all.at[c], n, me, c_send.at[1], c_recv.at[1])
    x_copy.wait()
    x_spread.drain()
    att_spread.start()
    own_a = pltpu.make_async_copy(own_att, att_all.at[me], keep_sem.at[5])
    own_a.start()
    keep(q_rot, q_out, 6)
    keep(lse, lse_out, 7)
    if planes > 2:
        gate_chain.advance(1)
        up_chain.advance(1)
    att_spread.pass_on()
    att_spread.late()
    own_a.wait()
    att_spread.finish()
    keep(att_all, att_out, 8)

    def out_block(i, _):
        rows = pl.ds(pl.multiple_of(i * ROWS, ROWS), ROWS)
        acc = jnp.zeros((ROWS, own_width), F32)
        for c in range(n):
            acc += dot_nn(att_all[c, rows, :], w_attn[c * own : (c + 1) * own, columns:])
        hidden = own_hid[rows, :].astype(F32) + RESIDUAL_SCALE * acc
        own_hid[rows, :] = hidden.astype(BF16)
        own_scaled[rows, :] = (hidden * (1.0 / RESIDUAL_SCALE)).astype(BF16)
        return 0

    lax.fori_loop(0, blocks, out_block, 0)
    def hid_slot(c):
        return x_all.at[:, pl.ds(pl.multiple_of(c * own_width, LANES), own_width)]

    hid_spread = spread_over(n, own_hid, hid_slot, n, me, c_send.at[2], c_recv.at[2])
    hid_spread.start()
    keep(own_scaled, mixed_out.at[:, pl.ds(own_ff, own_width)], 13)
    own_h = pltpu.make_async_copy(own_hid, hid_slot(me), keep_sem.at[5])
    own_h.start()
    for step in range(2, planes - 1):
        gate_chain.advance(step)
        up_chain.advance(step)
    down_chain.start(0)
    hid_spread.pass_on()
    hid_spread.late()
    own_h.wait()
    hid_spread.finish()
    keep(x_all, hid_out, 9)
    gate_chain.arrive(planes - 2)
    up_chain.arrive(planes - 2)
    keep(w_gate, gate_out, 10)
    keep(w_up, up_out, 11)
    if planes > 2:
        down_chain.advance(1)

    def mlp_copies(i, rows, wait):
        slot = lax.rem(i, 2)
        staged(wide, wide_sem, slot, normed2_out, rows, wait)
        for j, out in enumerate((a_out, b_out, mixed_out.at[:, pl.ds(0, own_ff)])):
            staged(narrow.at[j], narrow_sem.at[j], slot, out, rows, wait)

    def mlp_block(i, _):
        rows = pl.ds(pl.multiple_of(i * ROWS, ROWS), ROWS)
        slot = lax.rem(i, 2)

        @pl.when(i >= 2)
        def _():
            mlp_copies(i, rows, True)

        hidden = x_all[rows, :].astype(F32)
        r2 = lax.rsqrt(jnp.mean(hidden * hidden, axis=-1, keepdims=True) + EPSILON)
        normed = (hidden * r2 * mlp_gain).astype(BF16)
        wide[slot] = normed
        gate = dot_nn(normed, w_gate[...])
        up = dot_nn(normed, w_up[...])
        sig = jax.nn.sigmoid(gate)
        silu = gate * sig
        narrow[2, slot] = (silu * up).astype(BF16)
        narrow[1, slot] = silu.astype(BF16)
        narrow[0, slot] = (up * sig * (1.0 + gate * (1.0 - sig))).astype(BF16)
        mlp_copies(i, rows, False)
        return 0

    lax.fori_loop(0, blocks, mlp_block, 0)
    for step in range(2, planes - 1):
        down_chain.advance(step)
    for i in range(max(blocks - 2, 0), blocks):
        mlp_copies(i, pl.ds(i * ROWS, ROWS), True)
    down_chain.arrive(planes - 2)
    keep(w_down, down_out, 12)
    for c in (attn_chain, gain_chain, gate_chain, up_chain, down_chain):
        c.drain()
    for s in (att_spread, hid_spread):
        s.drain()
    for copy in local_copies:
        copy.wait()


def forward(n, planes, heads, slab, lengths, tokens, attn_shard, gate, up, down, gain_shard, cos, sin):
    per_device, width = tokens.shape
    total = per_device * n
    own = heads * HEAD_SIZE
    columns = own + 2 * HEAD_SIZE
    own_width = attn_shard.shape[1] - columns
    own_ff = planes * slab
    rows_shard = attn_shard.shape[0]
    pairs = heads // 2
    weights = [
        ((planes * rows_shard, attn_shard.shape[1]), BF16),
        ((planes * rows_shard, own_ff), BF16),
        ((planes * rows_shard, own_ff), BF16),
        ((own_ff, width), BF16),
        ((planes * gain_shard.shape[0], gain_shard.shape[1]), F32),
    ]
    outs = [
        ((total, width), BF16),
        ((total, width), BF16),
        ((total, own), BF16),
        ((total, LANES), BF16),
        ((total, LANES), BF16),
        ((pairs, total, LANES), F32),
        ((n, total, own), BF16),
        ((total, width), BF16),
        ((total, width), BF16),
        ((total, own_ff), BF16),
        ((total, own_ff), BF16),
        ((total, own_ff + own_width), BF16),
    ] + weights
    scratch = weights + [
        ((total, width), BF16),
        ((total, columns), F32),
        ((total, own), BF16),
        ((total, LANES), BF16),
        ((total, LANES), BF16),
        ((pairs, total, LANES), F32),
        ((total, own), BF16),
        ((n, total, own), BF16),
        ((total, own_width), BF16),
        ((total, own_width), BF16),
        ((2, ROWS, width), BF16),
        ((3, 2, ROWS, own_ff), BF16),
    ]
    steps = max(planes - 1, 1)
    dma = pltpu.SemaphoreType.DMA
    anywhere = pl.BlockSpec(memory_space=pl.ANY)
    vmem = pl.BlockSpec(memory_space=pltpu.VMEM)
    return pl.pallas_call(
        functools.partial(forward_kernel, n, planes, heads),
        in_specs=[pl.BlockSpec(memory_space=pltpu.SMEM), vmem] + [anywhere] * 5 + [vmem] * 2,
        out_specs=[anywhere] * len(outs),
        out_shape=[jax.ShapeDtypeStruct(*o) for o in outs],
        scratch_shapes=[pltpu.VMEM(*s) for s in scratch]
        + [dma((5, 2, steps)), dma((5, 2, steps)), dma((3, n)), dma((3, n)), dma((16,)), dma((3, planes)), dma((2,)), dma((3, 2))],
        compiler_params=pltpu.CompilerParams(
            vmem_limit_bytes=VMEM_LIMIT, collective_id=1, has_side_effects=True
        ),
        cost_estimate=pl.CostEstimate(
            flops=2 * total * width * (columns + own_width + 2 * own_ff),
            bytes_accessed=60 * 1024 * 1024,
            transcendentals=0,
        ),
        name="forward",
    )(lengths, tokens, attn_shard, gate, up, down, gain_shard, cos, sin)


def add_into(dst, src):
    rows_in, columns = dst.shape
    chunk = max(c for c in (256, 128, 64, 32) if c == 32 or (rows_in % c == 0 and c * columns <= 65536))

    def step(i, _):
        rows = pl.ds(pl.multiple_of(i * chunk, chunk), chunk)
        dst[rows, :] = (dst[rows, :].astype(F32) + src[rows, :].astype(F32)).astype(dst.dtype)
        return 0

    if rows_in < chunk:
        dst[...] = dst[...] + src[...]
    else:
        lax.fori_loop(0, rows_in // chunk, step, 0)


def fetch(src, dst, sem):
    copy = pltpu.make_async_copy(src, dst, sem)
    copy.start()
    copy.wait()


class Settle:
    def __init__(self, block, landed, stage, planes, plane, send_sem, recv_sem, load_sem):
        self.block, self.landed, self.stage = block, landed, stage
        self.planes, self.plane = planes, plane
        self.send_sem, self.recv_sem, self.load_sem = send_sem, recv_sem, load_sem

    def slot(self, way, shard, at):
        return shard if way == 0 else jnp.where(shard == at, self.planes, shard)

    def sends(self, step):
        p, last = self.plane, self.planes - 1
        return (
            (0, (p <= step) & (p < last), last - step + p, p + 1),
            (1, (last - p <= step) & (p > 0), step - last + p, p - 1),
        )

    def receives(self, step):
        p, last = self.plane, self.planes - 1
        return (
            (0, (p >= 1) & (p - 1 <= step), last - step + p - 1),
            (1, (p <= last - 1) & (last - p - 1 <= step), step - last + p + 1),
        )

    def copy(self, way, step, shard, to):
        return pltpu.make_async_remote_copy(
            src_ref=self.block(shard),
            dst_ref=self.landed.at[self.slot(way, shard, to)],
            send_sem=self.send_sem.at[way, step],
            recv_sem=self.recv_sem.at[way, step],
            device_id={"fsdp": to},
            device_id_type=MESH,
        )

    def start(self, step=0):
        for way, active, shard, to in self.sends(step):

            @pl.when(active)
            def _(way=way, shard=shard, to=to):
                self.copy(way, step, shard, to).start()

    def take(self, step):
        for way, active, shard in self.receives(step):

            @pl.when(active)
            def _(way=way, shard=shard):
                self.copy(way, step, shard, self.plane).wait_recv()
                fetch(self.landed.at[self.slot(way, shard, self.plane)], self.stage, self.load_sem)
                add_into(self.block(shard), self.stage)

    def advance(self, step):
        self.take(step - 1)
        self.start(step)

    def drain(self):
        for step in range(self.planes - 1):
            for way, active, shard, to in self.sends(step):

                @pl.when(active)
                def _(way=way, shard=shard, to=to, step=step):
                    self.copy(way, step, shard, to).wait_send()


class Scatter:
    def __init__(self, block, near, far, stage, me, send_sem, recv_sem, load_sem):
        self.block, self.landed, self.far, self.stage = block, near, far, stage
        self.send_sem, self.recv_sem, self.load_sem = send_sem, recv_sem, load_sem
        self.core = lax.rem(me, 2)
        self.chip = me // 2
        self.chips = (self.chip, *square(self.chip))
        self.half = stage[0].shape[0] // 2

    def rows(self, which):
        return pl.ds(which * self.half, self.half)

    def own(self, k):
        return self.block(self.chips[k] * 2 + self.core)

    def copy(self, src, dst, sem, chip, core):
        return pltpu.make_async_remote_copy(
            src_ref=src,
            dst_ref=dst,
            send_sem=self.send_sem.at[sem],
            recv_sem=self.recv_sem.at[sem],
            device_id={"ctx": chip * 2 + core},
            device_id_type=MESH,
        )

    def first(self, k):
        other = 1 - self.core
        return self.copy(self.block(self.chips[k] * 2 + other), self.landed.at[k], k, self.chip, other)

    def second(self, k, to, which):
        place = self.far.at[to - 1 if k == to else 2, self.rows(which)]
        sem = 4 + 2 * (to - 1) + which if k == to else 7 + to
        return self.copy(self.own(k).at[self.rows(which)], place, sem, self.chips[to], self.core)

    def start(self):
        for k in (3, 1, 2, 0):
            self.first(k).start()

    def add_all(self, items):
        pending = None

        def complete(copy, dst, stage, then):
            copy.wait()
            add_into(dst, stage)
            for remote in then:
                remote.start()

        for index, (arrivals, src, dst, then) in enumerate(items):
            for remote in arrivals:
                remote.wait_recv()
            stage = self.stage[index % 2].at[pl.ds(0, dst.shape[0])]
            copy = pltpu.make_async_copy(src, stage, self.load_sem.at[index % 2])
            copy.start()
            if pending is not None:
                complete(*pending)
            pending = (copy, dst, stage, then)
        complete(*pending)

    def pass_on(self):
        self.add_all(
            [
                ([self.first(3)], self.landed.at[3], self.own(3), [self.second(3, 1, 0), self.second(3, 2, 1)]),
                ([self.first(1)], self.landed.at[1], self.own(1), [self.second(1, 1, 0)]),
                ([self.first(2)], self.landed.at[2], self.own(2), [self.second(2, 2, 1)]),
            ]
        )

    def late(self):
        self.add_all(
            [
                (
                    [self.second(3, to, which)],
                    self.far.at[2, self.rows(which)],
                    self.own(k).at[self.rows(which)],
                    [self.second(k, k, which)],
                )
                for to, which, k in ((1, 0, 2), (2, 1, 1))
            ]
        )

    def finish(self, total):
        items = [([self.first(0)], self.landed.at[0], total, [])]
        for k in (1, 2):
            items.append(([self.second(k, k, which) for which in (0, 1)], self.far.at[k - 1], total, []))
        self.add_all(items)

    def drain(self):
        for k in range(4):
            self.first(k).wait_send()
        for k, to, which in ((3, 1, 0), (3, 2, 1), (1, 1, 0), (1, 1, 1), (2, 2, 0), (2, 2, 1)):
            self.second(k, to, which).wait_send()


def backward_kernel(
    n,
    planes,
    heads,
    length_ref,
    grad_in,
    mixed_in,
    a_in,
    b_in,
    hidden_in,
    normed2_in,
    normed_in,
    x_in,
    att_in,
    q_in,
    k_in,
    v_in,
    lse_in,
    cos_in,
    sin_in,
    attn_in,
    gate_in,
    up_in,
    down_in,
    gain_in,
    token_out,
    gain_out,
    down_all,
    gate_all,
    up_all,
    out_all,
    qkv_all,
    near1,
    far1,
    near2,
    far2,
    near3,
    far3,
    down_landed,
    gate_landed,
    up_landed,
    out_landed,
    qkv_landed,
    w_attn,
    w_gate,
    w_up,
    w_down,
    p_down,
    gains,
    grad,
    a_v,
    b_v,
    part,
    hid_stage,
    stage_tall,
    stage_wide,
    stage_col,
    hidden_grad,
    lse,
    cos,
    sin,
    dk_sum,
    dv_sum,
    gain_own,
    gain_all,
    gain_landed,
    gain_stage,
    z_send,
    z_recv,
    s_send,
    s_recv,
    g_send,
    g_recv,
    load_sem,
    hid_sem,
    add_sem,
    ring_sem,
):
    me, plane = lax.axis_index("ctx"), lax.axis_index("fsdp")
    total, width = grad.shape
    per_device = total // n
    own = heads * HEAD_SIZE
    own_width = width // n
    own_ff = a_v.shape[1]
    rows_shard = width // planes
    slab = own_ff // planes
    blocks = total // ROWS
    pairs = heads // 2
    columns = own + LANES
    last = planes - 2

    def load(src, dst, index):
        copy = pltpu.make_async_copy(src, dst, load_sem.at[index])
        copy.start()
        return copy

    mixed_loads = [load(mixed_in.at[:, pl.ds(d * own_width, own_width)], part.at[d], d) for d in range(own_ff // own_width)]
    grad_load = load(grad_in, grad, 8)
    down_load = load(down_in, w_down, 9)
    gate_load = load(gate_in, w_gate, 10)
    up_load = load(up_in, w_up, 11)
    a_load = load(a_in, a_v, 12)
    b_load = load(b_in, b_v, 13)
    attn_load = load(attn_in, w_attn, 14)
    gain_load = load(gain_in, gains, 15)
    greet(n, planes, me, plane, True)

    def settle(index, block, landed, stage):
        return Settle(block, landed, stage, planes, plane, z_send.at[index], z_recv.at[index], add_sem)

    def rows_of(ref, rows):
        return lambda d: ref.at[pl.ds(pl.multiple_of(d * rows, rows), rows)]

    def out_block_of(d):
        return w_down.at[pl.ds(0, rows_shard), pl.ds(pl.multiple_of(d * own_width, LANES), own_width)]

    def qkv_block_of(d):
        return w_down.at[pl.ds(rows_shard, rows_shard), pl.ds(pl.multiple_of(d * columns, LANES), columns)]

    def gain_block_of(d):
        return gain_own.at[:, pl.ds(pl.multiple_of(d * rows_shard, LANES), rows_shard)]

    down_sum = settle(0, rows_of(p_down, slab), down_landed, stage_wide)
    gate_sum = settle(1, rows_of(w_gate, rows_shard), gate_landed, stage_tall)
    up_sum = settle(2, rows_of(w_up, rows_shard), up_landed, stage_tall)
    out_sum = settle(3, out_block_of, out_landed, stage_tall.at[:, pl.ds(0, own_width)])
    qkv_sum = settle(4, qkv_block_of, qkv_landed, stage_tall.at[:, pl.ds(0, columns)])
    gain_sum = settle(5, gain_block_of, gain_landed, gain_stage)

    def spread(index, src, dst):
        return spread_over(n, src, lambda c: dst.at[c], n, me, g_send.at[index], g_recv.at[index])

    spreads = []

    def give(index, sums, dst):
        src = sums.block(plane)
        mine = load(src, dst.at[me], 16 + index)
        out = spread(index, src, dst)
        out.start()
        spreads.append((out, mine))
        return out

    def scatter(index, block, near, far, stage):
        return Scatter(block, near, far, stage, me, s_send.at[index], s_recv.at[index], ring_sem)

    part_rows = total // 2
    col_stages = [stage_col.at[pl.ds(i * part_rows, part_rows)] for i in range(2)]

    def half_scatter(index, near, far, side):
        rows = pl.ds(side * part_rows, part_rows)
        return scatter(
            2 * index + side, lambda c: part.at[c, rows], near.at[:, rows], far.at[:, rows], col_stages
        )

    first = [half_scatter(0, near1, far1, side) for side in range(2)]
    second = [half_scatter(1, near2, far2, side) for side in range(2)]

    grad_load.wait()

    def scale_block(i, _):
        rows = pl.ds(pl.multiple_of(i * ROWS, ROWS), ROWS)
        grad[rows, :] = (RESIDUAL_SCALE * grad[rows, :].astype(F32)).astype(BF16)
        return 0

    lax.fori_loop(0, blocks, scale_block, 0)
    for copy in mixed_loads:
        copy.wait()

    def down_block(d, _):
        p_down[pl.ds(pl.multiple_of(d * own_width, own_width), own_width), :] = dot_tn(part[d], grad[...]).astype(BF16)
        return 0

    lax.fori_loop(0, own_ff // own_width, down_block, 0)
    down_sum.start()

    for copy in (down_load, gate_load, up_load, a_load, b_load, attn_load, gain_load):
        copy.wait()
    half = gains.shape[1] // 2
    attn_gain = jnp.concatenate([gains[f * 8 : f * 8 + 1, :half] for f in range(planes)], axis=1)
    mlp_gain = jnp.concatenate([gains[f * 8 : f * 8 + 1, half:] for f in range(planes)], axis=1)
    gain_own[...] = jnp.zeros_like(gain_own)

    def stream(src, i, wait):
        rows = pl.ds(pl.multiple_of(i * ROWS, ROWS), ROWS)
        slot = lax.rem(i, 2)
        copy = pltpu.make_async_copy(src.at[rows], hid_stage.at[slot], hid_sem.at[slot])
        return copy.wait() if wait else copy.start()

    stream(hidden_in, jnp.int32(0), False)

    def mlp_block(i, _):
        rows = pl.ds(pl.multiple_of(i * ROWS, ROWS), ROWS)

        @pl.when(i + 1 < blocks)
        def _():
            stream(hidden_in, i + 1, False)

        mixed_grad = dot_nt(grad[rows, :], w_down[...])
        ggrad = (mixed_grad * a_v[rows, :].astype(F32)).astype(BF16)
        ugrad = (mixed_grad * b_v[rows, :].astype(F32)).astype(BF16)
        a_v[rows, :] = ggrad
        b_v[rows, :] = ugrad
        normed_grad = dot_nt(ggrad, w_gate[...]) + dot_nt(ugrad, w_up[...])
        stream(hidden_in, i, True)

        hidden = hid_stage[lax.rem(i, 2)].astype(F32)
        r2 = lax.rsqrt(jnp.mean(hidden * hidden, axis=-1, keepdims=True) + EPSILON)
        gain_own[0:1, :] += jnp.sum(normed_grad * (hidden * r2), axis=0, keepdims=True)
        weighted = normed_grad * mlp_gain
        mean = jnp.mean(weighted * hidden, axis=-1, keepdims=True)
        piece = r2 * weighted - hidden * (r2 * r2 * r2 * mean)
        for c in range(n):
            part[c, rows, :] = piece[:, c * own_width : (c + 1) * own_width].astype(BF16)

        @pl.when(i == blocks // 2 - 1)
        def _():
            first[0].start()

        @pl.when(i == blocks - 2)
        def _():
            down_sum.advance(1)
            first[0].pass_on()

        return 0

    lax.fori_loop(0, blocks, mlp_block, 0)
    first[1].start()
    normed2_load = load(normed2_in, grad, 8)
    normed2_load.wait()

    def columns_times(right, out, low, high):
        def block(j, _):
            lanes = pl.ds(pl.multiple_of(j * ROWS, ROWS), ROWS)
            out[lanes, :] = dot_tn(grad[:, lanes], right[...]).astype(BF16)
            return 0

        lax.fori_loop(low, high, block, 0)

    first[0].late()
    columns_times(a_v, w_gate, 0, width // ROWS)
    gate_sum.start()
    first[1].pass_on()
    columns_times(b_v, w_up, 0, width // ROWS // 2)
    first[1].late()
    columns_times(b_v, w_up, width // ROWS // 2, width // ROWS)
    down_sum.advance(2)

    att_loads = [load(att_in.at[c], grad.at[:, pl.ds(c * own, own)], c) for c in range(n)]
    own_grad = load(grad_in.at[:, pl.ds(pl.multiple_of(me * own_width, LANES), own_width)], b_v.at[:, pl.ds(LANES, own_width)], 8)
    q_load = load(q_in, a_v.at[:, pl.ds(0, own)], 9)
    k_load = load(k_in, a_v.at[:, pl.ds(own, LANES)], 10)
    v_load = load(v_in, a_v.at[:, pl.ds(own + LANES, LANES)], 11)
    lse_load = load(lse_in, lse, 12)
    cos_load = load(cos_in, cos, 13)
    sin_load = load(sin_in, sin, 14)
    own_grad.wait()

    def begin(i, _):
        rows = pl.ds(pl.multiple_of(i * ROWS, ROWS), ROWS)
        hidden_grad[rows, :] = b_v[rows, LANES : LANES + own_width].astype(F32) + part[me, rows, :].astype(F32)
        return 0

    lax.fori_loop(0, blocks, begin, 0)
    for side in range(2):
        first[side].finish(hidden_grad.at[pl.ds(side * part_rows, part_rows)])
        first[side].drain()

    def branch_block(i, _):
        rows = pl.ds(pl.multiple_of(i * ROWS, ROWS), ROWS)
        branch = (RESIDUAL_SCALE * hidden_grad[rows, :]).astype(BF16)
        b_v[rows, LANES : LANES + own_width] = branch
        for c in range(n):
            part[c, rows, :] = dot_nt(branch, w_attn[c * own : (c + 1) * own, columns:]).astype(BF16)

        @pl.when(i == blocks // 2 - 1)
        def _():
            second[0].start()

        return 0

    lax.fori_loop(0, blocks, branch_block, 0)
    second[1].start()
    second[0].pass_on()
    gate_sum.advance(1)
    for copy in att_loads:
        copy.wait()
    heads_per_shard = rows_shard // own
    for c in range(n):
        place = out_block_of(c // heads_per_shard).at[pl.ds((c % heads_per_shard) * own, own)]
        place[...] = dot_tn(grad[:, c * own : (c + 1) * own], b_v[:, LANES : LANES + own_width]).astype(BF16)
    second[1].pass_on()
    second[0].late()
    normed_load = load(normed_in, grad, 15)
    down_sum.take(last)
    up_sum.start()
    second[1].late()
    second[0].finish(part.at[me, pl.ds(0, part_rows)])
    down_give = give(0, down_sum, down_all)
    gate_sum.advance(2)

    for copy in (q_load, k_load, v_load, lse_load, cos_load, sin_load):
        copy.wait()
    dk_sum[...] = jnp.zeros_like(dk_sum)
    dv_sum[...] = jnp.zeros_like(dv_sum)
    first_len = length_ref[0]
    dq_at = own + 2 * LANES

    def attend_pair(side, pair, _):
        lanes = pl.ds(pl.multiple_of(pair * LANES, LANES), LANES)
        dq_lanes = pl.ds(pl.multiple_of(dq_at + pair * LANES, LANES), LANES)
        for block in range(side * (blocks // 2), (side + 1) * (blocks // 2)):
            rows = pl.ds(block * ROWS, ROWS)
            end = (block + 1) * ROWS
            bias = mask_bias(first_len, block * ROWS, ROWS, end)
            query, grads = a_v[rows, lanes], part[me, rows, lanes]
            low = low_half(query.shape)
            keys, values = a_v[:end, own : own + LANES], a_v[:end, own + LANES : own + 2 * LANES]
            parts = []
            for head in range(2):
                chosen = low if head == 0 else jnp.logical_not(low)
                own_query = jnp.where(chosen, query, jnp.zeros_like(query))
                own_grads = jnp.where(chosen, grads, jnp.zeros_like(grads))
                scores = dot_nt(own_query, keys) + bias
                probs = jnp.exp(scores - lse[pair, rows, head : head + 1])
                prob_grad = dot_nt(own_grads, values)
                delta = jnp.sum(probs * prob_grad, axis=-1, keepdims=True)
                score_grad = (probs * (prob_grad - delta)).astype(BF16)
                parts.append(dot_nn(score_grad, keys))
                dk_sum[:end, :] += dot_tn(score_grad, own_query)
                dv_sum[:end, :] += dot_tn(probs.astype(BF16), own_grads)
            dq = jnp.where(low_half(parts[0].shape), parts[0], parts[1]) * SCORE_SCALE
            a_v[rows, dq_lanes] = (dq * cos[rows, :] - swap_halves(dq) * sin[rows, :]).astype(BF16)

        if side:

            @pl.when(pair == 0)
            def _():
                down_give.pass_on()
                up_sum.advance(1)

        return 0

    lax.fori_loop(0, pairs, functools.partial(attend_pair, 0), 0)
    second[1].finish(part.at[me, pl.ds(part_rows, part_rows)])
    lax.fori_loop(0, pairs, functools.partial(attend_pair, 1), 0)
    dk = dk_sum[...]
    dk = dk + pltpu.roll(dk, HEAD_SIZE, 1)
    dk = dk * cos[...] - swap_halves(dk) * sin[...]
    dv = dv_sum[...]
    dv = dv + pltpu.roll(dv, HEAD_SIZE, 1)
    b_v[:, :LANES] = jnp.where(low_half(dk.shape), dk, dv).astype(BF16)
    down_give.late()
    gate_sum.take(last)
    gate_give = give(1, gate_sum, gate_all)
    up_sum.advance(2)
    out_sum.start()

    normed_load.wait()
    dq_end = dq_at + own
    for d in range(planes):
        for j in range(rows_shard // ROWS):
            lanes = slice(d * rows_shard + j * ROWS, d * rows_shard + (j + 1) * ROWS)
            place = qkv_block_of(d).at[pl.ds(j * ROWS, ROWS)]
            place[:, :own] = dot_tn(grad[:, lanes], a_v[:, dq_at:dq_end]).astype(BF16)
            place[:, own:] = dot_tn(grad[:, lanes], b_v[:, :LANES]).astype(BF16)
    gate_give.pass_on()
    out_sum.advance(1)
    qkv_sum.start()

    stream(x_in, jnp.int32(0), False)

    def token_block(i, _):
        rows = pl.ds(pl.multiple_of(i * ROWS, ROWS), ROWS)

        @pl.when(i + 1 < blocks)
        def _():
            stream(x_in, i + 1, False)

        normed_grad = dot_nt(a_v[rows, dq_at:dq_end], w_attn[:, :own]) + dot_nt(b_v[rows, :LANES], w_attn[:, own:columns])
        stream(x_in, i, True)
        x = hid_stage[lax.rem(i, 2)].astype(F32)
        r1 = lax.rsqrt(jnp.mean(x * x, axis=-1, keepdims=True) + EPSILON)
        gain_own[1:2, :] += jnp.sum(normed_grad * (x * r1), axis=0, keepdims=True)
        weighted = normed_grad * attn_gain
        mean = jnp.mean(weighted * x, axis=-1, keepdims=True)
        piece = r1 * weighted - x * (r1 * r1 * r1 * mean)
        for c in range(n):
            lanes = slice(c * own_width, (c + 1) * own_width)
            mine = jnp.where(me == c, hidden_grad[rows, :], 0.0)
            grad[rows, lanes] = (piece[:, lanes] + mine).astype(BF16)
        return 0

    lax.fori_loop(0, blocks, token_block, 0)

    def token_rows(c):
        return grad.at[pl.ds(pl.multiple_of(c * per_device, per_device), per_device)]

    third = scatter(4, token_rows, near3, far3, [hid_stage.at[i, pl.ds(0, per_device)] for i in range(2)])
    third.start()
    gain_give = spread(5, gain_own, gain_all)
    gain_mine = load(gain_own, gain_all.at[me], 21)
    gain_give.start()
    gate_give.late()
    third.pass_on()
    out_sum.advance(2)
    gain_give.pass_on()
    up_sum.take(last)
    up_give = give(2, up_sum, up_all)
    third.late()
    qkv_sum.advance(1)
    gain_give.finish()
    gain_mine.wait()
    gain_give.drain()
    gain_own[...] = sum(gain_all[c] for c in range(n))
    gain_sum.start()
    token_out[...] = token_rows(me)[...].astype(F32)
    third.finish(token_out)
    out_sum.take(last)
    out_give = give(3, out_sum, out_all)
    up_give.pass_on()
    qkv_sum.advance(2)
    gain_sum.advance(1)
    out_give.pass_on()
    up_give.late()
    gain_sum.advance(2)
    out_give.late()
    qkv_sum.take(last)
    qkv_give = give(4, qkv_sum, qkv_all)
    gain_sum.take(last)
    gain_out[...] = gain_block_of(plane)[...]
    qkv_give.pass_on()
    qkv_give.late()
    for out, mine in spreads:
        out.finish()
        out.drain()
        mine.wait()
    for s in (*second, third):
        s.drain()
    for s in (down_sum, gate_sum, up_sum, out_sum, qkv_sum, gain_sum):
        s.drain()


def backward(n, planes, heads, lengths, grad, saved, weights, cos, sin):
    x, normed, q_rot, k_rot, v_rows, lse, att_all, hidden, normed2, a, b, mixed = saved
    w_attn, w_gate, w_up, w_down, gains = weights
    total, width = grad.shape
    own = heads * HEAD_SIZE
    own_width = width // n
    own_ff = a.shape[1]
    rows_shard = width // planes
    slab = own_ff // planes
    columns = own + LANES
    chips = n // 2
    per_device = total // n
    col, row = (chips, total, own_width), (chips, per_device, width)
    outs = [
        ((per_device, width), F32),
        ((8, rows_shard), F32),
        ((n, slab, width), BF16),
        ((n, rows_shard, own_ff), BF16),
        ((n, rows_shard, own_ff), BF16),
        ((n, rows_shard, own_width), BF16),
        ((n, rows_shard, columns), BF16),
        (col, BF16),
        (col, BF16),
        (col, BF16),
        (col, BF16),
        (row, BF16),
        (row, BF16),
        ((planes + 1, slab, width), BF16),
        ((planes + 1, rows_shard, own_ff), BF16),
        ((planes + 1, rows_shard, own_ff), BF16),
        ((planes + 1, rows_shard, own_width), BF16),
        ((planes + 1, rows_shard, columns), BF16),
    ]
    scratch = [
        (w_attn.shape, BF16),
        (w_gate.shape, BF16),
        (w_up.shape, BF16),
        (w_down.shape, BF16),
        (w_down.shape, BF16),
        (gains.shape, F32),
        ((total, width), BF16),
        ((total, own_ff), BF16),
        ((total, own_ff), BF16),
        ((n, total, own_width), BF16),
        ((2, ROWS, width), BF16),
        ((rows_shard, own_ff), BF16),
        ((slab, width), BF16),
        ((total, own_width), BF16),
        ((total, own_width), F32),
        (lse.shape, F32),
        (cos.shape, F32),
        (sin.shape, F32),
        ((total, LANES), F32),
        ((total, LANES), F32),
        ((8, width), F32),
        ((n, 8, width), F32),
        ((planes + 1, 8, rows_shard), F32),
        ((8, rows_shard), F32),
    ]
    steps = planes - 1
    dma = pltpu.SemaphoreType.DMA
    anywhere = pl.BlockSpec(memory_space=pl.ANY)
    vmem = pl.BlockSpec(memory_space=pltpu.VMEM)
    return pl.pallas_call(
        functools.partial(backward_kernel, n, planes, heads),
        in_specs=[pl.BlockSpec(memory_space=pltpu.SMEM)] + [anywhere] * 20,
        out_specs=[vmem] * 2 + [anywhere] * (len(outs) - 2),
        out_shape=[jax.ShapeDtypeStruct(*o) for o in outs],
        scratch_shapes=[pltpu.VMEM(*s) for s in scratch]
        + [
            dma((6, 2, steps)),
            dma((6, 2, steps)),
            dma((5, 10)),
            dma((5, 10)),
            dma((6, n)),
            dma((6, n)),
            dma((24,)),
            dma((2,)),
            dma,
            dma((2,)),
        ],
        compiler_params=pltpu.CompilerParams(
            vmem_limit_bytes=60 * 1024 * 1024, collective_id=2, has_side_effects=True
        ),
        cost_estimate=pl.CostEstimate(
            flops=16 * total * width * own_ff, bytes_accessed=100 * 1024 * 1024, transcendentals=0
        ),
        name="backward",
    )(
        lengths,
        grad,
        mixed,
        a,
        b,
        hidden,
        normed2,
        normed,
        x,
        att_all,
        q_rot,
        k_rot,
        v_rows,
        lse,
        cos,
        sin,
        w_attn,
        w_gate,
        w_up,
        w_down,
        gains,
    )[:7]


def kernel_fits(n, planes, total, width, own_ff):
    held = 4 * width * own_ff + 2 * total * width + 2 * total * own_ff
    return planes == 4 and total % (2 * ROWS) == 0 and n == 8 and own_ff // planes >= total // n and n * own_ff >= 4 * width and 2 * held < 44 * 1024 * 1024 and (own_ff // planes) % LANES == 0


def own_columns(array, index, width):
    return lax.dynamic_slice_in_dim(array, index * width, width, axis=1)


def after(value, *others):
    return lax.optimization_barrier((value, *others))[0]


def local(
    tokens,
    lengths,
    deal,
    attn_gain,
    query_weight,
    key_matrix,
    value_matrix,
    out_weight,
    mlp_gain,
    gate_weight,
    up_weight,
    down_weight,
    cotangent,
):
    n_ctx = lax.axis_size("ctx")
    n_fsdp = lax.axis_size("fsdp")
    me = lax.axis_index("ctx")
    me_array = me.astype(jnp.int32).reshape(1)
    per_device, width = tokens.shape[1], tokens.shape[2]
    total = per_device * n_ctx
    block_rows = per_device // n_ctx
    heads = QUERY_HEADS // n_ctx
    sharing = n_ctx // KEY_VALUE_HEADS
    own_width = width // n_ctx
    ff = gate_weight.shape[1]
    slab = ff // (n_fsdp * n_ctx)
    own_ff = slab * n_fsdp
    rows_shard = query_weight.shape[0]

    kv_head = me // sharing
    split = heads * HEAD_SIZE
    attn_shard = jnp.concatenate(
        [
            own_columns(query_weight, me, split),
            own_columns(key_matrix, kv_head, HEAD_SIZE),
            own_columns(value_matrix, kv_head, HEAD_SIZE),
            own_columns(out_weight, me, own_width),
        ],
        axis=1,
    )

    def ff_columns(array):
        return jnp.concatenate([own_columns(array, f * n_ctx + me, slab) for f in range(n_fsdp)], axis=1)

    gain_shard = jnp.tile(jnp.concatenate([attn_gain, mlp_gain]).astype(F32)[None], (8, 1))

    first_len = lengths[0, 0]
    given = jnp.arange(total, dtype=jnp.int32)
    position = given - jnp.where(given >= first_len, first_len, 0)
    freq_index = jnp.arange(HEAD_SIZE // 2, dtype=F32)
    inverse = ROPE_BASE ** (-2.0 * freq_index / HEAD_SIZE)
    turns = jnp.tile(inverse, 4)
    sign = jnp.tile(jnp.repeat(jnp.array([-1.0, 1.0], F32), HEAD_SIZE // 2), 2)
    angles = position.astype(F32)[:, None] * turns[None, :]
    cos_table = jnp.cos(angles)
    sin_table = jnp.sin(angles) * sign[None, :]

    deal_rows = deal[0]
    slot_ids = jnp.arange(n_ctx, dtype=jnp.int32)
    dealt_of_given = (deal_rows * n_ctx + slot_ids[:, None]).reshape(-1)
    matched = deal_rows[:, :, None] == slot_ids[None, None, :]
    source_slot = jnp.sum(jnp.where(matched, slot_ids[None, :, None], 0), axis=1)
    given_of_dealt = (slot_ids[:, None] * n_ctx + source_slot).T.reshape(-1)

    def reorder(array, table):
        blocks = array.reshape(n_ctx * n_ctx, block_rows, array.shape[1])
        return jnp.take(blocks, table, axis=0, mode="clip").reshape(array.shape)

    ff_weights = gate_weight, up_weight, down_weight
    if slab % LANES:
        ff_weights = (
            ff_columns(gate_weight),
            ff_columns(up_weight),
            lax.dynamic_slice_in_dim(down_weight, me * slab, slab, axis=0),
        )

    cotangent_all = lax.all_gather(cotangent[0], "ctx", axis=0, tiled=True)
    (
        x, normed, q_rot, k_rot, v_rows, lse, attended_all, hidden_all, normed2, a, b, both, w_attn, w_gate, w_up, w_down, gains_all,
    ) = forward(
        n_ctx,
        n_fsdp,
        heads,
        slab,
        lengths[0],
        tokens[0],
        attn_shard,
        *ff_weights,
        gain_shard,
        cos_table,
        sin_table,
    )
    w_qkv, w_out = w_attn[:, : split + 2 * HEAD_SIZE], w_attn[:, split + 2 * HEAD_SIZE :]
    gains = gains_all.reshape(n_fsdp, 8, 2, rows_shard)[:, 0].transpose(1, 0, 2).reshape(2, 1, width)
    grad_result = reorder(cotangent_all, dealt_of_given)

    column = lax.broadcasted_iota(jnp.int32, (own_width, width), 1) - me * own_width
    place = (column == lax.broadcasted_iota(jnp.int32, (own_width, width), 0)).astype(BF16)
    result_part = RESIDUAL_SCALE * dot_nn(reorder(both, given_of_dealt), jnp.concatenate([w_down, place], axis=0))
    activations = lax.psum_scatter(
        result_part.astype(BF16), "ctx", scatter_dimension=0, tiled=True
    )[None]

    if kernel_fits(n_ctx, n_fsdp, total, width, own_ff):
        token_grad, gain_rows, down_part, gate_part, up_part, out_part, qkv_part = backward(
            n_ctx,
            n_fsdp,
            heads,
            lengths[0],
            grad_result,
            (x, normed, q_rot, k_rot, v_rows, lse, attended_all, hidden_all, normed2, a, b, both),
            (w_attn, w_gate, w_up, w_down, gains_all),
            cos_table,
            sin_table,
        )
        token_grad = token_grad[None]
        own_gains = gain_rows[1::-1]
    else:
        mlp_grad = (RESIDUAL_SCALE * grad_result.astype(F32)).astype(BF16)

        def settle(left, right):
            return lax.psum_scatter(dot_tn(left, right).astype(BF16), "fsdp", scatter_dimension=0, tiled=True)

        down_part = settle(both[:, :own_ff], mlp_grad)
        ggrad, ugrad, hidden_part, mlp_gain_part = mlp_backward(
            n_ctx, mlp_grad, a, b, hidden_all, gains[1], w_gate, w_up, w_down
        )
        hidden_sum = lax.psum_scatter(hidden_part, "ctx", scatter_dimension=0, tiled=False)
        gate_part = settle(normed2, ggrad)
        up_part = settle(normed2, ugrad)
        hidden_grad, branch_grad, attended_part = branch_backward(
            hidden_sum, own_columns(grad_result, me, own_width), w_out, n_ctx
        )
        attended_grad = lax.psum_scatter(attended_part, "ctx", scatter_dimension=0, tiled=False)
        out_part = lax.psum_scatter(
            jnp.einsum("ctk,to->cko", attended_all, branch_grad, preferred_element_type=F32)
            .astype(BF16)
            .reshape(width, own_width),
            "fsdp",
            scatter_dimension=0,
            tiled=True,
        )
        dq, dkv = attention_backward(attended_grad, q_rot, k_rot, v_rows, lse, cos_table, sin_table, lengths[0])
        qkv_part = settle(normed, jnp.concatenate([dq, dkv], axis=1))
        token_part, attn_gain_part = token_backward(me_array, dq, dkv, w_qkv, x, gains[0], hidden_grad)
        token_grad = lax.psum_scatter(token_part, "ctx", scatter_dimension=0, tiled=True).astype(F32)[None]

        gain_parts = jnp.concatenate([attn_gain_part, mlp_gain_part], axis=0)
        step = 1
        while step < n_ctx:
            gain_parts = gain_parts + lax.ppermute(gain_parts, "ctx", [(c, c ^ step) for c in range(n_ctx)])
            step *= 2
        gain_rows = gain_parts.reshape(2, n_fsdp, rows_shard).transpose(1, 0, 2).reshape(n_fsdp, 2 * rows_shard)
        own_gains = lax.psum_scatter(gain_rows, "fsdp", scatter_dimension=0, tiled=True).reshape(2, rows_shard)
        down_part, gate_part, up_part, out_part, qkv_part = [
            lax.all_gather(p, "ctx", axis=0, tiled=False) for p in (down_part, gate_part, up_part, out_part, qkv_part)
        ]

    if slab % LANES == 0 and sharing == 1 and heads % 4 == 0:
        gate_grad, up_grad, down_grad, out_grad, query_grad, key_grad, value_grad = finish(
            slab, gate_part, up_part, down_part.reshape(n_ctx * slab, width), out_part, qkv_part
        )
    else:
        down_grad = down_part.reshape(n_ctx * slab, width).astype(F32)
        if slab % LANES == 0:
            gate_grad = spread_columns(gate_part, slab, n_fsdp)
            up_grad = spread_columns(up_part, slab, n_fsdp)
        else:

            def ff_whole(part):
                pieces = part.reshape(n_ctx, rows_shard, n_fsdp, slab)
                return pieces.transpose(1, 2, 0, 3).reshape(rows_shard, ff).astype(F32)

            gate_grad = ff_whole(gate_part)
            up_grad = ff_whole(up_part)
        out_grad = spread_columns(out_part, own_width, 1)
        qkv_all = qkv_part
        query_grad = spread_columns(qkv_all, split, 1)

        def shared_heads(pieces):
            pieces = pieces.astype(F32).reshape(KEY_VALUE_HEADS, sharing, rows_shard, HEAD_SIZE).sum(axis=1)
            return pieces.transpose(1, 0, 2).reshape(rows_shard, KEY_VALUE_HEADS * HEAD_SIZE)

        key_grad = shared_heads(qkv_all[:, :, split : split + HEAD_SIZE])
        value_grad = shared_heads(qkv_all[:, :, split + HEAD_SIZE :])

    return (
        activations,
        token_grad,
        own_gains[0],
        query_grad,
        key_grad,
        value_grad,
        out_grad,
        own_gains[1],
        gate_grad,
        up_grad,
        down_grad,
    )


def solution(mesh):
    rows = P("fsdp", None)
    block = P("fsdp", "ctx", None)
    gain = P("fsdp")
    return jax.shard_map(
        local,
        mesh=mesh,
        in_specs=(block, rows, P("fsdp", None, None), gain, rows, rows, rows, rows, gain, rows, rows, rows, block),
        out_specs=(block, block, gain, rows, rows, rows, rows, gain, rows, rows, rows),
        check_vma=False,
    )
```

```python
import functools

import jax
import jax.numpy as jnp
from jax import lax
from jax.experimental import pallas as pl
from jax.experimental.pallas import tpu as pltpu
from jax.sharding import PartitionSpec as P

QUERY_HEADS = 32
KEY_VALUE_HEADS = 8
HEAD_SIZE = 64
EPSILON = 1e-05
ROPE_BASE = 10000000.0
SCORE_SCALE = 0.015625
RESIDUAL_SCALE = 0.22
NEGATIVE_BIG = -1e30
LANES = 128
ROWS = 256
BF16 = jnp.bfloat16
F32 = jnp.float32
VMEM_LIMIT = 59 * 1024 * 1024


def dot_nn(a, b):
    return lax.dot_general(a, b, (((1,), (0,)), ((), ())), preferred_element_type=F32)


def dot_nt(a, b):
    return lax.dot_general(a, b, (((1,), (1,)), ((), ())), preferred_element_type=F32)


def dot_tn(a, b):
    return lax.dot_general(a, b, (((0,), (0,)), ((), ())), preferred_element_type=F32)


def swap_halves(x):
    lane = lax.broadcasted_iota(jnp.int32, x.shape, 1)
    first = lax.rem(lane, HEAD_SIZE) < HEAD_SIZE // 2
    return jnp.where(first, pltpu.roll(x, LANES - HEAD_SIZE // 2, 1), pltpu.roll(x, HEAD_SIZE // 2, 1))


def low_half(shape):
    return lax.broadcasted_iota(jnp.int32, shape, 1) < HEAD_SIZE


def mask_bias(first_len, row0, rows, cols):
    query = row0 + lax.broadcasted_iota(jnp.int32, (rows, cols), 0)
    key = lax.broadcasted_iota(jnp.int32, (rows, cols), 1)
    start = jnp.where(query >= first_len, first_len, 0)
    return jnp.where((key <= query) & (key >= start), 0.0, NEGATIVE_BIG)


def attention_backward_kernel(length_ref, g_ref, q_ref, k_ref, v_ref, lse_ref, cos_ref, sin_ref, dq_ref, dkv_ref, dk_sum, dv_sum):
    pair = pl.program_id(0)
    tokens = q_ref.shape[0]

    @pl.when(pair == 0)
    def _():
        dk_sum[...] = jnp.zeros_like(dk_sum)
        dv_sum[...] = jnp.zeros_like(dv_sum)

    first_len = length_ref[0]
    for block in range(tokens // ROWS):
        rows = pl.ds(block * ROWS, ROWS)
        end = (block + 1) * ROWS
        bias = mask_bias(first_len, block * ROWS, ROWS, end)
        query, grad = q_ref[rows, :], g_ref[rows, :]
        low = low_half(query.shape)
        keys, values = k_ref[:end, :], v_ref[:end, :]
        parts = []
        for half in range(2):
            chosen = low if half == 0 else jnp.logical_not(low)
            own_query = jnp.where(chosen, query, jnp.zeros_like(query))
            own_grad = jnp.where(chosen, grad, jnp.zeros_like(grad))
            scores = dot_nt(own_query, keys) + bias
            probs = jnp.exp(scores - lse_ref[0, rows, half : half + 1])
            prob_grad = dot_nt(own_grad, values)
            delta = jnp.sum(probs * prob_grad, axis=-1, keepdims=True)
            score_grad = (probs * (prob_grad - delta)).astype(BF16)
            parts.append(dot_nn(score_grad, keys))
            dk_sum[:end, :] += dot_tn(score_grad, own_query)
            dv_sum[:end, :] += dot_tn(probs.astype(BF16), own_grad)
        dq = jnp.where(low_half(parts[0].shape), parts[0], parts[1]) * SCORE_SCALE
        dq_ref[rows, :] = (dq * cos_ref[rows, :] - swap_halves(dq) * sin_ref[rows, :]).astype(BF16)

    @pl.when(pair == pl.num_programs(0) - 1)
    def _():
        dk = dk_sum[...]
        dk = dk + pltpu.roll(dk, HEAD_SIZE, 1)
        dk = dk * cos_ref[...] - swap_halves(dk) * sin_ref[...]
        dv = dv_sum[...]
        dv = dv + pltpu.roll(dv, HEAD_SIZE, 1)
        dkv_ref[...] = jnp.where(low_half(dk.shape), dk, dv).astype(BF16)


def attention_backward(grads, q_rot, k_rot, v_rows, lse, cos, sin, lengths):
    tokens = q_rot.shape[0]
    pairs = q_rot.shape[1] // LANES
    one = pl.BlockSpec((tokens, LANES), lambda j: (0, 0))
    each = pl.BlockSpec((tokens, LANES), lambda j: (0, j))
    return pl.pallas_call(
        attention_backward_kernel,
        grid=(pairs,),
        in_specs=[
            pl.BlockSpec(memory_space=pltpu.SMEM),
            each,
            each,
            one,
            one,
            pl.BlockSpec((1, tokens, LANES), lambda j: (j, 0, 0)),
            one,
            one,
        ],
        out_specs=[each, one],
        out_shape=[
            jax.ShapeDtypeStruct((tokens, pairs * LANES), BF16),
            jax.ShapeDtypeStruct((tokens, LANES), BF16),
        ],
        scratch_shapes=[pltpu.VMEM((tokens, LANES), F32), pltpu.VMEM((tokens, LANES), F32)],
        compiler_params=pltpu.CompilerParams(vmem_limit_bytes=VMEM_LIMIT),
        cost_estimate=pl.CostEstimate(
            flops=10 * tokens * tokens * LANES * pairs,
            bytes_accessed=12 * tokens * pairs * LANES,
            transcendentals=tokens * tokens * pairs,
        ),
        name="attend_back",
    )(lengths, grads, q_rot, k_rot, v_rows, lse, cos, sin)


def row_block(width):
    return pl.BlockSpec((ROWS, width), lambda i: (i, 0))


def fixed(*shape):
    return pl.BlockSpec(shape, lambda i: (0,) * len(shape))


def params():
    return pltpu.CompilerParams(vmem_limit_bytes=VMEM_LIMIT)


def cost(flops, *arrays):
    moved = sum(a.size * a.dtype.itemsize for a in arrays)
    return pl.CostEstimate(flops=flops, bytes_accessed=moved, transcendentals=0)


def mlp_back_kernel(
    grad_ref, a_ref, b_ref, hidden_ref, gain_ref, gate_ref, up_ref, down_ref, ggrad_ref, ugrad_ref, part_ref, gain_out
):
    mixed_grad = dot_nt(grad_ref[...], down_ref[...])
    ggrad = (mixed_grad * a_ref[...].astype(F32)).astype(BF16)
    ugrad = (mixed_grad * b_ref[...].astype(F32)).astype(BF16)
    ggrad_ref[...] = ggrad
    ugrad_ref[...] = ugrad
    normed_grad = dot_nt(ggrad, gate_ref[...]) + dot_nt(ugrad, up_ref[...])
    hidden = hidden_ref[...].astype(F32)
    r2 = lax.rsqrt(jnp.mean(hidden * hidden, axis=-1, keepdims=True) + EPSILON)
    gain_part = jnp.sum(normed_grad * (hidden * r2), axis=0, keepdims=True)

    @pl.when(pl.program_id(0) == 0)
    def _():
        gain_out[...] = jnp.zeros_like(gain_out)

    gain_out[...] += gain_part
    weighted = normed_grad * gain_ref[...]
    mean = jnp.mean(weighted * hidden, axis=-1, keepdims=True)
    part = r2 * weighted - hidden * (r2 * r2 * r2 * mean)
    own = part_ref.shape[2]
    for c in range(part_ref.shape[0]):
        part_ref[c] = part[:, c * own : (c + 1) * own].astype(BF16)


def mlp_backward(n, mlp_grad, a, b, hidden_all, gain, w_gate, w_up, w_down):
    total, width = hidden_all.shape
    own = width // n
    own_ff = w_gate.shape[1]
    narrow = jax.ShapeDtypeStruct((total, own_ff), BF16)
    planes = pl.BlockSpec((n, ROWS, own), lambda i: (0, i, 0))
    return pl.pallas_call(
        mlp_back_kernel,
        grid=(total // ROWS,),
        in_specs=[
            row_block(width),
            row_block(own_ff),
            row_block(own_ff),
            row_block(width),
            fixed(1, width),
            fixed(width, own_ff),
            fixed(width, own_ff),
            fixed(own_ff, width),
        ],
        out_specs=[row_block(own_ff), row_block(own_ff), planes, fixed(1, width)],
        out_shape=[narrow, narrow, jax.ShapeDtypeStruct((n, total, own), BF16), jax.ShapeDtypeStruct((1, width), F32)],
        compiler_params=params(),
        cost_estimate=cost(6 * total * width * own_ff, mlp_grad, hidden_all, hidden_all, w_gate, w_up, w_down, a, b, a, b),
        name="mlp_backward",
    )(mlp_grad, a, b, hidden_all, gain, w_gate, w_up, w_down)


def branch_kernel(part_ref, grad_ref, w_ref, hidden_ref, branch_ref, out_ref):
    hidden_grad = part_ref[...].astype(F32) + grad_ref[...].astype(F32)
    hidden_ref[...] = hidden_grad
    branch = (RESIDUAL_SCALE * hidden_grad).astype(BF16)
    branch_ref[...] = branch
    own = out_ref.shape[2]
    for c in range(out_ref.shape[0]):
        out_ref[c] = dot_nt(branch, w_ref[c]).astype(BF16)


def branch_backward(hidden_part, grad_own, w_out, n):
    total, own_width = hidden_part.shape
    own = w_out.shape[0] // n
    w_heads = w_out.reshape(n, own, own_width)
    return pl.pallas_call(
        branch_kernel,
        grid=(total // ROWS,),
        in_specs=[row_block(own_width), row_block(own_width), fixed(n, own, own_width)],
        out_specs=[row_block(own_width), row_block(own_width), pl.BlockSpec((n, ROWS, own), lambda i: (0, i, 0))],
        out_shape=[
            jax.ShapeDtypeStruct((total, own_width), F32),
            jax.ShapeDtypeStruct((total, own_width), BF16),
            jax.ShapeDtypeStruct((n, total, own), BF16),
        ],
        compiler_params=params(),
        cost_estimate=cost(2 * total * own_width * own * n, hidden_part, hidden_part, hidden_part, w_out),
        name="branch_backward",
    )(hidden_part, grad_own, w_heads)


def token_kernel(me_ref, dq_ref, dkv_ref, w_ref, x_ref, gain_ref, hidden_ref, part_ref, gain_out):
    split = dq_ref.shape[1]
    normed_grad = dot_nt(dq_ref[...], w_ref[:, :split]) + dot_nt(dkv_ref[...], w_ref[:, split:])
    x = x_ref[...].astype(F32)
    r1 = lax.rsqrt(jnp.mean(x * x, axis=-1, keepdims=True) + EPSILON)

    @pl.when(pl.program_id(0) == 0)
    def _():
        gain_out[...] = jnp.zeros_like(gain_out)

    gain_out[...] += jnp.sum(normed_grad * (x * r1), axis=0, keepdims=True)
    weighted = normed_grad * gain_ref[...]
    mean = jnp.mean(weighted * x, axis=-1, keepdims=True)
    part = r1 * weighted - x * (r1 * r1 * r1 * mean)
    own_width = hidden_ref.shape[1]
    for c in range(part.shape[1] // own_width):
        piece = part[:, c * own_width : (c + 1) * own_width]
        piece = piece + jnp.where(me_ref[0] == c, hidden_ref[...], 0.0)
        part_ref[:, c * own_width : (c + 1) * own_width] = piece.astype(BF16)


def token_backward(me, dq, dkv, w_qkv, x, gain, hidden_grad):
    total, width = x.shape
    own_width = hidden_grad.shape[1]
    return pl.pallas_call(
        token_kernel,
        grid=(total // ROWS,),
        in_specs=[
            pl.BlockSpec(memory_space=pltpu.SMEM),
            row_block(dq.shape[1]),
            row_block(dkv.shape[1]),
            fixed(*w_qkv.shape),
            row_block(width),
            fixed(1, width),
            row_block(own_width),
        ],
        out_specs=[row_block(width), fixed(1, width)],
        out_shape=[jax.ShapeDtypeStruct((total, width), BF16), jax.ShapeDtypeStruct((1, width), F32)],
        compiler_params=params(),
        cost_estimate=cost(2 * total * width * w_qkv.shape[1], x, x, w_qkv, dq, dkv, hidden_grad),
        name="token_backward",
    )(me, dq, dkv, w_qkv, x, gain, hidden_grad)


def result_kernel(me_ref, rows_ref, w_ref, out_ref):
    depth = w_ref.shape[0]
    own = rows_ref.shape[1] - depth
    product = dot_nn(rows_ref[:, :depth], w_ref[...])
    hidden = rows_ref[:, depth:].astype(F32)
    for c in range(out_ref.shape[1] // own):
        lanes = slice(c * own, (c + 1) * own)
        mine = jnp.where(me_ref[0] == c, hidden, 0.0)
        out_ref[:, lanes] = (RESIDUAL_SCALE * (product[:, lanes] + mine)).astype(BF16)


def result_rows(me, rows, w_down):
    total, columns = rows.shape
    depth, width = w_down.shape
    out_shape = jax.ShapeDtypeStruct((total, width), BF16)
    return pl.pallas_call(
        result_kernel,
        grid=(total // ROWS,),
        in_specs=[pl.BlockSpec(memory_space=pltpu.SMEM), row_block(columns), fixed(depth, width)],
        out_specs=row_block(width),
        out_shape=out_shape,
        compiler_params=params(),
        cost_estimate=cost(2 * total * depth * width, rows, w_down, out_shape),
        name="result_rows",
    )(me, rows, w_down)


def finish_kernel(slab, gate_ref, up_ref, down_ref, out_ref, qkv_ref, gate_out, up_out, down_out, out_out, q_out, k_out, v_out):
    n = gate_ref.shape[0]
    for src, dst, piece in ((gate_ref, gate_out, slab), (up_ref, up_out, slab), (out_ref, out_out, out_ref.shape[2])):
        for c in range(n):
            for f in range(src.shape[2] // piece):
                at = (f * n + c) * piece
                dst[:, at : at + piece] = src[c, :, f * piece : (f + 1) * piece].astype(F32)
    down_out[...] = down_ref[...].astype(F32)
    split = qkv_ref.shape[2] - LANES
    for c in range(n):
        q_out[:, c * split : (c + 1) * split] = qkv_ref[c, :, :split].astype(F32)
    for pair in range(n // 2):
        even = qkv_ref[2 * pair, :, split:].astype(F32)
        odd = qkv_ref[2 * pair + 1, :, split:].astype(F32)
        low = low_half(even.shape)
        lanes = slice(pair * LANES, (pair + 1) * LANES)
        k_out[:, lanes] = jnp.where(low, even, pltpu.roll(odd, HEAD_SIZE, 1))
        v_out[:, lanes] = jnp.where(low, pltpu.roll(even, HEAD_SIZE, 1), odd)


def finish(slab, gate, up, down, out, qkv):
    n, rows, own_ff = gate.shape
    width = n * out.shape[2]
    steps = 16
    tile, down_tile = rows // steps, down.shape[0] // steps
    kv = n * HEAD_SIZE

    def by_device(columns):
        return pl.BlockSpec((n, tile, columns), lambda i: (0, i, 0))

    def flat(height, columns):
        return pl.BlockSpec((height, columns), lambda i: (i, 0))

    outs = [
        (flat(tile, n * own_ff), (rows, n * own_ff)),
        (flat(tile, n * own_ff), (rows, n * own_ff)),
        (flat(down_tile, width), down.shape),
        (flat(tile, width), (rows, width)),
        (flat(tile, width), (rows, width)),
        (flat(tile, kv), (rows, kv)),
        (flat(tile, kv), (rows, kv)),
    ]
    return pl.pallas_call(
        functools.partial(finish_kernel, slab),
        grid=(steps,),
        in_specs=[
            by_device(own_ff),
            by_device(own_ff),
            flat(down_tile, width),
            by_device(out.shape[2]),
            by_device(qkv.shape[2]),
        ],
        out_specs=[spec for spec, _ in outs],
        out_shape=[jax.ShapeDtypeStruct(shape, F32) for _, shape in outs],
        compiler_params=params(),
        cost_estimate=cost(0, gate, gate, gate, up, up, up, down, down, down),
        name="finish",
    )(gate, up, down, out, qkv)


def spread_kernel(in_ref, out_ref):
    slab = in_ref.shape[2]
    for c in range(in_ref.shape[0]):
        out_ref[:, c * slab : (c + 1) * slab] = in_ref[c].astype(F32)


def spread_columns(pieces, slab, groups):
    n, rows, _ = pieces.shape
    tile = 128
    out_shape = jax.ShapeDtypeStruct((rows, groups * n * slab), F32)
    return pl.pallas_call(
        spread_kernel,
        grid=(groups, rows // tile),
        in_specs=[pl.BlockSpec((n, tile, slab), lambda f, r: (0, r, f))],
        out_specs=pl.BlockSpec((tile, n * slab), lambda f, r: (r, f)),
        out_shape=out_shape,
        compiler_params=params(),
        cost_estimate=cost(0, pieces, out_shape),
        name="spread_columns",
    )(pieces)


MESH = pl.DeviceIdType.MESH


class Chain:
    def __init__(self, slot, planes, plane, send_sem, recv_sem):
        self.slot, self.planes, self.plane = slot, planes, plane
        self.send_sem, self.recv_sem = send_sem, recv_sem

    def copy(self, way, step, shard, to):
        return pltpu.make_async_remote_copy(
            src_ref=self.slot(shard),
            dst_ref=self.slot(shard),
            send_sem=self.send_sem.at[way, step],
            recv_sem=self.recv_sem.at[way, step],
            device_id={"fsdp": to},
            device_id_type=MESH,
        )

    def moves(self, step):
        p, last = self.plane, self.planes - 1
        return (
            (0, (p >= step) & (p < last), p - step, p + 1, p >= step + 1, p - 1 - step),
            (1, (p + step <= last) & (p > 0), p + step, p - 1, p + step + 1 <= last, p + 1 + step),
        )

    def start(self, step):
        for way, sends, shard, to, _, _ in self.moves(step):

            @pl.when(sends)
            def _(way=way, shard=shard, to=to):
                self.copy(way, step, shard, to).start()

    def arrive(self, step):
        for way, _, _, _, receives, shard in self.moves(step):

            @pl.when(receives)
            def _(way=way, shard=shard):
                self.copy(way, step, shard, self.plane).wait_recv()

    def advance(self, step):
        self.arrive(step - 1)
        self.start(step)

    def drain(self):
        for step in range(self.planes - 1):
            for way, sends, shard, to, _, _ in self.moves(step):

                @pl.when(sends)
                def _(way=way, shard=shard, to=to, step=step):
                    self.copy(way, step, shard, to).wait_send()


class Spread:
    def __init__(self, src, slot, n, me, send_sem, recv_sem):
        self.src, self.slot, self.n, self.me = src, slot, n, me
        self.send_sem, self.recv_sem = send_sem, recv_sem
        self.chips = n // 2
        self.chip, self.core = me // 2, lax.rem(me, 2)
        self.partner = me + 1 - 2 * self.core

    def at(self, k):
        return lax.rem(self.chip + k, self.chips) * 2 + self.core

    def copy(self, src, owner, sem, to):
        return pltpu.make_async_remote_copy(
            src_ref=src,
            dst_ref=self.slot(owner),
            send_sem=self.send_sem.at[sem],
            recv_sem=self.recv_sem.at[sem],
            device_id={"ctx": to},
            device_id_type=MESH,
        )

    def out(self, k):
        return self.copy(self.src, self.me, k, self.at(k))

    def relay(self, k):
        owner = self.at(self.chips - k) if k else self.me
        src = self.slot(owner) if k else self.src
        return self.copy(src, owner, self.chips + k, self.partner)

    def start(self):
        for k in range(1, self.chips):
            self.out(k).start()
        self.relay(0).start()

    def pass_on(self):
        for k in range(1, self.chips):
            self.copy(self.src, self.at(self.chips - k), k, self.me).wait_recv()
            self.relay(k).start()

    def late(self):
        pass

    def finish(self):
        other = 1 - 2 * self.core
        for k in range(self.chips):
            owner = (self.at(self.chips - k) if k else self.me) + other
            self.copy(self.slot(owner), owner, self.chips + k, self.me).wait_recv()

    def drain(self):
        for k in range(1, self.chips):
            self.out(k).wait_send()
        for k in range(self.chips):
            self.relay(k).wait_send()


class Spread4:
    def __init__(self, src, slot, n, me, send_sem, recv_sem):
        self.src, self.slot, self.me = src, slot, me
        self.send_sem, self.recv_sem = send_sem, recv_sem
        self.core = lax.rem(me, 2)
        self.other = 1 - self.core
        chip = me // 2
        self.near, self.side, self.far = square(chip)
        self.chip = chip
        self.half = src.shape[0] // 2

    def copy(self, src, dst, sem, to):
        return pltpu.make_async_remote_copy(
            src_ref=src,
            dst_ref=dst,
            send_sem=self.send_sem.at[sem],
            recv_sem=self.recv_sem.at[sem],
            device_id={"ctx": to},
            device_id_type=MESH,
        )

    def part(self, owner, which):
        return self.slot(owner).at[pl.ds(which * self.half, self.half)]

    def out(self, sem):
        chip = self.near if sem == 1 else self.side
        return self.copy(self.src, self.slot(self.me), sem, chip * 2 + self.core)

    def onward(self, sem):
        origin, to, which = (self.near, self.side, 0) if sem == 3 else (self.side, self.near, 1)
        owner = origin * 2 + self.core
        return self.copy(self.part(owner, which), self.part(owner, which), sem, to * 2 + self.core)

    def relay(self, k):
        owner = (self.chip, self.near, self.side, self.far)[k] * 2 + self.core
        src = self.slot(owner) if k else self.src
        return self.copy(src, self.slot(owner), 4 + k, self.chip * 2 + self.other)

    def start(self):
        self.out(1).start()
        self.out(2).start()
        self.relay(0).start()

    def pass_on(self):
        for k, chip in ((1, self.near), (2, self.side)):
            owner = chip * 2 + self.core
            self.copy(self.src, self.slot(owner), k, self.me).wait_recv()
            self.onward(3 if k == 1 else 0).start()
            self.relay(k).start()

    def late(self):
        owner = self.far * 2 + self.core
        for sem, which in ((3, 0), (0, 1)):
            self.copy(self.part(owner, which), self.part(owner, which), sem, self.me).wait_recv()
        self.relay(3).start()

    def finish(self):
        for k, chip in enumerate((self.chip, self.near, self.side, self.far)):
            owner = chip * 2 + self.other
            self.copy(self.slot(owner), self.slot(owner), 4 + k, self.me).wait_recv()

    def drain(self):
        for sem in (1, 2):
            self.out(sem).wait_send()
        for sem in (3, 0):
            self.onward(sem).wait_send()
        for k in range(4):
            self.relay(k).wait_send()


def square(chip):
    return chip + 1 - 2 * lax.rem(chip, 2), chip + 2 - 4 * (chip // 2), 3 - chip


def spread_over(n, src, *rest):
    return (Spread4 if n == 8 and src.shape[0] % 32 == 0 else Spread)(src, *rest)


def greet(n, planes, me, plane, across):
    barrier = pltpu.get_barrier_semaphore()
    chips = n // 2
    core = lax.rem(me, 2)
    others = [lax.rem(me // 2 + k, chips) * 2 + core for k in range(1, chips)] + [me + 1 - 2 * core]
    for other in others:
        pl.semaphore_signal(barrier, inc=1, device_id={"ctx": other}, device_id_type=MESH)
    if across:

        @pl.when(plane > 0)
        def _():
            pl.semaphore_signal(barrier, inc=1, device_id={"fsdp": plane - 1}, device_id_type=MESH)

        @pl.when(plane < planes - 1)
        def _():
            pl.semaphore_signal(barrier, inc=1, device_id={"fsdp": plane + 1}, device_id_type=MESH)

    count = len(others)
    if across:
        count = count + (plane > 0).astype(jnp.int32) + (plane < planes - 1).astype(jnp.int32)
    pl.semaphore_wait(barrier, count)


def forward_kernel(
    n,
    planes,
    heads,
    length_ref,
    tokens_ref,
    attn_shard,
    gate_ref,
    up_ref,
    down_ref,
    gain_shard,
    cos_ref,
    sin_ref,
    x_out,
    normed_out,
    q_out,
    k_out,
    v_out,
    lse_out,
    att_out,
    hid_out,
    normed2_out,
    a_out,
    b_out,
    mixed_out,
    attn_out,
    gate_out,
    up_out,
    down_out,
    gain_out,
    w_attn,
    w_gate,
    w_up,
    w_down,
    gains,
    x_all,
    qkv,
    q_rot,
    k_rot,
    v_rows,
    lse,
    own_att,
    att_all,
    own_hid,
    own_scaled,
    wide,
    narrow,
    z_send,
    z_recv,
    c_send,
    c_recv,
    keep_sem,
    load_sem,
    wide_sem,
    narrow_sem,
):
    me, plane = lax.axis_index("ctx"), lax.axis_index("fsdp")
    per_device, width = tokens_ref.shape
    total = x_all.shape[0]
    rows_shard = attn_shard.shape[0]
    own = own_att.shape[1]
    own_width = own_hid.shape[1]
    columns = qkv.shape[1]
    blocks = total // ROWS
    pairs = heads // 2

    local_copies = []

    def keep(src, dst, index):
        copy = pltpu.make_async_copy(src, dst, keep_sem.at[index])
        copy.start()
        local_copies.append(copy)

    def chain(index, ref, rows):
        return Chain(lambda s: ref.at[pl.ds(s * rows, rows)], planes, plane, z_send.at[index], z_recv.at[index])

    attn_chain = chain(0, w_attn, rows_shard)
    gate_chain = chain(1, w_gate, rows_shard)
    up_chain = chain(2, w_up, rows_shard)
    slab = w_down.shape[0] // planes
    down_chain = chain(3, w_down, slab)
    gain_chain = chain(4, gains, gain_shard.shape[0])
    own_ff = w_gate.shape[1]
    loads = [
        pltpu.make_async_copy(shard, c.slot(plane), keep_sem.at[i])
        for i, (c, shard) in enumerate(((attn_chain, attn_shard), (gain_chain, gain_shard)))
    ]
    for ref, c, at in ((gate_ref, gate_chain, 0), (up_ref, up_chain, 1)):
        for f in range(ref.shape[1] // (n * slab)):
            src = ref.at[:, pl.ds(pl.multiple_of((f * n + me) * slab, LANES), slab)]
            dst = c.slot(plane).at[:, pl.ds(f * slab, slab)]
            loads.append(pltpu.make_async_copy(src, dst, load_sem.at[at, f]))
        if ref.shape[1] == own_ff:
            loads.append(pltpu.make_async_copy(ref, c.slot(plane), load_sem.at[at, 0]))
    down_src = down_ref if down_ref.shape[0] == slab else down_ref.at[pl.ds(pl.multiple_of(me * slab, slab), slab)]
    loads.append(pltpu.make_async_copy(down_src, down_chain.slot(plane), load_sem.at[2, 0]))
    for load in loads:
        load.start()
    own_x = pltpu.make_async_copy(tokens_ref, x_all.at[pl.ds(me * per_device, per_device)], keep_sem.at[5])
    own_x.start()
    greet(n, planes, me, plane, True)
    loads[0].wait()
    attn_chain.start(0)
    loads[1].wait()
    gain_chain.start(0)
    x_spread = spread_over(
        n, tokens_ref, lambda c: x_all.at[pl.ds(c * per_device, per_device)], n, me, c_send.at[0], c_recv.at[0]
    )
    x_spread.start()
    for load in loads[2:]:
        load.wait()
    own_x.wait()
    for step in range(1, planes - 1):
        attn_chain.advance(step)
        gain_chain.advance(step)
    gate_chain.start(0)
    up_chain.start(0)
    x_spread.pass_on()
    x_spread.late()
    x_spread.finish()
    x_copy = pltpu.make_async_copy(x_all, x_out, keep_sem.at[0])
    x_copy.start()
    attn_chain.arrive(planes - 2)
    gain_chain.arrive(planes - 2)
    keep(w_attn, attn_out, 1)
    keep(gains, gain_out, 2)
    half = gain_shard.shape[1] // 2
    step_rows = gain_shard.shape[0]
    attn_gain = jnp.concatenate([gains[f * step_rows : f * step_rows + 1, :half] for f in range(planes)], axis=1)
    mlp_gain = jnp.concatenate([gains[f * step_rows : f * step_rows + 1, half:] for f in range(planes)], axis=1)

    def staged(stage, sem, slot, out, rows, wait_before):
        copy = pltpu.make_async_copy(stage.at[slot], out.at[rows], sem.at[slot])
        return copy.wait() if wait_before else copy.start()

    def project_block(i, _):
        rows = pl.ds(pl.multiple_of(i * ROWS, ROWS), ROWS)
        slot = lax.rem(i, 2)

        @pl.when(i >= 2)
        def _():
            staged(wide, wide_sem, slot, normed_out, rows, True)

        own_hid[rows, :] = x_all[rows, pl.ds(pl.multiple_of(me * own_width, LANES), own_width)]
        x = x_all[rows, :].astype(F32)
        r1 = lax.rsqrt(jnp.mean(x * x, axis=-1, keepdims=True) + EPSILON)
        normed = (x * r1 * attn_gain).astype(BF16)
        wide[slot] = normed
        staged(wide, wide_sem, slot, normed_out, rows, False)
        qkv[rows, :] = dot_nn(normed, w_attn[:, :columns])
        return 0

    lax.fori_loop(0, blocks, project_block, 0)
    for i in range(max(blocks - 2, 0), blocks):
        staged(wide, wide_sem, i % 2, normed_out, pl.ds(i * ROWS, ROWS), True)

    split = columns - LANES
    cos, sin = cos_ref[...], sin_ref[...]
    kv = qkv[:, split:]
    turned = pltpu.roll(kv, HEAD_SIZE, 1)
    low = low_half(kv.shape)
    k = jnp.where(low, kv, turned)
    k_rot[...] = (k * cos + swap_halves(k) * sin).astype(BF16)
    v_rows[...] = jnp.where(low, turned, kv).astype(BF16)
    keep(k_rot, k_out, 3)
    keep(v_rows, v_out, 4)
    first_len = length_ref[0]

    def attend_pair(pair, _):
        lanes = pl.ds(pl.multiple_of(pair * LANES, LANES), LANES)
        q = qkv[:, lanes]
        q_rot[:, lanes] = ((q * cos_ref[...] + swap_halves(q) * sin_ref[...]) * SCORE_SCALE).astype(BF16)
        for block in range(blocks):
            rows = pl.ds(block * ROWS, ROWS)
            end = (block + 1) * ROWS
            bias = mask_bias(first_len, block * ROWS, ROWS, end)
            query = q_rot[rows, lanes]
            lower = low_half(query.shape)
            keys, values = k_rot[:end, :], v_rows[:end, :]
            parts = []
            for side in range(2):
                chosen = lower if side == 0 else jnp.logical_not(lower)
                scores = dot_nt(jnp.where(chosen, query, jnp.zeros_like(query)), keys) + bias
                top = jnp.max(scores, axis=-1, keepdims=True)
                weights = jnp.exp(scores - top)
                whole = jnp.sum(weights, axis=-1, keepdims=True)
                probs = (weights * (1.0 / whole)).astype(BF16)
                parts.append(dot_nn(probs, values))
                lse[pair, rows, side : side + 1] = top + jnp.log(whole)
            own_att[rows, lanes] = jnp.where(low_half(parts[0].shape), parts[0], parts[1]).astype(BF16)
        return 0

    lax.fori_loop(0, pairs, attend_pair, 0)
    att_spread = spread_over(n, own_att, lambda c: att_all.at[c], n, me, c_send.at[1], c_recv.at[1])
    x_copy.wait()
    x_spread.drain()
    att_spread.start()
    own_a = pltpu.make_async_copy(own_att, att_all.at[me], keep_sem.at[5])
    own_a.start()
    keep(q_rot, q_out, 6)
    keep(lse, lse_out, 7)
    if planes > 2:
        gate_chain.advance(1)
        up_chain.advance(1)
    att_spread.pass_on()
    att_spread.late()
    own_a.wait()
    att_spread.finish()
    keep(att_all, att_out, 8)

    def out_block(i, _):
        rows = pl.ds(pl.multiple_of(i * ROWS, ROWS), ROWS)
        acc = jnp.zeros((ROWS, own_width), F32)
        for c in range(n):
            acc += dot_nn(att_all[c, rows, :], w_attn[c * own : (c + 1) * own, columns:])
        hidden = own_hid[rows, :].astype(F32) + RESIDUAL_SCALE * acc
        own_hid[rows, :] = hidden.astype(BF16)
        own_scaled[rows, :] = (hidden * (1.0 / RESIDUAL_SCALE)).astype(BF16)
        return 0

    lax.fori_loop(0, blocks, out_block, 0)
    def hid_slot(c):
        return x_all.at[:, pl.ds(pl.multiple_of(c * own_width, LANES), own_width)]

    hid_spread = spread_over(n, own_hid, hid_slot, n, me, c_send.at[2], c_recv.at[2])
    hid_spread.start()
    keep(own_scaled, mixed_out.at[:, pl.ds(own_ff, own_width)], 13)
    own_h = pltpu.make_async_copy(own_hid, hid_slot(me), keep_sem.at[5])
    own_h.start()
    for step in range(2, planes - 1):
        gate_chain.advance(step)
        up_chain.advance(step)
    down_chain.start(0)
    hid_spread.pass_on()
    hid_spread.late()
    own_h.wait()
    hid_spread.finish()
    keep(x_all, hid_out, 9)
    gate_chain.arrive(planes - 2)
    up_chain.arrive(planes - 2)
    keep(w_gate, gate_out, 10)
    keep(w_up, up_out, 11)
    if planes > 2:
        down_chain.advance(1)

    def mlp_copies(i, rows, wait):
        slot = lax.rem(i, 2)
        staged(wide, wide_sem, slot, normed2_out, rows, wait)
        for j, out in enumerate((a_out, b_out, mixed_out.at[:, pl.ds(0, own_ff)])):
            staged(narrow.at[j], narrow_sem.at[j], slot, out, rows, wait)

    def mlp_block(i, _):
        rows = pl.ds(pl.multiple_of(i * ROWS, ROWS), ROWS)
        slot = lax.rem(i, 2)

        @pl.when(i >= 2)
        def _():
            mlp_copies(i, rows, True)

        hidden = x_all[rows, :].astype(F32)
        r2 = lax.rsqrt(jnp.mean(hidden * hidden, axis=-1, keepdims=True) + EPSILON)
        normed = (hidden * r2 * mlp_gain).astype(BF16)
        wide[slot] = normed
        gate = dot_nn(normed, w_gate[...])
        up = dot_nn(normed, w_up[...])
        sig = jax.nn.sigmoid(gate)
        silu = gate * sig
        narrow[2, slot] = (silu * up).astype(BF16)
        narrow[1, slot] = silu.astype(BF16)
        narrow[0, slot] = (up * sig * (1.0 + gate * (1.0 - sig))).astype(BF16)
        mlp_copies(i, rows, False)
        return 0

    lax.fori_loop(0, blocks, mlp_block, 0)
    for step in range(2, planes - 1):
        down_chain.advance(step)
    for i in range(max(blocks - 2, 0), blocks):
        mlp_copies(i, pl.ds(i * ROWS, ROWS), True)
    down_chain.arrive(planes - 2)
    keep(w_down, down_out, 12)
    for c in (attn_chain, gain_chain, gate_chain, up_chain, down_chain):
        c.drain()
    for s in (att_spread, hid_spread):
        s.drain()
    for copy in local_copies:
        copy.wait()


def forward(n, planes, heads, slab, lengths, tokens, attn_shard, gate, up, down, gain_shard, cos, sin):
    per_device, width = tokens.shape
    total = per_device * n
    own = heads * HEAD_SIZE
    columns = own + 2 * HEAD_SIZE
    own_width = attn_shard.shape[1] - columns
    own_ff = planes * slab
    rows_shard = attn_shard.shape[0]
    pairs = heads // 2
    weights = [
        ((planes * rows_shard, attn_shard.shape[1]), BF16),
        ((planes * rows_shard, own_ff), BF16),
        ((planes * rows_shard, own_ff), BF16),
        ((own_ff, width), BF16),
        ((planes * gain_shard.shape[0], gain_shard.shape[1]), F32),
    ]
    outs = [
        ((total, width), BF16),
        ((total, width), BF16),
        ((total, own), BF16),
        ((total, LANES), BF16),
        ((total, LANES), BF16),
        ((pairs, total, LANES), F32),
        ((n, total, own), BF16),
        ((total, width), BF16),
        ((total, width), BF16),
        ((total, own_ff), BF16),
        ((total, own_ff), BF16),
        ((total, own_ff + own_width), BF16),
    ] + weights
    scratch = weights + [
        ((total, width), BF16),
        ((total, columns), F32),
        ((total, own), BF16),
        ((total, LANES), BF16),
        ((total, LANES), BF16),
        ((pairs, total, LANES), F32),
        ((total, own), BF16),
        ((n, total, own), BF16),
        ((total, own_width), BF16),
        ((total, own_width), BF16),
        ((2, ROWS, width), BF16),
        ((3, 2, ROWS, own_ff), BF16),
    ]
    steps = max(planes - 1, 1)
    dma = pltpu.SemaphoreType.DMA
    anywhere = pl.BlockSpec(memory_space=pl.ANY)
    vmem = pl.BlockSpec(memory_space=pltpu.VMEM)
    return pl.pallas_call(
        functools.partial(forward_kernel, n, planes, heads),
        in_specs=[pl.BlockSpec(memory_space=pltpu.SMEM), vmem] + [anywhere] * 5 + [vmem] * 2,
        out_specs=[anywhere] * len(outs),
        out_shape=[jax.ShapeDtypeStruct(*o) for o in outs],
        scratch_shapes=[pltpu.VMEM(*s) for s in scratch]
        + [dma((5, 2, steps)), dma((5, 2, steps)), dma((3, n)), dma((3, n)), dma((16,)), dma((3, planes)), dma((2,)), dma((3, 2))],
        compiler_params=pltpu.CompilerParams(
            vmem_limit_bytes=VMEM_LIMIT, collective_id=1, has_side_effects=True
        ),
        cost_estimate=pl.CostEstimate(
            flops=2 * total * width * (columns + own_width + 2 * own_ff),
            bytes_accessed=60 * 1024 * 1024,
            transcendentals=0,
        ),
        name="forward",
    )(lengths, tokens, attn_shard, gate, up, down, gain_shard, cos, sin)


def add_into(dst, src):
    rows_in, columns = dst.shape
    chunk = max(c for c in (256, 128, 64, 32) if c == 32 or (rows_in % c == 0 and c * columns <= 65536))

    def step(i, _):
        rows = pl.ds(pl.multiple_of(i * chunk, chunk), chunk)
        dst[rows, :] = (dst[rows, :].astype(F32) + src[rows, :].astype(F32)).astype(dst.dtype)
        return 0

    if rows_in < chunk:
        dst[...] = dst[...] + src[...]
    else:
        lax.fori_loop(0, rows_in // chunk, step, 0)


def fetch(src, dst, sem):
    copy = pltpu.make_async_copy(src, dst, sem)
    copy.start()
    copy.wait()


class Settle:
    def __init__(self, block, landed, stage, planes, plane, send_sem, recv_sem, load_sem):
        self.block, self.landed, self.stage = block, landed, stage
        self.planes, self.plane = planes, plane
        self.send_sem, self.recv_sem, self.load_sem = send_sem, recv_sem, load_sem

    def slot(self, way, shard, at):
        return shard if way == 0 else jnp.where(shard == at, self.planes, shard)

    def sends(self, step):
        p, last = self.plane, self.planes - 1
        return (
            (0, (p <= step) & (p < last), last - step + p, p + 1),
            (1, (last - p <= step) & (p > 0), step - last + p, p - 1),
        )

    def receives(self, step):
        p, last = self.plane, self.planes - 1
        return (
            (0, (p >= 1) & (p - 1 <= step), last - step + p - 1),
            (1, (p <= last - 1) & (last - p - 1 <= step), step - last + p + 1),
        )

    def copy(self, way, step, shard, to):
        return pltpu.make_async_remote_copy(
            src_ref=self.block(shard),
            dst_ref=self.landed.at[self.slot(way, shard, to)],
            send_sem=self.send_sem.at[way, step],
            recv_sem=self.recv_sem.at[way, step],
            device_id={"fsdp": to},
            device_id_type=MESH,
        )

    def start(self, step=0):
        for way, active, shard, to in self.sends(step):

            @pl.when(active)
            def _(way=way, shard=shard, to=to):
                self.copy(way, step, shard, to).start()

    def take(self, step):
        for way, active, shard in self.receives(step):

            @pl.when(active)
            def _(way=way, shard=shard):
                self.copy(way, step, shard, self.plane).wait_recv()
                fetch(self.landed.at[self.slot(way, shard, self.plane)], self.stage, self.load_sem)
                add_into(self.block(shard), self.stage)

    def advance(self, step):
        self.take(step - 1)
        self.start(step)

    def drain(self):
        for step in range(self.planes - 1):
            for way, active, shard, to in self.sends(step):

                @pl.when(active)
                def _(way=way, shard=shard, to=to, step=step):
                    self.copy(way, step, shard, to).wait_send()


class Scatter:
    def __init__(self, block, near, far, stage, me, send_sem, recv_sem, load_sem):
        self.block, self.landed, self.far, self.stage = block, near, far, stage
        self.send_sem, self.recv_sem, self.load_sem = send_sem, recv_sem, load_sem
        self.core = lax.rem(me, 2)
        self.chip = me // 2
        self.chips = (self.chip, *square(self.chip))
        self.half = stage[0].shape[0] // 2

    def rows(self, which):
        return pl.ds(which * self.half, self.half)

    def own(self, k):
        return self.block(self.chips[k] * 2 + self.core)

    def copy(self, src, dst, sem, chip, core):
        return pltpu.make_async_remote_copy(
            src_ref=src,
            dst_ref=dst,
            send_sem=self.send_sem.at[sem],
            recv_sem=self.recv_sem.at[sem],
            device_id={"ctx": chip * 2 + core},
            device_id_type=MESH,
        )

    def first(self, k):
        other = 1 - self.core
        return self.copy(self.block(self.chips[k] * 2 + other), self.landed.at[k], k, self.chip, other)

    def second(self, k, to, which):
        place = self.far.at[to - 1 if k == to else 2, self.rows(which)]
        sem = 4 + 2 * (to - 1) + which if k == to else 7 + to
        return self.copy(self.own(k).at[self.rows(which)], place, sem, self.chips[to], self.core)

    def start(self):
        for k in (3, 1, 2, 0):
            self.first(k).start()

    def add_all(self, items):
        pending = None

        def complete(copy, dst, stage, then):
            copy.wait()
            add_into(dst, stage)
            for remote in then:
                remote.start()

        for index, (arrivals, src, dst, then) in enumerate(items):
            for remote in arrivals:
                remote.wait_recv()
            stage = self.stage[index % 2].at[pl.ds(0, dst.shape[0])]
            copy = pltpu.make_async_copy(src, stage, self.load_sem.at[index % 2])
            copy.start()
            if pending is not None:
                complete(*pending)
            pending = (copy, dst, stage, then)
        complete(*pending)

    def pass_on(self):
        self.add_all(
            [
                ([self.first(3)], self.landed.at[3], self.own(3), [self.second(3, 1, 0), self.second(3, 2, 1)]),
                ([self.first(1)], self.landed.at[1], self.own(1), [self.second(1, 1, 0)]),
                ([self.first(2)], self.landed.at[2], self.own(2), [self.second(2, 2, 1)]),
            ]
        )

    def late(self):
        self.add_all(
            [
                (
                    [self.second(3, to, which)],
                    self.far.at[2, self.rows(which)],
                    self.own(k).at[self.rows(which)],
                    [self.second(k, k, which)],
                )
                for to, which, k in ((1, 0, 2), (2, 1, 1))
            ]
        )

    def finish(self, total):
        items = [([self.first(0)], self.landed.at[0], total, [])]
        for k in (1, 2):
            items.append(([self.second(k, k, which) for which in (0, 1)], self.far.at[k - 1], total, []))
        self.add_all(items)

    def drain(self):
        for k in range(4):
            self.first(k).wait_send()
        for k, to, which in ((3, 1, 0), (3, 2, 1), (1, 1, 0), (1, 1, 1), (2, 2, 0), (2, 2, 1)):
            self.second(k, to, which).wait_send()


def backward_kernel(
    n,
    planes,
    heads,
    length_ref,
    grad_in,
    mixed_in,
    a_in,
    b_in,
    hidden_in,
    normed2_in,
    normed_in,
    x_in,
    att_in,
    q_in,
    k_in,
    v_in,
    lse_in,
    cos_in,
    sin_in,
    attn_in,
    gate_in,
    up_in,
    down_in,
    gain_in,
    token_out,
    gain_out,
    down_all,
    gate_all,
    up_all,
    out_all,
    qkv_all,
    near1,
    far1,
    near2,
    far2,
    near3,
    far3,
    down_landed,
    gate_landed,
    up_landed,
    out_landed,
    qkv_landed,
    w_attn,
    w_gate,
    w_up,
    w_down,
    p_down,
    gains,
    grad,
    a_v,
    b_v,
    part,
    hid_stage,
    stage_tall,
    stage_wide,
    stage_col,
    hidden_grad,
    lse,
    cos,
    sin,
    dk_sum,
    dv_sum,
    gain_own,
    gain_all,
    gain_landed,
    gain_stage,
    z_send,
    z_recv,
    s_send,
    s_recv,
    g_send,
    g_recv,
    load_sem,
    hid_sem,
    add_sem,
    ring_sem,
):
    me, plane = lax.axis_index("ctx"), lax.axis_index("fsdp")
    total, width = grad.shape
    per_device = total // n
    own = heads * HEAD_SIZE
    own_width = width // n
    own_ff = a_v.shape[1]
    rows_shard = width // planes
    slab = own_ff // planes
    blocks = total // ROWS
    pairs = heads // 2
    columns = own + LANES
    last = planes - 2

    def load(src, dst, index):
        copy = pltpu.make_async_copy(src, dst, load_sem.at[index])
        copy.start()
        return copy

    mixed_loads = [load(mixed_in.at[:, pl.ds(d * own_width, own_width)], part.at[d], d) for d in range(own_ff // own_width)]
    grad_load = load(grad_in, grad, 8)
    down_load = load(down_in, w_down, 9)
    gate_load = load(gate_in, w_gate, 10)
    up_load = load(up_in, w_up, 11)
    a_load = load(a_in, a_v, 12)
    b_load = load(b_in, b_v, 13)
    attn_load = load(attn_in, w_attn, 14)
    gain_load = load(gain_in, gains, 15)
    greet(n, planes, me, plane, True)

    def settle(index, block, landed, stage):
        return Settle(block, landed, stage, planes, plane, z_send.at[index], z_recv.at[index], add_sem)

    def rows_of(ref, rows):
        return lambda d: ref.at[pl.ds(pl.multiple_of(d * rows, rows), rows)]

    def out_block_of(d):
        return w_down.at[pl.ds(0, rows_shard), pl.ds(pl.multiple_of(d * own_width, LANES), own_width)]

    def qkv_block_of(d):
        return w_down.at[pl.ds(rows_shard, rows_shard), pl.ds(pl.multiple_of(d * columns, LANES), columns)]

    def gain_block_of(d):
        return gain_own.at[:, pl.ds(pl.multiple_of(d * rows_shard, LANES), rows_shard)]

    down_sum = settle(0, rows_of(p_down, slab), down_landed, stage_wide)
    gate_sum = settle(1, rows_of(w_gate, rows_shard), gate_landed, stage_tall)
    up_sum = settle(2, rows_of(w_up, rows_shard), up_landed, stage_tall)
    out_sum = settle(3, out_block_of, out_landed, stage_tall.at[:, pl.ds(0, own_width)])
    qkv_sum = settle(4, qkv_block_of, qkv_landed, stage_tall.at[:, pl.ds(0, columns)])
    gain_sum = settle(5, gain_block_of, gain_landed, gain_stage)

    def spread(index, src, dst):
        return spread_over(n, src, lambda c: dst.at[c], n, me, g_send.at[index], g_recv.at[index])

    spreads = []

    def give(index, sums, dst):
        src = sums.block(plane)
        mine = load(src, dst.at[me], 16 + index)
        out = spread(index, src, dst)
        out.start()
        spreads.append((out, mine))
        return out

    def scatter(index, block, near, far, stage):
        return Scatter(block, near, far, stage, me, s_send.at[index], s_recv.at[index], ring_sem)

    part_rows = total // 2
    col_stages = [stage_col.at[pl.ds(i * part_rows, part_rows)] for i in range(2)]

    def half_scatter(index, near, far, side):
        rows = pl.ds(side * part_rows, part_rows)
        return scatter(
            2 * index + side, lambda c: part.at[c, rows], near.at[:, rows], far.at[:, rows], col_stages
        )

    first = [half_scatter(0, near1, far1, side) for side in range(2)]
    second = [half_scatter(1, near2, far2, side) for side in range(2)]

    grad_load.wait()

    for copy in mixed_loads:
        copy.wait()

    def down_block(i, _):
        d = jnp.where(i == 0, planes - 1, jnp.where(i == 1, 0, planes - i))
        rows = pl.ds(pl.multiple_of(d * own_width, own_width), own_width)
        p_down[rows, :] = (RESIDUAL_SCALE * dot_tn(part[d], grad[...])).astype(BF16)

        @pl.when(i == 1)
        def _():
            down_sum.start()

        return 0

    lax.fori_loop(0, planes, down_block, 0)

    for copy in (down_load, gate_load, up_load, a_load, b_load, attn_load, gain_load):
        copy.wait()
    half = gains.shape[1] // 2
    attn_gain = jnp.concatenate([gains[f * 8 : f * 8 + 1, :half] for f in range(planes)], axis=1)
    mlp_gain = jnp.concatenate([gains[f * 8 : f * 8 + 1, half:] for f in range(planes)], axis=1)
    gain_own[...] = jnp.zeros_like(gain_own)

    def stream(src, i, wait):
        rows = pl.ds(pl.multiple_of(i * ROWS, ROWS), ROWS)
        slot = lax.rem(i, 2)
        copy = pltpu.make_async_copy(src.at[rows], hid_stage.at[slot], hid_sem.at[slot])
        return copy.wait() if wait else copy.start()

    stream(hidden_in, jnp.int32(0), False)

    def mlp_block(i, _):
        rows = pl.ds(pl.multiple_of(i * ROWS, ROWS), ROWS)

        @pl.when(i + 1 < blocks)
        def _():
            stream(hidden_in, i + 1, False)

        mixed_grad = RESIDUAL_SCALE * dot_nt(grad[rows, :], w_down[...])
        ggrad = (mixed_grad * a_v[rows, :].astype(F32)).astype(BF16)
        ugrad = (mixed_grad * b_v[rows, :].astype(F32)).astype(BF16)
        a_v[rows, :] = ggrad
        b_v[rows, :] = ugrad
        normed_grad = dot_nt(ggrad, w_gate[...]) + dot_nt(ugrad, w_up[...])
        stream(hidden_in, i, True)

        hidden = hid_stage[lax.rem(i, 2)].astype(F32)
        r2 = lax.rsqrt(jnp.mean(hidden * hidden, axis=-1, keepdims=True) + EPSILON)
        gain_own[0:1, :] += jnp.sum(normed_grad * (hidden * r2), axis=0, keepdims=True)
        weighted = normed_grad * mlp_gain
        mean = jnp.mean(weighted * hidden, axis=-1, keepdims=True)
        piece = r2 * weighted - hidden * (r2 * r2 * r2 * mean)
        for c in range(n):
            part[c, rows, :] = piece[:, c * own_width : (c + 1) * own_width].astype(BF16)

        @pl.when(i == blocks // 2 - 1)
        def _():
            first[0].start()

        @pl.when(i == blocks - 2)
        def _():
            down_sum.advance(1)
            first[0].pass_on()

        return 0

    lax.fori_loop(0, blocks, mlp_block, 0)
    first[1].start()
    normed2_load = load(normed2_in, grad, 8)
    normed2_load.wait()

    def columns_times(right, out, low, high):
        def block(j, _):
            lanes = pl.ds(pl.multiple_of(j * ROWS, ROWS), ROWS)
            out[lanes, :] = dot_tn(grad[:, lanes], right[...]).astype(BF16)
            return 0

        lax.fori_loop(low, high, block, 0)

    first[0].late()
    columns_times(a_v, w_gate, 0, width // ROWS)
    gate_sum.start()
    first[1].pass_on()
    columns_times(b_v, w_up, 0, width // ROWS // 2)
    first[1].late()
    columns_times(b_v, w_up, width // ROWS // 2, width // ROWS)
    down_sum.advance(2)

    att_loads = [load(att_in.at[c], grad.at[:, pl.ds(c * own, own)], c) for c in range(n)]
    own_grad = load(grad_in.at[:, pl.ds(pl.multiple_of(me * own_width, LANES), own_width)], b_v.at[:, pl.ds(LANES, own_width)], 8)
    q_load = load(q_in, a_v.at[:, pl.ds(0, own)], 9)
    k_load = load(k_in, a_v.at[:, pl.ds(own, LANES)], 10)
    v_load = load(v_in, a_v.at[:, pl.ds(own + LANES, LANES)], 11)
    lse_load = load(lse_in, lse, 12)
    cos_load = load(cos_in, cos, 13)
    sin_load = load(sin_in, sin, 14)
    own_grad.wait()

    def begin(i, _):
        rows = pl.ds(pl.multiple_of(i * ROWS, ROWS), ROWS)
        hidden_grad[rows, :] = b_v[rows, LANES : LANES + own_width].astype(F32) + part[me, rows, :].astype(F32)
        return 0

    lax.fori_loop(0, blocks, begin, 0)
    for side in range(2):
        first[side].finish(hidden_grad.at[pl.ds(side * part_rows, part_rows)])
        first[side].drain()

    def branch_block(i, _):
        rows = pl.ds(pl.multiple_of(i * ROWS, ROWS), ROWS)
        branch = (RESIDUAL_SCALE * hidden_grad[rows, :]).astype(BF16)
        b_v[rows, LANES : LANES + own_width] = branch
        for c in range(n):
            part[c, rows, :] = dot_nt(branch, w_attn[c * own : (c + 1) * own, columns:]).astype(BF16)

        @pl.when(i == blocks // 2 - 1)
        def _():
            second[0].start()

        return 0

    lax.fori_loop(0, blocks, branch_block, 0)
    second[1].start()
    second[0].pass_on()
    gate_sum.advance(1)
    for copy in att_loads:
        copy.wait()
    heads_per_shard = rows_shard // own
    for c in range(n):
        place = out_block_of(c // heads_per_shard).at[pl.ds((c % heads_per_shard) * own, own)]
        place[...] = dot_tn(grad[:, c * own : (c + 1) * own], b_v[:, LANES : LANES + own_width]).astype(BF16)
    second[1].pass_on()
    second[0].late()
    normed_load = load(normed_in, grad, 15)
    down_sum.take(last)
    up_sum.start()
    second[1].late()
    second[0].finish(part.at[me, pl.ds(0, part_rows)])
    down_give = give(0, down_sum, down_all)
    gate_sum.advance(2)

    for copy in (q_load, k_load, v_load, lse_load, cos_load, sin_load):
        copy.wait()
    dk_sum[...] = jnp.zeros_like(dk_sum)
    dv_sum[...] = jnp.zeros_like(dv_sum)
    first_len = length_ref[0]
    dq_at = own + 2 * LANES

    def attend_pair(side, pair, _):
        lanes = pl.ds(pl.multiple_of(pair * LANES, LANES), LANES)
        dq_lanes = pl.ds(pl.multiple_of(dq_at + pair * LANES, LANES), LANES)
        for block in range(side * (blocks // 2), (side + 1) * (blocks // 2)):
            rows = pl.ds(block * ROWS, ROWS)
            end = (block + 1) * ROWS
            bias = mask_bias(first_len, block * ROWS, ROWS, end)
            query, grads = a_v[rows, lanes], part[me, rows, lanes]
            low = low_half(query.shape)
            keys, values = a_v[:end, own : own + LANES], a_v[:end, own + LANES : own + 2 * LANES]
            parts = []
            for head in range(2):
                chosen = low if head == 0 else jnp.logical_not(low)
                own_query = jnp.where(chosen, query, jnp.zeros_like(query))
                own_grads = jnp.where(chosen, grads, jnp.zeros_like(grads))
                scores = dot_nt(own_query, keys) + bias
                probs = jnp.exp(scores - lse[pair, rows, head : head + 1])
                prob_grad = dot_nt(own_grads, values)
                delta = jnp.sum(probs * prob_grad, axis=-1, keepdims=True)
                score_grad = (probs * (prob_grad - delta)).astype(BF16)
                parts.append(dot_nn(score_grad, keys))
                dk_sum[:end, :] += dot_tn(score_grad, own_query)
                dv_sum[:end, :] += dot_tn(probs.astype(BF16), own_grads)
            dq = jnp.where(low_half(parts[0].shape), parts[0], parts[1]) * SCORE_SCALE
            a_v[rows, dq_lanes] = (dq * cos[rows, :] - swap_halves(dq) * sin[rows, :]).astype(BF16)

        if side:

            @pl.when(pair == 0)
            def _():
                down_give.pass_on()
                up_sum.advance(1)

        return 0

    lax.fori_loop(0, pairs, functools.partial(attend_pair, 0), 0)
    second[1].finish(part.at[me, pl.ds(part_rows, part_rows)])
    lax.fori_loop(0, pairs, functools.partial(attend_pair, 1), 0)
    dk = dk_sum[...]
    dk = dk + pltpu.roll(dk, HEAD_SIZE, 1)
    dk = dk * cos[...] - swap_halves(dk) * sin[...]
    dv = dv_sum[...]
    dv = dv + pltpu.roll(dv, HEAD_SIZE, 1)
    b_v[:, :LANES] = jnp.where(low_half(dk.shape), dk, dv).astype(BF16)
    down_give.late()
    gate_sum.take(last)
    gate_give = give(1, gate_sum, gate_all)
    up_sum.advance(2)
    out_sum.start()

    normed_load.wait()
    dq_end = dq_at + own
    for d in range(planes):
        for j in range(rows_shard // ROWS):
            lanes = slice(d * rows_shard + j * ROWS, d * rows_shard + (j + 1) * ROWS)
            place = qkv_block_of(d).at[pl.ds(j * ROWS, ROWS)]
            place[:, :own] = dot_tn(grad[:, lanes], a_v[:, dq_at:dq_end]).astype(BF16)
            place[:, own:] = dot_tn(grad[:, lanes], b_v[:, :LANES]).astype(BF16)
    gate_give.pass_on()
    out_sum.advance(1)
    qkv_sum.start()

    stream(x_in, jnp.int32(0), False)

    def token_block(i, _):
        rows = pl.ds(pl.multiple_of(i * ROWS, ROWS), ROWS)

        @pl.when(i + 1 < blocks)
        def _():
            stream(x_in, i + 1, False)

        normed_grad = dot_nt(a_v[rows, dq_at:dq_end], w_attn[:, :own]) + dot_nt(b_v[rows, :LANES], w_attn[:, own:columns])
        stream(x_in, i, True)
        x = hid_stage[lax.rem(i, 2)].astype(F32)
        r1 = lax.rsqrt(jnp.mean(x * x, axis=-1, keepdims=True) + EPSILON)
        gain_own[1:2, :] += jnp.sum(normed_grad * (x * r1), axis=0, keepdims=True)
        weighted = normed_grad * attn_gain
        mean = jnp.mean(weighted * x, axis=-1, keepdims=True)
        piece = r1 * weighted - x * (r1 * r1 * r1 * mean)
        for c in range(n):
            lanes = slice(c * own_width, (c + 1) * own_width)
            mine = jnp.where(me == c, hidden_grad[rows, :], 0.0)
            grad[rows, lanes] = (piece[:, lanes] + mine).astype(BF16)
        return 0

    lax.fori_loop(0, blocks, token_block, 0)

    def token_rows(c):
        return grad.at[pl.ds(pl.multiple_of(c * per_device, per_device), per_device)]

    third = scatter(4, token_rows, near3, far3, [hid_stage.at[i, pl.ds(0, per_device)] for i in range(2)])
    third.start()
    gain_give = spread(5, gain_own, gain_all)
    gain_mine = load(gain_own, gain_all.at[me], 21)
    gain_give.start()
    gate_give.late()
    third.pass_on()
    gain_give.pass_on()
    out_sum.advance(2)
    third.late()
    gain_give.finish()
    gain_mine.wait()
    gain_give.drain()
    gain_own[...] = sum(gain_all[c] for c in range(n))
    gain_sum.start()
    token_out[...] = token_rows(me)[...].astype(F32)
    qkv_sum.advance(1)
    third.finish(token_out)
    up_sum.take(last)
    up_give = give(2, up_sum, up_all)
    gain_sum.advance(1)
    out_sum.take(last)
    out_give = give(3, out_sum, out_all)
    qkv_sum.advance(2)
    gain_sum.advance(2)
    up_give.pass_on()
    out_give.pass_on()
    up_give.late()
    gain_sum.take(last)
    gain_out[...] = gain_block_of(plane)[...]
    qkv_sum.take(last)
    qkv_give = give(4, qkv_sum, qkv_all)
    out_give.late()
    qkv_give.pass_on()
    qkv_give.late()
    for out, mine in spreads:
        out.finish()
        out.drain()
        mine.wait()
    for s in (*second, third):
        s.drain()
    for s in (down_sum, gate_sum, up_sum, out_sum, qkv_sum, gain_sum):
        s.drain()


def backward(n, planes, heads, lengths, grad, saved, weights, cos, sin):
    x, normed, q_rot, k_rot, v_rows, lse, att_all, hidden, normed2, a, b, mixed = saved
    w_attn, w_gate, w_up, w_down, gains = weights
    total, width = grad.shape
    own = heads * HEAD_SIZE
    own_width = width // n
    own_ff = a.shape[1]
    rows_shard = width // planes
    slab = own_ff // planes
    columns = own + LANES
    chips = n // 2
    per_device = total // n
    col, row = (chips, total, own_width), (chips, per_device, width)
    outs = [
        ((per_device, width), F32),
        ((8, rows_shard), F32),
        ((n, slab, width), BF16),
        ((n, rows_shard, own_ff), BF16),
        ((n, rows_shard, own_ff), BF16),
        ((n, rows_shard, own_width), BF16),
        ((n, rows_shard, columns), BF16),
        (col, BF16),
        (col, BF16),
        (col, BF16),
        (col, BF16),
        (row, BF16),
        (row, BF16),
        ((planes + 1, slab, width), BF16),
        ((planes + 1, rows_shard, own_ff), BF16),
        ((planes + 1, rows_shard, own_ff), BF16),
        ((planes + 1, rows_shard, own_width), BF16),
        ((planes + 1, rows_shard, columns), BF16),
    ]
    scratch = [
        (w_attn.shape, BF16),
        (w_gate.shape, BF16),
        (w_up.shape, BF16),
        (w_down.shape, BF16),
        (w_down.shape, BF16),
        (gains.shape, F32),
        ((total, width), BF16),
        ((total, own_ff), BF16),
        ((total, own_ff), BF16),
        ((n, total, own_width), BF16),
        ((2, ROWS, width), BF16),
        ((rows_shard, own_ff), BF16),
        ((slab, width), BF16),
        ((total, own_width), BF16),
        ((total, own_width), F32),
        (lse.shape, F32),
        (cos.shape, F32),
        (sin.shape, F32),
        ((total, LANES), F32),
        ((total, LANES), F32),
        ((8, width), F32),
        ((n, 8, width), F32),
        ((planes + 1, 8, rows_shard), F32),
        ((8, rows_shard), F32),
    ]
    steps = planes - 1
    dma = pltpu.SemaphoreType.DMA
    anywhere = pl.BlockSpec(memory_space=pl.ANY)
    vmem = pl.BlockSpec(memory_space=pltpu.VMEM)
    return pl.pallas_call(
        functools.partial(backward_kernel, n, planes, heads),
        in_specs=[pl.BlockSpec(memory_space=pltpu.SMEM)] + [anywhere] * 20,
        out_specs=[vmem] * 2 + [anywhere] * (len(outs) - 2),
        out_shape=[jax.ShapeDtypeStruct(*o) for o in outs],
        scratch_shapes=[pltpu.VMEM(*s) for s in scratch]
        + [
            dma((6, 2, steps)),
            dma((6, 2, steps)),
            dma((5, 10)),
            dma((5, 10)),
            dma((6, n)),
            dma((6, n)),
            dma((24,)),
            dma((2,)),
            dma,
            dma((2,)),
        ],
        compiler_params=pltpu.CompilerParams(
            vmem_limit_bytes=60 * 1024 * 1024, collective_id=2, has_side_effects=True
        ),
        cost_estimate=pl.CostEstimate(
            flops=16 * total * width * own_ff, bytes_accessed=100 * 1024 * 1024, transcendentals=0
        ),
        name="backward",
    )(
        lengths,
        grad,
        mixed,
        a,
        b,
        hidden,
        normed2,
        normed,
        x,
        att_all,
        q_rot,
        k_rot,
        v_rows,
        lse,
        cos,
        sin,
        w_attn,
        w_gate,
        w_up,
        w_down,
        gains,
    )[:7]


def kernel_fits(n, planes, total, width, own_ff):
    held = 4 * width * own_ff + 2 * total * width + 2 * total * own_ff
    return planes == 4 and total % (2 * ROWS) == 0 and n == 8 and own_ff // planes >= total // n and n * own_ff == planes * width and 2 * held < 44 * 1024 * 1024 and (own_ff // planes) % LANES == 0


def own_columns(array, index, width):
    return lax.dynamic_slice_in_dim(array, index * width, width, axis=1)


def after(value, *others):
    return lax.optimization_barrier((value, *others))[0]


def local(
    tokens,
    lengths,
    deal,
    attn_gain,
    query_weight,
    key_matrix,
    value_matrix,
    out_weight,
    mlp_gain,
    gate_weight,
    up_weight,
    down_weight,
    cotangent,
):
    n_ctx = lax.axis_size("ctx")
    n_fsdp = lax.axis_size("fsdp")
    me = lax.axis_index("ctx")
    me_array = me.astype(jnp.int32).reshape(1)
    per_device, width = tokens.shape[1], tokens.shape[2]
    total = per_device * n_ctx
    block_rows = per_device // n_ctx
    heads = QUERY_HEADS // n_ctx
    sharing = n_ctx // KEY_VALUE_HEADS
    own_width = width // n_ctx
    ff = gate_weight.shape[1]
    slab = ff // (n_fsdp * n_ctx)
    own_ff = slab * n_fsdp
    rows_shard = query_weight.shape[0]

    kv_head = me // sharing
    split = heads * HEAD_SIZE
    attn_shard = jnp.concatenate(
        [
            own_columns(query_weight, me, split),
            own_columns(key_matrix, kv_head, HEAD_SIZE),
            own_columns(value_matrix, kv_head, HEAD_SIZE),
            own_columns(out_weight, me, own_width),
        ],
        axis=1,
    )

    def ff_columns(array):
        return jnp.concatenate([own_columns(array, f * n_ctx + me, slab) for f in range(n_fsdp)], axis=1)

    gain_shard = jnp.tile(jnp.concatenate([attn_gain, mlp_gain]).astype(F32)[None], (8, 1))

    first_len = lengths[0, 0]
    given = jnp.arange(total, dtype=jnp.int32)
    position = given - jnp.where(given >= first_len, first_len, 0)
    freq_index = jnp.arange(HEAD_SIZE // 2, dtype=F32)
    inverse = ROPE_BASE ** (-2.0 * freq_index / HEAD_SIZE)
    turns = jnp.tile(inverse, 4)
    sign = jnp.tile(jnp.repeat(jnp.array([-1.0, 1.0], F32), HEAD_SIZE // 2), 2)
    angles = position.astype(F32)[:, None] * turns[None, :]
    cos_table = jnp.cos(angles)
    sin_table = jnp.sin(angles) * sign[None, :]

    deal_rows = deal[0]
    slot_ids = jnp.arange(n_ctx, dtype=jnp.int32)
    dealt_of_given = (deal_rows * n_ctx + slot_ids[:, None]).reshape(-1)
    matched = deal_rows[:, :, None] == slot_ids[None, None, :]
    source_slot = jnp.sum(jnp.where(matched, slot_ids[None, :, None], 0), axis=1)
    given_of_dealt = (slot_ids[:, None] * n_ctx + source_slot).T.reshape(-1)

    def reorder(array, table):
        blocks = array.reshape(n_ctx * n_ctx, block_rows, array.shape[1])
        return jnp.take(blocks, table, axis=0, mode="clip").reshape(array.shape)

    ff_weights = gate_weight, up_weight, down_weight
    if slab % LANES:
        ff_weights = (
            ff_columns(gate_weight),
            ff_columns(up_weight),
            lax.dynamic_slice_in_dim(down_weight, me * slab, slab, axis=0),
        )

    cotangent_all = lax.all_gather(cotangent[0], "ctx", axis=0, tiled=True)
    (
        x, normed, q_rot, k_rot, v_rows, lse, attended_all, hidden_all, normed2, a, b, both, w_attn, w_gate, w_up, w_down, gains_all,
    ) = forward(
        n_ctx,
        n_fsdp,
        heads,
        slab,
        lengths[0],
        tokens[0],
        attn_shard,
        *ff_weights,
        gain_shard,
        cos_table,
        sin_table,
    )
    w_qkv, w_out = w_attn[:, : split + 2 * HEAD_SIZE], w_attn[:, split + 2 * HEAD_SIZE :]
    gains = gains_all.reshape(n_fsdp, 8, 2, rows_shard)[:, 0].transpose(1, 0, 2).reshape(2, 1, width)
    grad_result = reorder(cotangent_all, dealt_of_given)

    result_part = result_rows(me_array, reorder(both, given_of_dealt), w_down)
    activations = lax.psum_scatter(
        result_part, "ctx", scatter_dimension=0, tiled=True
    )[None]

    if kernel_fits(n_ctx, n_fsdp, total, width, own_ff):
        token_grad, gain_rows, down_part, gate_part, up_part, out_part, qkv_part = backward(
            n_ctx,
            n_fsdp,
            heads,
            lengths[0],
            grad_result,
            (x, normed, q_rot, k_rot, v_rows, lse, attended_all, hidden_all, normed2, a, b, both),
            (w_attn, w_gate, w_up, w_down, gains_all),
            cos_table,
            sin_table,
        )
        token_grad = token_grad[None]
        own_gains = gain_rows[1::-1]
    else:
        mlp_grad = (RESIDUAL_SCALE * grad_result.astype(F32)).astype(BF16)

        def settle(left, right):
            return lax.psum_scatter(dot_tn(left, right).astype(BF16), "fsdp", scatter_dimension=0, tiled=True)

        down_part = settle(both[:, :own_ff], mlp_grad)
        ggrad, ugrad, hidden_part, mlp_gain_part = mlp_backward(
            n_ctx, mlp_grad, a, b, hidden_all, gains[1], w_gate, w_up, w_down
        )
        hidden_sum = lax.psum_scatter(hidden_part, "ctx", scatter_dimension=0, tiled=False)
        gate_part = settle(normed2, ggrad)
        up_part = settle(normed2, ugrad)
        hidden_grad, branch_grad, attended_part = branch_backward(
            hidden_sum, own_columns(grad_result, me, own_width), w_out, n_ctx
        )
        attended_grad = lax.psum_scatter(attended_part, "ctx", scatter_dimension=0, tiled=False)
        out_part = lax.psum_scatter(
            jnp.einsum("ctk,to->cko", attended_all, branch_grad, preferred_element_type=F32)
            .astype(BF16)
            .reshape(width, own_width),
            "fsdp",
            scatter_dimension=0,
            tiled=True,
        )
        dq, dkv = attention_backward(attended_grad, q_rot, k_rot, v_rows, lse, cos_table, sin_table, lengths[0])
        qkv_part = settle(normed, jnp.concatenate([dq, dkv], axis=1))
        token_part, attn_gain_part = token_backward(me_array, dq, dkv, w_qkv, x, gains[0], hidden_grad)
        token_grad = lax.psum_scatter(token_part, "ctx", scatter_dimension=0, tiled=True).astype(F32)[None]

        gain_parts = jnp.concatenate([attn_gain_part, mlp_gain_part], axis=0)
        step = 1
        while step < n_ctx:
            gain_parts = gain_parts + lax.ppermute(gain_parts, "ctx", [(c, c ^ step) for c in range(n_ctx)])
            step *= 2
        gain_rows = gain_parts.reshape(2, n_fsdp, rows_shard).transpose(1, 0, 2).reshape(n_fsdp, 2 * rows_shard)
        own_gains = lax.psum_scatter(gain_rows, "fsdp", scatter_dimension=0, tiled=True).reshape(2, rows_shard)
        down_part, gate_part, up_part, out_part, qkv_part = [
            lax.all_gather(p, "ctx", axis=0, tiled=False) for p in (down_part, gate_part, up_part, out_part, qkv_part)
        ]

    if slab % LANES == 0 and sharing == 1 and heads % 4 == 0:
        gate_grad, up_grad, down_grad, out_grad, query_grad, key_grad, value_grad = finish(
            slab, gate_part, up_part, down_part.reshape(n_ctx * slab, width), out_part, qkv_part
        )
    else:
        down_grad = down_part.reshape(n_ctx * slab, width).astype(F32)
        if slab % LANES == 0:
            gate_grad = spread_columns(gate_part, slab, n_fsdp)
            up_grad = spread_columns(up_part, slab, n_fsdp)
        else:

            def ff_whole(part):
                pieces = part.reshape(n_ctx, rows_shard, n_fsdp, slab)
                return pieces.transpose(1, 2, 0, 3).reshape(rows_shard, ff).astype(F32)

            gate_grad = ff_whole(gate_part)
            up_grad = ff_whole(up_part)
        out_grad = spread_columns(out_part, own_width, 1)
        qkv_all = qkv_part
        query_grad = spread_columns(qkv_all, split, 1)

        def shared_heads(pieces):
            pieces = pieces.astype(F32).reshape(KEY_VALUE_HEADS, sharing, rows_shard, HEAD_SIZE).sum(axis=1)
            return pieces.transpose(1, 0, 2).reshape(rows_shard, KEY_VALUE_HEADS * HEAD_SIZE)

        key_grad = shared_heads(qkv_all[:, :, split : split + HEAD_SIZE])
        value_grad = shared_heads(qkv_all[:, :, split + HEAD_SIZE :])

    return (
        activations,
        token_grad,
        own_gains[0],
        query_grad,
        key_grad,
        value_grad,
        out_grad,
        own_gains[1],
        gate_grad,
        up_grad,
        down_grad,
    )


def solution(mesh):
    rows = P("fsdp", None)
    block = P("fsdp", "ctx", None)
    gain = P("fsdp")
    return jax.shard_map(
        local,
        mesh=mesh,
        in_specs=(block, rows, P("fsdp", None, None), gain, rows, rows, rows, rows, gain, rows, rows, rows, block),
        out_specs=(block, block, gain, rows, rows, rows, rows, gain, rows, rows, rows),
        check_vma=False,
    )
```

```python
import functools

import jax
import jax.numpy as jnp
from jax import lax
from jax.experimental import pallas as pl
from jax.experimental.pallas import tpu as pltpu
from jax.sharding import PartitionSpec as P

QUERY_HEADS = 32
KEY_VALUE_HEADS = 8
HEAD_SIZE = 64
EPSILON = 1e-05
ROPE_BASE = 10000000.0
SCORE_SCALE = 0.015625
RESIDUAL_SCALE = 0.22
NEGATIVE_BIG = -1e30
LANES = 128
ROWS = 256
BF16 = jnp.bfloat16
F32 = jnp.float32
VMEM_LIMIT = 59 * 1024 * 1024


def dot_nn(a, b):
    return lax.dot_general(a, b, (((1,), (0,)), ((), ())), preferred_element_type=F32)


def dot_nt(a, b):
    return lax.dot_general(a, b, (((1,), (1,)), ((), ())), preferred_element_type=F32)


def dot_tn(a, b):
    return lax.dot_general(a, b, (((0,), (0,)), ((), ())), preferred_element_type=F32)


def swap_halves(x):
    lane = lax.broadcasted_iota(jnp.int32, x.shape, 1)
    first = lax.rem(lane, HEAD_SIZE) < HEAD_SIZE // 2
    return jnp.where(first, pltpu.roll(x, LANES - HEAD_SIZE // 2, 1), pltpu.roll(x, HEAD_SIZE // 2, 1))


def low_half(shape):
    return lax.broadcasted_iota(jnp.int32, shape, 1) < HEAD_SIZE


def mask_bias(first_len, row0, rows, cols):
    query = row0 + lax.broadcasted_iota(jnp.int32, (rows, cols), 0)
    key = lax.broadcasted_iota(jnp.int32, (rows, cols), 1)
    start = jnp.where(query >= first_len, first_len, 0)
    return jnp.where((key <= query) & (key >= start), 0.0, NEGATIVE_BIG)


def attention_backward_kernel(length_ref, g_ref, q_ref, k_ref, v_ref, lse_ref, cos_ref, sin_ref, dq_ref, dkv_ref, dk_sum, dv_sum):
    pair = pl.program_id(0)
    tokens = q_ref.shape[0]

    @pl.when(pair == 0)
    def _():
        dk_sum[...] = jnp.zeros_like(dk_sum)
        dv_sum[...] = jnp.zeros_like(dv_sum)

    first_len = length_ref[0]
    for block in range(tokens // ROWS):
        rows = pl.ds(block * ROWS, ROWS)
        end = (block + 1) * ROWS
        bias = mask_bias(first_len, block * ROWS, ROWS, end)
        query, grad = q_ref[rows, :], g_ref[rows, :]
        low = low_half(query.shape)
        keys, values = k_ref[:end, :], v_ref[:end, :]
        parts = []
        for half in range(2):
            chosen = low if half == 0 else jnp.logical_not(low)
            own_query = jnp.where(chosen, query, jnp.zeros_like(query))
            own_grad = jnp.where(chosen, grad, jnp.zeros_like(grad))
            scores = dot_nt(own_query, keys) + bias
            probs = jnp.exp(scores - lse_ref[0, rows, half : half + 1])
            prob_grad = dot_nt(own_grad, values)
            delta = jnp.sum(probs * prob_grad, axis=-1, keepdims=True)
            score_grad = (probs * (prob_grad - delta)).astype(BF16)
            parts.append(dot_nn(score_grad, keys))
            dk_sum[:end, :] += dot_tn(score_grad, own_query)
            dv_sum[:end, :] += dot_tn(probs.astype(BF16), own_grad)
        dq = jnp.where(low_half(parts[0].shape), parts[0], parts[1]) * SCORE_SCALE
        dq_ref[rows, :] = (dq * cos_ref[rows, :] - swap_halves(dq) * sin_ref[rows, :]).astype(BF16)

    @pl.when(pair == pl.num_programs(0) - 1)
    def _():
        dk = dk_sum[...]
        dk = dk + pltpu.roll(dk, HEAD_SIZE, 1)
        dk = dk * cos_ref[...] - swap_halves(dk) * sin_ref[...]
        dv = dv_sum[...]
        dv = dv + pltpu.roll(dv, HEAD_SIZE, 1)
        dkv_ref[...] = jnp.where(low_half(dk.shape), dk, dv).astype(BF16)


def attention_backward(grads, q_rot, k_rot, v_rows, lse, cos, sin, lengths):
    tokens = q_rot.shape[0]
    pairs = q_rot.shape[1] // LANES
    one = pl.BlockSpec((tokens, LANES), lambda j: (0, 0))
    each = pl.BlockSpec((tokens, LANES), lambda j: (0, j))
    return pl.pallas_call(
        attention_backward_kernel,
        grid=(pairs,),
        in_specs=[
            pl.BlockSpec(memory_space=pltpu.SMEM),
            each,
            each,
            one,
            one,
            pl.BlockSpec((1, tokens, LANES), lambda j: (j, 0, 0)),
            one,
            one,
        ],
        out_specs=[each, one],
        out_shape=[
            jax.ShapeDtypeStruct((tokens, pairs * LANES), BF16),
            jax.ShapeDtypeStruct((tokens, LANES), BF16),
        ],
        scratch_shapes=[pltpu.VMEM((tokens, LANES), F32), pltpu.VMEM((tokens, LANES), F32)],
        compiler_params=pltpu.CompilerParams(vmem_limit_bytes=VMEM_LIMIT),
        cost_estimate=pl.CostEstimate(
            flops=10 * tokens * tokens * LANES * pairs,
            bytes_accessed=12 * tokens * pairs * LANES,
            transcendentals=tokens * tokens * pairs,
        ),
        name="attend_back",
    )(lengths, grads, q_rot, k_rot, v_rows, lse, cos, sin)


def row_block(width):
    return pl.BlockSpec((ROWS, width), lambda i: (i, 0))


def fixed(*shape):
    return pl.BlockSpec(shape, lambda i: (0,) * len(shape))


def params():
    return pltpu.CompilerParams(vmem_limit_bytes=VMEM_LIMIT)


def cost(flops, *arrays):
    moved = sum(a.size * a.dtype.itemsize for a in arrays)
    return pl.CostEstimate(flops=flops, bytes_accessed=moved, transcendentals=0)


def mlp_back_kernel(
    grad_ref, a_ref, b_ref, hidden_ref, gain_ref, gate_ref, up_ref, down_ref, ggrad_ref, ugrad_ref, part_ref, gain_out
):
    mixed_grad = dot_nt(grad_ref[...], down_ref[...])
    ggrad = (mixed_grad * a_ref[...].astype(F32)).astype(BF16)
    ugrad = (mixed_grad * b_ref[...].astype(F32)).astype(BF16)
    ggrad_ref[...] = ggrad
    ugrad_ref[...] = ugrad
    normed_grad = dot_nt(ggrad, gate_ref[...]) + dot_nt(ugrad, up_ref[...])
    hidden = hidden_ref[...].astype(F32)
    r2 = lax.rsqrt(jnp.mean(hidden * hidden, axis=-1, keepdims=True) + EPSILON)
    gain_part = jnp.sum(normed_grad * (hidden * r2), axis=0, keepdims=True)

    @pl.when(pl.program_id(0) == 0)
    def _():
        gain_out[...] = jnp.zeros_like(gain_out)

    gain_out[...] += gain_part
    weighted = normed_grad * gain_ref[...]
    mean = jnp.mean(weighted * hidden, axis=-1, keepdims=True)
    part = r2 * weighted - hidden * (r2 * r2 * r2 * mean)
    own = part_ref.shape[2]
    for c in range(part_ref.shape[0]):
        part_ref[c] = part[:, c * own : (c + 1) * own].astype(BF16)


def mlp_backward(n, mlp_grad, a, b, hidden_all, gain, w_gate, w_up, w_down):
    total, width = hidden_all.shape
    own = width // n
    own_ff = w_gate.shape[1]
    narrow = jax.ShapeDtypeStruct((total, own_ff), BF16)
    planes = pl.BlockSpec((n, ROWS, own), lambda i: (0, i, 0))
    return pl.pallas_call(
        mlp_back_kernel,
        grid=(total // ROWS,),
        in_specs=[
            row_block(width),
            row_block(own_ff),
            row_block(own_ff),
            row_block(width),
            fixed(1, width),
            fixed(width, own_ff),
            fixed(width, own_ff),
            fixed(own_ff, width),
        ],
        out_specs=[row_block(own_ff), row_block(own_ff), planes, fixed(1, width)],
        out_shape=[narrow, narrow, jax.ShapeDtypeStruct((n, total, own), BF16), jax.ShapeDtypeStruct((1, width), F32)],
        compiler_params=params(),
        cost_estimate=cost(6 * total * width * own_ff, mlp_grad, hidden_all, hidden_all, w_gate, w_up, w_down, a, b, a, b),
        name="mlp_backward",
    )(mlp_grad, a, b, hidden_all, gain, w_gate, w_up, w_down)


def branch_kernel(part_ref, grad_ref, w_ref, hidden_ref, branch_ref, out_ref):
    hidden_grad = part_ref[...].astype(F32) + grad_ref[...].astype(F32)
    hidden_ref[...] = hidden_grad
    branch = (RESIDUAL_SCALE * hidden_grad).astype(BF16)
    branch_ref[...] = branch
    own = out_ref.shape[2]
    for c in range(out_ref.shape[0]):
        out_ref[c] = dot_nt(branch, w_ref[c]).astype(BF16)


def branch_backward(hidden_part, grad_own, w_out, n):
    total, own_width = hidden_part.shape
    own = w_out.shape[0] // n
    w_heads = w_out.reshape(n, own, own_width)
    return pl.pallas_call(
        branch_kernel,
        grid=(total // ROWS,),
        in_specs=[row_block(own_width), row_block(own_width), fixed(n, own, own_width)],
        out_specs=[row_block(own_width), row_block(own_width), pl.BlockSpec((n, ROWS, own), lambda i: (0, i, 0))],
        out_shape=[
            jax.ShapeDtypeStruct((total, own_width), F32),
            jax.ShapeDtypeStruct((total, own_width), BF16),
            jax.ShapeDtypeStruct((n, total, own), BF16),
        ],
        compiler_params=params(),
        cost_estimate=cost(2 * total * own_width * own * n, hidden_part, hidden_part, hidden_part, w_out),
        name="branch_backward",
    )(hidden_part, grad_own, w_heads)


def token_kernel(me_ref, dq_ref, dkv_ref, w_ref, x_ref, gain_ref, hidden_ref, part_ref, gain_out):
    split = dq_ref.shape[1]
    normed_grad = dot_nt(dq_ref[...], w_ref[:, :split]) + dot_nt(dkv_ref[...], w_ref[:, split:])
    x = x_ref[...].astype(F32)
    r1 = lax.rsqrt(jnp.mean(x * x, axis=-1, keepdims=True) + EPSILON)

    @pl.when(pl.program_id(0) == 0)
    def _():
        gain_out[...] = jnp.zeros_like(gain_out)

    gain_out[...] += jnp.sum(normed_grad * (x * r1), axis=0, keepdims=True)
    weighted = normed_grad * gain_ref[...]
    mean = jnp.mean(weighted * x, axis=-1, keepdims=True)
    part = r1 * weighted - x * (r1 * r1 * r1 * mean)
    own_width = hidden_ref.shape[1]
    for c in range(part.shape[1] // own_width):
        piece = part[:, c * own_width : (c + 1) * own_width]
        piece = piece + jnp.where(me_ref[0] == c, hidden_ref[...], 0.0)
        part_ref[:, c * own_width : (c + 1) * own_width] = piece.astype(BF16)


def token_backward(me, dq, dkv, w_qkv, x, gain, hidden_grad):
    total, width = x.shape
    own_width = hidden_grad.shape[1]
    return pl.pallas_call(
        token_kernel,
        grid=(total // ROWS,),
        in_specs=[
            pl.BlockSpec(memory_space=pltpu.SMEM),
            row_block(dq.shape[1]),
            row_block(dkv.shape[1]),
            fixed(*w_qkv.shape),
            row_block(width),
            fixed(1, width),
            row_block(own_width),
        ],
        out_specs=[row_block(width), fixed(1, width)],
        out_shape=[jax.ShapeDtypeStruct((total, width), BF16), jax.ShapeDtypeStruct((1, width), F32)],
        compiler_params=params(),
        cost_estimate=cost(2 * total * width * w_qkv.shape[1], x, x, w_qkv, dq, dkv, hidden_grad),
        name="token_backward",
    )(me, dq, dkv, w_qkv, x, gain, hidden_grad)


def result_kernel(me_ref, rows_ref, w_ref, out_ref):
    depth = w_ref.shape[0]
    own = rows_ref.shape[1] - depth
    product = dot_nn(rows_ref[:, :depth], w_ref[...])
    hidden = rows_ref[:, depth:].astype(F32)
    for c in range(out_ref.shape[1] // own):
        lanes = slice(c * own, (c + 1) * own)
        mine = jnp.where(me_ref[0] == c, hidden, 0.0)
        out_ref[:, lanes] = (RESIDUAL_SCALE * (product[:, lanes] + mine)).astype(BF16)


def result_rows(me, rows, w_down):
    total, columns = rows.shape
    depth, width = w_down.shape
    out_shape = jax.ShapeDtypeStruct((total, width), BF16)
    return pl.pallas_call(
        result_kernel,
        grid=(total // ROWS,),
        in_specs=[pl.BlockSpec(memory_space=pltpu.SMEM), row_block(columns), fixed(depth, width)],
        out_specs=row_block(width),
        out_shape=out_shape,
        compiler_params=params(),
        cost_estimate=cost(2 * total * depth * width, rows, w_down, out_shape),
        name="result_rows",
    )(me, rows, w_down)


def finish_kernel(slab, gate_ref, up_ref, down_ref, out_ref, qkv_ref, gate_out, up_out, down_out, out_out, q_out, k_out, v_out):
    n = gate_ref.shape[0]
    for src, dst, piece in ((gate_ref, gate_out, slab), (up_ref, up_out, slab), (out_ref, out_out, out_ref.shape[2])):
        for c in range(n):
            for f in range(src.shape[2] // piece):
                at = (f * n + c) * piece
                dst[:, at : at + piece] = src[c, :, f * piece : (f + 1) * piece].astype(F32)
    down_out[...] = down_ref[...].astype(F32)
    split = qkv_ref.shape[2] - LANES
    for c in range(n):
        q_out[:, c * split : (c + 1) * split] = qkv_ref[c, :, :split].astype(F32)
    for pair in range(n // 2):
        even = qkv_ref[2 * pair, :, split:].astype(F32)
        odd = qkv_ref[2 * pair + 1, :, split:].astype(F32)
        low = low_half(even.shape)
        lanes = slice(pair * LANES, (pair + 1) * LANES)
        k_out[:, lanes] = jnp.where(low, even, pltpu.roll(odd, HEAD_SIZE, 1))
        v_out[:, lanes] = jnp.where(low, pltpu.roll(even, HEAD_SIZE, 1), odd)


def finish(slab, gate, up, down, out, qkv):
    n, rows, own_ff = gate.shape
    width = n * out.shape[2]
    steps = 16
    tile, down_tile = rows // steps, down.shape[0] // steps
    kv = n * HEAD_SIZE

    def by_device(columns):
        return pl.BlockSpec((n, tile, columns), lambda i: (0, i, 0))

    def flat(height, columns):
        return pl.BlockSpec((height, columns), lambda i: (i, 0))

    outs = [
        (flat(tile, n * own_ff), (rows, n * own_ff)),
        (flat(tile, n * own_ff), (rows, n * own_ff)),
        (flat(down_tile, width), down.shape),
        (flat(tile, width), (rows, width)),
        (flat(tile, width), (rows, width)),
        (flat(tile, kv), (rows, kv)),
        (flat(tile, kv), (rows, kv)),
    ]
    return pl.pallas_call(
        functools.partial(finish_kernel, slab),
        grid=(steps,),
        in_specs=[
            by_device(own_ff),
            by_device(own_ff),
            flat(down_tile, width),
            by_device(out.shape[2]),
            by_device(qkv.shape[2]),
        ],
        out_specs=[spec for spec, _ in outs],
        out_shape=[jax.ShapeDtypeStruct(shape, F32) for _, shape in outs],
        compiler_params=params(),
        cost_estimate=cost(0, gate, gate, gate, up, up, up, down, down, down),
        name="finish",
    )(gate, up, down, out, qkv)


def spread_kernel(in_ref, out_ref):
    slab = in_ref.shape[2]
    for c in range(in_ref.shape[0]):
        out_ref[:, c * slab : (c + 1) * slab] = in_ref[c].astype(F32)


def spread_columns(pieces, slab, groups):
    n, rows, _ = pieces.shape
    tile = 128
    out_shape = jax.ShapeDtypeStruct((rows, groups * n * slab), F32)
    return pl.pallas_call(
        spread_kernel,
        grid=(groups, rows // tile),
        in_specs=[pl.BlockSpec((n, tile, slab), lambda f, r: (0, r, f))],
        out_specs=pl.BlockSpec((tile, n * slab), lambda f, r: (r, f)),
        out_shape=out_shape,
        compiler_params=params(),
        cost_estimate=cost(0, pieces, out_shape),
        name="spread_columns",
    )(pieces)


MESH = pl.DeviceIdType.MESH


class Chain:
    def __init__(self, slot, planes, plane, send_sem, recv_sem):
        self.slot, self.planes, self.plane = slot, planes, plane
        self.send_sem, self.recv_sem = send_sem, recv_sem

    def copy(self, way, step, shard, to):
        return pltpu.make_async_remote_copy(
            src_ref=self.slot(shard),
            dst_ref=self.slot(shard),
            send_sem=self.send_sem.at[way, step],
            recv_sem=self.recv_sem.at[way, step],
            device_id={"fsdp": to},
            device_id_type=MESH,
        )

    def moves(self, step):
        p, last = self.plane, self.planes - 1
        return (
            (0, (p >= step) & (p < last), p - step, p + 1, p >= step + 1, p - 1 - step),
            (1, (p + step <= last) & (p > 0), p + step, p - 1, p + step + 1 <= last, p + 1 + step),
        )

    def start(self, step):
        for way, sends, shard, to, _, _ in self.moves(step):

            @pl.when(sends)
            def _(way=way, shard=shard, to=to):
                self.copy(way, step, shard, to).start()

    def arrive(self, step):
        for way, _, _, _, receives, shard in self.moves(step):

            @pl.when(receives)
            def _(way=way, shard=shard):
                self.copy(way, step, shard, self.plane).wait_recv()

    def advance(self, step):
        self.arrive(step - 1)
        self.start(step)

    def drain(self):
        for step in range(self.planes - 1):
            for way, sends, shard, to, _, _ in self.moves(step):

                @pl.when(sends)
                def _(way=way, shard=shard, to=to, step=step):
                    self.copy(way, step, shard, to).wait_send()


class Spread:
    def __init__(self, src, slot, n, me, send_sem, recv_sem):
        self.src, self.slot, self.n, self.me = src, slot, n, me
        self.send_sem, self.recv_sem = send_sem, recv_sem
        self.chips = n // 2
        self.chip, self.core = me // 2, lax.rem(me, 2)
        self.partner = me + 1 - 2 * self.core

    def at(self, k):
        return lax.rem(self.chip + k, self.chips) * 2 + self.core

    def copy(self, src, owner, sem, to):
        return pltpu.make_async_remote_copy(
            src_ref=src,
            dst_ref=self.slot(owner),
            send_sem=self.send_sem.at[sem],
            recv_sem=self.recv_sem.at[sem],
            device_id={"ctx": to},
            device_id_type=MESH,
        )

    def out(self, k):
        return self.copy(self.src, self.me, k, self.at(k))

    def relay(self, k):
        owner = self.at(self.chips - k) if k else self.me
        src = self.slot(owner) if k else self.src
        return self.copy(src, owner, self.chips + k, self.partner)

    def start(self):
        for k in range(1, self.chips):
            self.out(k).start()
        self.relay(0).start()

    def pass_on(self):
        for k in range(1, self.chips):
            self.copy(self.src, self.at(self.chips - k), k, self.me).wait_recv()
            self.relay(k).start()

    def late(self):
        pass

    def finish(self):
        other = 1 - 2 * self.core
        for k in range(self.chips):
            owner = (self.at(self.chips - k) if k else self.me) + other
            self.copy(self.slot(owner), owner, self.chips + k, self.me).wait_recv()

    def drain(self):
        for k in range(1, self.chips):
            self.out(k).wait_send()
        for k in range(self.chips):
            self.relay(k).wait_send()


class Spread4:
    def __init__(self, src, slot, n, me, send_sem, recv_sem):
        self.src, self.slot, self.me = src, slot, me
        self.send_sem, self.recv_sem = send_sem, recv_sem
        self.core = lax.rem(me, 2)
        self.other = 1 - self.core
        chip = me // 2
        self.near, self.side, self.far = square(chip)
        self.chip = chip
        self.half = src.shape[0] // 2

    def copy(self, src, dst, sem, to):
        return pltpu.make_async_remote_copy(
            src_ref=src,
            dst_ref=dst,
            send_sem=self.send_sem.at[sem],
            recv_sem=self.recv_sem.at[sem],
            device_id={"ctx": to},
            device_id_type=MESH,
        )

    def part(self, owner, which):
        return self.slot(owner).at[pl.ds(which * self.half, self.half)]

    def out(self, sem):
        chip = self.near if sem == 1 else self.side
        return self.copy(self.src, self.slot(self.me), sem, chip * 2 + self.core)

    def onward(self, sem):
        origin, to, which = (self.near, self.side, 0) if sem == 3 else (self.side, self.near, 1)
        owner = origin * 2 + self.core
        return self.copy(self.part(owner, which), self.part(owner, which), sem, to * 2 + self.core)

    def relay(self, k):
        owner = (self.chip, self.near, self.side, self.far)[k] * 2 + self.core
        src = self.slot(owner) if k else self.src
        return self.copy(src, self.slot(owner), 4 + k, self.chip * 2 + self.other)

    def start(self):
        self.out(1).start()
        self.out(2).start()
        self.relay(0).start()

    def pass_on(self):
        for k, chip in ((1, self.near), (2, self.side)):
            owner = chip * 2 + self.core
            self.copy(self.src, self.slot(owner), k, self.me).wait_recv()
            self.onward(3 if k == 1 else 0).start()
            self.relay(k).start()

    def late(self):
        owner = self.far * 2 + self.core
        for sem, which in ((3, 0), (0, 1)):
            self.copy(self.part(owner, which), self.part(owner, which), sem, self.me).wait_recv()
        self.relay(3).start()

    def finish(self):
        for k, chip in enumerate((self.chip, self.near, self.side, self.far)):
            owner = chip * 2 + self.other
            self.copy(self.slot(owner), self.slot(owner), 4 + k, self.me).wait_recv()

    def drain(self):
        for sem in (1, 2):
            self.out(sem).wait_send()
        for sem in (3, 0):
            self.onward(sem).wait_send()
        for k in range(4):
            self.relay(k).wait_send()


def square(chip):
    return chip + 1 - 2 * lax.rem(chip, 2), chip + 2 - 4 * (chip // 2), 3 - chip


def spread_over(n, src, *rest):
    return (Spread4 if n == 8 and src.shape[0] % 32 == 0 else Spread)(src, *rest)


def greet(n, planes, me, plane, across):
    barrier = pltpu.get_barrier_semaphore()
    chips = n // 2
    core = lax.rem(me, 2)
    others = [lax.rem(me // 2 + k, chips) * 2 + core for k in range(1, chips)] + [me + 1 - 2 * core]
    for other in others:
        pl.semaphore_signal(barrier, inc=1, device_id={"ctx": other}, device_id_type=MESH)
    if across:

        @pl.when(plane > 0)
        def _():
            pl.semaphore_signal(barrier, inc=1, device_id={"fsdp": plane - 1}, device_id_type=MESH)

        @pl.when(plane < planes - 1)
        def _():
            pl.semaphore_signal(barrier, inc=1, device_id={"fsdp": plane + 1}, device_id_type=MESH)

    count = len(others)
    if across:
        count = count + (plane > 0).astype(jnp.int32) + (plane < planes - 1).astype(jnp.int32)
    pl.semaphore_wait(barrier, count)


def forward_kernel(
    n,
    planes,
    heads,
    length_ref,
    tokens_ref,
    attn_shard,
    gate_ref,
    up_ref,
    down_ref,
    gain_shard,
    cos_ref,
    sin_ref,
    x_out,
    normed_out,
    q_out,
    k_out,
    v_out,
    lse_out,
    att_out,
    hid_out,
    normed2_out,
    a_out,
    b_out,
    mixed_out,
    attn_out,
    gate_out,
    up_out,
    down_out,
    gain_out,
    w_attn,
    w_gate,
    w_up,
    w_down,
    gains,
    x_all,
    qkv,
    q_rot,
    k_rot,
    v_rows,
    lse,
    own_att,
    att_all,
    own_hid,
    own_scaled,
    wide,
    narrow,
    z_send,
    z_recv,
    c_send,
    c_recv,
    keep_sem,
    load_sem,
    wide_sem,
    narrow_sem,
):
    me, plane = lax.axis_index("ctx"), lax.axis_index("fsdp")
    per_device, width = tokens_ref.shape
    total = x_all.shape[0]
    rows_shard = attn_shard.shape[0]
    own = own_att.shape[1]
    own_width = own_hid.shape[1]
    columns = qkv.shape[1]
    blocks = total // ROWS
    pairs = heads // 2

    local_copies = []

    def keep(src, dst, index):
        copy = pltpu.make_async_copy(src, dst, keep_sem.at[index])
        copy.start()
        local_copies.append(copy)

    def chain(index, ref, rows):
        return Chain(lambda s: ref.at[pl.ds(s * rows, rows)], planes, plane, z_send.at[index], z_recv.at[index])

    attn_chain = chain(0, w_attn, rows_shard)
    gate_chain = chain(1, w_gate, rows_shard)
    up_chain = chain(2, w_up, rows_shard)
    slab = w_down.shape[0] // planes
    down_chain = chain(3, w_down, slab)
    gain_chain = chain(4, gains, gain_shard.shape[0])
    own_ff = w_gate.shape[1]
    loads = [
        pltpu.make_async_copy(shard, c.slot(plane), keep_sem.at[i])
        for i, (c, shard) in enumerate(((attn_chain, attn_shard), (gain_chain, gain_shard)))
    ]
    for ref, c, at in ((gate_ref, gate_chain, 0), (up_ref, up_chain, 1)):
        for f in range(ref.shape[1] // (n * slab)):
            src = ref.at[:, pl.ds(pl.multiple_of((f * n + me) * slab, LANES), slab)]
            dst = c.slot(plane).at[:, pl.ds(f * slab, slab)]
            loads.append(pltpu.make_async_copy(src, dst, load_sem.at[at, f]))
        if ref.shape[1] == own_ff:
            loads.append(pltpu.make_async_copy(ref, c.slot(plane), load_sem.at[at, 0]))
    down_src = down_ref if down_ref.shape[0] == slab else down_ref.at[pl.ds(pl.multiple_of(me * slab, slab), slab)]
    loads.append(pltpu.make_async_copy(down_src, down_chain.slot(plane), load_sem.at[2, 0]))
    for load in loads:
        load.start()
    own_x = pltpu.make_async_copy(tokens_ref, x_all.at[pl.ds(me * per_device, per_device)], keep_sem.at[5])
    own_x.start()
    greet(n, planes, me, plane, True)
    loads[0].wait()
    attn_chain.start(0)
    loads[1].wait()
    gain_chain.start(0)
    x_spread = spread_over(
        n, tokens_ref, lambda c: x_all.at[pl.ds(c * per_device, per_device)], n, me, c_send.at[0], c_recv.at[0]
    )
    x_spread.start()
    for load in loads[2:]:
        load.wait()
    own_x.wait()
    for step in range(1, planes - 1):
        attn_chain.advance(step)
        gain_chain.advance(step)
    gate_chain.start(0)
    up_chain.start(0)
    x_spread.pass_on()
    x_spread.late()
    x_spread.finish()
    x_copy = pltpu.make_async_copy(x_all, x_out, keep_sem.at[0])
    x_copy.start()
    attn_chain.arrive(planes - 2)
    gain_chain.arrive(planes - 2)
    keep(w_attn, attn_out, 1)
    keep(gains, gain_out, 2)
    half = gain_shard.shape[1] // 2
    step_rows = gain_shard.shape[0]
    attn_gain = jnp.concatenate([gains[f * step_rows : f * step_rows + 1, :half] for f in range(planes)], axis=1)
    mlp_gain = jnp.concatenate([gains[f * step_rows : f * step_rows + 1, half:] for f in range(planes)], axis=1)

    def staged(stage, sem, slot, out, rows, wait_before):
        copy = pltpu.make_async_copy(stage.at[slot], out.at[rows], sem.at[slot])
        return copy.wait() if wait_before else copy.start()

    def project_block(i, _):
        rows = pl.ds(pl.multiple_of(i * ROWS, ROWS), ROWS)
        slot = lax.rem(i, 2)

        @pl.when(i >= 2)
        def _():
            staged(wide, wide_sem, slot, normed_out, rows, True)

        own_hid[rows, :] = x_all[rows, pl.ds(pl.multiple_of(me * own_width, LANES), own_width)]
        x = x_all[rows, :].astype(F32)
        r1 = lax.rsqrt(jnp.mean(x * x, axis=-1, keepdims=True) + EPSILON)
        normed = (x * r1 * attn_gain).astype(BF16)
        wide[slot] = normed
        staged(wide, wide_sem, slot, normed_out, rows, False)
        qkv[rows, :] = dot_nn(normed, w_attn[:, :columns])
        return 0

    lax.fori_loop(0, blocks, project_block, 0)
    for i in range(max(blocks - 2, 0), blocks):
        staged(wide, wide_sem, i % 2, normed_out, pl.ds(i * ROWS, ROWS), True)

    split = columns - LANES
    cos, sin = cos_ref[...], sin_ref[...]
    kv = qkv[:, split:]
    turned = pltpu.roll(kv, HEAD_SIZE, 1)
    low = low_half(kv.shape)
    k = jnp.where(low, kv, turned)
    k_rot[...] = (k * cos + swap_halves(k) * sin).astype(BF16)
    v_rows[...] = jnp.where(low, turned, kv).astype(BF16)
    keep(k_rot, k_out, 3)
    keep(v_rows, v_out, 4)
    first_len = length_ref[0]

    def attend_pair(pair, _):
        lanes = pl.ds(pl.multiple_of(pair * LANES, LANES), LANES)
        q = qkv[:, lanes]
        q_rot[:, lanes] = ((q * cos_ref[...] + swap_halves(q) * sin_ref[...]) * SCORE_SCALE).astype(BF16)
        for block in range(blocks):
            rows = pl.ds(block * ROWS, ROWS)
            end = (block + 1) * ROWS
            bias = mask_bias(first_len, block * ROWS, ROWS, end)
            query = q_rot[rows, lanes]
            lower = low_half(query.shape)
            keys, values = k_rot[:end, :], v_rows[:end, :]
            parts = []
            for side in range(2):
                chosen = lower if side == 0 else jnp.logical_not(lower)
                scores = dot_nt(jnp.where(chosen, query, jnp.zeros_like(query)), keys) + bias
                top = jnp.max(scores, axis=-1, keepdims=True)
                weights = jnp.exp(scores - top)
                whole = jnp.sum(weights, axis=-1, keepdims=True)
                probs = (weights * (1.0 / whole)).astype(BF16)
                parts.append(dot_nn(probs, values))
                lse[pair, rows, side : side + 1] = top + jnp.log(whole)
            own_att[rows, lanes] = jnp.where(low_half(parts[0].shape), parts[0], parts[1]).astype(BF16)
        return 0

    lax.fori_loop(0, pairs, attend_pair, 0)
    att_spread = spread_over(n, own_att, lambda c: att_all.at[c], n, me, c_send.at[1], c_recv.at[1])
    x_copy.wait()
    x_spread.drain()
    att_spread.start()
    own_a = pltpu.make_async_copy(own_att, att_all.at[me], keep_sem.at[5])
    own_a.start()
    keep(q_rot, q_out, 6)
    keep(lse, lse_out, 7)
    if planes > 2:
        gate_chain.advance(1)
        up_chain.advance(1)
    att_spread.pass_on()
    att_spread.late()
    own_a.wait()
    att_spread.finish()
    keep(att_all, att_out, 8)

    def out_block(i, _):
        rows = pl.ds(pl.multiple_of(i * ROWS, ROWS), ROWS)
        acc = jnp.zeros((ROWS, own_width), F32)
        for c in range(n):
            acc += dot_nn(att_all[c, rows, :], w_attn[c * own : (c + 1) * own, columns:])
        hidden = own_hid[rows, :].astype(F32) + RESIDUAL_SCALE * acc
        own_hid[rows, :] = hidden.astype(BF16)
        own_scaled[rows, :] = (hidden * (1.0 / RESIDUAL_SCALE)).astype(BF16)
        return 0

    lax.fori_loop(0, blocks, out_block, 0)
    def hid_slot(c):
        return x_all.at[:, pl.ds(pl.multiple_of(c * own_width, LANES), own_width)]

    hid_spread = spread_over(n, own_hid, hid_slot, n, me, c_send.at[2], c_recv.at[2])
    hid_spread.start()
    keep(own_scaled, mixed_out.at[:, pl.ds(own_ff, own_width)], 13)
    own_h = pltpu.make_async_copy(own_hid, hid_slot(me), keep_sem.at[5])
    own_h.start()
    for step in range(2, planes - 1):
        gate_chain.advance(step)
        up_chain.advance(step)
    down_chain.start(0)
    hid_spread.pass_on()
    hid_spread.late()
    own_h.wait()
    hid_spread.finish()
    keep(x_all, hid_out, 9)
    gate_chain.arrive(planes - 2)
    up_chain.arrive(planes - 2)
    keep(w_gate, gate_out, 10)
    keep(w_up, up_out, 11)
    if planes > 2:
        down_chain.advance(1)

    def mlp_copies(i, rows, wait):
        slot = lax.rem(i, 2)
        staged(wide, wide_sem, slot, normed2_out, rows, wait)
        for j, out in enumerate((a_out, b_out, mixed_out.at[:, pl.ds(0, own_ff)])):
            staged(narrow.at[j], narrow_sem.at[j], slot, out, rows, wait)

    def mlp_block(i, _):
        rows = pl.ds(pl.multiple_of(i * ROWS, ROWS), ROWS)
        slot = lax.rem(i, 2)

        @pl.when(i >= 2)
        def _():
            mlp_copies(i, rows, True)

        hidden = x_all[rows, :].astype(F32)
        r2 = lax.rsqrt(jnp.mean(hidden * hidden, axis=-1, keepdims=True) + EPSILON)
        normed = (hidden * r2 * mlp_gain).astype(BF16)
        wide[slot] = normed
        gate = dot_nn(normed, w_gate[...])
        up = dot_nn(normed, w_up[...])
        sig = jax.nn.sigmoid(gate)
        silu = gate * sig
        narrow[2, slot] = (silu * up).astype(BF16)
        narrow[1, slot] = silu.astype(BF16)
        narrow[0, slot] = (up * sig * (1.0 + gate * (1.0 - sig))).astype(BF16)
        mlp_copies(i, rows, False)
        return 0

    lax.fori_loop(0, blocks, mlp_block, 0)
    for step in range(2, planes - 1):
        down_chain.advance(step)
    for i in range(max(blocks - 2, 0), blocks):
        mlp_copies(i, pl.ds(i * ROWS, ROWS), True)
    down_chain.arrive(planes - 2)
    keep(w_down, down_out, 12)
    for c in (attn_chain, gain_chain, gate_chain, up_chain, down_chain):
        c.drain()
    for s in (att_spread, hid_spread):
        s.drain()
    for copy in local_copies:
        copy.wait()


def forward(n, planes, heads, slab, lengths, tokens, attn_shard, gate, up, down, gain_shard, cos, sin):
    per_device, width = tokens.shape
    total = per_device * n
    own = heads * HEAD_SIZE
    columns = own + 2 * HEAD_SIZE
    own_width = attn_shard.shape[1] - columns
    own_ff = planes * slab
    rows_shard = attn_shard.shape[0]
    pairs = heads // 2
    weights = [
        ((planes * rows_shard, attn_shard.shape[1]), BF16),
        ((planes * rows_shard, own_ff), BF16),
        ((planes * rows_shard, own_ff), BF16),
        ((own_ff, width), BF16),
        ((planes * gain_shard.shape[0], gain_shard.shape[1]), F32),
    ]
    outs = [
        ((total, width), BF16),
        ((total, width), BF16),
        ((total, own), BF16),
        ((total, LANES), BF16),
        ((total, LANES), BF16),
        ((pairs, total, LANES), F32),
        ((n, total, own), BF16),
        ((total, width), BF16),
        ((total, width), BF16),
        ((total, own_ff), BF16),
        ((total, own_ff), BF16),
        ((total, own_ff + own_width), BF16),
    ] + weights
    scratch = weights + [
        ((total, width), BF16),
        ((total, columns), F32),
        ((total, own), BF16),
        ((total, LANES), BF16),
        ((total, LANES), BF16),
        ((pairs, total, LANES), F32),
        ((total, own), BF16),
        ((n, total, own), BF16),
        ((total, own_width), BF16),
        ((total, own_width), BF16),
        ((2, ROWS, width), BF16),
        ((3, 2, ROWS, own_ff), BF16),
    ]
    steps = max(planes - 1, 1)
    dma = pltpu.SemaphoreType.DMA
    anywhere = pl.BlockSpec(memory_space=pl.ANY)
    vmem = pl.BlockSpec(memory_space=pltpu.VMEM)
    return pl.pallas_call(
        functools.partial(forward_kernel, n, planes, heads),
        in_specs=[pl.BlockSpec(memory_space=pltpu.SMEM), vmem] + [anywhere] * 5 + [vmem] * 2,
        out_specs=[anywhere] * len(outs),
        out_shape=[jax.ShapeDtypeStruct(*o) for o in outs],
        scratch_shapes=[pltpu.VMEM(*s) for s in scratch]
        + [dma((5, 2, steps)), dma((5, 2, steps)), dma((3, n)), dma((3, n)), dma((16,)), dma((3, planes)), dma((2,)), dma((3, 2))],
        compiler_params=pltpu.CompilerParams(
            vmem_limit_bytes=VMEM_LIMIT, collective_id=1, has_side_effects=True
        ),
        cost_estimate=pl.CostEstimate(
            flops=2 * total * width * (columns + own_width + 2 * own_ff),
            bytes_accessed=60 * 1024 * 1024,
            transcendentals=0,
        ),
        name="forward",
    )(lengths, tokens, attn_shard, gate, up, down, gain_shard, cos, sin)


def add_into(dst, src):
    rows_in, columns = dst.shape
    chunk = max(c for c in (256, 128, 64, 32) if c == 32 or (rows_in % c == 0 and c * columns <= 65536))

    def step(i, _):
        rows = pl.ds(pl.multiple_of(i * chunk, chunk), chunk)
        dst[rows, :] = (dst[rows, :].astype(F32) + src[rows, :].astype(F32)).astype(dst.dtype)
        return 0

    if rows_in < chunk:
        dst[...] = dst[...] + src[...]
    else:
        lax.fori_loop(0, rows_in // chunk, step, 0)


def fetch(src, dst, sem):
    copy = pltpu.make_async_copy(src, dst, sem)
    copy.start()
    copy.wait()


class Settle:
    def __init__(self, block, landed, stage, planes, plane, send_sem, recv_sem, load_sem):
        self.block, self.landed, self.stage = block, landed, stage
        self.planes, self.plane = planes, plane
        self.send_sem, self.recv_sem, self.load_sem = send_sem, recv_sem, load_sem

    def slot(self, way, shard, at):
        return shard if way == 0 else jnp.where(shard == at, self.planes, shard)

    def sends(self, step):
        p, last = self.plane, self.planes - 1
        return (
            (0, (p <= step) & (p < last), last - step + p, p + 1),
            (1, (last - p <= step) & (p > 0), step - last + p, p - 1),
        )

    def receives(self, step):
        p, last = self.plane, self.planes - 1
        return (
            (0, (p >= 1) & (p - 1 <= step), last - step + p - 1),
            (1, (p <= last - 1) & (last - p - 1 <= step), step - last + p + 1),
        )

    def copy(self, way, step, shard, to):
        return pltpu.make_async_remote_copy(
            src_ref=self.block(shard),
            dst_ref=self.landed.at[self.slot(way, shard, to)],
            send_sem=self.send_sem.at[way, step],
            recv_sem=self.recv_sem.at[way, step],
            device_id={"fsdp": to},
            device_id_type=MESH,
        )

    def start(self, step=0):
        ahead = [step + 1] if step else [0, 1]
        for way in range(2):
            end = self.plane == (0, self.planes - 1)[way]
            _, active, shard, to = self.sends(step)[way]

            @pl.when(active & jnp.logical_not(end))
            def _(way=way, shard=shard, to=to):
                self.copy(way, step, shard, to).start()

            @pl.when(end)
            def _(way=way):
                for later in ahead:
                    if later < self.planes - 1:
                        _, _, shard, to = self.sends(later)[way]
                        self.copy(way, later, shard, to).start()

    def take(self, step):
        for way, active, shard in self.receives(step):

            @pl.when(active)
            def _(way=way, shard=shard):
                self.copy(way, step, shard, self.plane).wait_recv()
                fetch(self.landed.at[self.slot(way, shard, self.plane)], self.stage, self.load_sem)
                add_into(self.block(shard), self.stage)

    def advance(self, step):
        self.take(step - 1)
        self.start(step)

    def drain(self):
        for step in range(self.planes - 1):
            for way, active, shard, to in self.sends(step):

                @pl.when(active)
                def _(way=way, shard=shard, to=to, step=step):
                    self.copy(way, step, shard, to).wait_send()


class Scatter:
    def __init__(self, block, near, far, stage, me, send_sem, recv_sem, load_sem):
        self.block, self.landed, self.far, self.stage = block, near, far, stage
        self.send_sem, self.recv_sem, self.load_sem = send_sem, recv_sem, load_sem
        self.core = lax.rem(me, 2)
        self.chip = me // 2
        self.chips = (self.chip, *square(self.chip))
        self.half = stage[0].shape[0] // 2

    def rows(self, which):
        return pl.ds(which * self.half, self.half)

    def own(self, k):
        return self.block(self.chips[k] * 2 + self.core)

    def copy(self, src, dst, sem, chip, core):
        return pltpu.make_async_remote_copy(
            src_ref=src,
            dst_ref=dst,
            send_sem=self.send_sem.at[sem],
            recv_sem=self.recv_sem.at[sem],
            device_id={"ctx": chip * 2 + core},
            device_id_type=MESH,
        )

    def first(self, k):
        other = 1 - self.core
        return self.copy(self.block(self.chips[k] * 2 + other), self.landed.at[k], k, self.chip, other)

    def second(self, k, to, which):
        place = self.far.at[to - 1 if k == to else 2, self.rows(which)]
        sem = 4 + 2 * (to - 1) + which if k == to else 7 + to
        return self.copy(self.own(k).at[self.rows(which)], place, sem, self.chips[to], self.core)

    def start(self):
        for k in (3, 1, 2, 0):
            self.first(k).start()

    def add_all(self, items):
        pending = None

        def complete(copy, dst, stage, then):
            copy.wait()
            add_into(dst, stage)
            for remote in then:
                remote.start()

        for index, (arrivals, src, dst, then) in enumerate(items):
            for remote in arrivals:
                remote.wait_recv()
            stage = self.stage[index % 2].at[pl.ds(0, dst.shape[0])]
            copy = pltpu.make_async_copy(src, stage, self.load_sem.at[index % 2])
            copy.start()
            if pending is not None:
                complete(*pending)
            pending = (copy, dst, stage, then)
        complete(*pending)

    def pass_on(self):
        self.add_all(
            [
                ([self.first(3)], self.landed.at[3], self.own(3), [self.second(3, 1, 0), self.second(3, 2, 1)]),
                ([self.first(1)], self.landed.at[1], self.own(1), [self.second(1, 1, 0)]),
                ([self.first(2)], self.landed.at[2], self.own(2), [self.second(2, 2, 1)]),
            ]
        )

    def late(self):
        self.add_all(
            [
                (
                    [self.second(3, to, which)],
                    self.far.at[2, self.rows(which)],
                    self.own(k).at[self.rows(which)],
                    [self.second(k, k, which)],
                )
                for to, which, k in ((1, 0, 2), (2, 1, 1))
            ]
        )

    def finish(self, total):
        items = [([self.first(0)], self.landed.at[0], total, [])]
        for k in (1, 2):
            items.append(([self.second(k, k, which) for which in (0, 1)], self.far.at[k - 1], total, []))
        self.add_all(items)

    def drain(self):
        for k in range(4):
            self.first(k).wait_send()
        for k, to, which in ((3, 1, 0), (3, 2, 1), (1, 1, 0), (1, 1, 1), (2, 2, 0), (2, 2, 1)):
            self.second(k, to, which).wait_send()


def backward_kernel(
    n,
    planes,
    heads,
    length_ref,
    grad_in,
    mixed_in,
    a_in,
    b_in,
    hidden_in,
    normed2_in,
    normed_in,
    x_in,
    att_in,
    q_in,
    k_in,
    v_in,
    lse_in,
    cos_in,
    sin_in,
    attn_in,
    gate_in,
    up_in,
    down_in,
    gain_in,
    token_out,
    gain_out,
    down_all,
    gate_all,
    up_all,
    out_all,
    qkv_all,
    near1,
    far1,
    near2,
    far2,
    near3,
    far3,
    down_landed,
    gate_landed,
    up_landed,
    out_landed,
    qkv_landed,
    w_attn,
    w_gate,
    w_up,
    w_down,
    p_down,
    gains,
    grad,
    a_v,
    b_v,
    part,
    hid_stage,
    stage_tall,
    stage_wide,
    stage_col,
    hidden_grad,
    lse,
    cos,
    sin,
    dk_sum,
    dv_sum,
    gain_own,
    gain_all,
    gain_landed,
    gain_stage,
    z_send,
    z_recv,
    s_send,
    s_recv,
    g_send,
    g_recv,
    load_sem,
    hid_sem,
    add_sem,
    ring_sem,
):
    me, plane = lax.axis_index("ctx"), lax.axis_index("fsdp")
    total, width = grad.shape
    per_device = total // n
    own = heads * HEAD_SIZE
    own_width = width // n
    own_ff = a_v.shape[1]
    rows_shard = width // planes
    slab = own_ff // planes
    blocks = total // ROWS
    pairs = heads // 2
    columns = own + LANES
    last = planes - 2

    def load(src, dst, index):
        copy = pltpu.make_async_copy(src, dst, load_sem.at[index])
        copy.start()
        return copy

    mixed_loads = [load(mixed_in.at[:, pl.ds(d * own_width, own_width)], part.at[d], d) for d in range(own_ff // own_width)]
    grad_load = load(grad_in, grad, 8)
    down_load = load(down_in, w_down, 9)
    gate_load = load(gate_in, w_gate, 10)
    up_load = load(up_in, w_up, 11)
    a_load = load(a_in, a_v, 12)
    b_load = load(b_in, b_v, 13)
    attn_load = load(attn_in, w_attn, 14)
    gain_load = load(gain_in, gains, 15)
    greet(n, planes, me, plane, True)

    def settle(index, block, landed, stage):
        return Settle(block, landed, stage, planes, plane, z_send.at[index], z_recv.at[index], add_sem)

    def rows_of(ref, rows):
        return lambda d: ref.at[pl.ds(pl.multiple_of(d * rows, rows), rows)]

    def out_block_of(d):
        return w_down.at[pl.ds(0, rows_shard), pl.ds(pl.multiple_of(d * own_width, LANES), own_width)]

    def qkv_block_of(d):
        return w_down.at[pl.ds(rows_shard, rows_shard), pl.ds(pl.multiple_of(d * columns, LANES), columns)]

    def gain_block_of(d):
        return gain_own.at[:, pl.ds(pl.multiple_of(d * rows_shard, LANES), rows_shard)]

    down_sum = settle(0, rows_of(p_down, slab), down_landed, stage_wide)
    gate_sum = settle(1, rows_of(w_gate, rows_shard), gate_landed, stage_tall)
    up_sum = settle(2, rows_of(w_up, rows_shard), up_landed, stage_tall)
    out_sum = settle(3, out_block_of, out_landed, stage_tall.at[:, pl.ds(0, own_width)])
    qkv_sum = settle(4, qkv_block_of, qkv_landed, stage_tall.at[:, pl.ds(0, columns)])
    gain_sum = settle(5, gain_block_of, gain_landed, gain_stage)

    def spread(index, src, dst):
        return spread_over(n, src, lambda c: dst.at[c], n, me, g_send.at[index], g_recv.at[index])

    spreads = []

    def give(index, sums, dst):
        src = sums.block(plane)
        mine = load(src, dst.at[me], 16 + index)
        out = spread(index, src, dst)
        out.start()
        spreads.append((out, mine))
        return out

    def scatter(index, block, near, far, stage):
        return Scatter(block, near, far, stage, me, s_send.at[index], s_recv.at[index], ring_sem)

    part_rows = total // 2
    col_stages = [stage_col.at[pl.ds(i * part_rows, part_rows)] for i in range(2)]

    def half_scatter(index, near, far, side):
        rows = pl.ds(side * part_rows, part_rows)
        return scatter(
            2 * index + side, lambda c: part.at[c, rows], near.at[:, rows], far.at[:, rows], col_stages
        )

    first = [half_scatter(0, near1, far1, side) for side in range(2)]
    second = [half_scatter(1, near2, far2, side) for side in range(2)]

    grad_load.wait()

    for copy in mixed_loads:
        copy.wait()

    def down_block(i, _):
        d = jnp.where(i == 0, planes - 1, jnp.where(i == 1, 0, planes - i))
        rows = pl.ds(pl.multiple_of(d * own_width, own_width), own_width)
        p_down[rows, :] = (RESIDUAL_SCALE * dot_tn(part[d], grad[...])).astype(BF16)

        return 0

    lax.fori_loop(0, planes, down_block, 0)
    down_sum.start()

    for copy in (down_load, gate_load, up_load, a_load, b_load, attn_load, gain_load):
        copy.wait()
    half = gains.shape[1] // 2
    attn_gain = jnp.concatenate([gains[f * 8 : f * 8 + 1, :half] for f in range(planes)], axis=1)
    mlp_gain = jnp.concatenate([gains[f * 8 : f * 8 + 1, half:] for f in range(planes)], axis=1)
    gain_own[...] = jnp.zeros_like(gain_own)

    def stream(src, i, wait):
        rows = pl.ds(pl.multiple_of(i * ROWS, ROWS), ROWS)
        slot = lax.rem(i, 2)
        copy = pltpu.make_async_copy(src.at[rows], hid_stage.at[slot], hid_sem.at[slot])
        return copy.wait() if wait else copy.start()

    stream(hidden_in, jnp.int32(0), False)

    def mlp_block(i, _):
        rows = pl.ds(pl.multiple_of(i * ROWS, ROWS), ROWS)

        @pl.when(i + 1 < blocks)
        def _():
            stream(hidden_in, i + 1, False)

        mixed_grad = RESIDUAL_SCALE * dot_nt(grad[rows, :], w_down[...])
        ggrad = (mixed_grad * a_v[rows, :].astype(F32)).astype(BF16)
        ugrad = (mixed_grad * b_v[rows, :].astype(F32)).astype(BF16)
        a_v[rows, :] = ggrad
        b_v[rows, :] = ugrad
        normed_grad = dot_nt(ggrad, w_gate[...]) + dot_nt(ugrad, w_up[...])
        stream(hidden_in, i, True)

        hidden = hid_stage[lax.rem(i, 2)].astype(F32)
        r2 = lax.rsqrt(jnp.mean(hidden * hidden, axis=-1, keepdims=True) + EPSILON)
        gain_own[0:1, :] += jnp.sum(normed_grad * (hidden * r2), axis=0, keepdims=True)
        weighted = normed_grad * mlp_gain
        mean = jnp.mean(weighted * hidden, axis=-1, keepdims=True)
        piece = r2 * weighted - hidden * (r2 * r2 * r2 * mean)
        for c in range(n):
            part[c, rows, :] = piece[:, c * own_width : (c + 1) * own_width].astype(BF16)

        @pl.when(i == blocks // 2 - 1)
        def _():
            first[0].start()

        @pl.when(i == blocks - 2)
        def _():
            down_sum.advance(1)
            first[0].pass_on()

        return 0

    lax.fori_loop(0, blocks, mlp_block, 0)
    first[1].start()
    normed2_load = load(normed2_in, grad, 8)
    normed2_load.wait()

    def columns_times(right, out, low, high):
        def block(j, _):
            lanes = pl.ds(pl.multiple_of(j * ROWS, ROWS), ROWS)
            out[lanes, :] = dot_tn(grad[:, lanes], right[...]).astype(BF16)
            return 0

        lax.fori_loop(low, high, block, 0)

    first[0].late()
    columns_times(a_v, w_gate, 0, width // ROWS)
    gate_sum.start()
    first[1].pass_on()
    columns_times(b_v, w_up, 0, width // ROWS // 2)
    first[1].late()
    columns_times(b_v, w_up, width // ROWS // 2, width // ROWS)
    down_sum.advance(2)

    att_loads = [load(att_in.at[c], grad.at[:, pl.ds(c * own, own)], c) for c in range(n)]
    own_grad = load(grad_in.at[:, pl.ds(pl.multiple_of(me * own_width, LANES), own_width)], b_v.at[:, pl.ds(LANES, own_width)], 8)
    q_load = load(q_in, a_v.at[:, pl.ds(0, own)], 9)
    k_load = load(k_in, a_v.at[:, pl.ds(own, LANES)], 10)
    v_load = load(v_in, a_v.at[:, pl.ds(own + LANES, LANES)], 11)
    lse_load = load(lse_in, lse, 12)
    cos_load = load(cos_in, cos, 13)
    sin_load = load(sin_in, sin, 14)
    own_grad.wait()

    def begin(i, _):
        rows = pl.ds(pl.multiple_of(i * ROWS, ROWS), ROWS)
        hidden_grad[rows, :] = b_v[rows, LANES : LANES + own_width].astype(F32) + part[me, rows, :].astype(F32)
        return 0

    lax.fori_loop(0, blocks, begin, 0)
    for side in range(2):
        first[side].finish(hidden_grad.at[pl.ds(side * part_rows, part_rows)])
        first[side].drain()

    def branch_block(i, _):
        rows = pl.ds(pl.multiple_of(i * ROWS, ROWS), ROWS)
        branch = (RESIDUAL_SCALE * hidden_grad[rows, :]).astype(BF16)
        b_v[rows, LANES : LANES + own_width] = branch
        for c in range(n):
            part[c, rows, :] = dot_nt(branch, w_attn[c * own : (c + 1) * own, columns:]).astype(BF16)

        @pl.when(i == blocks // 2 - 1)
        def _():
            second[0].start()

        return 0

    lax.fori_loop(0, blocks, branch_block, 0)
    second[1].start()
    second[0].pass_on()
    gate_sum.advance(1)
    for copy in att_loads:
        copy.wait()
    heads_per_shard = rows_shard // own
    for c in range(n):
        place = out_block_of(c // heads_per_shard).at[pl.ds((c % heads_per_shard) * own, own)]
        place[...] = dot_tn(grad[:, c * own : (c + 1) * own], b_v[:, LANES : LANES + own_width]).astype(BF16)
    second[1].pass_on()
    second[0].late()
    normed_load = load(normed_in, grad, 15)
    down_sum.take(last)
    up_sum.start()
    second[1].late()
    second[0].finish(part.at[me, pl.ds(0, part_rows)])
    down_give = give(0, down_sum, down_all)
    gate_sum.advance(2)

    for copy in (q_load, k_load, v_load, lse_load, cos_load, sin_load):
        copy.wait()
    dk_sum[...] = jnp.zeros_like(dk_sum)
    dv_sum[...] = jnp.zeros_like(dv_sum)
    first_len = length_ref[0]
    dq_at = own + 2 * LANES

    def attend_pair(side, pair, _):
        lanes = pl.ds(pl.multiple_of(pair * LANES, LANES), LANES)
        dq_lanes = pl.ds(pl.multiple_of(dq_at + pair * LANES, LANES), LANES)
        for block in range(side * (blocks // 2), (side + 1) * (blocks // 2)):
            rows = pl.ds(block * ROWS, ROWS)
            end = (block + 1) * ROWS
            bias = mask_bias(first_len, block * ROWS, ROWS, end)
            query, grads = a_v[rows, lanes], part[me, rows, lanes]
            low = low_half(query.shape)
            keys, values = a_v[:end, own : own + LANES], a_v[:end, own + LANES : own + 2 * LANES]
            parts = []
            for head in range(2):
                chosen = low if head == 0 else jnp.logical_not(low)
                own_query = jnp.where(chosen, query, jnp.zeros_like(query))
                own_grads = jnp.where(chosen, grads, jnp.zeros_like(grads))
                scores = dot_nt(own_query, keys) + bias
                probs = jnp.exp(scores - lse[pair, rows, head : head + 1])
                prob_grad = dot_nt(own_grads, values)
                delta = jnp.sum(probs * prob_grad, axis=-1, keepdims=True)
                score_grad = (probs * (prob_grad - delta)).astype(BF16)
                parts.append(dot_nn(score_grad, keys))
                dk_sum[:end, :] += dot_tn(score_grad, own_query)
                dv_sum[:end, :] += dot_tn(probs.astype(BF16), own_grads)
            dq = jnp.where(low_half(parts[0].shape), parts[0], parts[1]) * SCORE_SCALE
            a_v[rows, dq_lanes] = (dq * cos[rows, :] - swap_halves(dq) * sin[rows, :]).astype(BF16)

        if side:

            @pl.when(pair == 0)
            def _():
                down_give.pass_on()
                up_sum.advance(1)

        return 0

    lax.fori_loop(0, pairs, functools.partial(attend_pair, 0), 0)
    second[1].finish(part.at[me, pl.ds(part_rows, part_rows)])
    lax.fori_loop(0, pairs, functools.partial(attend_pair, 1), 0)
    dk = dk_sum[...]
    dk = dk + pltpu.roll(dk, HEAD_SIZE, 1)
    dk = dk * cos[...] - swap_halves(dk) * sin[...]
    dv = dv_sum[...]
    dv = dv + pltpu.roll(dv, HEAD_SIZE, 1)
    b_v[:, :LANES] = jnp.where(low_half(dk.shape), dk, dv).astype(BF16)
    down_give.late()
    gate_sum.take(last)
    gate_give = give(1, gate_sum, gate_all)
    up_sum.advance(2)
    out_sum.start()

    normed_load.wait()
    dq_end = dq_at + own
    for d in range(planes):
        for j in range(rows_shard // ROWS):
            lanes = slice(d * rows_shard + j * ROWS, d * rows_shard + (j + 1) * ROWS)
            place = qkv_block_of(d).at[pl.ds(j * ROWS, ROWS)]
            place[:, :own] = dot_tn(grad[:, lanes], a_v[:, dq_at:dq_end]).astype(BF16)
            place[:, own:] = dot_tn(grad[:, lanes], b_v[:, :LANES]).astype(BF16)
    gate_give.pass_on()
    out_sum.advance(1)
    qkv_sum.start()

    stream(x_in, jnp.int32(0), False)

    def token_block(i, _):
        rows = pl.ds(pl.multiple_of(i * ROWS, ROWS), ROWS)

        @pl.when(i + 1 < blocks)
        def _():
            stream(x_in, i + 1, False)

        normed_grad = dot_nt(a_v[rows, dq_at:dq_end], w_attn[:, :own]) + dot_nt(b_v[rows, :LANES], w_attn[:, own:columns])
        stream(x_in, i, True)
        x = hid_stage[lax.rem(i, 2)].astype(F32)
        r1 = lax.rsqrt(jnp.mean(x * x, axis=-1, keepdims=True) + EPSILON)
        gain_own[1:2, :] += jnp.sum(normed_grad * (x * r1), axis=0, keepdims=True)
        weighted = normed_grad * attn_gain
        mean = jnp.mean(weighted * x, axis=-1, keepdims=True)
        piece = r1 * weighted - x * (r1 * r1 * r1 * mean)
        for c in range(n):
            lanes = slice(c * own_width, (c + 1) * own_width)
            mine = jnp.where(me == c, hidden_grad[rows, :], 0.0)
            grad[rows, lanes] = (piece[:, lanes] + mine).astype(BF16)
        return 0

    lax.fori_loop(0, blocks, token_block, 0)

    def token_rows(c):
        return grad.at[pl.ds(pl.multiple_of(c * per_device, per_device), per_device)]

    third = scatter(4, token_rows, near3, far3, [hid_stage.at[i, pl.ds(0, per_device)] for i in range(2)])
    third.start()
    gain_give = spread(5, gain_own, gain_all)
    gain_mine = load(gain_own, gain_all.at[me], 21)
    gain_give.start()
    gate_give.late()
    third.pass_on()
    gain_give.pass_on()
    out_sum.advance(2)
    third.late()
    gain_give.finish()
    gain_mine.wait()
    gain_give.drain()
    gain_own[...] = sum(gain_all[c] for c in range(n))
    gain_sum.start()
    token_out[...] = token_rows(me)[...].astype(F32)
    qkv_sum.advance(1)
    third.finish(token_out)
    up_sum.take(last)
    up_give = give(2, up_sum, up_all)
    gain_sum.advance(1)
    out_sum.take(last)
    out_give = give(3, out_sum, out_all)
    qkv_sum.advance(2)
    gain_sum.advance(2)
    up_give.pass_on()
    out_give.pass_on()
    up_give.late()
    gain_sum.take(last)
    gain_out[...] = gain_block_of(plane)[...]
    qkv_sum.take(last)
    qkv_give = give(4, qkv_sum, qkv_all)
    out_give.late()
    qkv_give.pass_on()
    qkv_give.late()
    for out, mine in spreads:
        out.finish()
        out.drain()
        mine.wait()
    for s in (*second, third):
        s.drain()
    for s in (down_sum, gate_sum, up_sum, out_sum, qkv_sum, gain_sum):
        s.drain()


def backward(n, planes, heads, lengths, grad, saved, weights, cos, sin):
    x, normed, q_rot, k_rot, v_rows, lse, att_all, hidden, normed2, a, b, mixed = saved
    w_attn, w_gate, w_up, w_down, gains = weights
    total, width = grad.shape
    own = heads * HEAD_SIZE
    own_width = width // n
    own_ff = a.shape[1]
    rows_shard = width // planes
    slab = own_ff // planes
    columns = own + LANES
    chips = n // 2
    per_device = total // n
    col, row = (chips, total, own_width), (chips, per_device, width)
    outs = [
        ((per_device, width), F32),
        ((8, rows_shard), F32),
        ((n, slab, width), BF16),
        ((n, rows_shard, own_ff), BF16),
        ((n, rows_shard, own_ff), BF16),
        ((n, rows_shard, own_width), BF16),
        ((n, rows_shard, columns), BF16),
        (col, BF16),
        (col, BF16),
        (col, BF16),
        (col, BF16),
        (row, BF16),
        (row, BF16),
        ((planes + 1, slab, width), BF16),
        ((planes + 1, rows_shard, own_ff), BF16),
        ((planes + 1, rows_shard, own_ff), BF16),
        ((planes + 1, rows_shard, own_width), BF16),
        ((planes + 1, rows_shard, columns), BF16),
    ]
    scratch = [
        (w_attn.shape, BF16),
        (w_gate.shape, BF16),
        (w_up.shape, BF16),
        (w_down.shape, BF16),
        (w_down.shape, BF16),
        (gains.shape, F32),
        ((total, width), BF16),
        ((total, own_ff), BF16),
        ((total, own_ff), BF16),
        ((n, total, own_width), BF16),
        ((2, ROWS, width), BF16),
        ((rows_shard, own_ff), BF16),
        ((slab, width), BF16),
        ((total, own_width), BF16),
        ((total, own_width), F32),
        (lse.shape, F32),
        (cos.shape, F32),
        (sin.shape, F32),
        ((total, LANES), F32),
        ((total, LANES), F32),
        ((8, width), F32),
        ((n, 8, width), F32),
        ((planes + 1, 8, rows_shard), F32),
        ((8, rows_shard), F32),
    ]
    steps = planes - 1
    dma = pltpu.SemaphoreType.DMA
    anywhere = pl.BlockSpec(memory_space=pl.ANY)
    vmem = pl.BlockSpec(memory_space=pltpu.VMEM)
    return pl.pallas_call(
        functools.partial(backward_kernel, n, planes, heads),
        in_specs=[pl.BlockSpec(memory_space=pltpu.SMEM)] + [anywhere] * 20,
        out_specs=[vmem] * 2 + [anywhere] * (len(outs) - 2),
        out_shape=[jax.ShapeDtypeStruct(*o) for o in outs],
        scratch_shapes=[pltpu.VMEM(*s) for s in scratch]
        + [
            dma((6, 2, steps)),
            dma((6, 2, steps)),
            dma((5, 10)),
            dma((5, 10)),
            dma((6, n)),
            dma((6, n)),
            dma((24,)),
            dma((2,)),
            dma,
            dma((2,)),
        ],
        compiler_params=pltpu.CompilerParams(
            vmem_limit_bytes=60 * 1024 * 1024, collective_id=2, has_side_effects=True
        ),
        cost_estimate=pl.CostEstimate(
            flops=16 * total * width * own_ff, bytes_accessed=100 * 1024 * 1024, transcendentals=0
        ),
        name="backward",
    )(
        lengths,
        grad,
        mixed,
        a,
        b,
        hidden,
        normed2,
        normed,
        x,
        att_all,
        q_rot,
        k_rot,
        v_rows,
        lse,
        cos,
        sin,
        w_attn,
        w_gate,
        w_up,
        w_down,
        gains,
    )[:7]


def kernel_fits(n, planes, total, width, own_ff):
    held = 4 * width * own_ff + 2 * total * width + 2 * total * own_ff
    return planes == 4 and total % (2 * ROWS) == 0 and n == 8 and own_ff // planes >= total // n and n * own_ff == planes * width and 2 * held < 44 * 1024 * 1024 and (own_ff // planes) % LANES == 0


def own_columns(array, index, width):
    return lax.dynamic_slice_in_dim(array, index * width, width, axis=1)


def after(value, *others):
    return lax.optimization_barrier((value, *others))[0]


def local(
    tokens,
    lengths,
    deal,
    attn_gain,
    query_weight,
    key_matrix,
    value_matrix,
    out_weight,
    mlp_gain,
    gate_weight,
    up_weight,
    down_weight,
    cotangent,
):
    n_ctx = lax.axis_size("ctx")
    n_fsdp = lax.axis_size("fsdp")
    me = lax.axis_index("ctx")
    me_array = me.astype(jnp.int32).reshape(1)
    per_device, width = tokens.shape[1], tokens.shape[2]
    total = per_device * n_ctx
    block_rows = per_device // n_ctx
    heads = QUERY_HEADS // n_ctx
    sharing = n_ctx // KEY_VALUE_HEADS
    own_width = width // n_ctx
    ff = gate_weight.shape[1]
    slab = ff // (n_fsdp * n_ctx)
    own_ff = slab * n_fsdp
    rows_shard = query_weight.shape[0]

    kv_head = me // sharing
    split = heads * HEAD_SIZE
    attn_shard = jnp.concatenate(
        [
            own_columns(query_weight, me, split),
            own_columns(key_matrix, kv_head, HEAD_SIZE),
            own_columns(value_matrix, kv_head, HEAD_SIZE),
            own_columns(out_weight, me, own_width),
        ],
        axis=1,
    )

    def ff_columns(array):
        return jnp.concatenate([own_columns(array, f * n_ctx + me, slab) for f in range(n_fsdp)], axis=1)

    gain_shard = jnp.tile(jnp.concatenate([attn_gain, mlp_gain]).astype(F32)[None], (8, 1))

    first_len = lengths[0, 0]
    given = jnp.arange(total, dtype=jnp.int32)
    position = given - jnp.where(given >= first_len, first_len, 0)
    freq_index = jnp.arange(HEAD_SIZE // 2, dtype=F32)
    inverse = ROPE_BASE ** (-2.0 * freq_index / HEAD_SIZE)
    turns = jnp.tile(inverse, 4)
    sign = jnp.tile(jnp.repeat(jnp.array([-1.0, 1.0], F32), HEAD_SIZE // 2), 2)
    angles = position.astype(F32)[:, None] * turns[None, :]
    cos_table = jnp.cos(angles)
    sin_table = jnp.sin(angles) * sign[None, :]

    deal_rows = deal[0]
    slot_ids = jnp.arange(n_ctx, dtype=jnp.int32)
    dealt_of_given = (deal_rows * n_ctx + slot_ids[:, None]).reshape(-1)
    matched = deal_rows[:, :, None] == slot_ids[None, None, :]
    source_slot = jnp.sum(jnp.where(matched, slot_ids[None, :, None], 0), axis=1)
    given_of_dealt = (slot_ids[:, None] * n_ctx + source_slot).T.reshape(-1)

    def reorder(array, table):
        blocks = array.reshape(n_ctx * n_ctx, block_rows, array.shape[1])
        return jnp.take(blocks, table, axis=0, mode="clip").reshape(array.shape)

    ff_weights = gate_weight, up_weight, down_weight
    if slab % LANES:
        ff_weights = (
            ff_columns(gate_weight),
            ff_columns(up_weight),
            lax.dynamic_slice_in_dim(down_weight, me * slab, slab, axis=0),
        )

    cotangent_all = lax.all_gather(cotangent[0], "ctx", axis=0, tiled=True)
    (
        x, normed, q_rot, k_rot, v_rows, lse, attended_all, hidden_all, normed2, a, b, both, w_attn, w_gate, w_up, w_down, gains_all,
    ) = forward(
        n_ctx,
        n_fsdp,
        heads,
        slab,
        lengths[0],
        tokens[0],
        attn_shard,
        *ff_weights,
        gain_shard,
        cos_table,
        sin_table,
    )
    w_qkv, w_out = w_attn[:, : split + 2 * HEAD_SIZE], w_attn[:, split + 2 * HEAD_SIZE :]
    gains = gains_all.reshape(n_fsdp, 8, 2, rows_shard)[:, 0].transpose(1, 0, 2).reshape(2, 1, width)
    grad_result = reorder(cotangent_all, dealt_of_given)

    result_part = result_rows(me_array, reorder(both, given_of_dealt), w_down)
    activations = lax.psum_scatter(
        result_part, "ctx", scatter_dimension=0, tiled=True
    )[None]

    if kernel_fits(n_ctx, n_fsdp, total, width, own_ff):
        token_grad, gain_rows, down_part, gate_part, up_part, out_part, qkv_part = backward(
            n_ctx,
            n_fsdp,
            heads,
            lengths[0],
            grad_result,
            (x, normed, q_rot, k_rot, v_rows, lse, attended_all, hidden_all, normed2, a, b, both),
            (w_attn, w_gate, w_up, w_down, gains_all),
            cos_table,
            sin_table,
        )
        token_grad = token_grad[None]
        own_gains = gain_rows[1::-1]
    else:
        mlp_grad = (RESIDUAL_SCALE * grad_result.astype(F32)).astype(BF16)

        def settle(left, right):
            return lax.psum_scatter(dot_tn(left, right).astype(BF16), "fsdp", scatter_dimension=0, tiled=True)

        down_part = settle(both[:, :own_ff], mlp_grad)
        ggrad, ugrad, hidden_part, mlp_gain_part = mlp_backward(
            n_ctx, mlp_grad, a, b, hidden_all, gains[1], w_gate, w_up, w_down
        )
        hidden_sum = lax.psum_scatter(hidden_part, "ctx", scatter_dimension=0, tiled=False)
        gate_part = settle(normed2, ggrad)
        up_part = settle(normed2, ugrad)
        hidden_grad, branch_grad, attended_part = branch_backward(
            hidden_sum, own_columns(grad_result, me, own_width), w_out, n_ctx
        )
        attended_grad = lax.psum_scatter(attended_part, "ctx", scatter_dimension=0, tiled=False)
        out_part = lax.psum_scatter(
            jnp.einsum("ctk,to->cko", attended_all, branch_grad, preferred_element_type=F32)
            .astype(BF16)
            .reshape(width, own_width),
            "fsdp",
            scatter_dimension=0,
            tiled=True,
        )
        dq, dkv = attention_backward(attended_grad, q_rot, k_rot, v_rows, lse, cos_table, sin_table, lengths[0])
        qkv_part = settle(normed, jnp.concatenate([dq, dkv], axis=1))
        token_part, attn_gain_part = token_backward(me_array, dq, dkv, w_qkv, x, gains[0], hidden_grad)
        token_grad = lax.psum_scatter(token_part, "ctx", scatter_dimension=0, tiled=True).astype(F32)[None]

        gain_parts = jnp.concatenate([attn_gain_part, mlp_gain_part], axis=0)
        step = 1
        while step < n_ctx:
            gain_parts = gain_parts + lax.ppermute(gain_parts, "ctx", [(c, c ^ step) for c in range(n_ctx)])
            step *= 2
        gain_rows = gain_parts.reshape(2, n_fsdp, rows_shard).transpose(1, 0, 2).reshape(n_fsdp, 2 * rows_shard)
        own_gains = lax.psum_scatter(gain_rows, "fsdp", scatter_dimension=0, tiled=True).reshape(2, rows_shard)
        down_part, gate_part, up_part, out_part, qkv_part = [
            lax.all_gather(p, "ctx", axis=0, tiled=False) for p in (down_part, gate_part, up_part, out_part, qkv_part)
        ]

    if slab % LANES == 0 and sharing == 1 and heads % 4 == 0:
        gate_grad, up_grad, down_grad, out_grad, query_grad, key_grad, value_grad = finish(
            slab, gate_part, up_part, down_part.reshape(n_ctx * slab, width), out_part, qkv_part
        )
    else:
        down_grad = down_part.reshape(n_ctx * slab, width).astype(F32)
        if slab % LANES == 0:
            gate_grad = spread_columns(gate_part, slab, n_fsdp)
            up_grad = spread_columns(up_part, slab, n_fsdp)
        else:

            def ff_whole(part):
                pieces = part.reshape(n_ctx, rows_shard, n_fsdp, slab)
                return pieces.transpose(1, 2, 0, 3).reshape(rows_shard, ff).astype(F32)

            gate_grad = ff_whole(gate_part)
            up_grad = ff_whole(up_part)
        out_grad = spread_columns(out_part, own_width, 1)
        qkv_all = qkv_part
        query_grad = spread_columns(qkv_all, split, 1)

        def shared_heads(pieces):
            pieces = pieces.astype(F32).reshape(KEY_VALUE_HEADS, sharing, rows_shard, HEAD_SIZE).sum(axis=1)
            return pieces.transpose(1, 0, 2).reshape(rows_shard, KEY_VALUE_HEADS * HEAD_SIZE)

        key_grad = shared_heads(qkv_all[:, :, split : split + HEAD_SIZE])
        value_grad = shared_heads(qkv_all[:, :, split + HEAD_SIZE :])

    return (
        activations,
        token_grad,
        own_gains[0],
        query_grad,
        key_grad,
        value_grad,
        out_grad,
        own_gains[1],
        gate_grad,
        up_grad,
        down_grad,
    )


def solution(mesh):
    rows = P("fsdp", None)
    block = P("fsdp", "ctx", None)
    gain = P("fsdp")
    return jax.shard_map(
        local,
        mesh=mesh,
        in_specs=(block, rows, P("fsdp", None, None), gain, rows, rows, rows, rows, gain, rows, rows, rows, block),
        out_specs=(block, block, gain, rows, rows, rows, rows, gain, rows, rows, rows),
        check_vma=False,
    )
```

```python
import functools

import jax
import jax.numpy as jnp
from jax import lax
from jax.experimental import pallas as pl
from jax.experimental.pallas import tpu as pltpu
from jax.sharding import PartitionSpec as P

QUERY_HEADS = 32
KEY_VALUE_HEADS = 8
HEAD_SIZE = 64
EPSILON = 1e-05
ROPE_BASE = 10000000.0
SCORE_SCALE = 0.015625
RESIDUAL_SCALE = 0.22
NEGATIVE_BIG = -1e30
LANES = 128
ROWS = 256
BF16 = jnp.bfloat16
F32 = jnp.float32
VMEM_LIMIT = 59 * 1024 * 1024


def dot_nn(a, b):
    return lax.dot_general(a, b, (((1,), (0,)), ((), ())), preferred_element_type=F32)


def dot_nt(a, b):
    return lax.dot_general(a, b, (((1,), (1,)), ((), ())), preferred_element_type=F32)


def dot_tn(a, b):
    return lax.dot_general(a, b, (((0,), (0,)), ((), ())), preferred_element_type=F32)


def swap_halves(x):
    lane = lax.broadcasted_iota(jnp.int32, x.shape, 1)
    first = lax.rem(lane, HEAD_SIZE) < HEAD_SIZE // 2
    return jnp.where(first, pltpu.roll(x, LANES - HEAD_SIZE // 2, 1), pltpu.roll(x, HEAD_SIZE // 2, 1))


def low_half(shape):
    return lax.broadcasted_iota(jnp.int32, shape, 1) < HEAD_SIZE


def mask_bias(first_len, row0, rows, cols):
    query = row0 + lax.broadcasted_iota(jnp.int32, (rows, cols), 0)
    key = lax.broadcasted_iota(jnp.int32, (rows, cols), 1)
    start = jnp.where(query >= first_len, first_len, 0)
    return jnp.where((key <= query) & (key >= start), 0.0, NEGATIVE_BIG)


def attention_backward_kernel(length_ref, g_ref, q_ref, k_ref, v_ref, lse_ref, cos_ref, sin_ref, dq_ref, dkv_ref, dk_sum, dv_sum):
    pair = pl.program_id(0)
    tokens = q_ref.shape[0]

    @pl.when(pair == 0)
    def _():
        dk_sum[...] = jnp.zeros_like(dk_sum)
        dv_sum[...] = jnp.zeros_like(dv_sum)

    first_len = length_ref[0]
    for block in range(tokens // ROWS):
        rows = pl.ds(block * ROWS, ROWS)
        end = (block + 1) * ROWS
        bias = mask_bias(first_len, block * ROWS, ROWS, end)
        query, grad = q_ref[rows, :], g_ref[rows, :]
        low = low_half(query.shape)
        keys, values = k_ref[:end, :], v_ref[:end, :]
        parts = []
        for half in range(2):
            chosen = low if half == 0 else jnp.logical_not(low)
            own_query = jnp.where(chosen, query, jnp.zeros_like(query))
            own_grad = jnp.where(chosen, grad, jnp.zeros_like(grad))
            scores = dot_nt(own_query, keys) + bias
            probs = jnp.exp(scores - lse_ref[0, rows, half : half + 1])
            prob_grad = dot_nt(own_grad, values)
            delta = jnp.sum(probs * prob_grad, axis=-1, keepdims=True)
            score_grad = (probs * (prob_grad - delta)).astype(BF16)
            parts.append(dot_nn(score_grad, keys))
            dk_sum[:end, :] += dot_tn(score_grad, own_query)
            dv_sum[:end, :] += dot_tn(probs.astype(BF16), own_grad)
        dq = jnp.where(low_half(parts[0].shape), parts[0], parts[1]) * SCORE_SCALE
        dq_ref[rows, :] = (dq * cos_ref[rows, :] - swap_halves(dq) * sin_ref[rows, :]).astype(BF16)

    @pl.when(pair == pl.num_programs(0) - 1)
    def _():
        dk = dk_sum[...]
        dk = dk + pltpu.roll(dk, HEAD_SIZE, 1)
        dk = dk * cos_ref[...] - swap_halves(dk) * sin_ref[...]
        dv = dv_sum[...]
        dv = dv + pltpu.roll(dv, HEAD_SIZE, 1)
        dkv_ref[...] = jnp.where(low_half(dk.shape), dk, dv).astype(BF16)


def attention_backward(grads, q_rot, k_rot, v_rows, lse, cos, sin, lengths):
    tokens = q_rot.shape[0]
    pairs = q_rot.shape[1] // LANES
    one = pl.BlockSpec((tokens, LANES), lambda j: (0, 0))
    each = pl.BlockSpec((tokens, LANES), lambda j: (0, j))
    return pl.pallas_call(
        attention_backward_kernel,
        grid=(pairs,),
        in_specs=[
            pl.BlockSpec(memory_space=pltpu.SMEM),
            each,
            each,
            one,
            one,
            pl.BlockSpec((1, tokens, LANES), lambda j: (j, 0, 0)),
            one,
            one,
        ],
        out_specs=[each, one],
        out_shape=[
            jax.ShapeDtypeStruct((tokens, pairs * LANES), BF16),
            jax.ShapeDtypeStruct((tokens, LANES), BF16),
        ],
        scratch_shapes=[pltpu.VMEM((tokens, LANES), F32), pltpu.VMEM((tokens, LANES), F32)],
        compiler_params=pltpu.CompilerParams(vmem_limit_bytes=VMEM_LIMIT),
        cost_estimate=pl.CostEstimate(
            flops=10 * tokens * tokens * LANES * pairs,
            bytes_accessed=12 * tokens * pairs * LANES,
            transcendentals=tokens * tokens * pairs,
        ),
        name="attend_back",
    )(lengths, grads, q_rot, k_rot, v_rows, lse, cos, sin)


def row_block(width):
    return pl.BlockSpec((ROWS, width), lambda i: (i, 0))


def fixed(*shape):
    return pl.BlockSpec(shape, lambda i: (0,) * len(shape))


def params():
    return pltpu.CompilerParams(vmem_limit_bytes=VMEM_LIMIT)


def cost(flops, *arrays):
    moved = sum(a.size * a.dtype.itemsize for a in arrays)
    return pl.CostEstimate(flops=flops, bytes_accessed=moved, transcendentals=0)


def mlp_back_kernel(
    grad_ref, a_ref, b_ref, hidden_ref, gain_ref, gate_ref, up_ref, down_ref, ggrad_ref, ugrad_ref, part_ref, gain_out
):
    mixed_grad = dot_nt(grad_ref[...], down_ref[...])
    ggrad = (mixed_grad * a_ref[...].astype(F32)).astype(BF16)
    ugrad = (mixed_grad * b_ref[...].astype(F32)).astype(BF16)
    ggrad_ref[...] = ggrad
    ugrad_ref[...] = ugrad
    normed_grad = dot_nt(ggrad, gate_ref[...]) + dot_nt(ugrad, up_ref[...])
    hidden = hidden_ref[...].astype(F32)
    r2 = lax.rsqrt(jnp.mean(hidden * hidden, axis=-1, keepdims=True) + EPSILON)
    gain_part = jnp.sum(normed_grad * (hidden * r2), axis=0, keepdims=True)

    @pl.when(pl.program_id(0) == 0)
    def _():
        gain_out[...] = jnp.zeros_like(gain_out)

    gain_out[...] += gain_part
    weighted = normed_grad * gain_ref[...]
    mean = jnp.mean(weighted * hidden, axis=-1, keepdims=True)
    part = r2 * weighted - hidden * (r2 * r2 * r2 * mean)
    own = part_ref.shape[2]
    for c in range(part_ref.shape[0]):
        part_ref[c] = part[:, c * own : (c + 1) * own].astype(BF16)


def mlp_backward(n, mlp_grad, a, b, hidden_all, gain, w_gate, w_up, w_down):
    total, width = hidden_all.shape
    own = width // n
    own_ff = w_gate.shape[1]
    narrow = jax.ShapeDtypeStruct((total, own_ff), BF16)
    planes = pl.BlockSpec((n, ROWS, own), lambda i: (0, i, 0))
    return pl.pallas_call(
        mlp_back_kernel,
        grid=(total // ROWS,),
        in_specs=[
            row_block(width),
            row_block(own_ff),
            row_block(own_ff),
            row_block(width),
            fixed(1, width),
            fixed(width, own_ff),
            fixed(width, own_ff),
            fixed(own_ff, width),
        ],
        out_specs=[row_block(own_ff), row_block(own_ff), planes, fixed(1, width)],
        out_shape=[narrow, narrow, jax.ShapeDtypeStruct((n, total, own), BF16), jax.ShapeDtypeStruct((1, width), F32)],
        compiler_params=params(),
        cost_estimate=cost(6 * total * width * own_ff, mlp_grad, hidden_all, hidden_all, w_gate, w_up, w_down, a, b, a, b),
        name="mlp_backward",
    )(mlp_grad, a, b, hidden_all, gain, w_gate, w_up, w_down)


def branch_kernel(part_ref, grad_ref, w_ref, hidden_ref, branch_ref, out_ref):
    hidden_grad = part_ref[...].astype(F32) + grad_ref[...].astype(F32)
    hidden_ref[...] = hidden_grad
    branch = (RESIDUAL_SCALE * hidden_grad).astype(BF16)
    branch_ref[...] = branch
    own = out_ref.shape[2]
    for c in range(out_ref.shape[0]):
        out_ref[c] = dot_nt(branch, w_ref[c]).astype(BF16)


def branch_backward(hidden_part, grad_own, w_out, n):
    total, own_width = hidden_part.shape
    own = w_out.shape[0] // n
    w_heads = w_out.reshape(n, own, own_width)
    return pl.pallas_call(
        branch_kernel,
        grid=(total // ROWS,),
        in_specs=[row_block(own_width), row_block(own_width), fixed(n, own, own_width)],
        out_specs=[row_block(own_width), row_block(own_width), pl.BlockSpec((n, ROWS, own), lambda i: (0, i, 0))],
        out_shape=[
            jax.ShapeDtypeStruct((total, own_width), F32),
            jax.ShapeDtypeStruct((total, own_width), BF16),
            jax.ShapeDtypeStruct((n, total, own), BF16),
        ],
        compiler_params=params(),
        cost_estimate=cost(2 * total * own_width * own * n, hidden_part, hidden_part, hidden_part, w_out),
        name="branch_backward",
    )(hidden_part, grad_own, w_heads)


def token_kernel(me_ref, dq_ref, dkv_ref, w_ref, x_ref, gain_ref, hidden_ref, part_ref, gain_out):
    split = dq_ref.shape[1]
    normed_grad = dot_nt(dq_ref[...], w_ref[:, :split]) + dot_nt(dkv_ref[...], w_ref[:, split:])
    x = x_ref[...].astype(F32)
    r1 = lax.rsqrt(jnp.mean(x * x, axis=-1, keepdims=True) + EPSILON)

    @pl.when(pl.program_id(0) == 0)
    def _():
        gain_out[...] = jnp.zeros_like(gain_out)

    gain_out[...] += jnp.sum(normed_grad * (x * r1), axis=0, keepdims=True)
    weighted = normed_grad * gain_ref[...]
    mean = jnp.mean(weighted * x, axis=-1, keepdims=True)
    part = r1 * weighted - x * (r1 * r1 * r1 * mean)
    own_width = hidden_ref.shape[1]
    for c in range(part.shape[1] // own_width):
        piece = part[:, c * own_width : (c + 1) * own_width]
        piece = piece + jnp.where(me_ref[0] == c, hidden_ref[...], 0.0)
        part_ref[:, c * own_width : (c + 1) * own_width] = piece.astype(BF16)


def token_backward(me, dq, dkv, w_qkv, x, gain, hidden_grad):
    total, width = x.shape
    own_width = hidden_grad.shape[1]
    return pl.pallas_call(
        token_kernel,
        grid=(total // ROWS,),
        in_specs=[
            pl.BlockSpec(memory_space=pltpu.SMEM),
            row_block(dq.shape[1]),
            row_block(dkv.shape[1]),
            fixed(*w_qkv.shape),
            row_block(width),
            fixed(1, width),
            row_block(own_width),
        ],
        out_specs=[row_block(width), fixed(1, width)],
        out_shape=[jax.ShapeDtypeStruct((total, width), BF16), jax.ShapeDtypeStruct((1, width), F32)],
        compiler_params=params(),
        cost_estimate=cost(2 * total * width * w_qkv.shape[1], x, x, w_qkv, dq, dkv, hidden_grad),
        name="token_backward",
    )(me, dq, dkv, w_qkv, x, gain, hidden_grad)


def result_kernel(me_ref, rows_ref, w_ref, out_ref):
    depth = w_ref.shape[0]
    own = rows_ref.shape[1] - depth
    product = dot_nn(rows_ref[:, :depth], w_ref[...])
    hidden = rows_ref[:, depth:].astype(F32)
    for c in range(out_ref.shape[1] // own):
        lanes = slice(c * own, (c + 1) * own)
        mine = jnp.where(me_ref[0] == c, hidden, 0.0)
        out_ref[:, lanes] = (RESIDUAL_SCALE * (product[:, lanes] + mine)).astype(BF16)


def result_rows(me, rows, w_down):
    total, columns = rows.shape
    depth, width = w_down.shape
    out_shape = jax.ShapeDtypeStruct((total, width), BF16)
    return pl.pallas_call(
        result_kernel,
        grid=(total // ROWS,),
        in_specs=[pl.BlockSpec(memory_space=pltpu.SMEM), row_block(columns), fixed(depth, width)],
        out_specs=row_block(width),
        out_shape=out_shape,
        compiler_params=params(),
        cost_estimate=cost(2 * total * depth * width, rows, w_down, out_shape),
        name="result_rows",
    )(me, rows, w_down)


def finish_kernel(slab, gate_ref, up_ref, down_ref, out_ref, qkv_ref, gate_out, up_out, down_out, out_out, q_out, k_out, v_out):
    n = gate_ref.shape[0]
    for src, dst, piece in ((gate_ref, gate_out, slab), (up_ref, up_out, slab), (out_ref, out_out, out_ref.shape[2])):
        for c in range(n):
            for f in range(src.shape[2] // piece):
                at = (f * n + c) * piece
                dst[:, at : at + piece] = src[c, :, f * piece : (f + 1) * piece].astype(F32)
    down_out[...] = down_ref[...].astype(F32)
    split = qkv_ref.shape[2] - LANES
    for c in range(n):
        q_out[:, c * split : (c + 1) * split] = qkv_ref[c, :, :split].astype(F32)
    for pair in range(n // 2):
        even = qkv_ref[2 * pair, :, split:].astype(F32)
        odd = qkv_ref[2 * pair + 1, :, split:].astype(F32)
        low = low_half(even.shape)
        lanes = slice(pair * LANES, (pair + 1) * LANES)
        k_out[:, lanes] = jnp.where(low, even, pltpu.roll(odd, HEAD_SIZE, 1))
        v_out[:, lanes] = jnp.where(low, pltpu.roll(even, HEAD_SIZE, 1), odd)


def finish(slab, gate, up, down, out, qkv):
    n, rows, own_ff = gate.shape
    width = n * out.shape[2]
    steps = 16
    tile, down_tile = rows // steps, down.shape[0] // steps
    kv = n * HEAD_SIZE

    def by_device(columns):
        return pl.BlockSpec((n, tile, columns), lambda i: (0, i, 0))

    def flat(height, columns):
        return pl.BlockSpec((height, columns), lambda i: (i, 0))

    outs = [
        (flat(tile, n * own_ff), (rows, n * own_ff)),
        (flat(tile, n * own_ff), (rows, n * own_ff)),
        (flat(down_tile, width), down.shape),
        (flat(tile, width), (rows, width)),
        (flat(tile, width), (rows, width)),
        (flat(tile, kv), (rows, kv)),
        (flat(tile, kv), (rows, kv)),
    ]
    return pl.pallas_call(
        functools.partial(finish_kernel, slab),
        grid=(steps,),
        in_specs=[
            by_device(own_ff),
            by_device(own_ff),
            flat(down_tile, width),
            by_device(out.shape[2]),
            by_device(qkv.shape[2]),
        ],
        out_specs=[spec for spec, _ in outs],
        out_shape=[jax.ShapeDtypeStruct(shape, F32) for _, shape in outs],
        compiler_params=params(),
        cost_estimate=cost(0, gate, gate, gate, up, up, up, down, down, down),
        name="finish",
    )(gate, up, down, out, qkv)


def spread_kernel(in_ref, out_ref):
    slab = in_ref.shape[2]
    for c in range(in_ref.shape[0]):
        out_ref[:, c * slab : (c + 1) * slab] = in_ref[c].astype(F32)


def spread_columns(pieces, slab, groups):
    n, rows, _ = pieces.shape
    tile = 128
    out_shape = jax.ShapeDtypeStruct((rows, groups * n * slab), F32)
    return pl.pallas_call(
        spread_kernel,
        grid=(groups, rows // tile),
        in_specs=[pl.BlockSpec((n, tile, slab), lambda f, r: (0, r, f))],
        out_specs=pl.BlockSpec((tile, n * slab), lambda f, r: (r, f)),
        out_shape=out_shape,
        compiler_params=params(),
        cost_estimate=cost(0, pieces, out_shape),
        name="spread_columns",
    )(pieces)


MESH = pl.DeviceIdType.MESH


class Chain:
    def __init__(self, slot, planes, plane, send_sem, recv_sem):
        self.slot, self.planes, self.plane = slot, planes, plane
        self.send_sem, self.recv_sem = send_sem, recv_sem

    def copy(self, way, step, shard, to):
        return pltpu.make_async_remote_copy(
            src_ref=self.slot(shard),
            dst_ref=self.slot(shard),
            send_sem=self.send_sem.at[way, step],
            recv_sem=self.recv_sem.at[way, step],
            device_id={"fsdp": to},
            device_id_type=MESH,
        )

    def moves(self, step):
        p, last = self.plane, self.planes - 1
        return (
            (0, (p >= step) & (p < last), p - step, p + 1, p >= step + 1, p - 1 - step),
            (1, (p + step <= last) & (p > 0), p + step, p - 1, p + step + 1 <= last, p + 1 + step),
        )

    def start(self, step):
        for way, sends, shard, to, _, _ in self.moves(step):

            @pl.when(sends)
            def _(way=way, shard=shard, to=to):
                self.copy(way, step, shard, to).start()

    def arrive(self, step):
        for way, _, _, _, receives, shard in self.moves(step):

            @pl.when(receives)
            def _(way=way, shard=shard):
                self.copy(way, step, shard, self.plane).wait_recv()

    def advance(self, step):
        self.arrive(step - 1)
        self.start(step)

    def drain(self):
        for step in range(self.planes - 1):
            for way, sends, shard, to, _, _ in self.moves(step):

                @pl.when(sends)
                def _(way=way, shard=shard, to=to, step=step):
                    self.copy(way, step, shard, to).wait_send()


class Spread:
    def __init__(self, src, slot, n, me, send_sem, recv_sem):
        self.src, self.slot, self.n, self.me = src, slot, n, me
        self.send_sem, self.recv_sem = send_sem, recv_sem
        self.chips = n // 2
        self.chip, self.core = me // 2, lax.rem(me, 2)
        self.partner = me + 1 - 2 * self.core

    def at(self, k):
        return lax.rem(self.chip + k, self.chips) * 2 + self.core

    def copy(self, src, owner, sem, to):
        return pltpu.make_async_remote_copy(
            src_ref=src,
            dst_ref=self.slot(owner),
            send_sem=self.send_sem.at[sem],
            recv_sem=self.recv_sem.at[sem],
            device_id={"ctx": to},
            device_id_type=MESH,
        )

    def out(self, k):
        return self.copy(self.src, self.me, k, self.at(k))

    def relay(self, k):
        owner = self.at(self.chips - k) if k else self.me
        src = self.slot(owner) if k else self.src
        return self.copy(src, owner, self.chips + k, self.partner)

    def start(self):
        for k in range(1, self.chips):
            self.out(k).start()
        self.relay(0).start()

    def pass_on(self):
        for k in range(1, self.chips):
            self.copy(self.src, self.at(self.chips - k), k, self.me).wait_recv()
            self.relay(k).start()

    def late(self):
        pass

    def finish(self):
        other = 1 - 2 * self.core
        for k in range(self.chips):
            owner = (self.at(self.chips - k) if k else self.me) + other
            self.copy(self.slot(owner), owner, self.chips + k, self.me).wait_recv()

    def drain(self):
        for k in range(1, self.chips):
            self.out(k).wait_send()
        for k in range(self.chips):
            self.relay(k).wait_send()


class Spread4:
    def __init__(self, src, slot, n, me, send_sem, recv_sem):
        self.src, self.slot, self.me = src, slot, me
        self.send_sem, self.recv_sem = send_sem, recv_sem
        self.core = lax.rem(me, 2)
        self.other = 1 - self.core
        chip = me // 2
        self.near, self.side, self.far = square(chip)
        self.chip = chip
        self.half = src.shape[0] // 2

    def copy(self, src, dst, sem, to):
        return pltpu.make_async_remote_copy(
            src_ref=src,
            dst_ref=dst,
            send_sem=self.send_sem.at[sem],
            recv_sem=self.recv_sem.at[sem],
            device_id={"ctx": to},
            device_id_type=MESH,
        )

    def part(self, owner, which):
        return self.slot(owner).at[pl.ds(which * self.half, self.half)]

    def out(self, sem):
        chip = self.near if sem == 1 else self.side
        return self.copy(self.src, self.slot(self.me), sem, chip * 2 + self.core)

    def onward(self, sem):
        origin, to, which = (self.near, self.side, 0) if sem == 3 else (self.side, self.near, 1)
        owner = origin * 2 + self.core
        return self.copy(self.part(owner, which), self.part(owner, which), sem, to * 2 + self.core)

    def relay(self, k):
        owner = (self.chip, self.near, self.side, self.far)[k] * 2 + self.core
        src = self.slot(owner) if k else self.src
        return self.copy(src, self.slot(owner), 4 + k, self.chip * 2 + self.other)

    def start(self):
        self.out(1).start()
        self.out(2).start()
        self.relay(0).start()

    def pass_on(self):
        for k, chip in ((1, self.near), (2, self.side)):
            owner = chip * 2 + self.core
            self.copy(self.src, self.slot(owner), k, self.me).wait_recv()
            self.onward(3 if k == 1 else 0).start()
            self.relay(k).start()

    def late(self):
        owner = self.far * 2 + self.core
        for sem, which in ((3, 0), (0, 1)):
            self.copy(self.part(owner, which), self.part(owner, which), sem, self.me).wait_recv()
        self.relay(3).start()

    def finish(self):
        for k, chip in enumerate((self.chip, self.near, self.side, self.far)):
            owner = chip * 2 + self.other
            self.copy(self.slot(owner), self.slot(owner), 4 + k, self.me).wait_recv()

    def drain(self):
        for sem in (1, 2):
            self.out(sem).wait_send()
        for sem in (3, 0):
            self.onward(sem).wait_send()
        for k in range(4):
            self.relay(k).wait_send()


def square(chip):
    return chip + 1 - 2 * lax.rem(chip, 2), chip + 2 - 4 * (chip // 2), 3 - chip


def spread_over(n, src, *rest):
    return (Spread4 if n == 8 and src.shape[0] % 32 == 0 else Spread)(src, *rest)


def greet(n, planes, me, plane, across):
    barrier = pltpu.get_barrier_semaphore()
    chips = n // 2
    core = lax.rem(me, 2)
    others = [lax.rem(me // 2 + k, chips) * 2 + core for k in range(1, chips)] + [me + 1 - 2 * core]
    for other in others:
        pl.semaphore_signal(barrier, inc=1, device_id={"ctx": other}, device_id_type=MESH)
    if across:

        @pl.when(plane > 0)
        def _():
            pl.semaphore_signal(barrier, inc=1, device_id={"fsdp": plane - 1}, device_id_type=MESH)

        @pl.when(plane < planes - 1)
        def _():
            pl.semaphore_signal(barrier, inc=1, device_id={"fsdp": plane + 1}, device_id_type=MESH)

    count = len(others)
    if across:
        count = count + (plane > 0).astype(jnp.int32) + (plane < planes - 1).astype(jnp.int32)
    pl.semaphore_wait(barrier, count)


def forward_kernel(
    n,
    planes,
    heads,
    length_ref,
    tokens_ref,
    attn_shard,
    gate_ref,
    up_ref,
    down_ref,
    gain_shard,
    turns_ref,
    x_out,
    normed_out,
    q_out,
    k_out,
    v_out,
    lse_out,
    att_out,
    hid_out,
    normed2_out,
    a_out,
    b_out,
    mixed_out,
    attn_out,
    gate_out,
    up_out,
    down_out,
    gain_out,
    cos_out,
    sin_out,
    w_attn,
    w_gate,
    w_up,
    w_down,
    gains,
    x_all,
    qkv,
    q_rot,
    k_rot,
    v_rows,
    lse,
    own_att,
    att_all,
    own_hid,
    own_scaled,
    wide,
    narrow,
    cos_ref,
    sin_ref,
    z_send,
    z_recv,
    c_send,
    c_recv,
    keep_sem,
    load_sem,
    wide_sem,
    narrow_sem,
):
    me, plane = lax.axis_index("ctx"), lax.axis_index("fsdp")
    per_device, width = tokens_ref.shape
    total = x_all.shape[0]
    rows_shard = attn_shard.shape[0]
    own = own_att.shape[1]
    own_width = own_hid.shape[1]
    columns = qkv.shape[1]
    blocks = total // ROWS
    pairs = heads // 2

    local_copies = []

    def keep(src, dst, index):
        copy = pltpu.make_async_copy(src, dst, keep_sem.at[index])
        copy.start()
        local_copies.append(copy)

    def chain(index, ref, rows):
        return Chain(lambda s: ref.at[pl.ds(s * rows, rows)], planes, plane, z_send.at[index], z_recv.at[index])

    attn_chain = chain(0, w_attn, rows_shard)
    gate_chain = chain(1, w_gate, rows_shard)
    up_chain = chain(2, w_up, rows_shard)
    slab = w_down.shape[0] // planes
    down_chain = chain(3, w_down, slab)
    gain_chain = chain(4, gains, gain_shard.shape[0])
    own_ff = w_gate.shape[1]
    loads = [
        pltpu.make_async_copy(shard, c.slot(plane), keep_sem.at[i])
        for i, (c, shard) in enumerate(((attn_chain, attn_shard), (gain_chain, gain_shard)))
    ]
    for ref, c, at in ((gate_ref, gate_chain, 0), (up_ref, up_chain, 1)):
        for f in range(ref.shape[1] // (n * slab)):
            src = ref.at[:, pl.ds(pl.multiple_of((f * n + me) * slab, LANES), slab)]
            dst = c.slot(plane).at[:, pl.ds(f * slab, slab)]
            loads.append(pltpu.make_async_copy(src, dst, load_sem.at[at, f]))
        if ref.shape[1] == own_ff:
            loads.append(pltpu.make_async_copy(ref, c.slot(plane), load_sem.at[at, 0]))
    down_src = down_ref if down_ref.shape[0] == slab else down_ref.at[pl.ds(pl.multiple_of(me * slab, slab), slab)]
    loads.append(pltpu.make_async_copy(down_src, down_chain.slot(plane), load_sem.at[2, 0]))
    for load in loads:
        load.start()
    own_x = pltpu.make_async_copy(tokens_ref, x_all.at[pl.ds(me * per_device, per_device)], keep_sem.at[5])
    own_x.start()
    greet(n, planes, me, plane, True)
    loads[0].wait()
    attn_chain.start(0)
    loads[1].wait()
    gain_chain.start(0)
    x_spread = spread_over(
        n, tokens_ref, lambda c: x_all.at[pl.ds(c * per_device, per_device)], n, me, c_send.at[0], c_recv.at[0]
    )
    x_spread.start()

    def rotary_block(i, _):
        rows = pl.ds(pl.multiple_of(i * ROWS, ROWS), ROWS)
        given = i * ROWS + lax.broadcasted_iota(jnp.int32, (ROWS, LANES), 0)
        lane = lax.broadcasted_iota(jnp.int32, (ROWS, LANES), 1)
        position = given - jnp.where(given >= length_ref[0], length_ref[0], 0)
        angle = position.astype(F32) * turns_ref[0:1, :]
        cos_ref[rows, :] = jnp.cos(angle)
        sine = jnp.sin(angle)
        sin_ref[rows, :] = jnp.where(lax.rem(lane, HEAD_SIZE) < HEAD_SIZE // 2, -sine, sine)
        return 0

    lax.fori_loop(0, blocks, rotary_block, 0)
    for load in loads[2:]:
        load.wait()
    own_x.wait()
    for step in range(1, planes - 1):
        attn_chain.advance(step)
        gain_chain.advance(step)
    gate_chain.start(0)
    up_chain.start(0)
    x_spread.pass_on()
    x_spread.late()
    x_spread.finish()
    x_copy = pltpu.make_async_copy(x_all, x_out, keep_sem.at[0])
    x_copy.start()
    attn_chain.arrive(planes - 2)
    gain_chain.arrive(planes - 2)
    keep(w_attn, attn_out, 1)
    keep(gains, gain_out, 2)
    half = gain_shard.shape[1] // 2
    step_rows = gain_shard.shape[0]
    attn_gain = jnp.concatenate([gains[f * step_rows : f * step_rows + 1, :half] for f in range(planes)], axis=1)
    mlp_gain = jnp.concatenate([gains[f * step_rows : f * step_rows + 1, half:] for f in range(planes)], axis=1)

    def staged(stage, sem, slot, out, rows, wait_before):
        copy = pltpu.make_async_copy(stage.at[slot], out.at[rows], sem.at[slot])
        return copy.wait() if wait_before else copy.start()

    def project_block(i, _):
        rows = pl.ds(pl.multiple_of(i * ROWS, ROWS), ROWS)
        slot = lax.rem(i, 2)

        @pl.when(i >= 2)
        def _():
            staged(wide, wide_sem, slot, normed_out, rows, True)

        own_hid[rows, :] = x_all[rows, pl.ds(pl.multiple_of(me * own_width, LANES), own_width)]
        x = x_all[rows, :].astype(F32)
        r1 = lax.rsqrt(jnp.mean(x * x, axis=-1, keepdims=True) + EPSILON)
        normed = (x * r1 * attn_gain).astype(BF16)
        wide[slot] = normed
        staged(wide, wide_sem, slot, normed_out, rows, False)
        qkv[rows, :] = dot_nn(normed, w_attn[:, :columns])
        return 0

    lax.fori_loop(0, blocks, project_block, 0)
    for i in range(max(blocks - 2, 0), blocks):
        staged(wide, wide_sem, i % 2, normed_out, pl.ds(i * ROWS, ROWS), True)

    split = columns - LANES
    cos, sin = cos_ref[...], sin_ref[...]
    kv = qkv[:, split:]
    turned = pltpu.roll(kv, HEAD_SIZE, 1)
    low = low_half(kv.shape)
    k = jnp.where(low, kv, turned)
    k_rot[...] = (k * cos + swap_halves(k) * sin).astype(BF16)
    v_rows[...] = jnp.where(low, turned, kv).astype(BF16)
    keep(k_rot, k_out, 3)
    keep(v_rows, v_out, 4)
    first_len = length_ref[0]

    def attend_pair(pair, _):
        lanes = pl.ds(pl.multiple_of(pair * LANES, LANES), LANES)
        q = qkv[:, lanes]
        q_rot[:, lanes] = ((q * cos_ref[...] + swap_halves(q) * sin_ref[...]) * SCORE_SCALE).astype(BF16)
        for block in range(blocks):
            rows = pl.ds(block * ROWS, ROWS)
            end = (block + 1) * ROWS
            bias = mask_bias(first_len, block * ROWS, ROWS, end)
            query = q_rot[rows, lanes]
            lower = low_half(query.shape)
            keys, values = k_rot[:end, :], v_rows[:end, :]
            parts = []
            for side in range(2):
                chosen = lower if side == 0 else jnp.logical_not(lower)
                scores = dot_nt(jnp.where(chosen, query, jnp.zeros_like(query)), keys) + bias
                top = jnp.max(scores, axis=-1, keepdims=True)
                weights = jnp.exp(scores - top)
                whole = jnp.sum(weights, axis=-1, keepdims=True)
                probs = (weights * (1.0 / whole)).astype(BF16)
                parts.append(dot_nn(probs, values))
                lse[pair, rows, side : side + 1] = top + jnp.log(whole)
            own_att[rows, lanes] = jnp.where(low_half(parts[0].shape), parts[0], parts[1]).astype(BF16)
        return 0

    lax.fori_loop(0, pairs, attend_pair, 0)
    att_spread = spread_over(n, own_att, lambda c: att_all.at[c], n, me, c_send.at[1], c_recv.at[1])
    x_copy.wait()
    x_spread.drain()
    att_spread.start()
    own_a = pltpu.make_async_copy(own_att, att_all.at[me], keep_sem.at[5])
    own_a.start()
    keep(q_rot, q_out, 6)
    keep(lse, lse_out, 7)
    if planes > 2:
        gate_chain.advance(1)
        up_chain.advance(1)
    att_spread.pass_on()
    att_spread.late()
    own_a.wait()
    att_spread.finish()
    keep(att_all, att_out, 8)

    def out_block(i, _):
        rows = pl.ds(pl.multiple_of(i * ROWS, ROWS), ROWS)
        acc = jnp.zeros((ROWS, own_width), F32)
        for c in range(n):
            acc += dot_nn(att_all[c, rows, :], w_attn[c * own : (c + 1) * own, columns:])
        hidden = own_hid[rows, :].astype(F32) + RESIDUAL_SCALE * acc
        own_hid[rows, :] = hidden.astype(BF16)
        own_scaled[rows, :] = (hidden * (1.0 / RESIDUAL_SCALE)).astype(BF16)
        return 0

    lax.fori_loop(0, blocks, out_block, 0)
    def hid_slot(c):
        return x_all.at[:, pl.ds(pl.multiple_of(c * own_width, LANES), own_width)]

    hid_spread = spread_over(n, own_hid, hid_slot, n, me, c_send.at[2], c_recv.at[2])
    hid_spread.start()
    keep(own_scaled, mixed_out.at[:, pl.ds(own_ff, own_width)], 13)
    own_h = pltpu.make_async_copy(own_hid, hid_slot(me), keep_sem.at[5])
    own_h.start()
    for step in range(2, planes - 1):
        gate_chain.advance(step)
        up_chain.advance(step)
    down_chain.start(0)
    hid_spread.pass_on()
    hid_spread.late()
    own_h.wait()
    hid_spread.finish()
    keep(x_all, hid_out, 9)
    keep(cos_ref, cos_out, 14)
    keep(sin_ref, sin_out, 15)
    gate_chain.arrive(planes - 2)
    up_chain.arrive(planes - 2)
    keep(w_gate, gate_out, 10)
    keep(w_up, up_out, 11)
    if planes > 2:
        down_chain.advance(1)

    def mlp_copies(i, rows, wait):
        slot = lax.rem(i, 2)
        staged(wide, wide_sem, slot, normed2_out, rows, wait)
        for j, out in enumerate((a_out, b_out, mixed_out.at[:, pl.ds(0, own_ff)])):
            staged(narrow.at[j], narrow_sem.at[j], slot, out, rows, wait)

    def mlp_block(i, _):
        rows = pl.ds(pl.multiple_of(i * ROWS, ROWS), ROWS)
        slot = lax.rem(i, 2)

        @pl.when(i >= 2)
        def _():
            mlp_copies(i, rows, True)

        hidden = x_all[rows, :].astype(F32)
        r2 = lax.rsqrt(jnp.mean(hidden * hidden, axis=-1, keepdims=True) + EPSILON)
        normed = (hidden * r2 * mlp_gain).astype(BF16)
        wide[slot] = normed
        gate = dot_nn(normed, w_gate[...])
        up = dot_nn(normed, w_up[...])
        sig = jax.nn.sigmoid(gate)
        silu = gate * sig
        narrow[2, slot] = (silu * up).astype(BF16)
        narrow[1, slot] = silu.astype(BF16)
        narrow[0, slot] = (up * sig * (1.0 + gate * (1.0 - sig))).astype(BF16)
        mlp_copies(i, rows, False)
        return 0

    lax.fori_loop(0, blocks, mlp_block, 0)
    for step in range(2, planes - 1):
        down_chain.advance(step)
    for i in range(max(blocks - 2, 0), blocks):
        mlp_copies(i, pl.ds(i * ROWS, ROWS), True)
    down_chain.arrive(planes - 2)
    keep(w_down, down_out, 12)
    for c in (attn_chain, gain_chain, gate_chain, up_chain, down_chain):
        c.drain()
    for s in (att_spread, hid_spread):
        s.drain()
    for copy in local_copies:
        copy.wait()


def forward(n, planes, heads, slab, lengths, tokens, attn_shard, gate, up, down, gain_shard, turns):
    per_device, width = tokens.shape
    total = per_device * n
    own = heads * HEAD_SIZE
    columns = own + 2 * HEAD_SIZE
    own_width = attn_shard.shape[1] - columns
    own_ff = planes * slab
    rows_shard = attn_shard.shape[0]
    pairs = heads // 2
    weights = [
        ((planes * rows_shard, attn_shard.shape[1]), BF16),
        ((planes * rows_shard, own_ff), BF16),
        ((planes * rows_shard, own_ff), BF16),
        ((own_ff, width), BF16),
        ((planes * gain_shard.shape[0], gain_shard.shape[1]), F32),
    ]
    outs = [
        ((total, width), BF16),
        ((total, width), BF16),
        ((total, own), BF16),
        ((total, LANES), BF16),
        ((total, LANES), BF16),
        ((pairs, total, LANES), F32),
        ((n, total, own), BF16),
        ((total, width), BF16),
        ((total, width), BF16),
        ((total, own_ff), BF16),
        ((total, own_ff), BF16),
        ((total, own_ff + own_width), BF16),
    ] + weights + [((total, LANES), F32)] * 2
    scratch = weights + [
        ((total, width), BF16),
        ((total, columns), F32),
        ((total, own), BF16),
        ((total, LANES), BF16),
        ((total, LANES), BF16),
        ((pairs, total, LANES), F32),
        ((total, own), BF16),
        ((n, total, own), BF16),
        ((total, own_width), BF16),
        ((total, own_width), BF16),
        ((2, ROWS, width), BF16),
        ((3, 2, ROWS, own_ff), BF16),
        ((total, LANES), F32),
        ((total, LANES), F32),
    ]
    steps = max(planes - 1, 1)
    dma = pltpu.SemaphoreType.DMA
    anywhere = pl.BlockSpec(memory_space=pl.ANY)
    vmem = pl.BlockSpec(memory_space=pltpu.VMEM)
    return pl.pallas_call(
        functools.partial(forward_kernel, n, planes, heads),
        in_specs=[pl.BlockSpec(memory_space=pltpu.SMEM), vmem] + [anywhere] * 5 + [vmem],
        out_specs=[anywhere] * len(outs),
        out_shape=[jax.ShapeDtypeStruct(*o) for o in outs],
        scratch_shapes=[pltpu.VMEM(*s) for s in scratch]
        + [dma((5, 2, steps)), dma((5, 2, steps)), dma((3, n)), dma((3, n)), dma((16,)), dma((3, planes)), dma((2,)), dma((3, 2))],
        compiler_params=pltpu.CompilerParams(
            vmem_limit_bytes=VMEM_LIMIT, collective_id=1, has_side_effects=True
        ),
        cost_estimate=pl.CostEstimate(
            flops=2 * total * width * (columns + own_width + 2 * own_ff),
            bytes_accessed=60 * 1024 * 1024,
            transcendentals=0,
        ),
        name="forward",
    )(lengths, tokens, attn_shard, gate, up, down, gain_shard, turns)


def add_into(dst, src):
    rows_in, columns = dst.shape
    chunk = max(c for c in (256, 128, 64, 32) if c == 32 or (rows_in % c == 0 and c * columns <= 65536))

    def step(i, _):
        rows = pl.ds(pl.multiple_of(i * chunk, chunk), chunk)
        dst[rows, :] = (dst[rows, :].astype(F32) + src[rows, :].astype(F32)).astype(dst.dtype)
        return 0

    if rows_in < chunk:
        dst[...] = dst[...] + src[...]
    else:
        lax.fori_loop(0, rows_in // chunk, step, 0)


def fetch(src, dst, sem):
    copy = pltpu.make_async_copy(src, dst, sem)
    copy.start()
    copy.wait()


class Settle:
    def __init__(self, block, landed, stage, planes, plane, send_sem, recv_sem, load_sem):
        self.block, self.landed, self.stage = block, landed, stage
        self.planes, self.plane = planes, plane
        self.send_sem, self.recv_sem, self.load_sem = send_sem, recv_sem, load_sem

    def slot(self, way, shard, at):
        return shard if way == 0 else jnp.where(shard == at, self.planes, shard)

    def sends(self, step):
        p, last = self.plane, self.planes - 1
        return (
            (0, (p <= step) & (p < last), last - step + p, p + 1),
            (1, (last - p <= step) & (p > 0), step - last + p, p - 1),
        )

    def receives(self, step):
        p, last = self.plane, self.planes - 1
        return (
            (0, (p >= 1) & (p - 1 <= step), last - step + p - 1),
            (1, (p <= last - 1) & (last - p - 1 <= step), step - last + p + 1),
        )

    def copy(self, way, step, shard, to):
        return pltpu.make_async_remote_copy(
            src_ref=self.block(shard),
            dst_ref=self.landed.at[self.slot(way, shard, to)],
            send_sem=self.send_sem.at[way, step],
            recv_sem=self.recv_sem.at[way, step],
            device_id={"fsdp": to},
            device_id_type=MESH,
        )

    def start(self, step=0):
        ahead = [step + 1] if step else [0, 1]
        for way in range(2):
            end = self.plane == (0, self.planes - 1)[way]
            _, active, shard, to = self.sends(step)[way]

            @pl.when(active & jnp.logical_not(end))
            def _(way=way, shard=shard, to=to):
                self.copy(way, step, shard, to).start()

            @pl.when(end)
            def _(way=way):
                for later in ahead:
                    if later < self.planes - 1:
                        _, _, shard, to = self.sends(later)[way]
                        self.copy(way, later, shard, to).start()

    def take(self, step):
        for way, active, shard in self.receives(step):

            @pl.when(active)
            def _(way=way, shard=shard):
                self.copy(way, step, shard, self.plane).wait_recv()
                fetch(self.landed.at[self.slot(way, shard, self.plane)], self.stage, self.load_sem)
                add_into(self.block(shard), self.stage)

    def advance(self, step):
        self.take(step - 1)
        self.start(step)

    def drain(self):
        for step in range(self.planes - 1):
            for way, active, shard, to in self.sends(step):

                @pl.when(active)
                def _(way=way, shard=shard, to=to, step=step):
                    self.copy(way, step, shard, to).wait_send()


class Scatter:
    def __init__(self, block, near, far, stage, me, send_sem, recv_sem, load_sem):
        self.block, self.landed, self.far, self.stage = block, near, far, stage
        self.send_sem, self.recv_sem, self.load_sem = send_sem, recv_sem, load_sem
        self.core = lax.rem(me, 2)
        self.chip = me // 2
        self.chips = (self.chip, *square(self.chip))
        self.half = stage[0].shape[0] // 2

    def rows(self, which):
        return pl.ds(which * self.half, self.half)

    def own(self, k):
        return self.block(self.chips[k] * 2 + self.core)

    def copy(self, src, dst, sem, chip, core):
        return pltpu.make_async_remote_copy(
            src_ref=src,
            dst_ref=dst,
            send_sem=self.send_sem.at[sem],
            recv_sem=self.recv_sem.at[sem],
            device_id={"ctx": chip * 2 + core},
            device_id_type=MESH,
        )

    def first(self, k):
        other = 1 - self.core
        return self.copy(self.block(self.chips[k] * 2 + other), self.landed.at[k], k, self.chip, other)

    def second(self, k, to, which):
        place = self.far.at[to - 1 if k == to else 2, self.rows(which)]
        sem = 4 + 2 * (to - 1) + which if k == to else 7 + to
        return self.copy(self.own(k).at[self.rows(which)], place, sem, self.chips[to], self.core)

    def start(self):
        for k in (3, 1, 2, 0):
            self.first(k).start()

    def add_all(self, items):
        pending = None

        def complete(copy, dst, stage, then):
            copy.wait()
            add_into(dst, stage)
            for remote in then:
                remote.start()

        for index, (arrivals, src, dst, then) in enumerate(items):
            for remote in arrivals:
                remote.wait_recv()
            stage = self.stage[index % 2].at[pl.ds(0, dst.shape[0])]
            copy = pltpu.make_async_copy(src, stage, self.load_sem.at[index % 2])
            copy.start()
            if pending is not None:
                complete(*pending)
            pending = (copy, dst, stage, then)
        complete(*pending)

    def pass_on(self):
        self.add_all(
            [
                ([self.first(3)], self.landed.at[3], self.own(3), [self.second(3, 1, 0), self.second(3, 2, 1)]),
                ([self.first(1)], self.landed.at[1], self.own(1), [self.second(1, 1, 0)]),
                ([self.first(2)], self.landed.at[2], self.own(2), [self.second(2, 2, 1)]),
            ]
        )

    def late(self):
        self.add_all(
            [
                (
                    [self.second(3, to, which)],
                    self.far.at[2, self.rows(which)],
                    self.own(k).at[self.rows(which)],
                    [self.second(k, k, which)],
                )
                for to, which, k in ((1, 0, 2), (2, 1, 1))
            ]
        )

    def finish(self, total):
        items = [([self.first(0)], self.landed.at[0], total, [])]
        for k in (1, 2):
            items.append(([self.second(k, k, which) for which in (0, 1)], self.far.at[k - 1], total, []))
        self.add_all(items)

    def drain(self):
        for k in range(4):
            self.first(k).wait_send()
        for k, to, which in ((3, 1, 0), (3, 2, 1), (1, 1, 0), (1, 1, 1), (2, 2, 0), (2, 2, 1)):
            self.second(k, to, which).wait_send()


def backward_kernel(
    n,
    planes,
    heads,
    length_ref,
    grad_in,
    mixed_in,
    a_in,
    b_in,
    hidden_in,
    normed2_in,
    normed_in,
    x_in,
    att_in,
    q_in,
    k_in,
    v_in,
    lse_in,
    cos_in,
    sin_in,
    attn_in,
    gate_in,
    up_in,
    down_in,
    gain_in,
    token_out,
    gain_out,
    down_all,
    gate_all,
    up_all,
    out_all,
    qkv_all,
    near1,
    far1,
    near2,
    far2,
    near3,
    far3,
    down_landed,
    gate_landed,
    up_landed,
    out_landed,
    qkv_landed,
    w_attn,
    w_gate,
    w_up,
    w_down,
    p_down,
    gains,
    grad,
    a_v,
    b_v,
    part,
    hid_stage,
    stage_tall,
    stage_wide,
    stage_col,
    hidden_grad,
    lse,
    cos,
    sin,
    dk_sum,
    dv_sum,
    gain_own,
    gain_all,
    gain_landed,
    gain_stage,
    z_send,
    z_recv,
    s_send,
    s_recv,
    g_send,
    g_recv,
    load_sem,
    hid_sem,
    add_sem,
    ring_sem,
):
    me, plane = lax.axis_index("ctx"), lax.axis_index("fsdp")
    total, width = grad.shape
    per_device = total // n
    own = heads * HEAD_SIZE
    own_width = width // n
    own_ff = a_v.shape[1]
    rows_shard = width // planes
    slab = own_ff // planes
    blocks = total // ROWS
    pairs = heads // 2
    columns = own + LANES
    last = planes - 2

    def load(src, dst, index):
        copy = pltpu.make_async_copy(src, dst, load_sem.at[index])
        copy.start()
        return copy

    mixed_loads = [load(mixed_in.at[:, pl.ds(d * own_width, own_width)], part.at[d], d) for d in range(own_ff // own_width)]
    grad_load = load(grad_in, grad, 8)
    down_load = load(down_in, w_down, 9)
    gate_load = load(gate_in, w_gate, 10)
    up_load = load(up_in, w_up, 11)
    a_load = load(a_in, a_v, 12)
    b_load = load(b_in, b_v, 13)
    attn_load = load(attn_in, w_attn, 14)
    gain_load = load(gain_in, gains, 15)
    greet(n, planes, me, plane, True)

    def settle(index, block, landed, stage):
        return Settle(block, landed, stage, planes, plane, z_send.at[index], z_recv.at[index], add_sem)

    def rows_of(ref, rows):
        return lambda d: ref.at[pl.ds(pl.multiple_of(d * rows, rows), rows)]

    def out_block_of(d):
        return w_down.at[pl.ds(0, rows_shard), pl.ds(pl.multiple_of(d * own_width, LANES), own_width)]

    def qkv_block_of(d):
        return w_down.at[pl.ds(rows_shard, rows_shard), pl.ds(pl.multiple_of(d * columns, LANES), columns)]

    def gain_block_of(d):
        return gain_own.at[:, pl.ds(pl.multiple_of(d * rows_shard, LANES), rows_shard)]

    down_sum = settle(0, rows_of(p_down, slab), down_landed, stage_wide)
    gate_sum = settle(1, rows_of(w_gate, rows_shard), gate_landed, stage_tall)
    up_sum = settle(2, rows_of(w_up, rows_shard), up_landed, stage_tall)
    out_sum = settle(3, out_block_of, out_landed, stage_tall.at[:, pl.ds(0, own_width)])
    qkv_sum = settle(4, qkv_block_of, qkv_landed, stage_tall.at[:, pl.ds(0, columns)])
    gain_sum = settle(5, gain_block_of, gain_landed, gain_stage)

    def spread(index, src, dst):
        return spread_over(n, src, lambda c: dst.at[c], n, me, g_send.at[index], g_recv.at[index])

    spreads = []

    def give(index, sums, dst):
        src = sums.block(plane)
        mine = load(src, dst.at[me], 16 + index)
        out = spread(index, src, dst)
        out.start()
        spreads.append((out, mine))
        return out

    def scatter(index, block, near, far, stage):
        return Scatter(block, near, far, stage, me, s_send.at[index], s_recv.at[index], ring_sem)

    part_rows = total // 2
    col_stages = [stage_col.at[pl.ds(i * part_rows, part_rows)] for i in range(2)]

    def half_scatter(index, near, far, side):
        rows = pl.ds(side * part_rows, part_rows)
        return scatter(
            2 * index + side, lambda c: part.at[c, rows], near.at[:, rows], far.at[:, rows], col_stages
        )

    first = [half_scatter(0, near1, far1, side) for side in range(2)]
    second = [half_scatter(1, near2, far2, side) for side in range(2)]

    grad_load.wait()

    for copy in mixed_loads:
        copy.wait()

    def down_block(i, _):
        d = jnp.where(i == 0, planes - 1, jnp.where(i == 1, 0, planes - i))
        rows = pl.ds(pl.multiple_of(d * own_width, own_width), own_width)
        p_down[rows, :] = (RESIDUAL_SCALE * dot_tn(part[d], grad[...])).astype(BF16)

        return 0

    lax.fori_loop(0, planes, down_block, 0)
    down_sum.start()

    for copy in (down_load, gate_load, up_load, a_load, b_load, attn_load, gain_load):
        copy.wait()
    half = gains.shape[1] // 2
    attn_gain = jnp.concatenate([gains[f * 8 : f * 8 + 1, :half] for f in range(planes)], axis=1)
    mlp_gain = jnp.concatenate([gains[f * 8 : f * 8 + 1, half:] for f in range(planes)], axis=1)
    gain_own[...] = jnp.zeros_like(gain_own)

    def stream(src, i, wait):
        rows = pl.ds(pl.multiple_of(i * ROWS, ROWS), ROWS)
        slot = lax.rem(i, 2)
        copy = pltpu.make_async_copy(src.at[rows], hid_stage.at[slot], hid_sem.at[slot])
        return copy.wait() if wait else copy.start()

    stream(hidden_in, jnp.int32(0), False)

    def mlp_block(i, _):
        rows = pl.ds(pl.multiple_of(i * ROWS, ROWS), ROWS)

        @pl.when(i + 1 < blocks)
        def _():
            stream(hidden_in, i + 1, False)

        mixed_grad = RESIDUAL_SCALE * dot_nt(grad[rows, :], w_down[...])
        ggrad = (mixed_grad * a_v[rows, :].astype(F32)).astype(BF16)
        ugrad = (mixed_grad * b_v[rows, :].astype(F32)).astype(BF16)
        a_v[rows, :] = ggrad
        b_v[rows, :] = ugrad
        normed_grad = dot_nt(ggrad, w_gate[...]) + dot_nt(ugrad, w_up[...])
        stream(hidden_in, i, True)

        hidden = hid_stage[lax.rem(i, 2)].astype(F32)
        r2 = lax.rsqrt(jnp.mean(hidden * hidden, axis=-1, keepdims=True) + EPSILON)
        gain_own[0:1, :] += jnp.sum(normed_grad * (hidden * r2), axis=0, keepdims=True)
        weighted = normed_grad * mlp_gain
        mean = jnp.mean(weighted * hidden, axis=-1, keepdims=True)
        piece = r2 * weighted - hidden * (r2 * r2 * r2 * mean)
        for c in range(n):
            part[c, rows, :] = piece[:, c * own_width : (c + 1) * own_width].astype(BF16)

        @pl.when(i == blocks // 2 - 1)
        def _():
            first[0].start()

        @pl.when(i == blocks - 2)
        def _():
            down_sum.advance(1)
            first[0].pass_on()

        return 0

    lax.fori_loop(0, blocks, mlp_block, 0)
    first[1].start()
    normed2_load = load(normed2_in, grad, 8)
    normed2_load.wait()

    def columns_times(right, out, low, high):
        def block(j, _):
            lanes = pl.ds(pl.multiple_of(j * ROWS, ROWS), ROWS)
            out[lanes, :] = dot_tn(grad[:, lanes], right[...]).astype(BF16)
            return 0

        lax.fori_loop(low, high, block, 0)

    first[0].late()
    columns_times(a_v, w_gate, 0, width // ROWS)
    gate_sum.start()
    first[1].pass_on()
    columns_times(b_v, w_up, 0, width // ROWS // 2)
    first[1].late()
    columns_times(b_v, w_up, width // ROWS // 2, width // ROWS)
    down_sum.advance(2)

    att_loads = [load(att_in.at[c], grad.at[:, pl.ds(c * own, own)], c) for c in range(n)]
    own_grad = load(grad_in.at[:, pl.ds(pl.multiple_of(me * own_width, LANES), own_width)], b_v.at[:, pl.ds(LANES, own_width)], 8)
    q_load = load(q_in, a_v.at[:, pl.ds(0, own)], 9)
    k_load = load(k_in, a_v.at[:, pl.ds(own, LANES)], 10)
    v_load = load(v_in, a_v.at[:, pl.ds(own + LANES, LANES)], 11)
    lse_load = load(lse_in, lse, 12)
    cos_load = load(cos_in, cos, 13)
    sin_load = load(sin_in, sin, 14)
    own_grad.wait()

    def begin(i, _):
        rows = pl.ds(pl.multiple_of(i * ROWS, ROWS), ROWS)
        hidden_grad[rows, :] = b_v[rows, LANES : LANES + own_width].astype(F32) + part[me, rows, :].astype(F32)
        return 0

    lax.fori_loop(0, blocks, begin, 0)
    for side in range(2):
        first[side].finish(hidden_grad.at[pl.ds(side * part_rows, part_rows)])
        first[side].drain()

    def branch_block(i, _):
        rows = pl.ds(pl.multiple_of(i * ROWS, ROWS), ROWS)
        branch = (RESIDUAL_SCALE * hidden_grad[rows, :]).astype(BF16)
        b_v[rows, LANES : LANES + own_width] = branch
        for c in range(n):
            part[c, rows, :] = dot_nt(branch, w_attn[c * own : (c + 1) * own, columns:]).astype(BF16)

        @pl.when(i == blocks // 2 - 1)
        def _():
            second[0].start()

        return 0

    lax.fori_loop(0, blocks, branch_block, 0)
    second[1].start()
    second[0].pass_on()
    gate_sum.advance(1)
    for copy in att_loads:
        copy.wait()
    heads_per_shard = rows_shard // own
    for c in range(n):
        place = out_block_of(c // heads_per_shard).at[pl.ds((c % heads_per_shard) * own, own)]
        place[...] = dot_tn(grad[:, c * own : (c + 1) * own], b_v[:, LANES : LANES + own_width]).astype(BF16)
    second[1].pass_on()
    second[0].late()
    normed_load = load(normed_in, grad, 15)
    down_sum.take(last)
    up_sum.start()
    second[1].late()
    second[0].finish(part.at[me, pl.ds(0, part_rows)])
    down_give = give(0, down_sum, down_all)
    gate_sum.advance(2)

    for copy in (q_load, k_load, v_load, lse_load, cos_load, sin_load):
        copy.wait()
    dk_sum[...] = jnp.zeros_like(dk_sum)
    dv_sum[...] = jnp.zeros_like(dv_sum)
    first_len = length_ref[0]
    dq_at = own + 2 * LANES

    def attend_pair(side, pair, _):
        lanes = pl.ds(pl.multiple_of(pair * LANES, LANES), LANES)
        dq_lanes = pl.ds(pl.multiple_of(dq_at + pair * LANES, LANES), LANES)
        for block in range(side * (blocks // 2), (side + 1) * (blocks // 2)):
            rows = pl.ds(block * ROWS, ROWS)
            end = (block + 1) * ROWS
            bias = mask_bias(first_len, block * ROWS, ROWS, end)
            query, grads = a_v[rows, lanes], part[me, rows, lanes]
            low = low_half(query.shape)
            keys, values = a_v[:end, own : own + LANES], a_v[:end, own + LANES : own + 2 * LANES]
            parts = []
            for head in range(2):
                chosen = low if head == 0 else jnp.logical_not(low)
                own_query = jnp.where(chosen, query, jnp.zeros_like(query))
                own_grads = jnp.where(chosen, grads, jnp.zeros_like(grads))
                scores = dot_nt(own_query, keys) + bias
                probs = jnp.exp(scores - lse[pair, rows, head : head + 1])
                prob_grad = dot_nt(own_grads, values)
                delta = jnp.sum(probs * prob_grad, axis=-1, keepdims=True)
                score_grad = (probs * (prob_grad - delta)).astype(BF16)
                parts.append(dot_nn(score_grad, keys))
                dk_sum[:end, :] += dot_tn(score_grad, own_query)
                dv_sum[:end, :] += dot_tn(probs.astype(BF16), own_grads)
            dq = jnp.where(low_half(parts[0].shape), parts[0], parts[1]) * SCORE_SCALE
            a_v[rows, dq_lanes] = (dq * cos[rows, :] - swap_halves(dq) * sin[rows, :]).astype(BF16)

        if side:

            @pl.when(pair == 0)
            def _():
                down_give.pass_on()
                up_sum.advance(1)

        return 0

    lax.fori_loop(0, pairs, functools.partial(attend_pair, 0), 0)
    second[1].finish(part.at[me, pl.ds(part_rows, part_rows)])
    lax.fori_loop(0, pairs, functools.partial(attend_pair, 1), 0)
    dk = dk_sum[...]
    dk = dk + pltpu.roll(dk, HEAD_SIZE, 1)
    dk = dk * cos[...] - swap_halves(dk) * sin[...]
    dv = dv_sum[...]
    dv = dv + pltpu.roll(dv, HEAD_SIZE, 1)
    b_v[:, :LANES] = jnp.where(low_half(dk.shape), dk, dv).astype(BF16)
    down_give.late()
    gate_sum.take(last)
    gate_give = give(1, gate_sum, gate_all)
    up_sum.advance(2)
    out_sum.start()

    normed_load.wait()
    dq_end = dq_at + own
    for d in range(planes):
        for j in range(rows_shard // ROWS):
            lanes = slice(d * rows_shard + j * ROWS, d * rows_shard + (j + 1) * ROWS)
            place = qkv_block_of(d).at[pl.ds(j * ROWS, ROWS)]
            place[:, :own] = dot_tn(grad[:, lanes], a_v[:, dq_at:dq_end]).astype(BF16)
            place[:, own:] = dot_tn(grad[:, lanes], b_v[:, :LANES]).astype(BF16)
    gate_give.pass_on()
    out_sum.advance(1)
    qkv_sum.start()

    stream(x_in, jnp.int32(0), False)

    def token_block(i, _):
        rows = pl.ds(pl.multiple_of(i * ROWS, ROWS), ROWS)

        @pl.when(i + 1 < blocks)
        def _():
            stream(x_in, i + 1, False)

        normed_grad = dot_nt(a_v[rows, dq_at:dq_end], w_attn[:, :own]) + dot_nt(b_v[rows, :LANES], w_attn[:, own:columns])
        stream(x_in, i, True)
        x = hid_stage[lax.rem(i, 2)].astype(F32)
        r1 = lax.rsqrt(jnp.mean(x * x, axis=-1, keepdims=True) + EPSILON)
        gain_own[1:2, :] += jnp.sum(normed_grad * (x * r1), axis=0, keepdims=True)
        weighted = normed_grad * attn_gain
        mean = jnp.mean(weighted * x, axis=-1, keepdims=True)
        piece = r1 * weighted - x * (r1 * r1 * r1 * mean)
        for c in range(n):
            lanes = slice(c * own_width, (c + 1) * own_width)
            mine = jnp.where(me == c, hidden_grad[rows, :], 0.0)
            grad[rows, lanes] = (piece[:, lanes] + mine).astype(BF16)
        return 0

    lax.fori_loop(0, blocks, token_block, 0)

    def token_rows(c):
        return grad.at[pl.ds(pl.multiple_of(c * per_device, per_device), per_device)]

    third = scatter(4, token_rows, near3, far3, [hid_stage.at[i, pl.ds(0, per_device)] for i in range(2)])
    third.start()
    gain_give = spread(5, gain_own, gain_all)
    gain_mine = load(gain_own, gain_all.at[me], 21)
    gain_give.start()
    gate_give.late()
    third.pass_on()
    gain_give.pass_on()
    out_sum.advance(2)
    third.late()
    gain_give.finish()
    gain_mine.wait()
    gain_give.drain()
    gain_own[...] = sum(gain_all[c] for c in range(n))
    gain_sum.start()
    token_out[...] = token_rows(me)[...].astype(F32)
    qkv_sum.advance(1)
    third.finish(token_out)
    up_sum.take(last)
    up_give = give(2, up_sum, up_all)
    gain_sum.advance(1)
    out_sum.take(last)
    out_give = give(3, out_sum, out_all)
    qkv_sum.advance(2)
    gain_sum.advance(2)
    up_give.pass_on()
    out_give.pass_on()
    up_give.late()
    gain_sum.take(last)
    gain_out[...] = gain_block_of(plane)[...]
    qkv_sum.take(last)
    qkv_give = give(4, qkv_sum, qkv_all)
    out_give.late()
    qkv_give.pass_on()
    qkv_give.late()
    for out, mine in spreads:
        out.finish()
        out.drain()
        mine.wait()
    for s in (*second, third):
        s.drain()
    for s in (down_sum, gate_sum, up_sum, out_sum, qkv_sum, gain_sum):
        s.drain()


def backward(n, planes, heads, lengths, grad, saved, weights, cos, sin):
    x, normed, q_rot, k_rot, v_rows, lse, att_all, hidden, normed2, a, b, mixed = saved
    w_attn, w_gate, w_up, w_down, gains = weights
    total, width = grad.shape
    own = heads * HEAD_SIZE
    own_width = width // n
    own_ff = a.shape[1]
    rows_shard = width // planes
    slab = own_ff // planes
    columns = own + LANES
    chips = n // 2
    per_device = total // n
    col, row = (chips, total, own_width), (chips, per_device, width)
    outs = [
        ((per_device, width), F32),
        ((8, rows_shard), F32),
        ((n, slab, width), BF16),
        ((n, rows_shard, own_ff), BF16),
        ((n, rows_shard, own_ff), BF16),
        ((n, rows_shard, own_width), BF16),
        ((n, rows_shard, columns), BF16),
        (col, BF16),
        (col, BF16),
        (col, BF16),
        (col, BF16),
        (row, BF16),
        (row, BF16),
        ((planes + 1, slab, width), BF16),
        ((planes + 1, rows_shard, own_ff), BF16),
        ((planes + 1, rows_shard, own_ff), BF16),
        ((planes + 1, rows_shard, own_width), BF16),
        ((planes + 1, rows_shard, columns), BF16),
    ]
    scratch = [
        (w_attn.shape, BF16),
        (w_gate.shape, BF16),
        (w_up.shape, BF16),
        (w_down.shape, BF16),
        (w_down.shape, BF16),
        (gains.shape, F32),
        ((total, width), BF16),
        ((total, own_ff), BF16),
        ((total, own_ff), BF16),
        ((n, total, own_width), BF16),
        ((2, ROWS, width), BF16),
        ((rows_shard, own_ff), BF16),
        ((slab, width), BF16),
        ((total, own_width), BF16),
        ((total, own_width), F32),
        (lse.shape, F32),
        (cos.shape, F32),
        (sin.shape, F32),
        ((total, LANES), F32),
        ((total, LANES), F32),
        ((8, width), F32),
        ((n, 8, width), F32),
        ((planes + 1, 8, rows_shard), F32),
        ((8, rows_shard), F32),
    ]
    steps = planes - 1
    dma = pltpu.SemaphoreType.DMA
    anywhere = pl.BlockSpec(memory_space=pl.ANY)
    vmem = pl.BlockSpec(memory_space=pltpu.VMEM)
    return pl.pallas_call(
        functools.partial(backward_kernel, n, planes, heads),
        in_specs=[pl.BlockSpec(memory_space=pltpu.SMEM)] + [anywhere] * 20,
        out_specs=[vmem] * 2 + [anywhere] * (len(outs) - 2),
        out_shape=[jax.ShapeDtypeStruct(*o) for o in outs],
        scratch_shapes=[pltpu.VMEM(*s) for s in scratch]
        + [
            dma((6, 2, steps)),
            dma((6, 2, steps)),
            dma((5, 10)),
            dma((5, 10)),
            dma((6, n)),
            dma((6, n)),
            dma((24,)),
            dma((2,)),
            dma,
            dma((2,)),
        ],
        compiler_params=pltpu.CompilerParams(
            vmem_limit_bytes=60 * 1024 * 1024, collective_id=2, has_side_effects=True
        ),
        cost_estimate=pl.CostEstimate(
            flops=16 * total * width * own_ff, bytes_accessed=100 * 1024 * 1024, transcendentals=0
        ),
        name="backward",
    )(
        lengths,
        grad,
        mixed,
        a,
        b,
        hidden,
        normed2,
        normed,
        x,
        att_all,
        q_rot,
        k_rot,
        v_rows,
        lse,
        cos,
        sin,
        w_attn,
        w_gate,
        w_up,
        w_down,
        gains,
    )[:7]


def kernel_fits(n, planes, total, width, own_ff):
    held = 4 * width * own_ff + 2 * total * width + 2 * total * own_ff
    return planes == 4 and total % (2 * ROWS) == 0 and n == 8 and own_ff // planes >= total // n and n * own_ff == planes * width and 2 * held < 44 * 1024 * 1024 and (own_ff // planes) % LANES == 0


def own_columns(array, index, width):
    return lax.dynamic_slice_in_dim(array, index * width, width, axis=1)


def after(value, *others):
    return lax.optimization_barrier((value, *others))[0]


def local(
    tokens,
    lengths,
    deal,
    attn_gain,
    query_weight,
    key_matrix,
    value_matrix,
    out_weight,
    mlp_gain,
    gate_weight,
    up_weight,
    down_weight,
    cotangent,
):
    n_ctx = lax.axis_size("ctx")
    n_fsdp = lax.axis_size("fsdp")
    me = lax.axis_index("ctx")
    me_array = me.astype(jnp.int32).reshape(1)
    per_device, width = tokens.shape[1], tokens.shape[2]
    total = per_device * n_ctx
    block_rows = per_device // n_ctx
    heads = QUERY_HEADS // n_ctx
    sharing = n_ctx // KEY_VALUE_HEADS
    own_width = width // n_ctx
    ff = gate_weight.shape[1]
    slab = ff // (n_fsdp * n_ctx)
    own_ff = slab * n_fsdp
    rows_shard = query_weight.shape[0]

    kv_head = me // sharing
    split = heads * HEAD_SIZE
    attn_shard = jnp.concatenate(
        [
            own_columns(query_weight, me, split),
            own_columns(key_matrix, kv_head, HEAD_SIZE),
            own_columns(value_matrix, kv_head, HEAD_SIZE),
            own_columns(out_weight, me, own_width),
        ],
        axis=1,
    )

    def ff_columns(array):
        return jnp.concatenate([own_columns(array, f * n_ctx + me, slab) for f in range(n_fsdp)], axis=1)

    gain_shard = jnp.tile(jnp.concatenate([attn_gain, mlp_gain]).astype(F32)[None], (8, 1))

    freq_index = jnp.arange(HEAD_SIZE // 2, dtype=F32)
    inverse = ROPE_BASE ** (-2.0 * freq_index / HEAD_SIZE)
    turns = jnp.tile(inverse, (8, 4))

    deal_rows = deal[0]
    slot_ids = jnp.arange(n_ctx, dtype=jnp.int32)
    dealt_of_given = (deal_rows * n_ctx + slot_ids[:, None]).reshape(-1)
    matched = deal_rows[:, :, None] == slot_ids[None, None, :]
    source_slot = jnp.sum(jnp.where(matched, slot_ids[None, :, None], 0), axis=1)
    given_of_dealt = (slot_ids[:, None] * n_ctx + source_slot).T.reshape(-1)

    def reorder(array, table):
        blocks = array.reshape(n_ctx * n_ctx, block_rows, array.shape[1])
        return jnp.take(blocks, table, axis=0, mode="clip").reshape(array.shape)

    ff_weights = gate_weight, up_weight, down_weight
    if slab % LANES:
        ff_weights = (
            ff_columns(gate_weight),
            ff_columns(up_weight),
            lax.dynamic_slice_in_dim(down_weight, me * slab, slab, axis=0),
        )

    cotangent_all = lax.all_gather(cotangent[0], "ctx", axis=0, tiled=True)
    (
        x, normed, q_rot, k_rot, v_rows, lse, attended_all, hidden_all, normed2, a, b, both, w_attn, w_gate, w_up, w_down, gains_all, cos_table, sin_table,
    ) = forward(
        n_ctx,
        n_fsdp,
        heads,
        slab,
        lengths[0],
        tokens[0],
        attn_shard,
        *ff_weights,
        gain_shard,
        turns,
    )
    w_qkv, w_out = w_attn[:, : split + 2 * HEAD_SIZE], w_attn[:, split + 2 * HEAD_SIZE :]
    gains = gains_all.reshape(n_fsdp, 8, 2, rows_shard)[:, 0].transpose(1, 0, 2).reshape(2, 1, width)
    grad_result = reorder(cotangent_all, dealt_of_given)

    result_part = result_rows(me_array, reorder(both, given_of_dealt), w_down)
    activations = lax.psum_scatter(
        result_part, "ctx", scatter_dimension=0, tiled=True
    )[None]

    if kernel_fits(n_ctx, n_fsdp, total, width, own_ff):
        token_grad, gain_rows, down_part, gate_part, up_part, out_part, qkv_part = backward(
            n_ctx,
            n_fsdp,
            heads,
            lengths[0],
            grad_result,
            (x, normed, q_rot, k_rot, v_rows, lse, attended_all, hidden_all, normed2, a, b, both),
            (w_attn, w_gate, w_up, w_down, gains_all),
            cos_table,
            sin_table,
        )
        token_grad = token_grad[None]
        own_gains = gain_rows[1], gain_rows[0]
    else:
        mlp_grad = (RESIDUAL_SCALE * grad_result.astype(F32)).astype(BF16)

        def settle(left, right):
            return lax.psum_scatter(dot_tn(left, right).astype(BF16), "fsdp", scatter_dimension=0, tiled=True)

        down_part = settle(both[:, :own_ff], mlp_grad)
        ggrad, ugrad, hidden_part, mlp_gain_part = mlp_backward(
            n_ctx, mlp_grad, a, b, hidden_all, gains[1], w_gate, w_up, w_down
        )
        hidden_sum = lax.psum_scatter(hidden_part, "ctx", scatter_dimension=0, tiled=False)
        gate_part = settle(normed2, ggrad)
        up_part = settle(normed2, ugrad)
        hidden_grad, branch_grad, attended_part = branch_backward(
            hidden_sum, own_columns(grad_result, me, own_width), w_out, n_ctx
        )
        attended_grad = lax.psum_scatter(attended_part, "ctx", scatter_dimension=0, tiled=False)
        out_part = lax.psum_scatter(
            jnp.einsum("ctk,to->cko", attended_all, branch_grad, preferred_element_type=F32)
            .astype(BF16)
            .reshape(width, own_width),
            "fsdp",
            scatter_dimension=0,
            tiled=True,
        )
        dq, dkv = attention_backward(attended_grad, q_rot, k_rot, v_rows, lse, cos_table, sin_table, lengths[0])
        qkv_part = settle(normed, jnp.concatenate([dq, dkv], axis=1))
        token_part, attn_gain_part = token_backward(me_array, dq, dkv, w_qkv, x, gains[0], hidden_grad)
        token_grad = lax.psum_scatter(token_part, "ctx", scatter_dimension=0, tiled=True).astype(F32)[None]

        gain_parts = jnp.concatenate([attn_gain_part, mlp_gain_part], axis=0)
        step = 1
        while step < n_ctx:
            gain_parts = gain_parts + lax.ppermute(gain_parts, "ctx", [(c, c ^ step) for c in range(n_ctx)])
            step *= 2
        gain_rows = gain_parts.reshape(2, n_fsdp, rows_shard).transpose(1, 0, 2).reshape(n_fsdp, 2 * rows_shard)
        own_gains = lax.psum_scatter(gain_rows, "fsdp", scatter_dimension=0, tiled=True).reshape(2, rows_shard)
        down_part, gate_part, up_part, out_part, qkv_part = [
            lax.all_gather(p, "ctx", axis=0, tiled=False) for p in (down_part, gate_part, up_part, out_part, qkv_part)
        ]

    if slab % LANES == 0 and sharing == 1 and heads % 4 == 0:
        gate_grad, up_grad, down_grad, out_grad, query_grad, key_grad, value_grad = finish(
            slab, gate_part, up_part, down_part.reshape(n_ctx * slab, width), out_part, qkv_part
        )
    else:
        down_grad = down_part.reshape(n_ctx * slab, width).astype(F32)
        if slab % LANES == 0:
            gate_grad = spread_columns(gate_part, slab, n_fsdp)
            up_grad = spread_columns(up_part, slab, n_fsdp)
        else:

            def ff_whole(part):
                pieces = part.reshape(n_ctx, rows_shard, n_fsdp, slab)
                return pieces.transpose(1, 2, 0, 3).reshape(rows_shard, ff).astype(F32)

            gate_grad = ff_whole(gate_part)
            up_grad = ff_whole(up_part)
        out_grad = spread_columns(out_part, own_width, 1)
        qkv_all = qkv_part
        query_grad = spread_columns(qkv_all, split, 1)

        def shared_heads(pieces):
            pieces = pieces.astype(F32).reshape(KEY_VALUE_HEADS, sharing, rows_shard, HEAD_SIZE).sum(axis=1)
            return pieces.transpose(1, 0, 2).reshape(rows_shard, KEY_VALUE_HEADS * HEAD_SIZE)

        key_grad = shared_heads(qkv_all[:, :, split : split + HEAD_SIZE])
        value_grad = shared_heads(qkv_all[:, :, split + HEAD_SIZE :])

    return (
        activations,
        token_grad,
        own_gains[0],
        query_grad,
        key_grad,
        value_grad,
        out_grad,
        own_gains[1],
        gate_grad,
        up_grad,
        down_grad,
    )


def solution(mesh):
    rows = P("fsdp", None)
    block = P("fsdp", "ctx", None)
    gain = P("fsdp")
    return jax.shard_map(
        local,
        mesh=mesh,
        in_specs=(block, rows, P("fsdp", None, None), gain, rows, rows, rows, rows, gain, rows, rows, rows, block),
        out_specs=(block, block, gain, rows, rows, rows, rows, gain, rows, rows, rows),
        check_vma=False,
    )
```

```python
import functools

import jax
import jax.numpy as jnp
import numpy as np
from jax import lax
from jax.experimental import pallas as pl
from jax.experimental.pallas import tpu as pltpu
from jax.sharding import PartitionSpec as P

QUERY_HEADS = 32
KEY_VALUE_HEADS = 8
HEAD_SIZE = 64
EPSILON = 1e-05
ROPE_BASE = 10000000.0
SCORE_SCALE = 0.015625
RESIDUAL_SCALE = 0.22
NEGATIVE_BIG = -1e30
LANES = 128
ROWS = 256
BF16 = jnp.bfloat16
F32 = jnp.float32
VMEM_LIMIT = 59 * 1024 * 1024


def dot_nn(a, b):
    return lax.dot_general(a, b, (((1,), (0,)), ((), ())), preferred_element_type=F32)


def dot_nt(a, b):
    return lax.dot_general(a, b, (((1,), (1,)), ((), ())), preferred_element_type=F32)


def dot_tn(a, b):
    return lax.dot_general(a, b, (((0,), (0,)), ((), ())), preferred_element_type=F32)


def swap_halves(x):
    lane = lax.broadcasted_iota(jnp.int32, x.shape, 1)
    first = lax.rem(lane, HEAD_SIZE) < HEAD_SIZE // 2
    return jnp.where(first, pltpu.roll(x, LANES - HEAD_SIZE // 2, 1), pltpu.roll(x, HEAD_SIZE // 2, 1))


def low_half(shape):
    return lax.broadcasted_iota(jnp.int32, shape, 1) < HEAD_SIZE


def mask_bias(first_len, row0, rows, cols):
    query = row0 + lax.broadcasted_iota(jnp.int32, (rows, cols), 0)
    key = lax.broadcasted_iota(jnp.int32, (rows, cols), 1)
    start = jnp.where(query >= first_len, first_len, 0)
    return jnp.where((key <= query) & (key >= start), 0.0, NEGATIVE_BIG)


def attention_backward_kernel(length_ref, g_ref, q_ref, k_ref, v_ref, lse_ref, cos_ref, sin_ref, dq_ref, dkv_ref, dk_sum, dv_sum):
    pair = pl.program_id(0)
    tokens = q_ref.shape[0]

    @pl.when(pair == 0)
    def _():
        dk_sum[...] = jnp.zeros_like(dk_sum)
        dv_sum[...] = jnp.zeros_like(dv_sum)

    first_len = length_ref[0]
    for block in range(tokens // ROWS):
        rows = pl.ds(block * ROWS, ROWS)
        end = (block + 1) * ROWS
        bias = mask_bias(first_len, block * ROWS, ROWS, end)
        query, grad = q_ref[rows, :], g_ref[rows, :]
        low = low_half(query.shape)
        keys, values = k_ref[:end, :], v_ref[:end, :]
        parts = []
        for half in range(2):
            chosen = low if half == 0 else jnp.logical_not(low)
            own_query = jnp.where(chosen, query, jnp.zeros_like(query))
            own_grad = jnp.where(chosen, grad, jnp.zeros_like(grad))
            scores = dot_nt(own_query, keys) + bias
            probs = jnp.exp(scores - lse_ref[0, rows, half : half + 1])
            prob_grad = dot_nt(own_grad, values)
            delta = jnp.sum(probs * prob_grad, axis=-1, keepdims=True)
            score_grad = (probs * (prob_grad - delta)).astype(BF16)
            parts.append(dot_nn(score_grad, keys))
            dk_sum[:end, :] += dot_tn(score_grad, own_query)
            dv_sum[:end, :] += dot_tn(probs.astype(BF16), own_grad)
        dq = jnp.where(low_half(parts[0].shape), parts[0], parts[1]) * SCORE_SCALE
        dq_ref[rows, :] = (dq * cos_ref[rows, :] - swap_halves(dq) * sin_ref[rows, :]).astype(BF16)

    @pl.when(pair == pl.num_programs(0) - 1)
    def _():
        dk = dk_sum[...]
        dk = dk + pltpu.roll(dk, HEAD_SIZE, 1)
        dk = dk * cos_ref[...] - swap_halves(dk) * sin_ref[...]
        dv = dv_sum[...]
        dv = dv + pltpu.roll(dv, HEAD_SIZE, 1)
        dkv_ref[...] = jnp.where(low_half(dk.shape), dk, dv).astype(BF16)


def attention_backward(grads, q_rot, k_rot, v_rows, lse, cos, sin, lengths):
    tokens = q_rot.shape[0]
    pairs = q_rot.shape[1] // LANES
    one = pl.BlockSpec((tokens, LANES), lambda j: (0, 0))
    each = pl.BlockSpec((tokens, LANES), lambda j: (0, j))
    return pl.pallas_call(
        attention_backward_kernel,
        grid=(pairs,),
        in_specs=[
            pl.BlockSpec(memory_space=pltpu.SMEM),
            each,
            each,
            one,
            one,
            pl.BlockSpec((1, tokens, LANES), lambda j: (j, 0, 0)),
            one,
            one,
        ],
        out_specs=[each, one],
        out_shape=[
            jax.ShapeDtypeStruct((tokens, pairs * LANES), BF16),
            jax.ShapeDtypeStruct((tokens, LANES), BF16),
        ],
        scratch_shapes=[pltpu.VMEM((tokens, LANES), F32), pltpu.VMEM((tokens, LANES), F32)],
        compiler_params=pltpu.CompilerParams(vmem_limit_bytes=VMEM_LIMIT),
        cost_estimate=pl.CostEstimate(
            flops=10 * tokens * tokens * LANES * pairs,
            bytes_accessed=12 * tokens * pairs * LANES,
            transcendentals=tokens * tokens * pairs,
        ),
        name="attend_back",
    )(lengths, grads, q_rot, k_rot, v_rows, lse, cos, sin)


def row_block(width):
    return pl.BlockSpec((ROWS, width), lambda i: (i, 0))


def fixed(*shape):
    return pl.BlockSpec(shape, lambda i: (0,) * len(shape))


def params():
    return pltpu.CompilerParams(vmem_limit_bytes=VMEM_LIMIT)


def cost(flops, *arrays):
    moved = sum(a.size * a.dtype.itemsize for a in arrays)
    return pl.CostEstimate(flops=flops, bytes_accessed=moved, transcendentals=0)


def mlp_back_kernel(
    grad_ref, a_ref, b_ref, hidden_ref, gain_ref, gate_ref, up_ref, down_ref, ggrad_ref, ugrad_ref, part_ref, gain_out
):
    mixed_grad = dot_nt(grad_ref[...], down_ref[...])
    ggrad = (mixed_grad * a_ref[...].astype(F32)).astype(BF16)
    ugrad = (mixed_grad * b_ref[...].astype(F32)).astype(BF16)
    ggrad_ref[...] = ggrad
    ugrad_ref[...] = ugrad
    normed_grad = dot_nt(ggrad, gate_ref[...]) + dot_nt(ugrad, up_ref[...])
    hidden = hidden_ref[...].astype(F32)
    r2 = lax.rsqrt(jnp.mean(hidden * hidden, axis=-1, keepdims=True) + EPSILON)
    gain_part = jnp.sum(normed_grad * (hidden * r2), axis=0, keepdims=True)

    @pl.when(pl.program_id(0) == 0)
    def _():
        gain_out[...] = jnp.zeros_like(gain_out)

    gain_out[...] += gain_part
    weighted = normed_grad * gain_ref[...]
    mean = jnp.mean(weighted * hidden, axis=-1, keepdims=True)
    part = r2 * weighted - hidden * (r2 * r2 * r2 * mean)
    own = part_ref.shape[2]
    for c in range(part_ref.shape[0]):
        part_ref[c] = part[:, c * own : (c + 1) * own].astype(BF16)


def mlp_backward(n, mlp_grad, a, b, hidden_all, gain, w_gate, w_up, w_down):
    total, width = hidden_all.shape
    own = width // n
    own_ff = w_gate.shape[1]
    narrow = jax.ShapeDtypeStruct((total, own_ff), BF16)
    planes = pl.BlockSpec((n, ROWS, own), lambda i: (0, i, 0))
    return pl.pallas_call(
        mlp_back_kernel,
        grid=(total // ROWS,),
        in_specs=[
            row_block(width),
            row_block(own_ff),
            row_block(own_ff),
            row_block(width),
            fixed(1, width),
            fixed(width, own_ff),
            fixed(width, own_ff),
            fixed(own_ff, width),
        ],
        out_specs=[row_block(own_ff), row_block(own_ff), planes, fixed(1, width)],
        out_shape=[narrow, narrow, jax.ShapeDtypeStruct((n, total, own), BF16), jax.ShapeDtypeStruct((1, width), F32)],
        compiler_params=params(),
        cost_estimate=cost(6 * total * width * own_ff, mlp_grad, hidden_all, hidden_all, w_gate, w_up, w_down, a, b, a, b),
        name="mlp_backward",
    )(mlp_grad, a, b, hidden_all, gain, w_gate, w_up, w_down)


def branch_kernel(part_ref, grad_ref, w_ref, hidden_ref, branch_ref, out_ref):
    hidden_grad = part_ref[...].astype(F32) + grad_ref[...].astype(F32)
    hidden_ref[...] = hidden_grad
    branch = (RESIDUAL_SCALE * hidden_grad).astype(BF16)
    branch_ref[...] = branch
    own = out_ref.shape[2]
    for c in range(out_ref.shape[0]):
        out_ref[c] = dot_nt(branch, w_ref[c]).astype(BF16)


def branch_backward(hidden_part, grad_own, w_out, n):
    total, own_width = hidden_part.shape
    own = w_out.shape[0] // n
    w_heads = w_out.reshape(n, own, own_width)
    return pl.pallas_call(
        branch_kernel,
        grid=(total // ROWS,),
        in_specs=[row_block(own_width), row_block(own_width), fixed(n, own, own_width)],
        out_specs=[row_block(own_width), row_block(own_width), pl.BlockSpec((n, ROWS, own), lambda i: (0, i, 0))],
        out_shape=[
            jax.ShapeDtypeStruct((total, own_width), F32),
            jax.ShapeDtypeStruct((total, own_width), BF16),
            jax.ShapeDtypeStruct((n, total, own), BF16),
        ],
        compiler_params=params(),
        cost_estimate=cost(2 * total * own_width * own * n, hidden_part, hidden_part, hidden_part, w_out),
        name="branch_backward",
    )(hidden_part, grad_own, w_heads)


def token_kernel(me_ref, dq_ref, dkv_ref, w_ref, x_ref, gain_ref, hidden_ref, part_ref, gain_out):
    split = dq_ref.shape[1]
    normed_grad = dot_nt(dq_ref[...], w_ref[:, :split]) + dot_nt(dkv_ref[...], w_ref[:, split:])
    x = x_ref[...].astype(F32)
    r1 = lax.rsqrt(jnp.mean(x * x, axis=-1, keepdims=True) + EPSILON)

    @pl.when(pl.program_id(0) == 0)
    def _():
        gain_out[...] = jnp.zeros_like(gain_out)

    gain_out[...] += jnp.sum(normed_grad * (x * r1), axis=0, keepdims=True)
    weighted = normed_grad * gain_ref[...]
    mean = jnp.mean(weighted * x, axis=-1, keepdims=True)
    part = r1 * weighted - x * (r1 * r1 * r1 * mean)
    own_width = hidden_ref.shape[1]
    for c in range(part.shape[1] // own_width):
        piece = part[:, c * own_width : (c + 1) * own_width]
        piece = piece + jnp.where(me_ref[0] == c, hidden_ref[...], 0.0)
        part_ref[:, c * own_width : (c + 1) * own_width] = piece.astype(BF16)


def token_backward(me, dq, dkv, w_qkv, x, gain, hidden_grad):
    total, width = x.shape
    own_width = hidden_grad.shape[1]
    return pl.pallas_call(
        token_kernel,
        grid=(total // ROWS,),
        in_specs=[
            pl.BlockSpec(memory_space=pltpu.SMEM),
            row_block(dq.shape[1]),
            row_block(dkv.shape[1]),
            fixed(*w_qkv.shape),
            row_block(width),
            fixed(1, width),
            row_block(own_width),
        ],
        out_specs=[row_block(width), fixed(1, width)],
        out_shape=[jax.ShapeDtypeStruct((total, width), BF16), jax.ShapeDtypeStruct((1, width), F32)],
        compiler_params=params(),
        cost_estimate=cost(2 * total * width * w_qkv.shape[1], x, x, w_qkv, dq, dkv, hidden_grad),
        name="token_backward",
    )(me, dq, dkv, w_qkv, x, gain, hidden_grad)


def result_kernel(me_ref, rows_ref, w_ref, out_ref):
    depth = w_ref.shape[0]
    own = rows_ref.shape[1] - depth
    product = dot_nn(rows_ref[:, :depth], w_ref[...])
    hidden = rows_ref[:, depth:].astype(F32)
    for c in range(out_ref.shape[1] // own):
        lanes = slice(c * own, (c + 1) * own)
        mine = jnp.where(me_ref[0] == c, hidden, 0.0)
        out_ref[:, lanes] = (RESIDUAL_SCALE * (product[:, lanes] + mine)).astype(BF16)


def result_rows(me, rows, w_down):
    total, columns = rows.shape
    depth, width = w_down.shape
    out_shape = jax.ShapeDtypeStruct((total, width), BF16)
    return pl.pallas_call(
        result_kernel,
        grid=(total // ROWS,),
        in_specs=[pl.BlockSpec(memory_space=pltpu.SMEM), row_block(columns), fixed(depth, width)],
        out_specs=row_block(width),
        out_shape=out_shape,
        compiler_params=params(),
        cost_estimate=cost(2 * total * depth * width, rows, w_down, out_shape),
        name="result_rows",
    )(me, rows, w_down)


def finish_kernel(slab, gate_ref, up_ref, down_ref, out_ref, qkv_ref, gate_out, up_out, down_out, out_out, q_out, k_out, v_out):
    n = gate_ref.shape[0]
    for src, dst, piece in ((gate_ref, gate_out, slab), (up_ref, up_out, slab), (out_ref, out_out, out_ref.shape[2])):
        for c in range(n):
            for f in range(src.shape[2] // piece):
                at = (f * n + c) * piece
                dst[:, at : at + piece] = src[c, :, f * piece : (f + 1) * piece].astype(F32)
    down_out[...] = down_ref[...].astype(F32)
    split = qkv_ref.shape[2] - LANES
    for c in range(n):
        q_out[:, c * split : (c + 1) * split] = qkv_ref[c, :, :split].astype(F32)
    for pair in range(n // 2):
        even = qkv_ref[2 * pair, :, split:].astype(F32)
        odd = qkv_ref[2 * pair + 1, :, split:].astype(F32)
        low = low_half(even.shape)
        lanes = slice(pair * LANES, (pair + 1) * LANES)
        k_out[:, lanes] = jnp.where(low, even, pltpu.roll(odd, HEAD_SIZE, 1))
        v_out[:, lanes] = jnp.where(low, pltpu.roll(even, HEAD_SIZE, 1), odd)


def finish(slab, gate, up, down, out, qkv):
    n, rows, own_ff = gate.shape
    width = n * out.shape[2]
    steps = 16
    tile, down_tile = rows // steps, down.shape[0] // steps
    kv = n * HEAD_SIZE

    def by_device(columns):
        return pl.BlockSpec((n, tile, columns), lambda i: (0, i, 0))

    def flat(height, columns):
        return pl.BlockSpec((height, columns), lambda i: (i, 0))

    outs = [
        (flat(tile, n * own_ff), (rows, n * own_ff)),
        (flat(tile, n * own_ff), (rows, n * own_ff)),
        (flat(down_tile, width), down.shape),
        (flat(tile, width), (rows, width)),
        (flat(tile, width), (rows, width)),
        (flat(tile, kv), (rows, kv)),
        (flat(tile, kv), (rows, kv)),
    ]
    return pl.pallas_call(
        functools.partial(finish_kernel, slab),
        grid=(steps,),
        in_specs=[
            by_device(own_ff),
            by_device(own_ff),
            flat(down_tile, width),
            by_device(out.shape[2]),
            by_device(qkv.shape[2]),
        ],
        out_specs=[spec for spec, _ in outs],
        out_shape=[jax.ShapeDtypeStruct(shape, F32) for _, shape in outs],
        compiler_params=params(),
        cost_estimate=cost(0, gate, gate, gate, up, up, up, down, down, down),
        name="finish",
    )(gate, up, down, out, qkv)


def spread_kernel(in_ref, out_ref):
    slab = in_ref.shape[2]
    for c in range(in_ref.shape[0]):
        out_ref[:, c * slab : (c + 1) * slab] = in_ref[c].astype(F32)


def spread_columns(pieces, slab, groups):
    n, rows, _ = pieces.shape
    tile = 128
    out_shape = jax.ShapeDtypeStruct((rows, groups * n * slab), F32)
    return pl.pallas_call(
        spread_kernel,
        grid=(groups, rows // tile),
        in_specs=[pl.BlockSpec((n, tile, slab), lambda f, r: (0, r, f))],
        out_specs=pl.BlockSpec((tile, n * slab), lambda f, r: (r, f)),
        out_shape=out_shape,
        compiler_params=params(),
        cost_estimate=cost(0, pieces, out_shape),
        name="spread_columns",
    )(pieces)


MESH = pl.DeviceIdType.MESH


class Chain:
    def __init__(self, slot, planes, plane, send_sem, recv_sem):
        self.slot, self.planes, self.plane = slot, planes, plane
        self.send_sem, self.recv_sem = send_sem, recv_sem

    def copy(self, way, step, shard, to):
        return pltpu.make_async_remote_copy(
            src_ref=self.slot(shard),
            dst_ref=self.slot(shard),
            send_sem=self.send_sem.at[way, step],
            recv_sem=self.recv_sem.at[way, step],
            device_id={"fsdp": to},
            device_id_type=MESH,
        )

    def moves(self, step):
        p, last = self.plane, self.planes - 1
        return (
            (0, (p >= step) & (p < last), p - step, p + 1, p >= step + 1, p - 1 - step),
            (1, (p + step <= last) & (p > 0), p + step, p - 1, p + step + 1 <= last, p + 1 + step),
        )

    def start(self, step):
        for way, sends, shard, to, _, _ in self.moves(step):

            @pl.when(sends)
            def _(way=way, shard=shard, to=to):
                self.copy(way, step, shard, to).start()

    def arrive(self, step):
        for way, _, _, _, receives, shard in self.moves(step):

            @pl.when(receives)
            def _(way=way, shard=shard):
                self.copy(way, step, shard, self.plane).wait_recv()

    def advance(self, step):
        self.arrive(step - 1)
        self.start(step)

    def drain(self):
        for step in range(self.planes - 1):
            for way, sends, shard, to, _, _ in self.moves(step):

                @pl.when(sends)
                def _(way=way, shard=shard, to=to, step=step):
                    self.copy(way, step, shard, to).wait_send()


class Spread:
    def __init__(self, src, slot, n, me, send_sem, recv_sem):
        self.src, self.slot, self.n, self.me = src, slot, n, me
        self.send_sem, self.recv_sem = send_sem, recv_sem
        self.chips = n // 2
        self.chip, self.core = me // 2, lax.rem(me, 2)
        self.partner = me + 1 - 2 * self.core

    def at(self, k):
        return lax.rem(self.chip + k, self.chips) * 2 + self.core

    def copy(self, src, owner, sem, to):
        return pltpu.make_async_remote_copy(
            src_ref=src,
            dst_ref=self.slot(owner),
            send_sem=self.send_sem.at[sem],
            recv_sem=self.recv_sem.at[sem],
            device_id={"ctx": to},
            device_id_type=MESH,
        )

    def out(self, k):
        return self.copy(self.src, self.me, k, self.at(k))

    def relay(self, k):
        owner = self.at(self.chips - k) if k else self.me
        src = self.slot(owner) if k else self.src
        return self.copy(src, owner, self.chips + k, self.partner)

    def start(self):
        for k in range(1, self.chips):
            self.out(k).start()
        self.relay(0).start()

    def pass_on(self):
        for k in range(1, self.chips):
            self.copy(self.src, self.at(self.chips - k), k, self.me).wait_recv()
            self.relay(k).start()

    def late(self):
        pass

    def finish(self):
        other = 1 - 2 * self.core
        for k in range(self.chips):
            owner = (self.at(self.chips - k) if k else self.me) + other
            self.copy(self.slot(owner), owner, self.chips + k, self.me).wait_recv()

    def drain(self):
        for k in range(1, self.chips):
            self.out(k).wait_send()
        for k in range(self.chips):
            self.relay(k).wait_send()


class Spread4:
    def __init__(self, src, slot, n, me, send_sem, recv_sem):
        self.src, self.slot, self.me = src, slot, me
        self.send_sem, self.recv_sem = send_sem, recv_sem
        self.core = lax.rem(me, 2)
        self.other = 1 - self.core
        chip = me // 2
        self.near, self.side, self.far = square(chip)
        self.chip = chip
        self.half = src.shape[0] // 2

    def copy(self, src, dst, sem, to):
        return pltpu.make_async_remote_copy(
            src_ref=src,
            dst_ref=dst,
            send_sem=self.send_sem.at[sem],
            recv_sem=self.recv_sem.at[sem],
            device_id={"ctx": to},
            device_id_type=MESH,
        )

    def part(self, owner, which):
        return self.slot(owner).at[pl.ds(which * self.half, self.half)]

    def out(self, sem):
        chip = self.near if sem == 1 else self.side
        return self.copy(self.src, self.slot(self.me), sem, chip * 2 + self.core)

    def onward(self, sem):
        origin, to, which = (self.near, self.side, 0) if sem == 3 else (self.side, self.near, 1)
        owner = origin * 2 + self.core
        return self.copy(self.part(owner, which), self.part(owner, which), sem, to * 2 + self.core)

    def relay(self, k):
        owner = (self.chip, self.near, self.side, self.far)[k] * 2 + self.core
        src = self.slot(owner) if k else self.src
        return self.copy(src, self.slot(owner), 4 + k, self.chip * 2 + self.other)

    def start(self):
        self.out(1).start()
        self.out(2).start()
        self.relay(0).start()

    def pass_on(self):
        for k, chip in ((1, self.near), (2, self.side)):
            owner = chip * 2 + self.core
            self.copy(self.src, self.slot(owner), k, self.me).wait_recv()
            self.onward(3 if k == 1 else 0).start()
            self.relay(k).start()

    def late(self):
        owner = self.far * 2 + self.core
        for sem, which in ((3, 0), (0, 1)):
            self.copy(self.part(owner, which), self.part(owner, which), sem, self.me).wait_recv()
        self.relay(3).start()

    def finish(self):
        for k, chip in enumerate((self.chip, self.near, self.side, self.far)):
            owner = chip * 2 + self.other
            self.copy(self.slot(owner), self.slot(owner), 4 + k, self.me).wait_recv()

    def drain(self):
        for sem in (1, 2):
            self.out(sem).wait_send()
        for sem in (3, 0):
            self.onward(sem).wait_send()
        for k in range(4):
            self.relay(k).wait_send()


def square(chip):
    return chip + 1 - 2 * lax.rem(chip, 2), chip + 2 - 4 * (chip // 2), 3 - chip


def spread_over(n, src, *rest):
    return (Spread4 if n == 8 and src.shape[0] % 32 == 0 else Spread)(src, *rest)


def greet(n, planes, me, plane, across):
    barrier = pltpu.get_barrier_semaphore()
    chips = n // 2
    core = lax.rem(me, 2)
    others = [lax.rem(me // 2 + k, chips) * 2 + core for k in range(1, chips)] + [me + 1 - 2 * core]
    for other in others:
        pl.semaphore_signal(barrier, inc=1, device_id={"ctx": other}, device_id_type=MESH)
    if across:

        @pl.when(plane > 0)
        def _():
            pl.semaphore_signal(barrier, inc=1, device_id={"fsdp": plane - 1}, device_id_type=MESH)

        @pl.when(plane < planes - 1)
        def _():
            pl.semaphore_signal(barrier, inc=1, device_id={"fsdp": plane + 1}, device_id_type=MESH)

    count = len(others)
    if across:
        count = count + (plane > 0).astype(jnp.int32) + (plane < planes - 1).astype(jnp.int32)
    pl.semaphore_wait(barrier, count)


def forward_kernel(
    n,
    planes,
    heads,
    length_ref,
    tokens_ref,
    query_ref,
    kv_shard,
    out_ref,
    gate_ref,
    up_ref,
    down_ref,
    gain_shard,
    turns_ref,
    x_out,
    normed_out,
    q_out,
    k_out,
    v_out,
    lse_out,
    att_out,
    hid_out,
    normed2_out,
    a_out,
    b_out,
    mixed_out,
    attn_out,
    gate_out,
    up_out,
    down_out,
    gain_out,
    cos_out,
    sin_out,
    w_attn,
    w_gate,
    w_up,
    w_down,
    gains,
    x_all,
    qkv,
    q_rot,
    k_rot,
    v_rows,
    lse,
    own_att,
    att_all,
    own_hid,
    own_scaled,
    wide,
    narrow,
    cos_ref,
    sin_ref,
    z_send,
    z_recv,
    c_send,
    c_recv,
    keep_sem,
    load_sem,
    wide_sem,
    narrow_sem,
):
    me, plane = lax.axis_index("ctx"), lax.axis_index("fsdp")
    per_device, width = tokens_ref.shape
    total = x_all.shape[0]
    rows_shard = kv_shard.shape[0]
    own = own_att.shape[1]
    own_width = own_hid.shape[1]
    columns = qkv.shape[1]
    blocks = total // ROWS
    pairs = heads // 2

    local_copies = []

    def keep(src, dst, index):
        copy = pltpu.make_async_copy(src, dst, keep_sem.at[index])
        copy.start()
        local_copies.append(copy)

    def chain(index, ref, rows):
        return Chain(lambda s: ref.at[pl.ds(s * rows, rows)], planes, plane, z_send.at[index], z_recv.at[index])

    attn_chain = chain(0, w_attn, rows_shard)
    gate_chain = chain(1, w_gate, rows_shard)
    up_chain = chain(2, w_up, rows_shard)
    slab = w_down.shape[0] // planes
    down_chain = chain(3, w_down, slab)
    gain_chain = chain(4, gains, gain_shard.shape[0])
    own_ff = w_gate.shape[1]
    attn_slot = attn_chain.slot(plane)
    query_src = query_ref.at[:, pl.ds(pl.multiple_of(me * own, LANES), own)]
    out_src = out_ref.at[:, pl.ds(pl.multiple_of(me * own_width, LANES), own_width)]
    attn_loads = [
        pltpu.make_async_copy(query_src, attn_slot.at[:, pl.ds(0, own)], load_sem.at[2, 1]),
        pltpu.make_async_copy(kv_shard, attn_slot.at[:, pl.ds(own, LANES)], load_sem.at[2, 2]),
        pltpu.make_async_copy(out_src, attn_slot.at[:, pl.ds(columns, own_width)], load_sem.at[2, 3]),
    ]
    loads = [pltpu.make_async_copy(gain_shard, gain_chain.slot(plane), keep_sem.at[1])]
    for ref, c, at in ((gate_ref, gate_chain, 0), (up_ref, up_chain, 1)):
        for f in range(ref.shape[1] // (n * slab)):
            src = ref.at[:, pl.ds(pl.multiple_of((f * n + me) * slab, LANES), slab)]
            dst = c.slot(plane).at[:, pl.ds(f * slab, slab)]
            loads.append(pltpu.make_async_copy(src, dst, load_sem.at[at, f]))
        if ref.shape[1] == own_ff:
            loads.append(pltpu.make_async_copy(ref, c.slot(plane), load_sem.at[at, 0]))
    down_src = down_ref if down_ref.shape[0] == slab else down_ref.at[pl.ds(pl.multiple_of(me * slab, slab), slab)]
    loads.append(pltpu.make_async_copy(down_src, down_chain.slot(plane), load_sem.at[2, 0]))
    for load in (*attn_loads, *loads):
        load.start()
    own_x = pltpu.make_async_copy(tokens_ref, x_all.at[pl.ds(me * per_device, per_device)], keep_sem.at[5])
    own_x.start()
    greet(n, planes, me, plane, True)
    for load in attn_loads:
        load.wait()
    attn_chain.start(0)
    loads[0].wait()
    gain_chain.start(0)
    x_spread = spread_over(
        n, tokens_ref, lambda c: x_all.at[pl.ds(c * per_device, per_device)], n, me, c_send.at[0], c_recv.at[0]
    )
    x_spread.start()

    def rotary_block(i, _):
        rows = pl.ds(pl.multiple_of(i * ROWS, ROWS), ROWS)
        given = i * ROWS + lax.broadcasted_iota(jnp.int32, (ROWS, LANES), 0)
        lane = lax.broadcasted_iota(jnp.int32, (ROWS, LANES), 1)
        position = given - jnp.where(given >= length_ref[0], length_ref[0], 0)
        angle = position.astype(F32) * turns_ref[0:1, :]
        cos_ref[rows, :] = jnp.cos(angle)
        sine = jnp.sin(angle)
        sin_ref[rows, :] = jnp.where(lax.rem(lane, HEAD_SIZE) < HEAD_SIZE // 2, -sine, sine)
        return 0

    lax.fori_loop(0, blocks, rotary_block, 0)
    for load in loads[1:]:
        load.wait()
    own_x.wait()
    for step in range(1, planes - 1):
        attn_chain.advance(step)
        gain_chain.advance(step)
    gate_chain.start(0)
    up_chain.start(0)
    x_spread.pass_on()
    x_spread.late()
    x_spread.finish()
    x_copy = pltpu.make_async_copy(x_all, x_out, keep_sem.at[0])
    x_copy.start()
    attn_chain.arrive(planes - 2)
    gain_chain.arrive(planes - 2)
    keep(w_attn, attn_out, 1)
    keep(gains, gain_out, 2)
    half = gain_shard.shape[1] // 2
    step_rows = gain_shard.shape[0]
    attn_gain = jnp.concatenate([gains[f * step_rows : f * step_rows + 1, :half] for f in range(planes)], axis=1)
    mlp_gain = jnp.concatenate([gains[f * step_rows : f * step_rows + 1, half:] for f in range(planes)], axis=1)

    def staged(stage, sem, slot, out, rows, wait_before):
        copy = pltpu.make_async_copy(stage.at[slot], out.at[rows], sem.at[slot])
        return copy.wait() if wait_before else copy.start()

    def project_block(i, _):
        rows = pl.ds(pl.multiple_of(i * ROWS, ROWS), ROWS)
        slot = lax.rem(i, 2)

        @pl.when(i >= 2)
        def _():
            staged(wide, wide_sem, slot, normed_out, rows, True)

        own_hid[rows, :] = x_all[rows, pl.ds(pl.multiple_of(me * own_width, LANES), own_width)]
        x = x_all[rows, :].astype(F32)
        r1 = lax.rsqrt(jnp.mean(x * x, axis=-1, keepdims=True) + EPSILON)
        normed = (x * r1 * attn_gain).astype(BF16)
        wide[slot] = normed
        staged(wide, wide_sem, slot, normed_out, rows, False)
        qkv[rows, :] = dot_nn(normed, w_attn[:, :columns])
        return 0

    lax.fori_loop(0, blocks, project_block, 0)
    for i in range(max(blocks - 2, 0), blocks):
        staged(wide, wide_sem, i % 2, normed_out, pl.ds(i * ROWS, ROWS), True)

    split = columns - LANES
    cos, sin = cos_ref[...], sin_ref[...]
    kv = qkv[:, split:]
    turned = pltpu.roll(kv, HEAD_SIZE, 1)
    low = low_half(kv.shape)
    k = jnp.where(low, kv, turned)
    k_rot[...] = (k * cos + swap_halves(k) * sin).astype(BF16)
    v_rows[...] = jnp.where(low, turned, kv).astype(BF16)
    keep(k_rot, k_out, 3)
    keep(v_rows, v_out, 4)
    first_len = length_ref[0]

    def attend_pair(pair, _):
        lanes = pl.ds(pl.multiple_of(pair * LANES, LANES), LANES)
        q = qkv[:, lanes]
        q_rot[:, lanes] = ((q * cos_ref[...] + swap_halves(q) * sin_ref[...]) * SCORE_SCALE).astype(BF16)
        for block in range(blocks):
            rows = pl.ds(block * ROWS, ROWS)
            end = (block + 1) * ROWS
            bias = mask_bias(first_len, block * ROWS, ROWS, end)
            query = q_rot[rows, lanes]
            lower = low_half(query.shape)
            keys, values = k_rot[:end, :], v_rows[:end, :]
            parts = []
            for side in range(2):
                chosen = lower if side == 0 else jnp.logical_not(lower)
                scores = dot_nt(jnp.where(chosen, query, jnp.zeros_like(query)), keys) + bias
                top = jnp.max(scores, axis=-1, keepdims=True)
                weights = jnp.exp(scores - top)
                whole = jnp.sum(weights, axis=-1, keepdims=True)
                probs = (weights * (1.0 / whole)).astype(BF16)
                parts.append(dot_nn(probs, values))
                lse[pair, rows, side : side + 1] = top + jnp.log(whole)
            own_att[rows, lanes] = jnp.where(low_half(parts[0].shape), parts[0], parts[1]).astype(BF16)
        return 0

    lax.fori_loop(0, pairs, attend_pair, 0)
    att_spread = spread_over(n, own_att, lambda c: att_all.at[c], n, me, c_send.at[1], c_recv.at[1])
    x_copy.wait()
    x_spread.drain()
    att_spread.start()
    own_a = pltpu.make_async_copy(own_att, att_all.at[me], keep_sem.at[5])
    own_a.start()
    keep(q_rot, q_out, 6)
    keep(lse, lse_out, 7)
    if planes > 2:
        gate_chain.advance(1)
        up_chain.advance(1)
    att_spread.pass_on()
    att_spread.late()
    own_a.wait()
    att_spread.finish()
    keep(att_all, att_out, 8)

    def out_block(i, _):
        rows = pl.ds(pl.multiple_of(i * ROWS, ROWS), ROWS)
        acc = jnp.zeros((ROWS, own_width), F32)
        for c in range(n):
            acc += dot_nn(att_all[c, rows, :], w_attn[c * own : (c + 1) * own, columns:])
        hidden = own_hid[rows, :].astype(F32) + RESIDUAL_SCALE * acc
        own_hid[rows, :] = hidden.astype(BF16)
        own_scaled[rows, :] = (hidden * (1.0 / RESIDUAL_SCALE)).astype(BF16)
        return 0

    lax.fori_loop(0, blocks, out_block, 0)
    def hid_slot(c):
        return x_all.at[:, pl.ds(pl.multiple_of(c * own_width, LANES), own_width)]

    hid_spread = spread_over(n, own_hid, hid_slot, n, me, c_send.at[2], c_recv.at[2])
    hid_spread.start()
    keep(own_scaled, mixed_out.at[:, pl.ds(own_ff, own_width)], 13)
    own_h = pltpu.make_async_copy(own_hid, hid_slot(me), keep_sem.at[5])
    own_h.start()
    for step in range(2, planes - 1):
        gate_chain.advance(step)
        up_chain.advance(step)
    down_chain.start(0)
    hid_spread.pass_on()
    hid_spread.late()
    own_h.wait()
    hid_spread.finish()
    keep(x_all, hid_out, 9)
    keep(cos_ref, cos_out, 14)
    keep(sin_ref, sin_out, 15)
    gate_chain.arrive(planes - 2)
    up_chain.arrive(planes - 2)
    keep(w_gate, gate_out, 10)
    keep(w_up, up_out, 11)
    if planes > 2:
        down_chain.advance(1)

    def mlp_copies(i, rows, wait):
        slot = lax.rem(i, 2)
        staged(wide, wide_sem, slot, normed2_out, rows, wait)
        for j, out in enumerate((a_out, b_out, mixed_out.at[:, pl.ds(0, own_ff)])):
            staged(narrow.at[j], narrow_sem.at[j], slot, out, rows, wait)

    def mlp_block(i, _):
        rows = pl.ds(pl.multiple_of(i * ROWS, ROWS), ROWS)
        slot = lax.rem(i, 2)

        @pl.when(i >= 2)
        def _():
            mlp_copies(i, rows, True)

        hidden = x_all[rows, :].astype(F32)
        r2 = lax.rsqrt(jnp.mean(hidden * hidden, axis=-1, keepdims=True) + EPSILON)
        normed = (hidden * r2 * mlp_gain).astype(BF16)
        wide[slot] = normed
        gate = dot_nn(normed, w_gate[...])
        up = dot_nn(normed, w_up[...])
        sig = jax.nn.sigmoid(gate)
        silu = gate * sig
        narrow[2, slot] = (silu * up).astype(BF16)
        narrow[1, slot] = silu.astype(BF16)
        narrow[0, slot] = (up * sig * (1.0 + gate * (1.0 - sig))).astype(BF16)
        mlp_copies(i, rows, False)
        return 0

    lax.fori_loop(0, blocks, mlp_block, 0)
    for step in range(2, planes - 1):
        down_chain.advance(step)
    for i in range(max(blocks - 2, 0), blocks):
        mlp_copies(i, pl.ds(i * ROWS, ROWS), True)
    down_chain.arrive(planes - 2)
    keep(w_down, down_out, 12)
    for c in (attn_chain, gain_chain, gate_chain, up_chain, down_chain):
        c.drain()
    for s in (att_spread, hid_spread):
        s.drain()
    for copy in local_copies:
        copy.wait()


def forward(n, planes, heads, slab, lengths, tokens, query, kv_shard, out, gate, up, down, gain_shard, turns):
    per_device, width = tokens.shape
    total = per_device * n
    own = heads * HEAD_SIZE
    columns = own + 2 * HEAD_SIZE
    own_width = width // n
    own_ff = planes * slab
    rows_shard = kv_shard.shape[0]
    pairs = heads // 2
    weights = [
        ((planes * rows_shard, columns + own_width), BF16),
        ((planes * rows_shard, own_ff), BF16),
        ((planes * rows_shard, own_ff), BF16),
        ((own_ff, width), BF16),
        ((planes * gain_shard.shape[0], gain_shard.shape[1]), F32),
    ]
    outs = [
        ((total, width), BF16),
        ((total, width), BF16),
        ((total, own), BF16),
        ((total, LANES), BF16),
        ((total, LANES), BF16),
        ((pairs, total, LANES), F32),
        ((n, total, own), BF16),
        ((total, width), BF16),
        ((total, width), BF16),
        ((total, own_ff), BF16),
        ((total, own_ff), BF16),
        ((total, own_ff + own_width), BF16),
    ] + weights + [((total, LANES), F32)] * 2
    scratch = weights + [
        ((total, width), BF16),
        ((total, columns), F32),
        ((total, own), BF16),
        ((total, LANES), BF16),
        ((total, LANES), BF16),
        ((pairs, total, LANES), F32),
        ((total, own), BF16),
        ((n, total, own), BF16),
        ((total, own_width), BF16),
        ((total, own_width), BF16),
        ((2, ROWS, width), BF16),
        ((3, 2, ROWS, own_ff), BF16),
        ((total, LANES), F32),
        ((total, LANES), F32),
    ]
    steps = max(planes - 1, 1)
    dma = pltpu.SemaphoreType.DMA
    anywhere = pl.BlockSpec(memory_space=pl.ANY)
    vmem = pl.BlockSpec(memory_space=pltpu.VMEM)
    return pl.pallas_call(
        functools.partial(forward_kernel, n, planes, heads),
        in_specs=[pl.BlockSpec(memory_space=pltpu.SMEM), vmem] + [anywhere] * 7 + [vmem],
        out_specs=[anywhere] * len(outs),
        out_shape=[jax.ShapeDtypeStruct(*o) for o in outs],
        scratch_shapes=[pltpu.VMEM(*s) for s in scratch]
        + [dma((5, 2, steps)), dma((5, 2, steps)), dma((3, n)), dma((3, n)), dma((16,)), dma((3, max(planes, 4))), dma((2,)), dma((3, 2))],
        compiler_params=pltpu.CompilerParams(
            vmem_limit_bytes=VMEM_LIMIT, collective_id=1, has_side_effects=True
        ),
        cost_estimate=pl.CostEstimate(
            flops=2 * total * width * (columns + own_width + 2 * own_ff),
            bytes_accessed=60 * 1024 * 1024,
            transcendentals=0,
        ),
        name="forward",
    )(lengths, tokens, query, kv_shard, out, gate, up, down, gain_shard, turns)


def add_into(dst, src):
    rows_in, columns = dst.shape
    chunk = max(c for c in (256, 128, 64, 32) if c == 32 or (rows_in % c == 0 and c * columns <= 65536))

    def step(i, _):
        rows = pl.ds(pl.multiple_of(i * chunk, chunk), chunk)
        dst[rows, :] = (dst[rows, :].astype(F32) + src[rows, :].astype(F32)).astype(dst.dtype)
        return 0

    if rows_in < chunk:
        dst[...] = dst[...] + src[...]
    else:
        lax.fori_loop(0, rows_in // chunk, step, 0)


def fetch(src, dst, sem):
    copy = pltpu.make_async_copy(src, dst, sem)
    copy.start()
    copy.wait()


class Settle:
    def __init__(self, block, landed, stage, planes, plane, send_sem, recv_sem, load_sem):
        self.block, self.landed, self.stage = block, landed, stage
        self.planes, self.plane = planes, plane
        self.send_sem, self.recv_sem, self.load_sem = send_sem, recv_sem, load_sem

    def slot(self, way, shard, at):
        return shard if way == 0 else jnp.where(shard == at, self.planes, shard)

    def sends(self, step):
        p, last = self.plane, self.planes - 1
        return (
            (0, (p <= step) & (p < last), last - step + p, p + 1),
            (1, (last - p <= step) & (p > 0), step - last + p, p - 1),
        )

    def receives(self, step):
        p, last = self.plane, self.planes - 1
        return (
            (0, (p >= 1) & (p - 1 <= step), last - step + p - 1),
            (1, (p <= last - 1) & (last - p - 1 <= step), step - last + p + 1),
        )

    def copy(self, way, step, shard, to):
        return pltpu.make_async_remote_copy(
            src_ref=self.block(shard),
            dst_ref=self.landed.at[self.slot(way, shard, to)],
            send_sem=self.send_sem.at[way, step],
            recv_sem=self.recv_sem.at[way, step],
            device_id={"fsdp": to},
            device_id_type=MESH,
        )

    def start(self, step=0):
        ahead = [step + 1] if step else [0, 1]
        for way in range(2):
            end = self.plane == (0, self.planes - 1)[way]
            _, active, shard, to = self.sends(step)[way]

            @pl.when(active & jnp.logical_not(end))
            def _(way=way, shard=shard, to=to):
                self.copy(way, step, shard, to).start()

            @pl.when(end)
            def _(way=way):
                for later in ahead:
                    if later < self.planes - 1:
                        _, _, shard, to = self.sends(later)[way]
                        self.copy(way, later, shard, to).start()

    def take(self, step):
        for way, active, shard in self.receives(step):

            @pl.when(active)
            def _(way=way, shard=shard):
                self.copy(way, step, shard, self.plane).wait_recv()
                fetch(self.landed.at[self.slot(way, shard, self.plane)], self.stage, self.load_sem)
                add_into(self.block(shard), self.stage)

    def advance(self, step):
        self.take(step - 1)
        self.start(step)

    def drain(self):
        for step in range(self.planes - 1):
            for way, active, shard, to in self.sends(step):

                @pl.when(active)
                def _(way=way, shard=shard, to=to, step=step):
                    self.copy(way, step, shard, to).wait_send()


class Scatter:
    def __init__(self, block, near, far, stage, me, send_sem, recv_sem, load_sem):
        self.block, self.landed, self.far, self.stage = block, near, far, stage
        self.send_sem, self.recv_sem, self.load_sem = send_sem, recv_sem, load_sem
        self.core = lax.rem(me, 2)
        self.chip = me // 2
        self.chips = (self.chip, *square(self.chip))
        self.half = stage[0].shape[0] // 2

    def rows(self, which):
        return pl.ds(which * self.half, self.half)

    def own(self, k):
        return self.block(self.chips[k] * 2 + self.core)

    def copy(self, src, dst, sem, chip, core):
        return pltpu.make_async_remote_copy(
            src_ref=src,
            dst_ref=dst,
            send_sem=self.send_sem.at[sem],
            recv_sem=self.recv_sem.at[sem],
            device_id={"ctx": chip * 2 + core},
            device_id_type=MESH,
        )

    def first(self, k):
        other = 1 - self.core
        return self.copy(self.block(self.chips[k] * 2 + other), self.landed.at[k], k, self.chip, other)

    def second(self, k, to, which):
        place = self.far.at[to - 1 if k == to else 2, self.rows(which)]
        sem = 4 + 2 * (to - 1) + which if k == to else 7 + to
        return self.copy(self.own(k).at[self.rows(which)], place, sem, self.chips[to], self.core)

    def start(self):
        for k in (3, 1, 2, 0):
            self.first(k).start()

    def add_all(self, items):
        pending = None

        def complete(copy, dst, stage, then):
            copy.wait()
            add_into(dst, stage)
            for remote in then:
                remote.start()

        for index, (arrivals, src, dst, then) in enumerate(items):
            for remote in arrivals:
                remote.wait_recv()
            stage = self.stage[index % 2].at[pl.ds(0, dst.shape[0])]
            copy = pltpu.make_async_copy(src, stage, self.load_sem.at[index % 2])
            copy.start()
            if pending is not None:
                complete(*pending)
            pending = (copy, dst, stage, then)
        complete(*pending)

    def pass_on(self):
        self.add_all(
            [
                ([self.first(3)], self.landed.at[3], self.own(3), [self.second(3, 1, 0), self.second(3, 2, 1)]),
                ([self.first(1)], self.landed.at[1], self.own(1), [self.second(1, 1, 0)]),
                ([self.first(2)], self.landed.at[2], self.own(2), [self.second(2, 2, 1)]),
            ]
        )

    def late(self):
        self.add_all(
            [
                (
                    [self.second(3, to, which)],
                    self.far.at[2, self.rows(which)],
                    self.own(k).at[self.rows(which)],
                    [self.second(k, k, which)],
                )
                for to, which, k in ((1, 0, 2), (2, 1, 1))
            ]
        )

    def finish(self, total):
        items = [([self.first(0)], self.landed.at[0], total, [])]
        for k in (1, 2):
            items.append(([self.second(k, k, which) for which in (0, 1)], self.far.at[k - 1], total, []))
        self.add_all(items)

    def drain(self):
        for k in range(4):
            self.first(k).wait_send()
        for k, to, which in ((3, 1, 0), (3, 2, 1), (1, 1, 0), (1, 1, 1), (2, 2, 0), (2, 2, 1)):
            self.second(k, to, which).wait_send()


def backward_kernel(
    n,
    planes,
    heads,
    length_ref,
    grad_in,
    mixed_in,
    a_in,
    b_in,
    hidden_in,
    normed2_in,
    normed_in,
    x_in,
    att_in,
    q_in,
    k_in,
    v_in,
    lse_in,
    cos_in,
    sin_in,
    attn_in,
    gate_in,
    up_in,
    down_in,
    gain_in,
    token_out,
    gain_out,
    down_all,
    gate_all,
    up_all,
    out_all,
    qkv_all,
    near1,
    far1,
    near2,
    far2,
    near3,
    far3,
    down_landed,
    gate_landed,
    up_landed,
    out_landed,
    qkv_landed,
    w_attn,
    w_gate,
    w_up,
    w_down,
    p_down,
    gains,
    grad,
    a_v,
    b_v,
    part,
    hid_stage,
    stage_tall,
    stage_wide,
    stage_col,
    hidden_grad,
    lse,
    cos,
    sin,
    dk_sum,
    dv_sum,
    gain_own,
    gain_all,
    gain_landed,
    gain_stage,
    z_send,
    z_recv,
    s_send,
    s_recv,
    g_send,
    g_recv,
    load_sem,
    hid_sem,
    add_sem,
    ring_sem,
):
    me, plane = lax.axis_index("ctx"), lax.axis_index("fsdp")
    total, width = grad.shape
    per_device = total // n
    own = heads * HEAD_SIZE
    own_width = width // n
    own_ff = a_v.shape[1]
    rows_shard = width // planes
    slab = own_ff // planes
    blocks = total // ROWS
    pairs = heads // 2
    columns = own + LANES
    last = planes - 2

    def load(src, dst, index):
        copy = pltpu.make_async_copy(src, dst, load_sem.at[index])
        copy.start()
        return copy

    mixed_loads = [load(mixed_in.at[:, pl.ds(d * own_width, own_width)], part.at[d], d) for d in range(own_ff // own_width)]
    grad_load = load(grad_in, grad, 8)
    down_load = load(down_in, w_down, 9)
    gate_load = load(gate_in, w_gate, 10)
    up_load = load(up_in, w_up, 11)
    a_load = load(a_in, a_v, 12)
    b_load = load(b_in, b_v, 13)
    attn_load = load(attn_in, w_attn, 14)
    gain_load = load(gain_in, gains, 15)
    greet(n, planes, me, plane, True)

    def settle(index, block, landed, stage):
        return Settle(block, landed, stage, planes, plane, z_send.at[index], z_recv.at[index], add_sem)

    def rows_of(ref, rows):
        return lambda d: ref.at[pl.ds(pl.multiple_of(d * rows, rows), rows)]

    def out_block_of(d):
        return w_down.at[pl.ds(0, rows_shard), pl.ds(pl.multiple_of(d * own_width, LANES), own_width)]

    def qkv_block_of(d):
        return w_down.at[pl.ds(rows_shard, rows_shard), pl.ds(pl.multiple_of(d * columns, LANES), columns)]

    def gain_block_of(d):
        return gain_own.at[:, pl.ds(pl.multiple_of(d * rows_shard, LANES), rows_shard)]

    down_sum = settle(0, rows_of(p_down, slab), down_landed, stage_wide)
    gate_sum = settle(1, rows_of(w_gate, rows_shard), gate_landed, stage_tall)
    up_sum = settle(2, rows_of(w_up, rows_shard), up_landed, stage_tall)
    out_sum = settle(3, out_block_of, out_landed, stage_tall.at[:, pl.ds(0, own_width)])
    qkv_sum = settle(4, qkv_block_of, qkv_landed, stage_tall.at[:, pl.ds(0, columns)])
    gain_sum = settle(5, gain_block_of, gain_landed, gain_stage)

    def spread(index, src, dst):
        return spread_over(n, src, lambda c: dst.at[c], n, me, g_send.at[index], g_recv.at[index])

    spreads = []

    def give(index, sums, dst):
        src = sums.block(plane)
        mine = load(src, dst.at[me], 16 + index)
        out = spread(index, src, dst)
        out.start()
        spreads.append((out, mine))
        return out

    def scatter(index, block, near, far, stage):
        return Scatter(block, near, far, stage, me, s_send.at[index], s_recv.at[index], ring_sem)

    part_rows = total // 2
    col_stages = [stage_col.at[pl.ds(i * part_rows, part_rows)] for i in range(2)]

    def half_scatter(index, near, far, side):
        rows = pl.ds(side * part_rows, part_rows)
        return scatter(
            2 * index + side, lambda c: part.at[c, rows], near.at[:, rows], far.at[:, rows], col_stages
        )

    first = [half_scatter(0, near1, far1, side) for side in range(2)]
    second = [half_scatter(1, near2, far2, side) for side in range(2)]

    grad_load.wait()

    for copy in mixed_loads:
        copy.wait()

    def down_block(i, _):
        d = jnp.where(i == 0, planes - 1, jnp.where(i == 1, 0, planes - i))
        rows = pl.ds(pl.multiple_of(d * own_width, own_width), own_width)
        p_down[rows, :] = (RESIDUAL_SCALE * dot_tn(part[d], grad[...])).astype(BF16)

        return 0

    lax.fori_loop(0, planes, down_block, 0)
    down_sum.start()

    for copy in (down_load, gate_load, up_load, a_load, b_load, attn_load, gain_load):
        copy.wait()
    half = gains.shape[1] // 2
    attn_gain = jnp.concatenate([gains[f * 8 : f * 8 + 1, :half] for f in range(planes)], axis=1)
    mlp_gain = jnp.concatenate([gains[f * 8 : f * 8 + 1, half:] for f in range(planes)], axis=1)
    gain_own[...] = jnp.zeros_like(gain_own)

    def stream(src, i, wait):
        rows = pl.ds(pl.multiple_of(i * ROWS, ROWS), ROWS)
        slot = lax.rem(i, 2)
        copy = pltpu.make_async_copy(src.at[rows], hid_stage.at[slot], hid_sem.at[slot])
        return copy.wait() if wait else copy.start()

    stream(hidden_in, jnp.int32(0), False)

    def mlp_block(i, _):
        rows = pl.ds(pl.multiple_of(i * ROWS, ROWS), ROWS)

        @pl.when(i + 1 < blocks)
        def _():
            stream(hidden_in, i + 1, False)

        mixed_grad = RESIDUAL_SCALE * dot_nt(grad[rows, :], w_down[...])
        ggrad = (mixed_grad * a_v[rows, :].astype(F32)).astype(BF16)
        ugrad = (mixed_grad * b_v[rows, :].astype(F32)).astype(BF16)
        a_v[rows, :] = ggrad
        b_v[rows, :] = ugrad
        normed_grad = dot_nt(ggrad, w_gate[...]) + dot_nt(ugrad, w_up[...])
        stream(hidden_in, i, True)

        hidden = hid_stage[lax.rem(i, 2)].astype(F32)
        r2 = lax.rsqrt(jnp.mean(hidden * hidden, axis=-1, keepdims=True) + EPSILON)
        gain_own[0:1, :] += jnp.sum(normed_grad * (hidden * r2), axis=0, keepdims=True)
        weighted = normed_grad * mlp_gain
        mean = jnp.mean(weighted * hidden, axis=-1, keepdims=True)
        piece = r2 * weighted - hidden * (r2 * r2 * r2 * mean)
        for c in range(n):
            part[c, rows, :] = piece[:, c * own_width : (c + 1) * own_width].astype(BF16)

        @pl.when(i == blocks // 2 - 1)
        def _():
            first[0].start()

        @pl.when(i == blocks - 2)
        def _():
            down_sum.advance(1)
            first[0].pass_on()

        return 0

    lax.fori_loop(0, blocks, mlp_block, 0)
    first[1].start()
    normed2_load = load(normed2_in, grad, 8)
    normed2_load.wait()

    def columns_times(right, out, low, high):
        def block(j, _):
            lanes = pl.ds(pl.multiple_of(j * ROWS, ROWS), ROWS)
            out[lanes, :] = dot_tn(grad[:, lanes], right[...]).astype(BF16)
            return 0

        lax.fori_loop(low, high, block, 0)

    first[0].late()
    columns_times(a_v, w_gate, 0, width // ROWS)
    gate_sum.start()
    first[1].pass_on()
    columns_times(b_v, w_up, 0, width // ROWS // 2)
    first[1].late()
    columns_times(b_v, w_up, width // ROWS // 2, width // ROWS)
    down_sum.advance(2)

    att_loads = [load(att_in.at[c], grad.at[:, pl.ds(c * own, own)], c) for c in range(n)]
    own_grad = load(grad_in.at[:, pl.ds(pl.multiple_of(me * own_width, LANES), own_width)], b_v.at[:, pl.ds(LANES, own_width)], 8)
    q_load = load(q_in, a_v.at[:, pl.ds(0, own)], 9)
    k_load = load(k_in, a_v.at[:, pl.ds(own, LANES)], 10)
    v_load = load(v_in, a_v.at[:, pl.ds(own + LANES, LANES)], 11)
    lse_load = load(lse_in, lse, 12)
    cos_load = load(cos_in, cos, 13)
    sin_load = load(sin_in, sin, 14)
    own_grad.wait()

    def begin(i, _):
        rows = pl.ds(pl.multiple_of(i * ROWS, ROWS), ROWS)
        hidden_grad[rows, :] = b_v[rows, LANES : LANES + own_width].astype(F32) + part[me, rows, :].astype(F32)
        return 0

    lax.fori_loop(0, blocks, begin, 0)
    for side in range(2):
        first[side].finish(hidden_grad.at[pl.ds(side * part_rows, part_rows)])
        first[side].drain()

    def branch_block(i, _):
        rows = pl.ds(pl.multiple_of(i * ROWS, ROWS), ROWS)
        branch = (RESIDUAL_SCALE * hidden_grad[rows, :]).astype(BF16)
        b_v[rows, LANES : LANES + own_width] = branch
        for c in range(n):
            part[c, rows, :] = dot_nt(branch, w_attn[c * own : (c + 1) * own, columns:]).astype(BF16)

        @pl.when(i == blocks // 2 - 1)
        def _():
            second[0].start()

        return 0

    lax.fori_loop(0, blocks, branch_block, 0)
    second[1].start()
    second[0].pass_on()
    gate_sum.advance(1)
    for copy in att_loads:
        copy.wait()
    heads_per_shard = rows_shard // own
    for c in range(n):
        place = out_block_of(c // heads_per_shard).at[pl.ds((c % heads_per_shard) * own, own)]
        place[...] = dot_tn(grad[:, c * own : (c + 1) * own], b_v[:, LANES : LANES + own_width]).astype(BF16)
    second[1].pass_on()
    second[0].late()
    normed_load = load(normed_in, grad, 15)
    down_sum.take(last)
    up_sum.start()
    second[1].late()
    second[0].finish(part.at[me, pl.ds(0, part_rows)])
    down_give = give(0, down_sum, down_all)
    gate_sum.advance(2)

    for copy in (q_load, k_load, v_load, lse_load, cos_load, sin_load):
        copy.wait()
    dk_sum[...] = jnp.zeros_like(dk_sum)
    dv_sum[...] = jnp.zeros_like(dv_sum)
    first_len = length_ref[0]
    dq_at = own + 2 * LANES

    def attend_pair(side, pair, _):
        lanes = pl.ds(pl.multiple_of(pair * LANES, LANES), LANES)
        dq_lanes = pl.ds(pl.multiple_of(dq_at + pair * LANES, LANES), LANES)
        for block in range(side * (blocks // 2), (side + 1) * (blocks // 2)):
            rows = pl.ds(block * ROWS, ROWS)
            end = (block + 1) * ROWS
            bias = mask_bias(first_len, block * ROWS, ROWS, end)
            query, grads = a_v[rows, lanes], part[me, rows, lanes]
            low = low_half(query.shape)
            keys, values = a_v[:end, own : own + LANES], a_v[:end, own + LANES : own + 2 * LANES]
            parts = []
            for head in range(2):
                chosen = low if head == 0 else jnp.logical_not(low)
                own_query = jnp.where(chosen, query, jnp.zeros_like(query))
                own_grads = jnp.where(chosen, grads, jnp.zeros_like(grads))
                scores = dot_nt(own_query, keys) + bias
                probs = jnp.exp(scores - lse[pair, rows, head : head + 1])
                prob_grad = dot_nt(own_grads, values)
                delta = jnp.sum(probs * prob_grad, axis=-1, keepdims=True)
                score_grad = (probs * (prob_grad - delta)).astype(BF16)
                parts.append(dot_nn(score_grad, keys))
                dk_sum[:end, :] += dot_tn(score_grad, own_query)
                dv_sum[:end, :] += dot_tn(probs.astype(BF16), own_grads)
            dq = jnp.where(low_half(parts[0].shape), parts[0], parts[1]) * SCORE_SCALE
            a_v[rows, dq_lanes] = (dq * cos[rows, :] - swap_halves(dq) * sin[rows, :]).astype(BF16)

        if side:

            @pl.when(pair == 0)
            def _():
                down_give.pass_on()
                up_sum.advance(1)

        return 0

    lax.fori_loop(0, pairs, functools.partial(attend_pair, 0), 0)
    second[1].finish(part.at[me, pl.ds(part_rows, part_rows)])
    lax.fori_loop(0, pairs, functools.partial(attend_pair, 1), 0)
    dk = dk_sum[...]
    dk = dk + pltpu.roll(dk, HEAD_SIZE, 1)
    dk = dk * cos[...] - swap_halves(dk) * sin[...]
    dv = dv_sum[...]
    dv = dv + pltpu.roll(dv, HEAD_SIZE, 1)
    b_v[:, :LANES] = jnp.where(low_half(dk.shape), dk, dv).astype(BF16)
    down_give.late()
    gate_sum.take(last)
    gate_give = give(1, gate_sum, gate_all)
    up_sum.advance(2)
    out_sum.start()

    normed_load.wait()
    dq_end = dq_at + own
    for d in range(planes):
        for j in range(rows_shard // ROWS):
            lanes = slice(d * rows_shard + j * ROWS, d * rows_shard + (j + 1) * ROWS)
            place = qkv_block_of(d).at[pl.ds(j * ROWS, ROWS)]
            place[:, :own] = dot_tn(grad[:, lanes], a_v[:, dq_at:dq_end]).astype(BF16)
            place[:, own:] = dot_tn(grad[:, lanes], b_v[:, :LANES]).astype(BF16)
    gate_give.pass_on()
    out_sum.advance(1)
    qkv_sum.start()

    stream(x_in, jnp.int32(0), False)

    def token_block(i, _):
        rows = pl.ds(pl.multiple_of(i * ROWS, ROWS), ROWS)

        @pl.when(i + 1 < blocks)
        def _():
            stream(x_in, i + 1, False)

        normed_grad = dot_nt(a_v[rows, dq_at:dq_end], w_attn[:, :own]) + dot_nt(b_v[rows, :LANES], w_attn[:, own:columns])
        stream(x_in, i, True)
        x = hid_stage[lax.rem(i, 2)].astype(F32)
        r1 = lax.rsqrt(jnp.mean(x * x, axis=-1, keepdims=True) + EPSILON)
        gain_own[1:2, :] += jnp.sum(normed_grad * (x * r1), axis=0, keepdims=True)
        weighted = normed_grad * attn_gain
        mean = jnp.mean(weighted * x, axis=-1, keepdims=True)
        piece = r1 * weighted - x * (r1 * r1 * r1 * mean)
        for c in range(n):
            lanes = slice(c * own_width, (c + 1) * own_width)
            mine = jnp.where(me == c, hidden_grad[rows, :], 0.0)
            grad[rows, lanes] = (piece[:, lanes] + mine).astype(BF16)
        return 0

    lax.fori_loop(0, blocks, token_block, 0)

    def token_rows(c):
        return grad.at[pl.ds(pl.multiple_of(c * per_device, per_device), per_device)]

    third = scatter(4, token_rows, near3, far3, [hid_stage.at[i, pl.ds(0, per_device)] for i in range(2)])
    third.start()
    gain_give = spread(5, gain_own, gain_all)
    gain_mine = load(gain_own, gain_all.at[me], 21)
    gain_give.start()
    gate_give.late()
    third.pass_on()
    gain_give.pass_on()
    out_sum.advance(2)
    third.late()
    gain_give.finish()
    gain_mine.wait()
    gain_give.drain()
    gain_own[...] = sum(gain_all[c] for c in range(n))
    gain_sum.start()
    token_out[...] = token_rows(me)[...].astype(F32)
    qkv_sum.advance(1)
    third.finish(token_out)
    up_sum.take(last)
    up_give = give(2, up_sum, up_all)
    gain_sum.advance(1)
    out_sum.take(last)
    out_give = give(3, out_sum, out_all)
    qkv_sum.advance(2)
    gain_sum.advance(2)
    up_give.pass_on()
    out_give.pass_on()
    up_give.late()
    gain_sum.take(last)
    gain_out[...] = gain_block_of(plane)[...]
    qkv_sum.take(last)
    qkv_give = give(4, qkv_sum, qkv_all)
    out_give.late()
    qkv_give.pass_on()
    qkv_give.late()
    for out, mine in spreads:
        out.finish()
        out.drain()
        mine.wait()
    for s in (*second, third):
        s.drain()
    for s in (down_sum, gate_sum, up_sum, out_sum, qkv_sum, gain_sum):
        s.drain()


def backward(n, planes, heads, lengths, grad, saved, weights, cos, sin):
    x, normed, q_rot, k_rot, v_rows, lse, att_all, hidden, normed2, a, b, mixed = saved
    w_attn, w_gate, w_up, w_down, gains = weights
    total, width = grad.shape
    own = heads * HEAD_SIZE
    own_width = width // n
    own_ff = a.shape[1]
    rows_shard = width // planes
    slab = own_ff // planes
    columns = own + LANES
    chips = n // 2
    per_device = total // n
    col, row = (chips, total, own_width), (chips, per_device, width)
    outs = [
        ((per_device, width), F32),
        ((8, rows_shard), F32),
        ((n, slab, width), BF16),
        ((n, rows_shard, own_ff), BF16),
        ((n, rows_shard, own_ff), BF16),
        ((n, rows_shard, own_width), BF16),
        ((n, rows_shard, columns), BF16),
        (col, BF16),
        (col, BF16),
        (col, BF16),
        (col, BF16),
        (row, BF16),
        (row, BF16),
        ((planes + 1, slab, width), BF16),
        ((planes + 1, rows_shard, own_ff), BF16),
        ((planes + 1, rows_shard, own_ff), BF16),
        ((planes + 1, rows_shard, own_width), BF16),
        ((planes + 1, rows_shard, columns), BF16),
    ]
    scratch = [
        (w_attn.shape, BF16),
        (w_gate.shape, BF16),
        (w_up.shape, BF16),
        (w_down.shape, BF16),
        (w_down.shape, BF16),
        (gains.shape, F32),
        ((total, width), BF16),
        ((total, own_ff), BF16),
        ((total, own_ff), BF16),
        ((n, total, own_width), BF16),
        ((2, ROWS, width), BF16),
        ((rows_shard, own_ff), BF16),
        ((slab, width), BF16),
        ((total, own_width), BF16),
        ((total, own_width), F32),
        (lse.shape, F32),
        (cos.shape, F32),
        (sin.shape, F32),
        ((total, LANES), F32),
        ((total, LANES), F32),
        ((8, width), F32),
        ((n, 8, width), F32),
        ((planes + 1, 8, rows_shard), F32),
        ((8, rows_shard), F32),
    ]
    steps = planes - 1
    dma = pltpu.SemaphoreType.DMA
    anywhere = pl.BlockSpec(memory_space=pl.ANY)
    vmem = pl.BlockSpec(memory_space=pltpu.VMEM)
    return pl.pallas_call(
        functools.partial(backward_kernel, n, planes, heads),
        in_specs=[pl.BlockSpec(memory_space=pltpu.SMEM)] + [anywhere] * 20,
        out_specs=[vmem] * 2 + [anywhere] * (len(outs) - 2),
        out_shape=[jax.ShapeDtypeStruct(*o) for o in outs],
        scratch_shapes=[pltpu.VMEM(*s) for s in scratch]
        + [
            dma((6, 2, steps)),
            dma((6, 2, steps)),
            dma((5, 10)),
            dma((5, 10)),
            dma((6, n)),
            dma((6, n)),
            dma((24,)),
            dma((2,)),
            dma,
            dma((2,)),
        ],
        compiler_params=pltpu.CompilerParams(
            vmem_limit_bytes=60 * 1024 * 1024, collective_id=2, has_side_effects=True
        ),
        cost_estimate=pl.CostEstimate(
            flops=16 * total * width * own_ff, bytes_accessed=100 * 1024 * 1024, transcendentals=0
        ),
        name="backward",
    )(
        lengths,
        grad,
        mixed,
        a,
        b,
        hidden,
        normed2,
        normed,
        x,
        att_all,
        q_rot,
        k_rot,
        v_rows,
        lse,
        cos,
        sin,
        w_attn,
        w_gate,
        w_up,
        w_down,
        gains,
    )[:7]


def kernel_fits(n, planes, total, width, own_ff):
    held = 4 * width * own_ff + 2 * total * width + 2 * total * own_ff
    return planes == 4 and total % (2 * ROWS) == 0 and n == 8 and own_ff // planes >= total // n and n * own_ff == planes * width and 2 * held < 44 * 1024 * 1024 and (own_ff // planes) % LANES == 0


def own_columns(array, index, width):
    return lax.dynamic_slice_in_dim(array, index * width, width, axis=1)


def after(value, *others):
    return lax.optimization_barrier((value, *others))[0]


def local(
    tokens,
    lengths,
    deal,
    attn_gain,
    query_weight,
    key_matrix,
    value_matrix,
    out_weight,
    mlp_gain,
    gate_weight,
    up_weight,
    down_weight,
    cotangent,
):
    n_ctx = lax.axis_size("ctx")
    n_fsdp = lax.axis_size("fsdp")
    me = lax.axis_index("ctx")
    me_array = me.astype(jnp.int32).reshape(1)
    per_device, width = tokens.shape[1], tokens.shape[2]
    total = per_device * n_ctx
    block_rows = per_device // n_ctx
    heads = QUERY_HEADS // n_ctx
    sharing = n_ctx // KEY_VALUE_HEADS
    own_width = width // n_ctx
    ff = gate_weight.shape[1]
    slab = ff // (n_fsdp * n_ctx)
    own_ff = slab * n_fsdp
    rows_shard = query_weight.shape[0]

    kv_head = me // sharing
    split = heads * HEAD_SIZE
    kv_shard = jnp.concatenate(
        [
            own_columns(key_matrix, kv_head, HEAD_SIZE),
            own_columns(value_matrix, kv_head, HEAD_SIZE),
        ],
        axis=1,
    )

    def ff_columns(array):
        return jnp.concatenate([own_columns(array, f * n_ctx + me, slab) for f in range(n_fsdp)], axis=1)

    gain_shard = jnp.tile(jnp.concatenate([attn_gain, mlp_gain]).astype(F32)[None], (8, 1))

    freq_index = np.arange(HEAD_SIZE // 2)
    turns = jnp.asarray(np.tile(ROPE_BASE ** (-2.0 * freq_index / HEAD_SIZE), (8, 4)), F32)

    deal_rows = deal[0]
    slot_ids = jnp.arange(n_ctx, dtype=jnp.int32)
    dealt_of_given = (deal_rows * n_ctx + slot_ids[:, None]).reshape(-1)
    matched = deal_rows[:, :, None] == slot_ids[None, None, :]
    source_slot = jnp.sum(jnp.where(matched, slot_ids[None, :, None], 0), axis=1)
    given_of_dealt = (slot_ids[:, None] * n_ctx + source_slot).T.reshape(-1)

    def reorder(array, table):
        blocks = array.reshape(n_ctx * n_ctx, block_rows, array.shape[1])
        return jnp.take(blocks, table, axis=0, mode="clip").reshape(array.shape)

    ff_weights = gate_weight, up_weight, down_weight
    if slab % LANES:
        ff_weights = (
            ff_columns(gate_weight),
            ff_columns(up_weight),
            lax.dynamic_slice_in_dim(down_weight, me * slab, slab, axis=0),
        )

    cotangent_all = lax.all_gather(cotangent[0], "ctx", axis=0, tiled=True)
    (
        x, normed, q_rot, k_rot, v_rows, lse, attended_all, hidden_all, normed2, a, b, both, w_attn, w_gate, w_up, w_down, gains_all, cos_table, sin_table,
    ) = forward(
        n_ctx,
        n_fsdp,
        heads,
        slab,
        lengths[0],
        tokens[0],
        query_weight,
        kv_shard,
        out_weight,
        *ff_weights,
        gain_shard,
        turns,
    )
    w_qkv, w_out = w_attn[:, : split + 2 * HEAD_SIZE], w_attn[:, split + 2 * HEAD_SIZE :]
    gains = gains_all.reshape(n_fsdp, 8, 2, rows_shard)[:, 0].transpose(1, 0, 2).reshape(2, 1, width)
    grad_result = reorder(cotangent_all, dealt_of_given)

    result_part = result_rows(me_array, reorder(both, given_of_dealt), w_down)
    activations = lax.psum_scatter(
        result_part, "ctx", scatter_dimension=0, tiled=True
    )[None]

    if kernel_fits(n_ctx, n_fsdp, total, width, own_ff):
        token_grad, gain_rows, down_part, gate_part, up_part, out_part, qkv_part = backward(
            n_ctx,
            n_fsdp,
            heads,
            lengths[0],
            grad_result,
            (x, normed, q_rot, k_rot, v_rows, lse, attended_all, hidden_all, normed2, a, b, both),
            (w_attn, w_gate, w_up, w_down, gains_all),
            cos_table,
            sin_table,
        )
        token_grad = token_grad[None]
        own_gains = gain_rows[1], gain_rows[0]
    else:
        mlp_grad = (RESIDUAL_SCALE * grad_result.astype(F32)).astype(BF16)

        def settle(left, right):
            return lax.psum_scatter(dot_tn(left, right).astype(BF16), "fsdp", scatter_dimension=0, tiled=True)

        down_part = settle(both[:, :own_ff], mlp_grad)
        ggrad, ugrad, hidden_part, mlp_gain_part = mlp_backward(
            n_ctx, mlp_grad, a, b, hidden_all, gains[1], w_gate, w_up, w_down
        )
        hidden_sum = lax.psum_scatter(hidden_part, "ctx", scatter_dimension=0, tiled=False)
        gate_part = settle(normed2, ggrad)
        up_part = settle(normed2, ugrad)
        hidden_grad, branch_grad, attended_part = branch_backward(
            hidden_sum, own_columns(grad_result, me, own_width), w_out, n_ctx
        )
        attended_grad = lax.psum_scatter(attended_part, "ctx", scatter_dimension=0, tiled=False)
        out_part = lax.psum_scatter(
            jnp.einsum("ctk,to->cko", attended_all, branch_grad, preferred_element_type=F32)
            .astype(BF16)
            .reshape(width, own_width),
            "fsdp",
            scatter_dimension=0,
            tiled=True,
        )
        dq, dkv = attention_backward(attended_grad, q_rot, k_rot, v_rows, lse, cos_table, sin_table, lengths[0])
        qkv_part = settle(normed, jnp.concatenate([dq, dkv], axis=1))
        token_part, attn_gain_part = token_backward(me_array, dq, dkv, w_qkv, x, gains[0], hidden_grad)
        token_grad = lax.psum_scatter(token_part, "ctx", scatter_dimension=0, tiled=True).astype(F32)[None]

        gain_parts = jnp.concatenate([attn_gain_part, mlp_gain_part], axis=0)
        step = 1
        while step < n_ctx:
            gain_parts = gain_parts + lax.ppermute(gain_parts, "ctx", [(c, c ^ step) for c in range(n_ctx)])
            step *= 2
        gain_rows = gain_parts.reshape(2, n_fsdp, rows_shard).transpose(1, 0, 2).reshape(n_fsdp, 2 * rows_shard)
        own_gains = lax.psum_scatter(gain_rows, "fsdp", scatter_dimension=0, tiled=True).reshape(2, rows_shard)
        down_part, gate_part, up_part, out_part, qkv_part = [
            lax.all_gather(p, "ctx", axis=0, tiled=False) for p in (down_part, gate_part, up_part, out_part, qkv_part)
        ]

    if slab % LANES == 0 and sharing == 1 and heads % 4 == 0:
        gate_grad, up_grad, down_grad, out_grad, query_grad, key_grad, value_grad = finish(
            slab, gate_part, up_part, down_part.reshape(n_ctx * slab, width), out_part, qkv_part
        )
    else:
        down_grad = down_part.reshape(n_ctx * slab, width).astype(F32)
        if slab % LANES == 0:
            gate_grad = spread_columns(gate_part, slab, n_fsdp)
            up_grad = spread_columns(up_part, slab, n_fsdp)
        else:

            def ff_whole(part):
                pieces = part.reshape(n_ctx, rows_shard, n_fsdp, slab)
                return pieces.transpose(1, 2, 0, 3).reshape(rows_shard, ff).astype(F32)

            gate_grad = ff_whole(gate_part)
            up_grad = ff_whole(up_part)
        out_grad = spread_columns(out_part, own_width, 1)
        qkv_all = qkv_part
        query_grad = spread_columns(qkv_all, split, 1)

        def shared_heads(pieces):
            pieces = pieces.astype(F32).reshape(KEY_VALUE_HEADS, sharing, rows_shard, HEAD_SIZE).sum(axis=1)
            return pieces.transpose(1, 0, 2).reshape(rows_shard, KEY_VALUE_HEADS * HEAD_SIZE)

        key_grad = shared_heads(qkv_all[:, :, split : split + HEAD_SIZE])
        value_grad = shared_heads(qkv_all[:, :, split + HEAD_SIZE :])

    return (
        activations,
        token_grad,
        own_gains[0],
        query_grad,
        key_grad,
        value_grad,
        out_grad,
        own_gains[1],
        gate_grad,
        up_grad,
        down_grad,
    )


def solution(mesh):
    rows = P("fsdp", None)
    block = P("fsdp", "ctx", None)
    gain = P("fsdp")
    return jax.shard_map(
        local,
        mesh=mesh,
        in_specs=(block, rows, P("fsdp", None, None), gain, rows, rows, rows, rows, gain, rows, rows, rows, block),
        out_specs=(block, block, gain, rows, rows, rows, rows, gain, rows, rows, rows),
        check_vma=False,
    )
```
